32 devices in a mesh: dp: 16 (over z, y, core), head: 2 (over x).
Axes of the slice: x: 2, y: 2, z: 4, core: 2. Of those that a mesh axis runs over, the one named last changes fastest.
Arguments:
- segment: bfloat16 [32, 512, 1024], P(('dp', 'head')), may hold values from -6 to 6
- memory: bfloat16 [32, 512, 1024], P('dp'), may hold values from -6 to 6
- compressed: bfloat16 [32, 512, 1024], P('dp'), may hold values from -6 to 6
- doc_lengths: int32 [32, 4], P('dp'), may hold values from 1 to 256, 512 in all within a row
- memory_valid: int32 [32], P('dp'), may hold values from 1 to 1024
- query_weight: bfloat16 [1024, 1024], P('dp', 'head'), may hold values from -0.1875 to 0.1875
- key_weight: bfloat16 [1024, 1024], P('dp', 'head'), may hold values from -0.1875 to 0.1875
- value_weight: bfloat16 [1024, 1024], P('dp', 'head'), may hold values from -0.1875 to 0.1875
- position_weight: bfloat16 [1024, 1024], P('dp', 'head'), may hold values from -0.1875 to 0.1875
- content_bias: bfloat16 [8, 128], P('head', 'dp'), may hold values from -3 to 3
- position_bias: bfloat16 [8, 128], P('head', 'dp'), may hold values from -3 to 3
- output_weight: bfloat16 [1024, 1024], P(('dp', 'head')), may hold values from -0.75 to 0.75
- up_weight: bfloat16 [1024, 4096], P(('dp', 'head')), may hold values from -0.1875 to 0.1875
- down_weight: bfloat16 [4096, 1024], P(('dp', 'head')), may hold values from -0.09375 to 0.09375
- compress_weight: bfloat16 [3072, 1024], P(('dp', 'head')), may hold values from -0.109375 to 0.109375
- norm_gain: bfloat16 [1024], P(('dp', 'head')), may hold values from 0.099609375 to 1.8984375
- norm_shift: bfloat16 [1024], P(('dp', 'head')), may hold values from -3 to 3
- post_gain: bfloat16 [1024], P(('dp', 'head')), may hold values from 0.099609375 to 1.8984375
- post_shift: bfloat16 [1024], P(('dp', 'head')), may hold values from -3 to 3
- cotangent: bfloat16 [32, 512, 1024], P(('dp', 'head')), may hold values from -6 to 6
- compress_cotangent: bfloat16 [32, 170, 1024], P(('dp', 'head')), may hold values from -6 to 6
Outputs:
- output: bfloat16 [32, 512, 1024], P(('dp', 'head'))
- new_compressed: bfloat16 [32, 170, 1024], P(('dp', 'head'))
- segment_gradient: bfloat16 [32, 512, 1024], P(('dp', 'head'))
- query_gradient: float32 [1024, 1024], P('dp', 'head')
- key_gradient: float32 [1024, 1024], P('dp', 'head')
- value_gradient: float32 [1024, 1024], P('dp', 'head')
- position_gradient: float32 [1024, 1024], P('dp', 'head')
- content_bias_gradient: float32 [8, 128], P('head', 'dp')
- position_bias_gradient: float32 [8, 128], P('head', 'dp')
- output_gradient: float32 [1024, 1024], P(('dp', 'head'))
- up_gradient: float32 [1024, 4096], P(('dp', 'head'))
- down_gradient: float32 [4096, 1024], P(('dp', 'head'))
- compress_gradient: float32 [3072, 1024], P(('dp', 'head'))
- norm_gain_gradient: float32 [1024], P(('dp', 'head'))
- norm_shift_gradient: float32 [1024], P(('dp', 'head'))
- post_gain_gradient: float32 [1024], P(('dp', 'head'))
- post_shift_gradient: float32 [1024], P(('dp', 'head'))
The draws below stay inside these ranges and needn't reach their ends.
Inputs may be any that keep to these rules, and one draw needn't show every extreme that they name: `doc_lengths`: each row gives the lengths, in order, of the 4 documents packed into a segment of 512 tokens; the first continues from the memory. `memory_valid`: the first document sees this many of the most recent rows of compressed then memory.
All inputs are finite; a program needn't handle non-finite values.
Results may differ from the reference program's by a relative error of at most 0.028.
Values may be sent and summed in bfloat16 or wider, within the bound.
A program may use at most 384 MiB of HBM per device.

```python
import math
import jax
import jax.numpy as jnp
import numpy as np
from jax import lax

D = 1024
H = 8
DH = 128
FF = 4096
SEG = 512
MEM = 512
CMEM = 512
NDOC = 4
SEQS = 32
CNEW = 170
CTX = 1536


def set_ends(drawn, rng, low, largest):
    longest = drawn.shape.index(max(drawn.shape))
    spots = []
    for shift in (0, 1):
        where = [jax.random.randint(jax.random.fold_in(rng, axis), (), 0, length) for axis, length in enumerate(drawn.shape)]
        where[longest] = (where[longest] + shift) % drawn.shape[longest]
        spots.append(tuple(where))
    return drawn.at[spots[0]].set(low).at[spots[1]].set(largest)


def block_levels(rng, extent, split, smallest, top_value):
    def one(dim, parts):
        draws = jax.random.uniform(jax.random.fold_in(jax.random.fold_in(rng, 6), dim), (parts,), jnp.float32, smallest / len(split), top_value / len(split))
        return jnp.repeat(jnp.exp(draws), extent[dim] // parts).reshape((-1,) + (1,) * (len(extent) - dim - 1))

    level = one(*split[0])
    for cut in split[1:]:
        level = level * one(*cut)
    return level


def profile(amount, total, reach, lean):
    weights = [(1 << 20) // math.isqrt(standing ** lean) + 1 for standing in range(2, amount + 1)]
    spare, given = total - reach - (amount - 1), [1] * (amount - 1)
    while spare > 0:
        candidates = [i for i in range(amount - 1) if given[i] < reach]
        whole, budget = sum([weights[i] for i in candidates]), spare
        for i in candidates:
            more = min(reach - given[i], max(1, budget * weights[i] // whole), spare)
            given[i] = given[i] + more
            spare = spare - more
    return np.array([reach] + given)


def ragged(key, count, total, limit, lean):
    if count == 2:
        one = jax.random.randint(key, (), max(1, total - limit), min(limit, total - 1) + 1)
        return jnp.stack([one, total - one])
    tallies = jnp.asarray(profile(count, total, limit, lean), jnp.int32)
    pairs = (count - 1) // 2
    source_of, sink = tallies[1:1 + 2 * pairs:2], tallies[2:2 + 2 * pairs:2]
    slack = jnp.minimum(source_of - 1, limit - sink)
    moved = jax.random.randint(jax.random.fold_in(key, 1), (pairs,), 0, 1 << 20) % (slack + 1)
    tallies = tallies.at[1:1 + 2 * pairs:2].set(source_of - moved).at[2:2 + 2 * pairs:2].set(sink + moved)
    return tallies[jax.random.permutation(jax.random.fold_in(key, 2), count)]


def normal_values(stream_key, dims, scale, bound, shards=(), kind=jnp.bfloat16):
    values = jax.random.normal(stream_key, dims, jnp.float32) * scale
    if len(shards) > 0:
        values = block_levels(stream_key, dims, shards, -0.22, 0.18) * values
    return jnp.clip(values, min=-bound, max=bound).astype(kind)


def setup_inputs(seed: int = 0) -> dict:
    key_list = jax.random.split(jax.random.key(seed), 22)
    segment = normal_values(key_list[0], (SEQS, SEG, D), 1.0, 6.0, ((0, 32),))
    memory = normal_values(key_list[1], (SEQS, MEM, D), 1.0, 6.0, ((0, 16),))
    compressed = normal_values(key_list[2], (SEQS, CMEM, D), 1.0, 6.0, ((0, 16),))
    doc_lengths = jax.vmap(lambda own: ragged(own, NDOC, SEG, SEG // 2, 2))(jax.random.split(key_list[3], SEQS)).reshape((SEQS, NDOC)).astype(jnp.int32)
    memory_valid = set_ends(jax.random.randint(key_list[4], (SEQS,), 1, CMEM + MEM + 1), jax.random.fold_in(key_list[4], 1), 1, CMEM + MEM).astype(jnp.int32)
    query_weight = normal_values(key_list[5], (D, D), D ** -0.5, 0.1875, ((0, 16), (1, 2)))
    key_weight = normal_values(key_list[6], (D, D), D ** -0.5, 0.1875, ((0, 16), (1, 2)))
    value_weight = normal_values(key_list[7], (D, D), D ** -0.5, 0.1875, ((0, 16), (1, 2)))
    position_weight = normal_values(key_list[8], (D, D), D ** -0.5, 0.1875, ((0, 16), (1, 2)))
    content_bias = normal_values(key_list[9], (H, DH), 0.5, 3.0, ((0, 2), (1, 16)))
    position_bias = normal_values(key_list[10], (H, DH), 0.5, 3.0, ((0, 2), (1, 16)))
    output_weight = normal_values(key_list[11], (D, D), (D // 16) ** -0.5, 0.75, ((0, 32),))
    up_weight = normal_values(key_list[12], (D, FF), D ** -0.5, 0.1875, ((0, 32),))
    down_weight = normal_values(key_list[13], (FF, D), FF ** -0.5, 0.09375, ((0, 32),))
    compress_weight = normal_values(key_list[14], (3 * D, D), (3 * D) ** -0.5, 0.109375, ((0, 32),))
    norm_gain = jnp.clip(1.0 + 0.18 * jax.random.normal(key_list[15], (D,), jnp.float32), 0.099609375, 1.8984375).astype(jnp.bfloat16)
    norm_shift = normal_values(key_list[16], (D,), 0.3, 3.0, ((0, 32),))
    post_gain = jnp.clip(1.0 + 0.18 * jax.random.normal(key_list[17], (D,), jnp.float32), 0.099609375, 1.8984375).astype(jnp.bfloat16)
    post_shift = normal_values(key_list[18], (D,), 0.3, 3.0, ((0, 32),))
    cotangent = normal_values(key_list[19], (SEQS, SEG, D), 1.0, 6.0, ((0, 32),))
    compress_cotangent = normal_values(key_list[20], (SEQS, CNEW, D), 1.0, 6.0, ((0, 32),))
    return dict(segment=segment, memory=memory, compressed=compressed, doc_lengths=doc_lengths, memory_valid=memory_valid, query_weight=query_weight, key_weight=key_weight, value_weight=value_weight, position_weight=position_weight, content_bias=content_bias, position_bias=position_bias, output_weight=output_weight, up_weight=up_weight, down_weight=down_weight, compress_weight=compress_weight, norm_gain=norm_gain, norm_shift=norm_shift, post_gain=post_gain, post_shift=post_shift, cotangent=cotangent, compress_cotangent=compress_cotangent)


@jax.custom_vjp
def low(v):
    return lax.optimization_barrier(v.astype(jnp.bfloat16)).astype(jnp.float32)

@jax.custom_vjp
def low_back(v):
    return v

def low_keep(v):
    return (low(v), None)

def low_pass(kept, grad):
    return (grad,)

def back_keep(v):
    return (v, None)

def back_low(kept, grad):
    return (low(grad),)
low.defvjp(low_keep, low_pass)
low_back.defvjp(back_keep, back_low)

def both_ways(values):
    return low(low_back(values))

def matmul_hi(left, right):
    return jnp.dot(left, right, precision=lax.Precision.HIGHEST)

def layer_norm(values, gain, shift):
    row_mean = lax.optimization_barrier(jnp.mean(values, axis=-1, keepdims=True))
    centred = values - row_mean
    row_variance = lax.optimization_barrier(jnp.mean(centred * centred, axis=-1, keepdims=True))
    return centred * lax.rsqrt(row_variance + 1e-05) * gain + shift

def position_table():
    distance = jnp.arange(CTX, dtype=jnp.float32)[:, None]
    frequency = jnp.exp(jnp.arange(D // 2, dtype=jnp.float32) * (-2.0 * math.log(10000.0) / D))
    phases = distance * frequency[None, :]
    return jnp.concatenate([jnp.sin(phases), jnp.cos(phases)], axis=1)

def visible(lengths, valid_len):
    doc_ends = jnp.cumsum(lengths).astype(jnp.int32)
    position = jnp.arange(SEG, dtype=jnp.int32)
    doc_index = lax.optimization_barrier(jnp.sum((position[:, None] >= doc_ends[None, :]).astype(jnp.int32), axis=1))
    same_doc = (doc_index[:, None] == doc_index[None, :]) & (position[None, :] <= position[:, None])
    slots = jnp.arange(CMEM + MEM, dtype=jnp.int32)
    mem_seen = (doc_index[:, None] == 0) & (slots[None, :] >= CMEM + MEM - valid_len)
    return jnp.concatenate([mem_seen, same_doc], axis=1)

def reference(segment, memory, compressed, doc_lengths, memory_valid, query_weight, key_weight, value_weight, position_weight, content_bias, position_bias, output_weight, up_weight, down_weight, compress_weight, norm_gain, norm_shift, post_gain, post_shift, cotangent, compress_cotangent):
    memory_f = memory.astype(jnp.float32)
    compressed_f = compressed.astype(jnp.float32)
    pos_table = low(position_table())
    past_rows = CMEM + MEM
    score_scale = 1.0 / math.sqrt(DH)
    distance = jnp.clip(past_rows + jnp.arange(SEG, dtype=jnp.int32)[:, None] - jnp.arange(CTX, dtype=jnp.int32)[None, :], 0, CTX - 1).astype(jnp.int32)
    distance = jnp.broadcast_to(distance[None], (H, SEG, CTX))

    def forward(segment_f, query_mat, key_mat, value_mat, place_mat, content_vec, place_vec, out_mat, up_mat, down_mat, comp_mat, gain_one, shift_one, gain_two, shift_two):

        def one(element):
            row_block, memory_rows, compressed_rows, lengths, valid_len = element
            place_keys = both_ways(matmul_hi(pos_table, place_mat))
            context_in = jnp.concatenate([compressed_rows, memory_rows, row_block], axis=0)
            normed = low(layer_norm(context_in, gain_one, shift_one))
            queries = low_back(matmul_hi(normed[past_rows:], query_mat))
            keys_proj = both_ways(matmul_hi(normed, key_mat))
            values_proj = both_ways(matmul_hi(normed, value_mat))
            query_content = both_ways(queries + content_vec.reshape(-1))
            query_place = both_ways(queries + place_vec.reshape(-1))
            content_heads = query_content.reshape(SEG, H, DH)
            position_head_rows = query_place.reshape(SEG, H, DH)
            key_heads = keys_proj.reshape(CTX, H, DH)
            value_heads = values_proj.reshape(CTX, H, DH)
            position_key_heads = place_keys.reshape(CTX, H, DH)
            content = jnp.einsum('ihd,jhd->hij', content_heads, key_heads, precision=lax.Precision.HIGHEST)
            relative_offset = jnp.einsum('fuw,buw->ufb', position_head_rows, position_key_heads, precision=lax.Precision.HIGHEST)
            shifted = jnp.take_along_axis(relative_offset, distance, axis=2)
            scores = low_back(content + shifted) * score_scale
            seen_mask = visible(lengths, valid_len)
            scores = jnp.where(seen_mask[None], scores, -1e+30)
            row_max = lax.optimization_barrier(jnp.max(scores, axis=2, keepdims=True))
            expo_vals = jnp.exp(scores - row_max)
            attn_low = low(expo_vals / lax.optimization_barrier(jnp.sum(expo_vals, axis=2, keepdims=True)))
            attended = jnp.einsum('hij,jhd->ihd', attn_low, value_heads, precision=lax.Precision.HIGHEST).reshape(SEG, D)
            attended = both_ways(attended)
            residual = row_block + low_back(matmul_hi(attended, out_mat))
            normed_two = low(layer_norm(residual, gain_two, shift_two))
            hidden_pre = low_back(matmul_hi(normed_two, up_mat))
            hidden_act = both_ways(jax.nn.gelu(hidden_pre))
            return residual + low_back(matmul_hi(hidden_act, down_mat))
        result = lax.map(jax.checkpoint(one), (segment_f, memory_f, compressed_f, doc_lengths, memory_valid))
        windows = memory_f[:, :3 * CNEW].reshape(SEQS, CNEW, 3 * D)
        made = jnp.einsum('sca,ab->scb', windows, comp_mat, precision=lax.Precision.HIGHEST)
        return (result, made)
    primals = [segment, query_weight, key_weight, value_weight, position_weight, content_bias, position_bias, output_weight, up_weight, down_weight, compress_weight, norm_gain, norm_shift, post_gain, post_shift]
    primals = [entry.astype(jnp.float32) for entry in primals]
    (result, made), pull_back = jax.vjp(forward, *primals)
    grads = pull_back((cotangent.astype(jnp.float32), compress_cotangent.astype(jnp.float32)))
    return (result.astype(jnp.bfloat16), made.astype(jnp.bfloat16), grads[0].astype(jnp.bfloat16), grads[1], grads[2], grads[3], grads[4], grads[5], grads[6], grads[7], grads[8], grads[9], grads[10], grads[11], grads[12], grads[13], grads[14])
```

```python
import functools
import math

import jax
import jax.numpy as jnp
import numpy as np
from jax import lax
from jax.experimental import pallas as pl
from jax.experimental.pallas import tpu as pltpu
from jax.sharding import PartitionSpec as P

F32 = jnp.float32
BF16 = jnp.bfloat16
MESH = pl.DeviceIdType.MESH
VMEM_LIMIT = 62 * 1024 * 1024
HALF = 256
LANES = 512
SMALL = 16


def dot(a, b):
    return lax.dot_general(a, b, (((1,), (0,)), ((), ())), preferred_element_type=F32)


def dot_nt(a, b):
    return lax.dot_general(a, b, (((1,), (1,)), ((), ())), preferred_element_type=F32)


def dot_tn(a, b):
    return lax.dot_general(a, b, (((0,), (0,)), ((), ())), preferred_element_type=F32)


def position_rows(context, width, used):
    distance = np.arange(context, dtype=np.float32)[:, None]
    frequency = np.exp(
        np.arange(width // 2, dtype=np.float32) * np.float32(-2.0 * math.log(10000.0) / width)
    )
    phases = distance * frequency[None, :].astype(np.float32)
    table = np.concatenate([np.sin(phases), np.cos(phases)], axis=1)
    return table[::-1][context - used :].astype(jnp.bfloat16)


def place(n):
    me = lax.axis_index("dp")
    core = lax.rem(me, 2)
    low = lax.rem(me // 2, 2)
    high = me // 4
    return core, low, high, n // 4


def meet(core, low, high, nhi, more=0):
    barrier = pltpu.get_barrier_semaphore()

    def tell(index):
        pl.semaphore_signal(barrier, inc=1, device_id={"dp": index}, device_id_type=MESH)

    for k in range(1, nhi):
        tell(lax.rem(high + k, nhi) * 4 + low * 2 + core)
    tell(high * 4 + (1 - low) * 2 + core)
    tell(high * 4 + low * 2 + (1 - core))
    pl.semaphore_wait(barrier, nhi + 1 + more)


def remote(src, dst, send, recv, index):
    return pltpu.make_async_remote_copy(
        src_ref=src,
        dst_ref=dst,
        send_sem=send,
        recv_sem=recv,
        device_id={"dp": index},
        device_id_type=MESH,
    )


class Gather:
    def __init__(self, n, pairs, sems):
        self.core, self.low, self.high, self.nhi = place(n)
        self.pairs = pairs
        (self.zs, self.zr, self.ys, self.yr, self.cs, self.cr, self.own) = sems

    def z_copies(self, c):
        shard, whole = self.pairs[c]
        return [
            remote(
                shard,
                whole.at[self.high, self.low, self.core],
                self.zs.at[c, k - 1],
                self.zr.at[c, k - 1],
                lax.rem(self.high + k, self.nhi) * 4 + self.low * 2 + self.core,
            )
            for k in range(1, self.nhi)
        ]

    def own_copy(self, c):
        shard, whole = self.pairs[c]
        return pltpu.make_async_copy(
            shard, whole.at[self.high, self.low, self.core], self.own.at[c]
        )

    def y_copy(self, c):
        _, whole = self.pairs[c]
        part = whole.at[:, self.low, self.core]
        return remote(
            part,
            part,
            self.ys.at[c],
            self.yr.at[c],
            self.high * 4 + (1 - self.low) * 2 + self.core,
        )

    def c_copy(self, c):
        _, whole = self.pairs[c]
        part = whole.at[:, :, self.core]
        return remote(
            part,
            part,
            self.cs.at[c],
            self.cr.at[c],
            self.high * 4 + self.low * 2 + (1 - self.core),
        )

    def start(self, c):
        for copy in self.z_copies(c):
            copy.start()
        self.own_copy(c).start()

    def pass_y(self, c):
        self.own_copy(c).wait()
        for copy in self.z_copies(c):
            copy.wait_recv()
        self.y_copy(c).start()

    def pass_core(self, c):
        self.y_copy(c).wait_recv()
        self.c_copy(c).start()

    def arrive(self, c):
        self.c_copy(c).wait_recv()

    def close(self, c):
        for copy in self.z_copies(c):
            copy.wait_send()
        self.y_copy(c).wait_send()
        self.c_copy(c).wait_send()

    @staticmethod
    def semaphores(count, nhi):
        dma = pltpu.SemaphoreType.DMA
        return [
            dma((count, nhi - 1)),
            dma((count, nhi - 1)),
            dma((count,)),
            dma((count,)),
            dma((count,)),
            dma((count,)),
            dma((count,)),
        ]


class Scatter:
    def __init__(self, n, items, mine, mine_sem, sems):
        self.core, self.low, self.high, self.nhi = place(n)
        self.items = items
        self.mine, self.mine_sem = mine, mine_sem
        (self.cs, self.cr, self.ys, self.yr, self.zs, self.zr) = sems

    def c_copy(self, c):
        return remote(
            self.items[c][0].at[:, :, 1 - self.core],
            self.items[c][2],
            self.cs.at[c],
            self.cr.at[c],
            self.high * 4 + self.low * 2 + (1 - self.core),
        )

    def mine_copy(self, c):
        slot = c % 2
        return pltpu.make_async_copy(
            self.items[c][0].at[:, :, self.core], self.mine.at[slot], self.mine_sem.at[slot]
        )

    def y_copy(self, c):
        return remote(
            self.items[c][2].at[:, 1 - self.low],
            self.items[c][3],
            self.ys.at[c],
            self.yr.at[c],
            self.high * 4 + (1 - self.low) * 2 + self.core,
        )

    def z_copies(self, c):
        return [
            remote(
                self.items[c][3].at[lax.rem(self.high + k, self.nhi)],
                self.items[c][4].at[k - 1],
                self.zs.at[c, k - 1],
                self.zr.at[c, k - 1],
                lax.rem(self.high + k, self.nhi) * 4 + self.low * 2 + self.core,
            )
            for k in range(1, self.nhi)
        ]

    def start(self, c):
        self.c_copy(c).start()
        if not self.items[c][1]:
            self.mine_copy(c).start()

    def add_core(self, c):
        here = self.items[c][1]
        if not here:
            self.mine_copy(c).wait()
        self.c_copy(c).wait_recv()
        land = self.items[c][2]

        def body(i, carry):
            for j in range(2):
                own = self.items[c][0][i, j, self.core] if here else self.mine[c % 2, i, j]
                land[i, j] = (land[i, j].astype(F32) + own.astype(F32)).astype(BF16)
            return carry

        lax.fori_loop(0, self.nhi, body, 0)
        self.y_copy(c).start()

    def add_y(self, c):
        self.y_copy(c).wait_recv()
        src, land = self.items[c][2], self.items[c][3]

        def body(i, carry):
            land[i] = (land[i].astype(F32) + src[i, self.low].astype(F32)).astype(BF16)
            return carry

        lax.fori_loop(0, self.nhi, body, 0)
        for copy in self.z_copies(c):
            copy.start()

    def add_z(self, c):
        for copy in self.z_copies(c):
            copy.wait_recv()
        land, last, done = self.items[c][3:]
        total = land[self.high].astype(F32)
        for k in range(self.nhi - 1):
            total = total + last[k].astype(F32)
        done(total)

    def tick(self, t):
        count = len(self.items)
        if 0 <= t - 1 < count:
            self.add_core(t - 1)
        if t < count:
            self.start(t)
        if 0 <= t - 2 < count:
            self.add_y(t - 2)
        if 0 <= t - 3 < count:
            self.add_z(t - 3)

    def close(self, c):
        self.c_copy(c).wait_send()
        self.y_copy(c).wait_send()
        for copy in self.z_copies(c):
            copy.wait_send()

    @staticmethod
    def scratch(count, nhi, rows):
        dma = pltpu.SemaphoreType.DMA
        return [
            pltpu.VMEM((count, nhi, 2, rows, LANES), BF16),
            pltpu.VMEM((count, nhi, rows, LANES), BF16),
            pltpu.VMEM((count, nhi - 1, rows, LANES), BF16),
            pltpu.VMEM((2, nhi, 2, rows, LANES), BF16),
            dma((2,)),
            dma((count,)),
            dma((count,)),
            dma((count,)),
            dma((count,)),
            dma((count, nhi - 1)),
            dma((count, nhi - 1)),
        ]


def norm_rows(values):
    mean = jnp.mean(values, axis=-1, keepdims=True)
    centred = values - mean
    variance = jnp.mean(centred * centred, axis=-1, keepdims=True)
    return centred * lax.rsqrt(variance + 1e-05)


def attend_rows(query_content, query_place, keys, place_keys, first_seen, last_seen, scale):
    width = keys.shape[0]
    content = dot_nt(query_content, keys)
    by_place = pltpu.roll(
        dot_nt(query_place, place_keys), width - (HALF - 1), 1, stride=1, stride_axis=0
    )
    column = lax.broadcasted_iota(jnp.int32, (HALF, width), 1)
    seen = (column >= first_seen) & (column <= last_seen)
    scores = jnp.where(seen, (content + by_place) * (scale * math.log2(math.e)), -1e30)
    top = jnp.max(scores, axis=1, keepdims=True)
    expo = jnp.exp2(scores - top)
    return expo * (1.0 / jnp.sum(expo, axis=1, keepdims=True))


def forward_kernel(
    n,
    past,
    seg_len,
    docs,
    compressed,
    memory,
    segment,
    cotangent,
    query_w,
    key_w,
    value_w,
    place_w,
    out_w,
    up_parts,
    down_w,
    comp_w,
    small,
    table,
    attended,
    seg_other,
    cot_other,
    params,
    kv_out,
    q_out,
    wide_out,
    near_out,
    place_out,
    xhat_out,
    query_whole,
    key_whole,
    value_whole,
    place_whole,
    out_whole,
    up_whole,
    down_whole,
    comp_whole,
    small_whole,
    out_shard,
    up_shard,
    comp_shard,
    small_shard,
    normed,
    past_rows,
    seg_rows,
    flat,
    small_rows,
    att,
    load_sem,
    flat_sem,
    own_sem,
    pair_send,
    pair_recv,
    att_own,
    att_send,
    att_recv,
    *sems,
):
    step = pl.program_id(0)
    x = lax.axis_index("head")
    core, low, high, nhi = place(n)
    tile = 256
    width = normed.shape[2]
    context = past + seg_len
    head = jnp.maximum(step - 2, 0) // 2
    half = comp_w.shape[1] // 2

    items = [(small_shard, small_whole)]
    items += [(query_w, query_whole), (key_w, key_whole), (value_w, value_whole), (place_w, place_whole)]
    items += [(out_shard, out_whole)]
    items += [(up_shard.at[f], up_whole.at[f]) for f in range(4)]
    mid = down_w.shape[0] // 2
    for part in range(2):
        at = pl.ds(part * mid, mid)
        items.append((down_w.at[at], down_whole.at[:, :, :, at]))
    items.append((comp_shard, comp_whole))
    gather = Gather(n, items, sems)
    count = len(items)
    needs = {0: 0, 5: 1, 6: 2, 7: 2, 8: 2, 9: 2, 12: 3}

    def pair(src, dst, k):
        return pltpu.make_async_remote_copy(
            src_ref=src,
            dst_ref=dst,
            send_sem=pair_send.at[k],
            recv_sem=pair_recv.at[k],
            device_id={"head": 1 - x},
            device_id_type=MESH,
        )

    mine_at = pl.ds(pl.multiple_of(x * half, half), half)
    other_at = pl.ds(pl.multiple_of((1 - x) * half, half), half)
    pairs = [
        pair(small, small_shard.at[x], 0),
        pair(out_w, out_shard.at[x], 1),
        pair(up_parts.at[1 - x], up_shard.at[:, x], 2),
        pair(comp_w.at[:, other_at], comp_shard.at[x], 3),
        pair(segment.at[0], seg_other, 4),
        pair(cotangent.at[0], cot_other, 5),
    ]
    owns = [
        pltpu.make_async_copy(small, small_shard.at[x], own_sem.at[0]),
        pltpu.make_async_copy(out_w, out_shard.at[x], own_sem.at[1]),
        pltpu.make_async_copy(up_parts.at[x], up_shard.at[:, x], own_sem.at[2]),
        pltpu.make_async_copy(comp_w.at[:, mine_at], comp_shard.at[x], own_sem.at[3]),
    ]
    loads = []
    for i in range(2):
        s = lax.rem(x + i, 2)
        loads.append(pltpu.make_async_copy(compressed.at[s], past_rows.at[i, 0], load_sem.at[i, 0]))
        loads.append(pltpu.make_async_copy(memory.at[s], past_rows.at[i, 1], load_sem.at[i, 1]))
    loads.append(pltpu.make_async_copy(segment.at[0], seg_rows.at[0], load_sem.at[0, 2]))
    load_other = pltpu.make_async_copy(seg_other, seg_rows.at[1], load_sem.at[1, 2])

    joined = set()

    def join(k):
        if k not in joined:
            joined.add(k)
            owns[k].wait()
            pairs[k].wait_recv()

    def tick(t):
        lead = t + 4
        if lead < count:
            if lead in needs:
                join(needs[lead])
            gather.start(lead)
        if t < count:
            gather.pass_y(t)
        if 0 <= t - 1 < count:
            gather.pass_core(t - 1)
        if 0 <= t - 2 < count:
            gather.arrive(t - 2)

    def flat_copies(h, slot):
        at = pl.ds(h * 128, 128)
        return [
            pltpu.make_async_copy(
                whole.at[:, :, :, :, at],
                flat.at[slot, :, :, :, :, pl.ds(j * 128, 128)],
                flat_sem.at[slot, j],
            )
            for j, whole in enumerate((query_whole, key_whole, value_whole, place_whole))
        ]

    def norm_into(i, values, at):
        eye = (
            lax.broadcasted_iota(jnp.int32, (tile, tile), 0)
            == lax.broadcasted_iota(jnp.int32, (tile, tile), 1)
        ).astype(BF16)
        gain = jnp.concatenate([params[0:1, :], params[1:2, :]], axis=1)
        shift = jnp.concatenate([params[2:3, :], params[3:4, :]], axis=1)
        xhat = norm_rows(values.astype(F32))
        normed[i, pl.ds(at, tile)] = (xhat * gain + shift).astype(BF16)
        xhat = xhat.astype(BF16)
        for b in range(width // tile):
            xhat_out[i, b * tile : (b + 1) * tile, pl.ds(at, tile)] = dot_nt(
                eye, xhat[:, b * tile : (b + 1) * tile]
            ).astype(BF16)

    def norm_past(i):
        per = past // 2 // tile

        def one(k, carry):
            at = pl.multiple_of(k * tile, tile)
            inner = pl.multiple_of(lax.rem(k, per) * tile, tile)
            norm_into(i, past_rows[i, k // per, pl.ds(inner, tile)], at)
            return carry

        lax.fori_loop(0, past // tile, one, 0)

    def norm_segment(i):
        def one(k, carry):
            at = pl.multiple_of(k * tile, tile)
            norm_into(i, seg_rows[i, pl.ds(at, tile)], past + at)
            return carry

        lax.fori_loop(0, seg_len // tile, one, 0)

    @pl.when(step == 0)
    def _():
        barrier = pltpu.get_barrier_semaphore()
        pl.semaphore_signal(
            barrier, inc=1, device_id={"head": 1 - x}, device_id_type=MESH
        )
        meet(core, low, high, nhi, 1)
        for k in (0, 1, 2):
            pairs[k].start()
            owns[k].start()
        for copy in loads:
            copy.start()
        for c in range(1, 4):
            gather.start(c)
        join(0)
        gather.start(0)
        for k in (4, 3, 5):
            pairs[k].start()
        owns[3].start()
        tick(0)
        tick(1)
        tick(2)
        summed = pltpu.make_async_copy(small_whole, small_rows, load_sem.at[0, 3])
        summed.start()
        summed.wait()
        both = jnp.sum(small_rows[...].reshape(n, 2, SMALL, LANES).astype(F32), axis=0)
        row = lax.broadcasted_iota(jnp.int32, (SMALL, LANES), 0)
        by_head = jnp.where(x == 0, both[0], both[1])
        params[...] = jnp.where(row < 8, both[0] + both[1], by_head)
        for copy in (loads[0], loads[1], loads[4]):
            copy.wait()
        norm_past(0)
        tick(3)
        norm_segment(0)
        tick(4)

    @pl.when(step == 1)
    def _():
        for copy in loads[2:4]:
            copy.wait()
        norm_past(1)
        tick(5)
        tick(6)
        for copy in flat_copies(0, 0):
            copy.start()

    for k in range(2, 10):

        @pl.when(step == k)
        def _(k=k):
            tick(k + 5)
            h, slot = (k - 2) // 2, ((k - 2) // 2) % 2
            if k % 2 == 0:
                for copy in flat_copies(h, slot):
                    copy.wait()
                if h < 3:
                    for copy in flat_copies(h + 1, 1 - slot):
                        copy.start()
            if k == 3:
                pairs[4].wait_recv()
                load_other.start()
                load_other.wait()
                norm_segment(1)

    def att_pair(h, i):
        at = pl.ds(pl.multiple_of(x * LANES + h * 128, 128), 128)
        return pltpu.make_async_remote_copy(
            src_ref=att.at[h, i],
            dst_ref=attended.at[1 - i, :, at],
            send_sem=att_send.at[h, i],
            recv_sem=att_recv.at[h, i],
            device_id={"head": 1 - x},
            device_id_type=MESH,
        )

    def att_local(h, i):
        at = pl.ds(pl.multiple_of(x * LANES + h * 128, 128), 128)
        return pltpu.make_async_copy(att.at[h, i], attended.at[i, :, at], att_own.at[h, i])

    @pl.when(step >= 2)
    def _():
        i = lax.rem(step, 2)
        s = lax.rem(x + i, 2)
        slot = lax.rem(head, 2)

        def weights(a, b):
            return flat[slot, :, :, :, :, a:b].reshape(width, b - a)

        @pl.when(i == 0)
        def _():
            mat = weights(384, 512)
            for k in range(table.shape[0] // tile):
                place_out[0, k * tile : (k + 1) * tile] = dot(
                    table[k * tile : (k + 1) * tile], mat
                ).astype(BF16)

        mat = weights(128, 384)
        for k in range(context // tile):
            kv_out[0, 0, k * tile : (k + 1) * tile] = dot(
                normed[i, pl.ds(k * tile, tile)], mat
            ).astype(BF16)
        mat = weights(0, 128)
        bias_at = pl.ds(pl.multiple_of(head * 128, 128), 128)
        for k in range(seg_len // tile):
            queries = dot(normed[i, pl.ds(past + k * tile, tile)], mat)
            at = slice(k * tile, (k + 1) * tile)
            q_out[0, 0, at, 0:128] = (queries + params[8:9, bias_at]).astype(BF16)
            q_out[0, 0, at, 128:256] = (queries + params[9:10, bias_at]).astype(BF16)

        scale = 1.0 / math.sqrt(128)
        for part, out, key_start, key_count, place_start in (
            (0, wide_out, 0, past + HALF, 0),
            (1, near_out, past, seg_len, past - HALF),
        ):
            token = lax.broadcasted_iota(jnp.int32, (HALF, 1), 0) + part * HALF
            first = jnp.where(token >= docs[s, 0], past + docs[s, 0], past - docs[s, 3])
            first = jnp.where(token >= docs[s, 1], past + docs[s, 1], first)
            first = jnp.where(token >= docs[s, 2], past + docs[s, 2], first)
            at = slice(part * HALF, (part + 1) * HALF)
            weights_low = attend_rows(
                q_out[0, 0, at, 0:128],
                q_out[0, 0, at, 128:256],
                kv_out[0, 0, key_start : key_start + key_count, 0:128],
                place_out[0, place_start : place_start + key_count],
                first - key_start,
                token + (past - key_start),
                scale,
            ).astype(BF16)
            out[0, 0] = weights_low
            att[head, i, at] = dot(
                weights_low, kv_out[0, 0, key_start : key_start + key_count, 128:256]
            ).astype(BF16)
        att_pair(head, i).start()
        att_local(head, i).start()

    @pl.when(step == pl.num_programs(0) - 1)
    def _():
        for t in range(15, count + 2):
            tick(t)
        for h in range(4):
            for i in range(2):
                att_local(h, i).wait()
                att_pair(h, i).wait()
        for copy in pairs:
            copy.wait_send()
        pairs[5].wait_recv()
        for c in range(count):
            gather.close(c)


def attention_forward(
    n, docs, compressed, memory, segment, cotangent, mats, out_w, up_parts, down_w, comp_w, small, table
):
    _, seg_len, width = segment.shape
    past = compressed.shape[1] + memory.shape[1]
    context = past + seg_len
    nhi = n // 4
    lead = (nhi, 2, 2)
    half_rows = out_w.shape[0]
    comp_rows = comp_w.shape[0]
    any_spec = pl.BlockSpec(memory_space=pl.ANY)
    single = pl.Buffered(1)
    bf = lambda *shape: jax.ShapeDtypeStruct(shape, BF16)
    head = lambda t: jnp.maximum(t - 2, 0) // 2
    which = lambda t: lax.rem(jnp.maximum(t, 2), 2)
    by_both = lambda t: (head(t), which(t), 0, 0)
    dma = pltpu.SemaphoreType.DMA
    count = 13
    return pl.pallas_call(
        functools.partial(forward_kernel, n, past, seg_len),
        grid=(10,),
        out_shape=(
            bf(2, seg_len, width),
            bf(seg_len, width),
            bf(seg_len, width),
            jax.ShapeDtypeStruct((SMALL, LANES), F32),
            bf(4, 2, context, 256),
            bf(4, 2, seg_len, 256),
            bf(4, 2, HALF, past + HALF),
            bf(4, 2, HALF, seg_len),
            bf(4, past + HALF, 128),
            bf(2, width, context),
            *[bf(*lead, *w.shape) for w in mats],
            bf(*lead, 2, half_rows, width),
            bf(4, *lead, 2, half_rows, LANES),
            bf(*lead, *down_w.shape),
            bf(*lead, 2, comp_rows, LANES),
            bf(*lead, 2, SMALL, LANES),
            bf(2, half_rows, width),
            bf(4, 2, half_rows, LANES),
            bf(2, comp_rows, LANES),
            bf(2, SMALL, LANES),
        ),
        in_specs=[pl.BlockSpec(memory_space=pltpu.SMEM)]
        + [any_spec] * 13
        + [pl.BlockSpec(table.shape, lambda t: (0, 0), pipeline_mode=single)],
        out_specs=(
            any_spec,
            any_spec,
            any_spec,
            pl.BlockSpec((SMALL, LANES), lambda t: (0, 0)),
            pl.BlockSpec((1, 1, context, 256), by_both),
            pl.BlockSpec((1, 1, seg_len, 256), by_both),
            pl.BlockSpec((1, 1, HALF, past + HALF), by_both),
            pl.BlockSpec((1, 1, HALF, seg_len), by_both),
            pl.BlockSpec((1, past + HALF, 128), lambda t: (head(t), 0, 0)),
            pl.BlockSpec((2, width, context), lambda t: (0, 0, 0), pipeline_mode=single),
            *[any_spec] * 13,
        ),
        scratch_shapes=[
            pltpu.VMEM((2, context, width), BF16),
            pltpu.VMEM((2, 2, past // 2, width), BF16),
            pltpu.VMEM((2, seg_len, width), BF16),
            pltpu.VMEM((2,) + lead + (mats[0].shape[0], LANES), BF16),
            pltpu.VMEM(lead + (2, SMALL, LANES), BF16),
            pltpu.VMEM((4, 2, seg_len, 128), BF16),
            dma((2, 4)),
            dma((2, 4)),
            dma((4,)),
            dma((6,)),
            dma((6,)),
            dma((4, 2)),
            dma((4, 2)),
            dma((4, 2)),
        ]
        + Gather.semaphores(count, nhi),
        compiler_params=pltpu.CompilerParams(
            vmem_limit_bytes=VMEM_LIMIT,
            dimension_semantics=("arbitrary",),
            collective_id=0,
            has_side_effects=True,
        ),
        name="attention_forward",
    )(docs, compressed, memory, segment, cotangent, *mats, out_w, up_parts, down_w, comp_w, small, table)


def gelu_parts(v):
    c = math.sqrt(2.0 / math.pi)
    square = v * v
    t = jnp.tanh(c * (v + 0.044715 * square * v))
    half = 0.5 * (1.0 + t)
    slope = half + 0.5 * v * (1.0 - t * t) * (c * (1.0 + 3 * 0.044715 * square))
    return v * half, slope


def feed_kernel(
    att,
    segment,
    cot,
    out_w,
    up,
    down,
    gain,
    shift,
    residual_out,
    branch_out,
    terms_out,
    up_out,
    down_out,
    residual,
    low,
    low_t,
    act,
    pre,
    branch,
    terms,
):
    f = pl.program_id(0)
    tile = 256
    total, width = residual.shape

    @pl.when(f == 0)
    def _():
        eye = (
            lax.broadcasted_iota(jnp.int32, (tile, tile), 0)
            == lax.broadcasted_iota(jnp.int32, (tile, tile), 1)
        ).astype(BF16)

        def project(i, carry):
            at = pl.ds(pl.multiple_of(i * tile, tile), tile)
            residual[at, :] = segment[at, :].astype(F32) + dot(att[at, :], out_w[...])
            return carry

        lax.fori_loop(0, total // tile, project, 0)
        for i in range(total // tile):
            at = slice(i * tile, (i + 1) * tile)
            value = (norm_rows(residual[at, :]) * gain[...] + shift[...]).astype(BF16)
            low[at, :] = value
            for b in range(width // tile):
                low_t[b * tile : (b + 1) * tile, at] = dot_nt(
                    eye, value[:, b * tile : (b + 1) * tile]
                ).astype(BF16)
        residual_out[...] = residual[0 : total // 2, :]
        branch[...] = jnp.zeros_like(branch)
        terms[...] = jnp.zeros_like(terms)

    def rows_body(i, carry):
        at = pl.ds(pl.multiple_of(i * tile, tile), tile)
        value, slope = gelu_parts(dot(low[at, :], up[0]))
        value = value.astype(BF16)
        act[at, :] = value
        back = dot_nt(cot[at, :], down[...]).astype(BF16).astype(F32)
        back = (back * slope).astype(BF16)
        pre[at, :] = back
        branch[at, :] += dot(value, down[...])
        terms[at, :] += dot_nt(back, up[0])
        return carry

    lax.fori_loop(0, total // tile, rows_body, 0)

    for i in range(width // tile):
        at = slice(i * tile, (i + 1) * tile)
        up_out[0, at, :] = dot(low_t[at, :], pre[...]).astype(BF16)
    for i in range(LANES // tile):
        at = slice(i * tile, (i + 1) * tile)
        down_out[at, :] = dot_tn(act[:, at], cot[...]).astype(BF16)

    @pl.when(f == pl.num_programs(0) - 1)
    def _():
        branch_out[...] = branch[...].astype(BF16)
        terms_out[...] = terms[...].astype(BF16)


def feed_forward(att, segment, cot, out_w, up, down, gain, shift):
    total, width = segment.shape
    const2 = lambda f: (0, 0)
    single = pl.Buffered(1)
    full = lambda: pl.BlockSpec((total, width), const2, pipeline_mode=single)
    return pl.pallas_call(
        feed_kernel,
        grid=(4,),
        out_shape=(
            jax.ShapeDtypeStruct((total // 2, width), F32),
            jax.ShapeDtypeStruct((total, width), BF16),
            jax.ShapeDtypeStruct((total, width), BF16),
            jax.ShapeDtypeStruct((4, width, LANES), BF16),
            jax.ShapeDtypeStruct((4 * LANES, width), BF16),
        ),
        in_specs=[
            full(),
            full(),
            full(),
            pl.BlockSpec((width, width), const2, pipeline_mode=single),
            pl.BlockSpec((1, width, LANES), lambda f: (f, 0, 0)),
            pl.BlockSpec((LANES, width), lambda f: (f, 0)),
            pl.BlockSpec((1, width), const2),
            pl.BlockSpec((1, width), const2),
        ],
        out_specs=(
            pl.BlockSpec((total // 2, width), const2, pipeline_mode=single),
            full(),
            full(),
            pl.BlockSpec((1, width, LANES), lambda f: (f, 0, 0)),
            pl.BlockSpec((LANES, width), lambda f: (f, 0)),
        ),
        scratch_shapes=[
            pltpu.VMEM((total, width), F32),
            pltpu.VMEM((total, width), BF16),
            pltpu.VMEM((width, total), BF16),
            pltpu.VMEM((total, LANES), BF16),
            pltpu.VMEM((total, LANES), BF16),
            pltpu.VMEM((total, width), F32),
            pltpu.VMEM((total, width), F32),
        ],
        compiler_params=pltpu.CompilerParams(
            vmem_limit_bytes=VMEM_LIMIT, dimension_semantics=("arbitrary",)
        ),
        name="feed_forward",
    )(att, segment, cot, out_w, up, down, gain, shift)


def norm_back(xhat, rstd, grad):
    a = jnp.mean(grad, axis=-1, keepdims=True)
    b = jnp.mean(grad * xhat, axis=-1, keepdims=True)
    return rstd * (grad - a - xhat * b)


def backward_kernel(
    n,
    past,
    seg_len,
    dout,
    kv,
    q,
    wide,
    near,
    place_keys,
    xhat_t,
    query_w,
    key_w,
    value_w,
    table_t,
    gain_row,
    gain_col,
    shift_col,
    segment,
    residual_grad,
    small_in,
    comp,
    up,
    down,
    out,
    segment_out,
    query_out,
    key_out,
    value_out,
    place_out,
    out_out,
    up_out,
    down_out,
    comp_out,
    small_out,
    flat,
    raw,
    sums,
    place_sum,
    input_grad,
    dkv,
    gain_sum,
    shift_sum,
    head_grads,
    context_land,
    context_send,
    up_send,
    up_land,
    comp_stage,
    comp_send,
    comp_land,
    out_keep,
    out_send,
    out_land,
    small_mine,
    small_c,
    small_y,
    small_z,
    small_x,
    pair_send,
    pair_recv,
    small_send,
    small_recv,
    land_c,
    land_y,
    land_z,
    mine,
    mine_sem,
    *sems,
):
    step = pl.program_id(0)
    x = lax.axis_index("head")
    core, low, high, nhi = place(n)
    head = lax.rem(step, 4)
    tile = 256
    context = past + seg_len
    width = flat.shape[0]
    rows = width // n
    half_rows = rows // 2
    comp_rows = comp_send.shape[0]
    scale = 1.0 / math.sqrt(128)
    flip = (
        lax.broadcasted_iota(jnp.int32, (HALF, HALF), 0)
        + lax.broadcasted_iota(jnp.int32, (HALF, HALF), 1)
        == HALF - 1
    ).astype(BF16)

    def pair(src, dst, k):
        return pltpu.make_async_remote_copy(
            src_ref=src,
            dst_ref=dst,
            send_sem=pair_send.at[k],
            recv_sem=pair_recv.at[k],
            device_id={"head": 1 - x},
            device_id_type=MESH,
        )

    context_pair = pair(context_send, context_land, 0)
    comp_pair = pair(comp_send, comp_land, 1)
    up_pairs = [pair(up_send.at[f], up_land.at[f], 2 + f) for f in range(4)]
    out_pairs = [pair(out_send.at[b], out_land.at[b], 6 + b) for b in range(2)]

    def comp_done(m):
        def done(total):
            comp_stage[m * rows : (m + 1) * rows, :] = total
            if m == 2:
                upper, lower = comp_stage[0:comp_rows, :], comp_stage[comp_rows:, :]
                to = pl.ds(pl.multiple_of(x * LANES, LANES), LANES)
                comp_out[:, to] = jnp.where(x == 0, upper, lower)
                comp_send[...] = jnp.where(x == 0, lower, upper).astype(BF16)
                comp_pair.start()

        return done

    def up_done(f):
        def done(total):
            upper, lower = total[0:half_rows], total[half_rows:]
            up_out[x, f] = jnp.where(x == 0, upper, lower)
            up_send[f] = jnp.where(x == 0, lower, upper).astype(BF16)
            up_pairs[f].start()

        return done

    def down_done(a, b):
        def done(total):
            down_out[a * rows : (a + 1) * rows, b * LANES : (b + 1) * LANES] = total

        return done

    def out_done(b):
        def done(total):
            upper, lower = total[0:half_rows], total[half_rows:]
            out_keep[b] = jnp.where(x == 0, upper, lower)
            out_send[b] = jnp.where(x == 0, lower, upper).astype(BF16)
            out_pairs[b].start()

        return done

    def head_done(h):
        def done(total):
            for j, ref in enumerate((query_out, key_out, value_out, place_out)):
                ref[:, h * 128 : (h + 1) * 128] = total[:, j * 128 : (j + 1) * 128]

        return done

    parts = [
        (comp.at[:, :, :, pl.ds(m * rows, rows)], False, comp_done(m)) for m in range(3)
    ]
    parts += [(up.at[f], False, up_done(f)) for f in range(4)]
    for a in range(2):
        for b in range(2):
            at, to = pl.ds(a * rows, rows), pl.ds(b * LANES, LANES)
            parts.append((down.at[:, :, :, at, to], False, down_done(a, b)))
    parts += [
        (out.at[:, :, :, :, pl.ds(b * LANES, LANES)], False, out_done(b)) for b in range(2)
    ]
    parts += [(head_grads.at[h], True, head_done(h)) for h in range(4)]
    scatter = Scatter(
        n,
        [
            (part, here, land_c.at[c], land_y.at[c], land_z.at[c], done)
            for c, (part, here, done) in enumerate(parts)
        ],
        mine,
        mine_sem,
        sems,
    )
    count = len(parts)

    @pl.when(step == 0)
    def _():
        barrier = pltpu.get_barrier_semaphore()
        pl.semaphore_signal(barrier, inc=1, device_id={"head": 1 - x}, device_id_type=MESH)
        meet(core, low, high, nhi, 1)
        raw[...] = jnp.zeros_like(raw)
        sums[...] = jnp.zeros_like(sums)
        place_sum[...] = jnp.zeros_like(place_sum)
        gain_sum[...] = jnp.zeros_like(gain_sum)
        shift_sum[...] = jnp.zeros_like(shift_sum)
        small_mine[...] = small_in[...]

    @pl.when(head == 0)
    def _():
        input_grad[...] = jnp.zeros_like(input_grad)

    for k in range(8):
        pl.when(step == k)(functools.partial(scatter.tick, 2 * k))

    for j, mat in enumerate((query_w, key_w, value_w)):
        flat[:, j * 128 : (j + 1) * 128] = mat[...]

    query_grads = []
    key_rows = []
    value_rows = []
    place_rows = []
    bias_at = pl.ds(pl.multiple_of(head * 128, 128), 128)
    for part, weights_ref, key_start, key_count, place_start in (
        (0, wide, 0, past + HALF, 0),
        (1, near, past, seg_len, past - HALF),
    ):
        at = slice(part * HALF, (part + 1) * HALF)
        keys_at = slice(key_start, key_start + key_count)
        attn = weights_ref[0, 0]
        grad = dout[0, at]
        value_rows.append(dot_tn(grad, attn))
        weights_grad = dot_nt(grad, kv[0, 0, keys_at, 128:256])
        attn = attn.astype(F32)
        row = jnp.sum(weights_grad * attn, axis=1, keepdims=True)
        scores_grad = (attn * (weights_grad - row) * scale).astype(BF16)
        content_grad = dot(scores_grad, kv[0, 0, keys_at, 0:128]).astype(BF16)
        key_rows.append(dot_tn(q[0, 0, at, 0:128], scores_grad))
        by_place = pltpu.roll(dot(flip, scores_grad), 0, 1, stride=1, stride_axis=0).astype(BF16)
        place_grad = dot(by_place, place_keys[0, place_start : place_start + key_count])
        place_grad = dot(flip, place_grad.astype(BF16)).astype(BF16)
        flipped_q = dot(flip, q[0, 0, at, 128:256]).astype(BF16)
        place_rows.append(dot_tn(flipped_q, by_place))
        content_f = content_grad.astype(F32)
        place_f = place_grad.astype(F32)
        small_mine[8:9, bias_at] += jnp.sum(content_f, axis=0, keepdims=True)
        small_mine[9:10, bias_at] += jnp.sum(place_f, axis=0, keepdims=True)
        query_grads.append((content_f + place_f).astype(BF16))

    for j, (wide_rows, near_rows) in enumerate((key_rows, value_rows)):
        at = slice(j * 128, (j + 1) * 128)
        dkv[at, 0:past] = wide_rows[:, 0:past].astype(BF16)
        dkv[at, past : past + HALF] = (wide_rows[:, past:] + near_rows[:, 0:HALF]).astype(BF16)
        dkv[at, past + HALF :] = near_rows[:, HALF:].astype(BF16)
    split = past - HALF
    for at, rows_grad in (
        (slice(0, split), place_rows[0][:, 0:split]),
        (slice(split, None), place_rows[0][:, split:] + place_rows[1]),
    ):
        place_sum[head, :, at] = (
            place_sum[head, :, at].astype(F32) + rows_grad.astype(BF16).astype(F32)
        ).astype(BF16)
    dq = jnp.concatenate(query_grads, axis=0)
    stacked = jnp.concatenate([dq, dkv[:, past:].astype(F32).T.astype(BF16)], axis=1)

    for k in range(8):
        pl.when(step == k)(functools.partial(scatter.tick, 2 * k + 1))

    ones = jnp.ones((8, context), BF16)
    sums[head, :, 0:128] += dot(ones[:, 0:seg_len], dq)
    sums[head, :, 128:384] += dot_nt(ones, dkv[...])
    for k in range(width // tile):
        at = slice(k * tile, (k + 1) * tile)
        raw[head, at, 0:128] += dot(xhat_t[0, at, past:], dq)
        raw[head, at, 128:384] += dot_nt(xhat_t[0, at, :], dkv[...])
        input_grad[:, at] += dot_nt(stacked, flat[at, 0:384])

    @pl.when(step >= 4)
    def _():
        place_low = place_sum[head]
        block = tile // (4 * rows)
        total = sums[head, 0:1, :]
        for k in range(width // tile):
            at = slice(k * tile, (k + 1) * tile)
            to = slice(k * block, (k + 1) * block)
            got = raw[head, at, :]
            mats = flat[at, 0:384].astype(F32)
            for acc, term in ((gain_sum, mats * got), (shift_sum, mats * total)):
                acc[at, :] += term[:, 0:128] + term[:, 128:256] + term[:, 256:384]
            grad = (gain_col[at, :] * got + shift_col[at, :] * total).astype(BF16)
            head_grads[head, to, :, :, :, 0:384] = grad.reshape(block, 2, 2, rows, 384)
            grad = dot_nt(table_t[at, :], place_low).astype(BF16)
            head_grads[head, to, :, :, :, 384:512] = grad.reshape(block, 2, 2, rows, 128)

    def own_rows(k):
        at = slice(k * tile, (k + 1) * tile)
        values = segment[0, at].astype(F32)
        mean = jnp.mean(values, axis=-1, keepdims=True)
        centred = values - mean
        rstd = lax.rsqrt(jnp.mean(centred * centred, axis=-1, keepdims=True) + 1e-05)
        return norm_back(centred * rstd, rstd, input_grad[at, :] * gain_row[...])

    @pl.when(step == 3)
    def _():
        for k in range(seg_len // tile):
            context_send[k * tile : (k + 1) * tile, :] = own_rows(k).astype(BF16)
        context_pair.start()

    @pl.when(step == 7)
    def _():
        scatter.tick(16)
        one = jnp.ones((8, 128), F32)
        for acc, row in ((gain_sum, 0), (shift_sum, 2)):
            line = lax.dot_general(
                one,
                acc[...],
                (((1,), (1,)), ((), ())),
                precision=lax.Precision.HIGHEST,
                preferred_element_type=F32,
            )
            small_mine[row : row + 1, :] = line[0:1, 0:LANES]
            small_mine[row + 1 : row + 2, :] = line[0:1, LANES:]

        def to_dp(src, dst, k, index):
            return remote(src, dst, small_send.at[k], small_recv.at[k], index)

        copies = [to_dp(small_mine, small_c.at[1], 0, high * 4 + low * 2 + (1 - core))]
        copies[0].start()
        context_pair.wait_recv()
        for k in range(seg_len // tile):
            at = slice(k * tile, (k + 1) * tile)
            segment_out[0, at] = (
                residual_grad[at, :] + own_rows(k) + context_land[at, :].astype(F32)
            ).astype(BF16)
        copies[0].wait_recv()
        small_c[0] = small_mine[...] + small_c[1]
        copies.append(to_dp(small_c.at[0], small_y.at[1], 1, high * 4 + (1 - low) * 2 + core))
        copies[1].start()
        scatter.tick(17)
        copies[1].wait_recv()
        small_y[0] = small_c[0] + small_y[1]
        along = []
        for k in range(1, nhi):
            to = lax.rem(high + k, nhi) * 4 + low * 2 + core
            along.append(to_dp(small_y.at[0], small_z.at[k], 2 + k, to))
        for copy in along:
            copy.start()
        scatter.tick(18)
        for copy in along:
            copy.wait_recv()
        line = small_y[0]
        for k in range(1, nhi):
            line = line + small_z[k]
        small_z[0] = line
        last = pltpu.make_async_remote_copy(
            src_ref=small_z.at[0],
            dst_ref=small_x,
            send_sem=small_send.at[2],
            recv_sem=small_recv.at[2],
            device_id={"head": 1 - x},
            device_id_type=MESH,
        )
        last.start()
        scatter.tick(19)
        comp_pair.wait_recv()
        to = pl.ds(pl.multiple_of((1 - x) * LANES, LANES), LANES)
        comp_out[:, to] = comp_land[...].astype(F32)
        for f in range(4):
            up_pairs[f].wait_recv()
            up_out[1 - x, f] = up_land[f].astype(F32)
        for b in range(2):
            out_pairs[b].wait_recv()
            out_out[:, b * LANES : (b + 1) * LANES] = out_keep[b] + out_land[b].astype(F32)
        last.wait_recv()
        line = lax.broadcasted_iota(jnp.int32, (SMALL, LANES), 0)
        small_out[...] = small_z[0] + jnp.where(line < 8, small_x[...], 0.0)
        for copy in [context_pair, comp_pair, *up_pairs, *out_pairs, *copies, *along, last]:
            copy.wait_send()
        for c in range(count):
            scatter.close(c)


def attention_backward(
    n, dout, kv, q, wide, near, place_keys, xhat_t, mats, table_t, gain, shift, segment,
    residual_grad, small_in, comp, up, down, out,
):
    _, seg_len, width = segment.shape
    context = kv.shape[2]
    past = context - seg_len
    rows = width // n
    nhi = n // 4
    half_rows = rows // 2
    comp_rows = comp.shape[3] // 2
    const2 = lambda t: (0, 0)
    seq = lambda t: 1 - t // 4
    head = lambda t: lax.rem(t, 4)
    by_both = lambda t: (head(t), seq(t), 0, 0)
    single = pl.Buffered(1)
    any_spec = pl.BlockSpec(memory_space=pl.ANY)
    vmem = pl.BlockSpec(memory_space=pltpu.VMEM)
    dma = pltpu.SemaphoreType.DMA
    f32 = lambda *shape: jax.ShapeDtypeStruct(shape, F32)
    lead = (nhi, 2, 2)
    full = lambda shape: pl.BlockSpec(shape, lambda t: (0,) * len(shape), pipeline_mode=single)
    outs = (
        jax.ShapeDtypeStruct((1, seg_len, width), BF16),
        f32(rows, LANES),
        f32(rows, LANES),
        f32(rows, LANES),
        f32(rows, LANES),
        f32(half_rows, width),
        f32(2, 4, half_rows, LANES),
        f32(2 * rows, width),
        f32(comp_rows, width),
        f32(SMALL, LANES),
    )
    return pl.pallas_call(
        functools.partial(backward_kernel, n, past, seg_len),
        grid=(8,),
        out_shape=outs,
        in_specs=[
            pl.BlockSpec((1, seg_len, 128), lambda t: (seq(t), 0, head(t))),
            pl.BlockSpec((1, 1, context, 256), by_both),
            pl.BlockSpec((1, 1, seg_len, 256), by_both),
            pl.BlockSpec((1, 1, HALF, past + HALF), by_both),
            pl.BlockSpec((1, 1, HALF, seg_len), by_both),
            pl.BlockSpec((1, past + HALF, 128), lambda t: (head(t), 0, 0)),
            pl.BlockSpec((1, width, context), lambda t: (seq(t), 0, 0), pipeline_mode=single),
            *[pl.BlockSpec((width, 128), lambda t: (0, head(t)))] * 3,
            full(table_t.shape),
            full((1, width)),
            full((width, 1)),
            full((width, 1)),
            pl.BlockSpec((1, seg_len, width), lambda t: (seq(t), 0, 0), pipeline_mode=single),
            full((seg_len, width)),
            full((SMALL, LANES)),
            any_spec,
            any_spec,
            any_spec,
            any_spec,
        ],
        out_specs=tuple(full(o.shape) for o in outs),
        scratch_shapes=[
            pltpu.VMEM((width, 384), BF16),
            pltpu.VMEM((4, width, 384), F32),
            pltpu.VMEM((4, 8, 384), F32),
            pltpu.VMEM((4, 128, past + HALF), BF16),
            pltpu.VMEM((seg_len, width), F32),
            pltpu.VMEM((256, context), BF16),
            pltpu.VMEM((width, 128), F32),
            pltpu.VMEM((width, 128), F32),
            pltpu.VMEM((4,) + lead + (rows, LANES), BF16),
            pltpu.VMEM((seg_len, width), BF16),
            pltpu.VMEM((seg_len, width), BF16),
            pltpu.VMEM((4, half_rows, LANES), BF16),
            pltpu.VMEM((4, half_rows, LANES), BF16),
            pltpu.VMEM((3 * rows, LANES), F32),
            pltpu.VMEM((comp_rows, LANES), BF16),
            pltpu.VMEM((comp_rows, LANES), BF16),
            pltpu.VMEM((2, half_rows, LANES), F32),
            pltpu.VMEM((2, half_rows, LANES), BF16),
            pltpu.VMEM((2, half_rows, LANES), BF16),
            pltpu.VMEM((SMALL, LANES), F32),
            pltpu.VMEM((2, SMALL, LANES), F32),
            pltpu.VMEM((2, SMALL, LANES), F32),
            pltpu.VMEM((nhi, SMALL, LANES), F32),
            pltpu.VMEM((SMALL, LANES), F32),
            dma((8,)),
            dma((8,)),
            dma((2 + nhi,)),
            dma((2 + nhi,)),
        ]
        + Scatter.scratch(17, nhi, rows),
        compiler_params=pltpu.CompilerParams(
            vmem_limit_bytes=VMEM_LIMIT,
            dimension_semantics=("arbitrary",),
            collective_id=1,
            has_side_effects=True,
        ),
        name="attention_backward",
    )(
        dout, kv, q, wide, near, place_keys, xhat_t, *mats, table_t,
        gain.reshape(1, width), gain.reshape(width, 1), shift.reshape(width, 1), segment,
        residual_grad, small_in, comp, up, down, out,
    )


def body(
    n,
    segment,
    memory,
    compressed,
    doc_lengths,
    memory_valid,
    query_weight,
    key_weight,
    value_weight,
    position_weight,
    content_bias,
    position_bias,
    output_weight,
    up_weight,
    down_weight,
    compress_weight,
    norm_gain,
    norm_shift,
    post_gain,
    post_shift,
    cotangent,
    compress_cotangent,
):
    x = lax.axis_index("head")
    dp = lax.axis_index("dp")
    first = x == 0
    nhi = n // 4
    width = segment.shape[2]
    seg_len = segment.shape[1]
    past = memory.shape[1] + compressed.shape[1]
    context = past + seg_len
    rows = query_weight.shape[0]
    half_rows = output_weight.shape[0]
    new_count = compress_cotangent.shape[1]
    comp_rows = compress_weight.shape[0]

    def swap(a):
        return lax.ppermute(a, "head", [(0, 1), (1, 0)])

    def pick(a, index):
        return jnp.where(index == 0, a[0], a[1])

    def in_order(own, got, axis):
        return jnp.where(
            first,
            jnp.concatenate([own, got], axis=axis),
            jnp.concatenate([got, own], axis=axis),
        )

    ffr = down_weight.shape[0]
    up_parts = (
        up_weight.reshape(half_rows, 4, n // 4, 2, ffr)
        .transpose(3, 1, 0, 2, 4)
        .reshape(2, 4, half_rows, LANES)
    )
    lane = jnp.arange(width, dtype=jnp.int32)

    def spread(vector, index, size):
        return jnp.where(lane // size == index, jnp.tile(vector, width // size), 0).reshape(2, LANES)

    bias_lane = jnp.arange(LANES, dtype=jnp.int32) % 128
    per = content_bias.shape[1]

    def spread_bias(bias):
        tiled = jnp.tile(bias, (1, n)).reshape(1, LANES)
        return jnp.where((bias_lane // per == dp), tiled, 0)

    small = jnp.concatenate(
        [
            spread(v, dp * 2 + x, half_rows)
            for v in (norm_gain, norm_shift, post_gain, post_shift)
        ]
        + [
            spread_bias(content_bias),
            spread_bias(position_bias),
            jnp.zeros((SMALL - 10, LANES), BF16),
        ]
    ).astype(BF16)

    end_one = doc_lengths[:, 0]
    end_two = end_one + doc_lengths[:, 1]
    docs = jnp.stack([end_one, end_two, end_two + doc_lengths[:, 2], memory_valid], axis=1)
    table = position_rows(context, width, past + HALF)

    (
        att, seg_other, cot_other, params, kv, q, wide, near, place_keys, xhat_t,
        query_whole, key_whole, value_whole, _, out_whole, up_whole, down_whole, comp_whole, *_,
    ) = attention_forward(
        n, docs, compressed, memory, segment, cotangent,
        (query_weight, key_weight, value_weight, position_weight),
        output_weight, up_parts, down_weight, compress_weight, small, jnp.asarray(table),
    )
    mats = [w.reshape(width, LANES) for w in (query_whole, key_whole, value_whole)]
    out_mat = out_whole.reshape(width, width)
    comp_mat = comp_whole.reshape(3 * width, LANES)
    gain_one, shift_one, gain_two, shift_two = (
        params[2 * i : 2 * i + 2].reshape(1, width) for i in range(4)
    )
    segment_both = jnp.concatenate([segment, seg_other[None]])
    cot_both = jnp.concatenate([cotangent[0], cot_other])

    att = att.reshape(-1, width)
    residual, branch, terms, up_grads, down_grads = feed_forward(
        att, segment_both.reshape(-1, width), cot_both, out_mat,
        up_whole.reshape(4, width, LANES), down_whole.reshape(4 * LANES, width), gain_two, shift_two,
    )

    input_terms = terms[:seg_len].astype(F32) + swap(terms[seg_len:]).astype(F32)
    result = (
        residual + branch[:seg_len].astype(F32) + swap(branch[seg_len:]).astype(F32)
    ).astype(BF16)
    mean = jnp.mean(residual, axis=-1, keepdims=True)
    centred = residual - mean
    rstd = lax.rsqrt(jnp.mean(centred * centred, axis=-1, keepdims=True) + 1e-05)
    xhat_two = centred * rstd
    gain_two_grad = jnp.sum(input_terms * xhat_two, axis=0)
    shift_two_grad = jnp.sum(input_terms, axis=0)
    residual_grad = cotangent[0].astype(F32) + norm_back(xhat_two, rstd, input_terms * gain_two)
    branch_grad = residual_grad.astype(BF16)
    out_grads = dot_tn(att[:seg_len], branch_grad).astype(BF16)
    mixed_grad = dot_nt(branch_grad, out_mat).astype(BF16)
    mixed_halves = (mixed_grad[:, :LANES], mixed_grad[:, LANES:])
    dout = jnp.stack([pick(mixed_halves, x), swap(pick(mixed_halves, 1 - x))])

    comp_cot = in_order(compress_cotangent, swap(compress_cotangent), 0)
    windows = memory[:, : 3 * new_count].reshape(-1, 3 * width)
    made_half = dot(windows, comp_mat).astype(BF16).reshape(2, new_count, LANES)
    made = in_order(pick(made_half, x), swap(pick(made_half, 1 - x)), 1)
    comp_cot_half = pick(comp_cot.reshape(-1, 2, LANES).transpose(1, 0, 2), x)
    comp_grads = dot_tn(windows, comp_cot_half).astype(BF16)

    small_in = jnp.concatenate(
        [
            jnp.zeros((4, LANES), F32),
            gain_two_grad.reshape(2, LANES),
            shift_two_grad.reshape(2, LANES),
            jnp.zeros((SMALL - 8, LANES), F32),
        ]
    )
    lead = (nhi, 2, 2)
    (
        segment_grad, query_done, key_done, value_done, place_done,
        out_done, up_done, down_done, comp_done, small_done,
    ) = attention_backward(
        n, dout, kv, q, wide, near, place_keys, xhat_t, mats, jnp.asarray(table.T.copy()),
        gain_one, shift_one, segment_both, residual_grad, small_in,
        comp_grads.reshape(lead + (3 * rows, LANES)),
        up_grads.reshape((4,) + lead + (rows, LANES)),
        down_grads.reshape(lead + (2 * rows, 2 * LANES)),
        out_grads.reshape(lead + (rows, 2 * LANES)),
    )

    up_final = (
        up_done.reshape(2, 4, half_rows, n // 4, ffr)
        .transpose(2, 1, 3, 0, 4)
        .reshape(half_rows, -1)
    )
    vectors = lax.dynamic_slice_in_dim(
        small_done[0:8].reshape(4, width), (dp * 2 + x) * half_rows, half_rows, 1
    )
    biases = lax.dynamic_slice_in_dim(small_done[8:10].reshape(2, 4, 128), dp * per, per, 2)
    return (
        result[None],
        made[None],
        segment_grad,
        query_done,
        key_done,
        value_done,
        place_done,
        biases[0],
        biases[1],
        out_done,
        up_final,
        down_done,
        comp_done,
        vectors[0],
        vectors[1],
        vectors[2],
        vectors[3],
    )


def solution(mesh):
    split = P(("dp", "head"))
    wide = P(("dp", "head"), None)
    deep = P(("dp", "head"), None, None)
    return jax.shard_map(
        functools.partial(body, mesh.shape["dp"]),
        mesh=mesh,
        in_specs=(
            deep,
            P("dp", None, None),
            P("dp", None, None),
            P("dp", None),
            P("dp"),
            P("dp", "head"),
            P("dp", "head"),
            P("dp", "head"),
            P("dp", "head"),
            P("head", "dp"),
            P("head", "dp"),
            wide,
            wide,
            wide,
            wide,
            split,
            split,
            split,
            split,
            deep,
            deep,
        ),
        out_specs=(
            deep,
            deep,
            deep,
            P("dp", "head"),
            P("dp", "head"),
            P("dp", "head"),
            P("dp", "head"),
            P("head", "dp"),
            P("head", "dp"),
            wide,
            wide,
            wide,
            wide,
            split,
            split,
            split,
            split,
        ),
        check_vma=False,
    )
```

```python
import functools
import math

import jax
import jax.numpy as jnp
import numpy as np
from jax import lax
from jax.experimental import pallas as pl
from jax.experimental.pallas import tpu as pltpu
from jax.sharding import PartitionSpec as P

F32 = jnp.float32
BF16 = jnp.bfloat16
MESH = pl.DeviceIdType.MESH
VMEM_LIMIT = 62 * 1024 * 1024
HALF = 256
LANES = 512
SMALL = 16


def dot(a, b):
    return lax.dot_general(a, b, (((1,), (0,)), ((), ())), preferred_element_type=F32)


def dot_nt(a, b):
    return lax.dot_general(a, b, (((1,), (1,)), ((), ())), preferred_element_type=F32)


def dot_tn(a, b):
    return lax.dot_general(a, b, (((0,), (0,)), ((), ())), preferred_element_type=F32)


def position_rows(context, width, used):
    distance = np.arange(context, dtype=np.float32)[:, None]
    frequency = np.exp(
        np.arange(width // 2, dtype=np.float32) * np.float32(-2.0 * math.log(10000.0) / width)
    )
    phases = distance * frequency[None, :].astype(np.float32)
    table = np.concatenate([np.sin(phases), np.cos(phases)], axis=1)
    return table[::-1][context - used :].astype(jnp.bfloat16)


def place(n):
    me = lax.axis_index("dp")
    core = lax.rem(me, 2)
    low = lax.rem(me // 2, 2)
    high = me // 4
    return core, low, high, n // 4


def meet(core, low, high, nhi, more=0):
    barrier = pltpu.get_barrier_semaphore()

    def tell(index):
        pl.semaphore_signal(barrier, inc=1, device_id={"dp": index}, device_id_type=MESH)

    for k in range(1, nhi):
        tell(lax.rem(high + k, nhi) * 4 + low * 2 + core)
    tell(high * 4 + (1 - low) * 2 + core)
    tell(high * 4 + low * 2 + (1 - core))
    pl.semaphore_wait(barrier, nhi + 1 + more)


def remote(src, dst, send, recv, index):
    return pltpu.make_async_remote_copy(
        src_ref=src,
        dst_ref=dst,
        send_sem=send,
        recv_sem=recv,
        device_id={"dp": index},
        device_id_type=MESH,
    )


class Gather:
    def __init__(self, n, pairs, sems):
        self.core, self.low, self.high, self.nhi = place(n)
        self.pairs = pairs
        (self.zs, self.zr, self.ys, self.yr, self.cs, self.cr, self.own) = sems

    def z_copies(self, c):
        shard, whole = self.pairs[c]
        return [
            remote(
                shard,
                whole.at[self.high, self.low, self.core],
                self.zs.at[c, k - 1],
                self.zr.at[c, k - 1],
                lax.rem(self.high + k, self.nhi) * 4 + self.low * 2 + self.core,
            )
            for k in range(1, self.nhi)
        ]

    def own_copy(self, c):
        shard, whole = self.pairs[c]
        return pltpu.make_async_copy(
            shard, whole.at[self.high, self.low, self.core], self.own.at[c]
        )

    def y_copy(self, c):
        _, whole = self.pairs[c]
        part = whole.at[:, self.low, self.core]
        return remote(
            part,
            part,
            self.ys.at[c],
            self.yr.at[c],
            self.high * 4 + (1 - self.low) * 2 + self.core,
        )

    def c_copy(self, c):
        _, whole = self.pairs[c]
        part = whole.at[:, :, self.core]
        return remote(
            part,
            part,
            self.cs.at[c],
            self.cr.at[c],
            self.high * 4 + self.low * 2 + (1 - self.core),
        )

    def start(self, c):
        for copy in self.z_copies(c):
            copy.start()
        self.own_copy(c).start()

    def pass_y(self, c):
        self.own_copy(c).wait()
        for copy in self.z_copies(c):
            copy.wait_recv()
        self.y_copy(c).start()

    def pass_core(self, c):
        self.y_copy(c).wait_recv()
        self.c_copy(c).start()

    def arrive(self, c):
        self.c_copy(c).wait_recv()

    def close(self, c):
        for copy in self.z_copies(c):
            copy.wait_send()
        self.y_copy(c).wait_send()
        self.c_copy(c).wait_send()

    @staticmethod
    def semaphores(count, nhi):
        dma = pltpu.SemaphoreType.DMA
        return [
            dma((count, nhi - 1)),
            dma((count, nhi - 1)),
            dma((count,)),
            dma((count,)),
            dma((count,)),
            dma((count,)),
            dma((count,)),
        ]


class Scatter:
    def __init__(self, n, items, mine, mine_sem, sems):
        self.core, self.low, self.high, self.nhi = place(n)
        self.items = items
        self.mine, self.mine_sem = mine, mine_sem
        (self.cs, self.cr, self.ys, self.yr, self.zs, self.zr) = sems

    def c_copy(self, c):
        return remote(
            self.items[c][0].at[:, :, 1 - self.core],
            self.items[c][2],
            self.cs.at[c],
            self.cr.at[c],
            self.high * 4 + self.low * 2 + (1 - self.core),
        )

    def mine_copy(self, c):
        slot = c % 2
        return pltpu.make_async_copy(
            self.items[c][0].at[:, :, self.core], self.mine.at[slot], self.mine_sem.at[slot]
        )

    def y_copy(self, c):
        return remote(
            self.items[c][2].at[:, 1 - self.low],
            self.items[c][3],
            self.ys.at[c],
            self.yr.at[c],
            self.high * 4 + (1 - self.low) * 2 + self.core,
        )

    def z_copies(self, c):
        return [
            remote(
                self.items[c][3].at[lax.rem(self.high + k, self.nhi)],
                self.items[c][4].at[k - 1],
                self.zs.at[c, k - 1],
                self.zr.at[c, k - 1],
                lax.rem(self.high + k, self.nhi) * 4 + self.low * 2 + self.core,
            )
            for k in range(1, self.nhi)
        ]

    def start(self, c):
        self.c_copy(c).start()
        if not self.items[c][1]:
            self.mine_copy(c).start()

    def add_core(self, c):
        here = self.items[c][1]
        if not here:
            self.mine_copy(c).wait()
        self.c_copy(c).wait_recv()
        land = self.items[c][2]

        def body(i, carry):
            for j in range(2):
                own = self.items[c][0][i, j, self.core] if here else self.mine[c % 2, i, j]
                land[i, j] = (land[i, j].astype(F32) + own.astype(F32)).astype(BF16)
            return carry

        lax.fori_loop(0, self.nhi, body, 0)
        self.y_copy(c).start()

    def add_y(self, c):
        self.y_copy(c).wait_recv()
        src, land = self.items[c][2], self.items[c][3]

        def body(i, carry):
            land[i] = (land[i].astype(F32) + src[i, self.low].astype(F32)).astype(BF16)
            return carry

        lax.fori_loop(0, self.nhi, body, 0)
        for copy in self.z_copies(c):
            copy.start()

    def add_z(self, c):
        for copy in self.z_copies(c):
            copy.wait_recv()
        land, last, done = self.items[c][3:]
        total = land[self.high].astype(F32)
        for k in range(self.nhi - 1):
            total = total + last[k].astype(F32)
        done(total)

    def tick(self, t):
        count = len(self.items)
        if 0 <= t - 1 < count:
            self.add_core(t - 1)
        if t < count:
            self.start(t)
        if 0 <= t - 2 < count:
            self.add_y(t - 2)
        if 0 <= t - 3 < count:
            self.add_z(t - 3)

    def close(self, c):
        self.c_copy(c).wait_send()
        self.y_copy(c).wait_send()
        for copy in self.z_copies(c):
            copy.wait_send()

    @staticmethod
    def scratch(count, nhi, rows):
        dma = pltpu.SemaphoreType.DMA
        return [
            pltpu.VMEM((count, nhi, 2, rows, LANES), BF16),
            pltpu.VMEM((count, nhi, rows, LANES), BF16),
            pltpu.VMEM((count, nhi - 1, rows, LANES), BF16),
            pltpu.VMEM((2, nhi, 2, rows, LANES), BF16),
            dma((2,)),
            dma((count,)),
            dma((count,)),
            dma((count,)),
            dma((count,)),
            dma((count, nhi - 1)),
            dma((count, nhi - 1)),
        ]


def norm_rows(values):
    mean = jnp.mean(values, axis=-1, keepdims=True)
    centred = values - mean
    variance = jnp.mean(centred * centred, axis=-1, keepdims=True)
    return centred * lax.rsqrt(variance + 1e-05)


def attend_rows(query_content, query_place, keys, place_keys, first_seen, last_seen, scale):
    width = keys.shape[0]
    content = dot_nt(query_content, keys)
    by_place = pltpu.roll(
        dot_nt(query_place, place_keys), width - (HALF - 1), 1, stride=1, stride_axis=0
    )
    column = lax.broadcasted_iota(jnp.int32, (HALF, width), 1)
    seen = (column >= first_seen) & (column <= last_seen)
    scores = jnp.where(seen, (content + by_place) * (scale * math.log2(math.e)), -1e30)
    top = jnp.max(scores, axis=1, keepdims=True)
    expo = jnp.exp2(scores - top)
    return expo * (1.0 / jnp.sum(expo, axis=1, keepdims=True))


def forward_kernel(
    n,
    past,
    seg_len,
    docs,
    compressed,
    memory,
    segment,
    cotangent,
    query_w,
    key_w,
    value_w,
    place_w,
    out_w,
    up_parts,
    down_w,
    comp_w,
    small,
    table,
    attended,
    seg_other,
    cot_other,
    params,
    kv_out,
    q_out,
    wide_out,
    near_out,
    place_out,
    xhat_out,
    query_whole,
    key_whole,
    value_whole,
    place_whole,
    out_whole,
    up_whole,
    down_whole,
    comp_whole,
    small_whole,
    out_shard,
    up_shard,
    comp_shard,
    small_shard,
    normed,
    past_rows,
    seg_rows,
    flat,
    small_rows,
    att,
    load_sem,
    flat_sem,
    own_sem,
    pair_send,
    pair_recv,
    att_own,
    att_send,
    att_recv,
    *sems,
):
    step = pl.program_id(0)
    x = lax.axis_index("head")
    core, low, high, nhi = place(n)
    tile = 256
    width = normed.shape[2]
    context = past + seg_len
    head = jnp.maximum(step - 2, 0) // 2
    half = comp_w.shape[1] // 2

    items = [(small_shard, small_whole)]
    items += [(query_w, query_whole), (key_w, key_whole), (value_w, value_whole), (place_w, place_whole)]
    items += [(out_shard, out_whole)]
    items += [(up_shard.at[f], up_whole.at[f]) for f in range(4)]
    mid = down_w.shape[0] // 2
    for part in range(2):
        at = pl.ds(part * mid, mid)
        items.append((down_w.at[at], down_whole.at[:, :, :, at]))
    items.append((comp_shard, comp_whole))
    gather = Gather(n, items, sems)
    count = len(items)
    needs = {0: 0, 5: 1, 6: 2, 7: 2, 8: 2, 9: 2, 12: 3}

    def pair(src, dst, k):
        return pltpu.make_async_remote_copy(
            src_ref=src,
            dst_ref=dst,
            send_sem=pair_send.at[k],
            recv_sem=pair_recv.at[k],
            device_id={"head": 1 - x},
            device_id_type=MESH,
        )

    mine_at = pl.ds(pl.multiple_of(x * half, half), half)
    other_at = pl.ds(pl.multiple_of((1 - x) * half, half), half)
    pairs = [
        pair(small, small_shard.at[x], 0),
        pair(out_w, out_shard.at[x], 1),
        pair(up_parts.at[1 - x], up_shard.at[:, x], 2),
        pair(comp_w.at[:, other_at], comp_shard.at[x], 3),
        pair(segment.at[0], seg_other, 4),
        pair(cotangent.at[0], cot_other, 5),
    ]
    owns = [
        pltpu.make_async_copy(small, small_shard.at[x], own_sem.at[0]),
        pltpu.make_async_copy(out_w, out_shard.at[x], own_sem.at[1]),
        pltpu.make_async_copy(up_parts.at[x], up_shard.at[:, x], own_sem.at[2]),
        pltpu.make_async_copy(comp_w.at[:, mine_at], comp_shard.at[x], own_sem.at[3]),
    ]
    loads = []
    for i in range(2):
        s = lax.rem(x + i, 2)
        loads.append(pltpu.make_async_copy(compressed.at[s], past_rows.at[i, 0], load_sem.at[i, 0]))
        loads.append(pltpu.make_async_copy(memory.at[s], past_rows.at[i, 1], load_sem.at[i, 1]))
    loads.append(pltpu.make_async_copy(segment.at[0], seg_rows.at[0], load_sem.at[0, 2]))
    load_other = pltpu.make_async_copy(seg_other, seg_rows.at[1], load_sem.at[1, 2])

    joined = set()

    def join(k):
        if k not in joined:
            joined.add(k)
            owns[k].wait()
            pairs[k].wait_recv()

    def tick(t):
        lead = t + 4
        if lead < count:
            if lead in needs:
                join(needs[lead])
            gather.start(lead)
        if t < count:
            gather.pass_y(t)
        if 0 <= t - 1 < count:
            gather.pass_core(t - 1)
        if 0 <= t - 2 < count:
            gather.arrive(t - 2)

    def flat_copies(h, slot):
        at = pl.ds(h * 128, 128)
        return [
            pltpu.make_async_copy(
                whole.at[:, :, :, :, at],
                flat.at[slot, :, :, :, :, pl.ds(j * 128, 128)],
                flat_sem.at[slot, j],
            )
            for j, whole in enumerate((query_whole, key_whole, value_whole, place_whole))
        ]

    def norm_into(i, values, at):
        eye = (
            lax.broadcasted_iota(jnp.int32, (tile, tile), 0)
            == lax.broadcasted_iota(jnp.int32, (tile, tile), 1)
        ).astype(BF16)
        gain = jnp.concatenate([params[0:1, :], params[1:2, :]], axis=1)
        shift = jnp.concatenate([params[2:3, :], params[3:4, :]], axis=1)
        xhat = norm_rows(values.astype(F32))
        normed[i, pl.ds(at, tile)] = (xhat * gain + shift).astype(BF16)
        xhat = xhat.astype(BF16)
        for b in range(width // tile):
            xhat_out[i, b * tile : (b + 1) * tile, pl.ds(at, tile)] = dot_nt(
                eye, xhat[:, b * tile : (b + 1) * tile]
            ).astype(BF16)

    def norm_past(i):
        per = past // 2 // tile

        def one(k, carry):
            at = pl.multiple_of(k * tile, tile)
            inner = pl.multiple_of(lax.rem(k, per) * tile, tile)
            norm_into(i, past_rows[i, k // per, pl.ds(inner, tile)], at)
            return carry

        lax.fori_loop(0, past // tile, one, 0)

    def norm_segment(i):
        def one(k, carry):
            at = pl.multiple_of(k * tile, tile)
            norm_into(i, seg_rows[i, pl.ds(at, tile)], past + at)
            return carry

        lax.fori_loop(0, seg_len // tile, one, 0)

    @pl.when(step == 0)
    def _():
        barrier = pltpu.get_barrier_semaphore()
        pl.semaphore_signal(
            barrier, inc=1, device_id={"head": 1 - x}, device_id_type=MESH
        )
        meet(core, low, high, nhi, 1)
        for k in (0, 1, 2):
            pairs[k].start()
            owns[k].start()
        for copy in loads:
            copy.start()
        for c in range(1, 4):
            gather.start(c)
        join(0)
        gather.start(0)
        for k in (4, 3, 5):
            pairs[k].start()
        owns[3].start()
        tick(0)
        tick(1)
        tick(2)
        summed = pltpu.make_async_copy(small_whole, small_rows, load_sem.at[0, 3])
        summed.start()
        summed.wait()
        both = jnp.sum(small_rows[...].reshape(n, 2, SMALL, LANES).astype(F32), axis=0)
        row = lax.broadcasted_iota(jnp.int32, (SMALL, LANES), 0)
        by_head = jnp.where(x == 0, both[0], both[1])
        params[...] = jnp.where(row < 8, both[0] + both[1], by_head)
        for copy in (loads[0], loads[1], loads[4]):
            copy.wait()
        norm_past(0)
        tick(3)
        norm_segment(0)
        tick(4)

    @pl.when(step == 1)
    def _():
        for copy in loads[2:4]:
            copy.wait()
        norm_past(1)
        tick(5)
        tick(6)
        for copy in flat_copies(0, 0):
            copy.start()

    for k in range(2, 10):

        @pl.when(step == k)
        def _(k=k):
            tick(k + 5)
            h, slot = (k - 2) // 2, ((k - 2) // 2) % 2
            if k % 2 == 0:
                for copy in flat_copies(h, slot):
                    copy.wait()
                if h < 3:
                    for copy in flat_copies(h + 1, 1 - slot):
                        copy.start()
            if k == 3:
                pairs[4].wait_recv()
                load_other.start()
                load_other.wait()
                norm_segment(1)

    def att_pair(h, i):
        at = pl.ds(pl.multiple_of(x * LANES + h * 128, 128), 128)
        return pltpu.make_async_remote_copy(
            src_ref=att.at[h, i],
            dst_ref=attended.at[1 - i, :, at],
            send_sem=att_send.at[h, i],
            recv_sem=att_recv.at[h, i],
            device_id={"head": 1 - x},
            device_id_type=MESH,
        )

    def att_local(h, i):
        at = pl.ds(pl.multiple_of(x * LANES + h * 128, 128), 128)
        return pltpu.make_async_copy(att.at[h, i], attended.at[i, :, at], att_own.at[h, i])

    @pl.when(step >= 2)
    def _():
        i = lax.rem(step, 2)
        s = lax.rem(x + i, 2)
        slot = lax.rem(head, 2)

        def weights(a, b):
            return flat[slot, :, :, :, :, a:b].reshape(width, b - a)

        @pl.when(i == 0)
        def _():
            mat = weights(384, 512)
            for k in range(table.shape[0] // tile):
                place_out[0, k * tile : (k + 1) * tile] = dot(
                    table[k * tile : (k + 1) * tile], mat
                ).astype(BF16)

        mat = weights(128, 384)
        for k in range(context // tile):
            kv_out[0, 0, k * tile : (k + 1) * tile] = dot(
                normed[i, pl.ds(k * tile, tile)], mat
            ).astype(BF16)
        mat = weights(0, 128)
        bias_at = pl.ds(pl.multiple_of(head * 128, 128), 128)
        for k in range(seg_len // tile):
            queries = dot(normed[i, pl.ds(past + k * tile, tile)], mat)
            at = slice(k * tile, (k + 1) * tile)
            q_out[0, 0, at, 0:128] = (queries + params[8:9, bias_at]).astype(BF16)
            q_out[0, 0, at, 128:256] = (queries + params[9:10, bias_at]).astype(BF16)

        scale = 1.0 / math.sqrt(128)
        for part, out, key_start, key_count, place_start in (
            (0, wide_out, 0, past + HALF, 0),
            (1, near_out, past, seg_len, past - HALF),
        ):
            token = lax.broadcasted_iota(jnp.int32, (HALF, 1), 0) + part * HALF
            first = jnp.where(token >= docs[s, 0], past + docs[s, 0], past - docs[s, 3])
            first = jnp.where(token >= docs[s, 1], past + docs[s, 1], first)
            first = jnp.where(token >= docs[s, 2], past + docs[s, 2], first)
            at = slice(part * HALF, (part + 1) * HALF)
            weights_low = attend_rows(
                q_out[0, 0, at, 0:128],
                q_out[0, 0, at, 128:256],
                kv_out[0, 0, key_start : key_start + key_count, 0:128],
                place_out[0, place_start : place_start + key_count],
                first - key_start,
                token + (past - key_start),
                scale,
            ).astype(BF16)
            out[0, 0] = weights_low
            att[head, i, at] = dot(
                weights_low, kv_out[0, 0, key_start : key_start + key_count, 128:256]
            ).astype(BF16)
        att_pair(head, i).start()
        att_local(head, i).start()

    @pl.when(step == pl.num_programs(0) - 1)
    def _():
        for t in range(15, count + 2):
            tick(t)
        for h in range(4):
            for i in range(2):
                att_local(h, i).wait()
                att_pair(h, i).wait()
        for copy in pairs:
            copy.wait_send()
        pairs[5].wait_recv()
        for c in range(count):
            gather.close(c)


def attention_forward(
    n, docs, compressed, memory, segment, cotangent, mats, out_w, up_parts, down_w, comp_w, small, table
):
    _, seg_len, width = segment.shape
    past = compressed.shape[1] + memory.shape[1]
    context = past + seg_len
    nhi = n // 4
    lead = (nhi, 2, 2)
    half_rows = out_w.shape[0]
    comp_rows = comp_w.shape[0]
    any_spec = pl.BlockSpec(memory_space=pl.ANY)
    single = pl.Buffered(1)
    bf = lambda *shape: jax.ShapeDtypeStruct(shape, BF16)
    head = lambda t: jnp.maximum(t - 2, 0) // 2
    which = lambda t: lax.rem(jnp.maximum(t, 2), 2)
    by_both = lambda t: (head(t), which(t), 0, 0)
    dma = pltpu.SemaphoreType.DMA
    count = 13
    return pl.pallas_call(
        functools.partial(forward_kernel, n, past, seg_len),
        grid=(10,),
        out_shape=(
            bf(2, seg_len, width),
            bf(seg_len, width),
            bf(seg_len, width),
            jax.ShapeDtypeStruct((SMALL, LANES), F32),
            bf(4, 2, context, 256),
            bf(4, 2, seg_len, 256),
            bf(4, 2, HALF, past + HALF),
            bf(4, 2, HALF, seg_len),
            bf(4, past + HALF, 128),
            bf(2, width, context),
            *[bf(*lead, *w.shape) for w in mats],
            bf(*lead, 2, half_rows, width),
            bf(4, *lead, 2, half_rows, LANES),
            bf(*lead, *down_w.shape),
            bf(*lead, 2, comp_rows, LANES),
            bf(*lead, 2, SMALL, LANES),
            bf(2, half_rows, width),
            bf(4, 2, half_rows, LANES),
            bf(2, comp_rows, LANES),
            bf(2, SMALL, LANES),
        ),
        in_specs=[pl.BlockSpec(memory_space=pltpu.SMEM)]
        + [any_spec] * 13
        + [pl.BlockSpec(table.shape, lambda t: (0, 0), pipeline_mode=single)],
        out_specs=(
            any_spec,
            any_spec,
            any_spec,
            pl.BlockSpec((SMALL, LANES), lambda t: (0, 0)),
            pl.BlockSpec((1, 1, context, 256), by_both),
            pl.BlockSpec((1, 1, seg_len, 256), by_both),
            pl.BlockSpec((1, 1, HALF, past + HALF), by_both),
            pl.BlockSpec((1, 1, HALF, seg_len), by_both),
            pl.BlockSpec((1, past + HALF, 128), lambda t: (head(t), 0, 0)),
            pl.BlockSpec((2, width, context), lambda t: (0, 0, 0), pipeline_mode=single),
            *[any_spec] * 13,
        ),
        scratch_shapes=[
            pltpu.VMEM((2, context, width), BF16),
            pltpu.VMEM((2, 2, past // 2, width), BF16),
            pltpu.VMEM((2, seg_len, width), BF16),
            pltpu.VMEM((2,) + lead + (mats[0].shape[0], LANES), BF16),
            pltpu.VMEM(lead + (2, SMALL, LANES), BF16),
            pltpu.VMEM((4, 2, seg_len, 128), BF16),
            dma((2, 4)),
            dma((2, 4)),
            dma((4,)),
            dma((6,)),
            dma((6,)),
            dma((4, 2)),
            dma((4, 2)),
            dma((4, 2)),
        ]
        + Gather.semaphores(count, nhi),
        compiler_params=pltpu.CompilerParams(
            vmem_limit_bytes=VMEM_LIMIT,
            dimension_semantics=("arbitrary",),
            collective_id=0,
            has_side_effects=True,
        ),
        name="attention_forward",
    )(docs, compressed, memory, segment, cotangent, *mats, out_w, up_parts, down_w, comp_w, small, table)


def gelu_parts(v):
    c = math.sqrt(2.0 / math.pi)
    square = v * v
    t = jnp.tanh(c * (v + 0.044715 * square * v))
    half = 0.5 * (1.0 + t)
    value = v * half
    return value, half + value * (1.0 - half) * (2 * c + (6 * 0.044715 * c) * square)


def feed_kernel(
    n,
    att_in,
    segment,
    seg_other,
    cotangent,
    cot_other,
    out_in,
    up_in,
    down_in,
    params,
    comp,
    own_out,
    branch_out,
    residual_out,
    dout,
    out_grads,
    down_grads,
    small_out,
    comp_out,
    up_out,
    att,
    seg,
    cot,
    out_w,
    up,
    down,
    residual,
    low,
    low_t,
    act,
    pre,
    branch,
    terms,
    terms_land,
    cast,
    up_grads,
    mixed,
    stage,
    up_send,
    up_land,
    comp_stage,
    comp_send,
    comp_land,
    load_sem,
    store_sem,
    stage_sem,
    pair_send,
    pair_recv,
    land_c,
    land_y,
    land_z,
    mine,
    mine_sem,
    *sems,
):
    x = lax.axis_index("head")
    core, low_y, high, nhi = place(n)
    tile = 256
    _, seg_len, width = att.shape
    rows = width // n
    half_rows = rows // 2
    comp_rows = comp_send.shape[0]

    def pair(src, dst, k):
        return pltpu.make_async_remote_copy(
            src_ref=src,
            dst_ref=dst,
            send_sem=pair_send.at[k],
            recv_sem=pair_recv.at[k],
            device_id={"head": 1 - x},
            device_id_type=MESH,
        )

    terms_pair = pair(cast.at[0], terms_land, 0)
    mixed_pair = pair(mixed.at[1 - x], dout.at[1], 1)
    comp_pair = pair(comp_send, comp_land, 2)
    up_pairs = [pair(up_send.at[f], up_land.at[f], 3 + f) for f in range(4)]
    scatter = Scatter(
        n,
        [
            (part, here, land_c.at[c], land_y.at[c], land_z.at[c], done)
            for c, (part, here, done) in enumerate(
                [
                    (
                        comp.at[:, :, :, pl.ds(m * rows, rows)],
                        False,
                        comp_block(m, x, rows, comp_stage, comp_out, comp_send, comp_pair),
                    )
                    for m in range(3)
                ]
                + [
                    (up_grads.at[f], True, up_block(f, x, up_out, up_send, up_pairs[f]))
                    for f in range(4)
                ]
            )
        ],
        mine,
        mine_sem,
        sems,
    )

    def load(src, dst, k):
        return pltpu.make_async_copy(src, dst, load_sem.at[k])

    loads = {
        "att1": load(att_in.at[1], att.at[1], 0),
        "out": load(out_in, out_w, 1),
        "seg1": load(seg_other, seg.at[1], 2),
        "cot1": load(cot_other, cot.at[1], 3),
        "up": load(up_in, up, 4),
        "down": load(down_in, down, 5),
        "att0": load(att_in.at[0], att.at[0], 6),
        "seg0": load(segment.at[0], seg.at[0], 7),
        "cot0": load(cotangent.at[0], cot.at[0], 8),
    }
    for copy in loads.values():
        copy.start()
    barrier = pltpu.get_barrier_semaphore()
    pl.semaphore_signal(barrier, inc=1, device_id={"head": 1 - x}, device_id_type=MESH)
    meet(core, low_y, high, nhi, 1)
    scatter.start(0)
    scatter.start(1)

    eye = (
        lax.broadcasted_iota(jnp.int32, (tile, tile), 0)
        == lax.broadcasted_iota(jnp.int32, (tile, tile), 1)
    ).astype(BF16)
    gain = jnp.concatenate([params[4:5, :], params[5:6, :]], axis=1)
    shift = jnp.concatenate([params[6:7, :], params[7:8, :]], axis=1)

    def project(i):
        for k in range(seg_len // tile):
            at = slice(k * tile, (k + 1) * tile)
            whole_at = slice(i * seg_len + k * tile, i * seg_len + (k + 1) * tile)
            value = seg[i, at].astype(F32) + dot(att[i, at], out_w[...])
            residual[at, :] = value
            value = (norm_rows(value) * gain + shift).astype(BF16)
            low[whole_at, :] = value
            for b in range(width // tile):
                low_t[b * tile : (b + 1) * tile, whole_at] = dot_nt(
                    eye, value[:, b * tile : (b + 1) * tile]
                ).astype(BF16)

    def hidden(i):
        whole_at = slice(i * seg_len, (i + 1) * seg_len)
        branch[...] = jnp.zeros_like(branch)
        terms[...] = jnp.zeros_like(terms)

        def one(f, carry):
            down_at = pl.ds(pl.multiple_of(f * LANES, LANES), LANES)
            value, slope = gelu_parts(dot(low[whole_at, :], up[f]))
            value = value.astype(BF16)
            act[f, whole_at, :] = value
            back = dot_nt(cot[i], down[down_at, :]).astype(BF16).astype(F32)
            back = (back * slope).astype(BF16)
            pre[f, whole_at, :] = back
            branch[...] += dot(value, down[down_at, :])
            terms[...] += dot_nt(back, up[f])
            return carry

        lax.fori_loop(0, 4, one, 0)

    for name in ("att1", "out", "seg1"):
        loads[name].wait()
    project(1)
    scatter.add_core(0)
    scatter.start(2)
    for name in ("cot1", "up", "down"):
        loads[name].wait()
    hidden(1)
    cast[0] = terms[...].astype(BF16)
    terms_pair.start()
    cast[1] = branch[...].astype(BF16)
    store_branch = pltpu.make_async_copy(cast.at[1], branch_out, store_sem.at[0])
    store_branch.start()
    scatter.add_core(1)
    scatter.add_y(0)
    for name in ("att0", "seg0", "cot0"):
        loads[name].wait()
    project(0)
    scatter.add_core(2)
    scatter.add_y(1)
    scatter.add_z(0)
    hidden(0)
    branch[...] += residual[...]
    store_own = pltpu.make_async_copy(branch, own_out, store_sem.at[1])
    store_own.start()
    scatter.add_y(2)
    scatter.add_z(1)

    block = tile // (4 * rows)

    def up_grad(f):
        for k in range(width // tile):
            grad = dot(low_t[k * tile : (k + 1) * tile, :], pre[f]).astype(BF16)
            up_grads[f, k * block : (k + 1) * block] = grad.reshape(block, 2, 2, rows, LANES)
        scatter.start(3 + f)

    up_grad(0)
    scatter.add_z(2)
    up_grad(1)
    scatter.add_core(3)
    up_grad(2)
    scatter.add_core(4)
    scatter.add_y(3)
    up_grad(3)
    scatter.add_core(5)
    scatter.add_y(4)
    scatter.add_z(3)

    terms_pair.wait_recv()
    gain_grad = jnp.zeros((1, width), F32)
    shift_grad = jnp.zeros((1, width), F32)
    terms_pair.wait_send()
    for k in range(seg_len // tile):
        at = slice(k * tile, (k + 1) * tile)
        grad = terms[at, :] + terms_land[at, :].astype(F32)
        value = residual[at, :]
        mean = jnp.mean(value, axis=-1, keepdims=True)
        centred = value - mean
        rstd = lax.rsqrt(jnp.mean(centred * centred, axis=-1, keepdims=True) + 1e-05)
        xhat = centred * rstd
        gain_grad += jnp.sum(grad * xhat, axis=0, keepdims=True)
        shift_grad += jnp.sum(grad, axis=0, keepdims=True)
        grad = cot[0, at].astype(F32) + norm_back(xhat, rstd, grad * gain)
        residual[at, :] = grad
        grad = grad.astype(BF16)
        cast[0, at, :] = grad
        back = dot_nt(grad, out_w[...]).astype(BF16)
        mixed[0, at, :] = back[:, 0:LANES]
        mixed[1, at, :] = back[:, LANES:]
    mixed_pair.start()
    store_dout = pltpu.make_async_copy(mixed.at[x], dout.at[0], store_sem.at[2])
    store_dout.start()
    store_residual = pltpu.make_async_copy(residual, residual_out, store_sem.at[3])
    store_residual.start()
    small_out[...] = jnp.zeros_like(small_out)
    small_out[4:5, :] = gain_grad[:, 0:LANES]
    small_out[5:6, :] = gain_grad[:, LANES:]
    small_out[6:7, :] = shift_grad[:, 0:LANES]
    small_out[7:8, :] = shift_grad[:, LANES:]
    scatter.add_core(6)
    scatter.add_y(5)
    scatter.add_z(4)

    staged = [None, None]
    jobs = [(out_grads, k * tile, None, k) for k in range(width // tile)]
    jobs += [
        (down_grads, f * LANES + k * tile, f, k) for f in range(4) for k in range(LANES // tile)
    ]
    for j, (target, start, f, k) in enumerate(jobs):
        slot = j % 2
        at = slice(k * tile, (k + 1) * tile)
        if f is None:
            grad = dot_tn(att[0, :, at], cast[0])
        else:
            grad = dot_tn(act[f, 0:seg_len, at], cot[0]) + dot_tn(act[f, seg_len:, at], cot[1])
        if staged[slot] is not None:
            staged[slot].wait()
        stage[slot] = grad.astype(BF16)
        staged[slot] = pltpu.make_async_copy(
            stage.at[slot], target.at[pl.ds(start, tile)], stage_sem.at[slot]
        )
        staged[slot].start()
        if j == 5:
            scatter.add_y(6)
            scatter.add_z(5)
    scatter.add_z(6)
    comp_pair.wait_recv()
    to = pl.ds(pl.multiple_of((1 - x) * LANES, LANES), LANES)
    comp_out[:, to] = comp_land[...].astype(F32)
    for f in range(4):
        up_pairs[f].wait_recv()
        up_out[1 - x, f] = up_land[f].astype(F32)
    mixed_pair.wait_recv()
    for copy in [mixed_pair, comp_pair, *up_pairs]:
        copy.wait_send()
    for copy in [*staged, store_branch, store_own, store_dout, store_residual]:
        copy.wait()
    for c in range(7):
        scatter.close(c)


def comp_block(m, x, rows, stage, out, send, pair):
    def done(total):
        stage[m * rows : (m + 1) * rows, :] = total
        if m == 2:
            half = send.shape[0]
            upper, lower = stage[0:half, :], stage[half:, :]
            to = pl.ds(pl.multiple_of(x * LANES, LANES), LANES)
            out[:, to] = jnp.where(x == 0, upper, lower)
            send[...] = jnp.where(x == 0, lower, upper).astype(BF16)
            pair.start()

    return done


def up_block(f, x, out, send, pair):
    def done(total):
        half = send.shape[1]
        upper, lower = total[0:half], total[half:]
        out[x, f] = jnp.where(x == 0, upper, lower)
        send[f] = jnp.where(x == 0, lower, upper).astype(BF16)
        pair.start()

    return done


def feed_forward(n, att, segment, seg_other, cotangent, cot_other, out_w, up, down, params, comp):
    _, seg_len, width = att.shape
    rows = width // n
    half_rows = rows // 2
    nhi = n // 4
    comp_rows = comp.shape[3] // 2
    total = 2 * seg_len
    any_spec = pl.BlockSpec(memory_space=pl.ANY)
    vmem = pl.BlockSpec(memory_space=pltpu.VMEM)
    dma = pltpu.SemaphoreType.DMA
    f32 = lambda *shape: jax.ShapeDtypeStruct(shape, F32)
    bf = lambda *shape: jax.ShapeDtypeStruct(shape, BF16)
    return pl.pallas_call(
        functools.partial(feed_kernel, n),
        out_shape=(
            f32(seg_len, width),
            bf(seg_len, width),
            f32(seg_len, width),
            bf(2, seg_len, LANES),
            bf(width, width),
            bf(4 * LANES, width),
            f32(SMALL, LANES),
            f32(comp_rows, width),
            f32(2, 4, half_rows, LANES),
        ),
        in_specs=[any_spec] * 8 + [vmem, any_spec],
        out_specs=(any_spec,) * 6 + (vmem,) * 3,
        scratch_shapes=[
            pltpu.VMEM((2, seg_len, width), BF16),
            pltpu.VMEM((2, seg_len, width), BF16),
            pltpu.VMEM((2, seg_len, width), BF16),
            pltpu.VMEM((width, width), BF16),
            pltpu.VMEM((4, width, LANES), BF16),
            pltpu.VMEM((4 * LANES, width), BF16),
            pltpu.VMEM((seg_len, width), F32),
            pltpu.VMEM((total, width), BF16),
            pltpu.VMEM((width, total), BF16),
            pltpu.VMEM((4, total, LANES), BF16),
            pltpu.VMEM((4, total, LANES), BF16),
            pltpu.VMEM((seg_len, width), F32),
            pltpu.VMEM((seg_len, width), F32),
            pltpu.VMEM((seg_len, width), BF16),
            pltpu.VMEM((2, seg_len, width), BF16),
            pltpu.VMEM((4, nhi, 2, 2, rows, LANES), BF16),
            pltpu.VMEM((2, seg_len, LANES), BF16),
            pltpu.VMEM((2, 256, width), BF16),
            pltpu.VMEM((4, half_rows, LANES), BF16),
            pltpu.VMEM((4, half_rows, LANES), BF16),
            pltpu.VMEM((3 * rows, LANES), F32),
            pltpu.VMEM((comp_rows, LANES), BF16),
            pltpu.VMEM((comp_rows, LANES), BF16),
            dma((9,)),
            dma((4,)),
            dma((2,)),
            dma((7,)),
            dma((7,)),
        ]
        + Scatter.scratch(7, nhi, rows),
        compiler_params=pltpu.CompilerParams(
            vmem_limit_bytes=VMEM_LIMIT, collective_id=2, has_side_effects=True
        ),
        name="feed_forward",
    )(att, segment, seg_other, cotangent, cot_other, out_w, up, down, params, comp)


def norm_back(xhat, rstd, grad):
    a = jnp.mean(grad, axis=-1, keepdims=True)
    b = jnp.mean(grad * xhat, axis=-1, keepdims=True)
    return rstd * (grad - a - xhat * b)


def backward_kernel(
    n,
    past,
    seg_len,
    dout,
    kv,
    q,
    wide,
    near,
    place_keys,
    xhat_t,
    query_w,
    key_w,
    value_w,
    table_t,
    gain_row,
    gain_col,
    shift_col,
    segment,
    residual_grad,
    small_in,
    own_sum,
    branch,
    down,
    out,
    result_out,
    segment_out,
    query_out,
    key_out,
    value_out,
    place_out,
    out_out,
    down_out,
    small_out,
    flat,
    raw,
    sums,
    place_sum,
    input_grad,
    dkv,
    gain_sum,
    shift_sum,
    head_grads,
    context_land,
    context_send,
    branch_land,
    own_rows_sum,
    own_sem,
    out_keep,
    out_send,
    out_land,
    small_mine,
    small_c,
    small_y,
    small_z,
    small_x,
    pair_send,
    pair_recv,
    small_send,
    small_recv,
    land_c,
    land_y,
    land_z,
    mine,
    mine_sem,
    *sems,
):
    step = pl.program_id(0)
    x = lax.axis_index("head")
    core, low, high, nhi = place(n)
    head = lax.rem(step, 4)
    tile = 256
    context = past + seg_len
    width = flat.shape[0]
    rows = width // n
    half_rows = rows // 2
    scale = 1.0 / math.sqrt(128)
    flip = (
        lax.broadcasted_iota(jnp.int32, (HALF, HALF), 0)
        + lax.broadcasted_iota(jnp.int32, (HALF, HALF), 1)
        == HALF - 1
    ).astype(BF16)

    def pair(src, dst, k):
        return pltpu.make_async_remote_copy(
            src_ref=src,
            dst_ref=dst,
            send_sem=pair_send.at[k],
            recv_sem=pair_recv.at[k],
            device_id={"head": 1 - x},
            device_id_type=MESH,
        )

    context_pair = pair(context_send, context_land, 0)
    branch_pair = pair(branch, branch_land, 1)
    out_pairs = [pair(out_send.at[b], out_land.at[b], 2 + b) for b in range(2)]
    load_own = pltpu.make_async_copy(own_sum, own_rows_sum, own_sem)

    def down_done(a, b):
        def done(total):
            down_out[a * rows : (a + 1) * rows, b * LANES : (b + 1) * LANES] = total

        return done

    def out_done(b):
        def done(total):
            upper, lower = total[0:half_rows], total[half_rows:]
            out_keep[b] = jnp.where(x == 0, upper, lower)
            out_send[b] = jnp.where(x == 0, lower, upper).astype(BF16)
            out_pairs[b].start()

        return done

    def head_done(h):
        def done(total):
            for j, ref in enumerate((query_out, key_out, value_out, place_out)):
                ref[:, h * 128 : (h + 1) * 128] = total[:, j * 128 : (j + 1) * 128]

        return done

    parts = []
    for a in range(2):
        for b in range(2):
            at, to = pl.ds(a * rows, rows), pl.ds(b * LANES, LANES)
            parts.append((down.at[:, :, :, at, to], False, down_done(a, b)))
    parts += [
        (out.at[:, :, :, :, pl.ds(b * LANES, LANES)], False, out_done(b)) for b in range(2)
    ]
    parts += [(head_grads.at[h], True, head_done(h)) for h in range(4)]
    scatter = Scatter(
        n,
        [
            (part, here, land_c.at[c], land_y.at[c], land_z.at[c], done)
            for c, (part, here, done) in enumerate(parts)
        ],
        mine,
        mine_sem,
        sems,
    )
    count = len(parts)

    @pl.when(step == 0)
    def _():
        barrier = pltpu.get_barrier_semaphore()
        pl.semaphore_signal(barrier, inc=1, device_id={"head": 1 - x}, device_id_type=MESH)
        meet(core, low, high, nhi, 1)
        load_own.start()
        raw[...] = jnp.zeros_like(raw)
        sums[...] = jnp.zeros_like(sums)
        place_sum[...] = jnp.zeros_like(place_sum)
        gain_sum[...] = jnp.zeros_like(gain_sum)
        shift_sum[...] = jnp.zeros_like(shift_sum)
        small_mine[...] = small_in[...]

    @pl.when(head == 0)
    def _():
        input_grad[...] = jnp.zeros_like(input_grad)

    before = {0: 0, 1: 2, 2: 4, 3: None, 4: None, 5: 6, 6: 7, 7: 8}
    within = {0: 1, 1: 3, 2: 5}
    for k, t in before.items():
        if t is not None:
            pl.when(step == k)(functools.partial(scatter.tick, t))

    for j, mat in enumerate((query_w, key_w, value_w)):
        flat[:, j * 128 : (j + 1) * 128] = mat[...]

    query_grads = []
    key_rows = []
    value_rows = []
    place_rows = []
    bias_at = pl.ds(pl.multiple_of(head * 128, 128), 128)
    for part, weights_ref, key_start, key_count, place_start in (
        (0, wide, 0, past + HALF, 0),
        (1, near, past, seg_len, past - HALF),
    ):
        at = slice(part * HALF, (part + 1) * HALF)
        keys_at = slice(key_start, key_start + key_count)
        attn = weights_ref[0, 0]
        grad = dout[0, at]
        value_rows.append(dot_tn(grad, attn))
        weights_grad = dot_nt(grad, kv[0, 0, keys_at, 128:256])
        attn = attn.astype(F32)
        row = jnp.sum(weights_grad * attn, axis=1, keepdims=True)
        scores_grad = (attn * (weights_grad - row) * scale).astype(BF16)
        content_grad = dot(scores_grad, kv[0, 0, keys_at, 0:128]).astype(BF16)
        key_rows.append(dot_tn(q[0, 0, at, 0:128], scores_grad))
        by_place = pltpu.roll(dot(flip, scores_grad), 0, 1, stride=1, stride_axis=0).astype(BF16)
        place_grad = dot(by_place, place_keys[0, place_start : place_start + key_count])
        place_grad = dot(flip, place_grad.astype(BF16)).astype(BF16)
        flipped_q = dot(flip, q[0, 0, at, 128:256]).astype(BF16)
        place_rows.append(dot_tn(flipped_q, by_place))
        content_f = content_grad.astype(F32)
        place_f = place_grad.astype(F32)
        small_mine[8:9, bias_at] += jnp.sum(content_f, axis=0, keepdims=True)
        small_mine[9:10, bias_at] += jnp.sum(place_f, axis=0, keepdims=True)
        query_grads.append((content_f + place_f).astype(BF16))

    for j, (wide_rows, near_rows) in enumerate((key_rows, value_rows)):
        at = slice(j * 128, (j + 1) * 128)
        dkv[at, 0:past] = wide_rows[:, 0:past].astype(BF16)
        dkv[at, past : past + HALF] = (wide_rows[:, past:] + near_rows[:, 0:HALF]).astype(BF16)
        dkv[at, past + HALF :] = near_rows[:, HALF:].astype(BF16)
    split = past - HALF
    for at, rows_grad in (
        (slice(0, split), place_rows[0][:, 0:split]),
        (slice(split, None), place_rows[0][:, split:] + place_rows[1]),
    ):
        place_sum[head, :, at] = (
            place_sum[head, :, at].astype(F32) + rows_grad.astype(BF16).astype(F32)
        ).astype(BF16)
    dq = jnp.concatenate(query_grads, axis=0)
    stacked = jnp.concatenate([dq, dkv[:, past:].astype(F32).T.astype(BF16)], axis=1)

    for k, t in within.items():
        pl.when(step == k)(functools.partial(scatter.tick, t))

    ones = jnp.ones((8, context), BF16)
    sums[head, :, 0:128] += dot(ones[:, 0:seg_len], dq)
    sums[head, :, 128:384] += dot_nt(ones, dkv[...])
    for k in range(width // tile):
        at = slice(k * tile, (k + 1) * tile)
        raw[head, at, 0:128] += dot(xhat_t[0, at, past:], dq)
        raw[head, at, 128:384] += dot_nt(xhat_t[0, at, :], dkv[...])
        input_grad[:, at] += dot_nt(stacked, flat[at, 0:384])

    @pl.when(step >= 4)
    def _():
        place_low = place_sum[head]
        block = tile // (4 * rows)
        total = sums[head, 0:1, :]
        for k in range(width // tile):
            at = slice(k * tile, (k + 1) * tile)
            to = slice(k * block, (k + 1) * block)
            got = raw[head, at, :]
            mats = flat[at, 0:384].astype(F32)
            for acc, term in ((gain_sum, mats * got), (shift_sum, mats * total)):
                acc[at, :] += term[:, 0:128] + term[:, 128:256] + term[:, 256:384]
            grad = (gain_col[at, :] * got + shift_col[at, :] * total).astype(BF16)
            head_grads[head, to, :, :, :, 0:384] = grad.reshape(block, 2, 2, rows, 384)
            grad = dot_nt(table_t[at, :], place_low).astype(BF16)
            head_grads[head, to, :, :, :, 384:512] = grad.reshape(block, 2, 2, rows, 128)

    def own_rows(k):
        at = slice(k * tile, (k + 1) * tile)
        values = segment[0, at].astype(F32)
        mean = jnp.mean(values, axis=-1, keepdims=True)
        centred = values - mean
        rstd = lax.rsqrt(jnp.mean(centred * centred, axis=-1, keepdims=True) + 1e-05)
        return norm_back(centred * rstd, rstd, input_grad[at, :] * gain_row[...])

    @pl.when(step == 3)
    def _():
        for k in range(seg_len // tile):
            context_send[k * tile : (k + 1) * tile, :] = own_rows(k).astype(BF16)
        context_pair.start()
        branch_pair.start()

    @pl.when(step == 7)
    def _():
        scatter.tick(9)
        one = jnp.ones((8, 128), F32)
        for acc, row in ((gain_sum, 0), (shift_sum, 2)):
            line = lax.dot_general(
                one,
                acc[...],
                (((1,), (1,)), ((), ())),
                precision=lax.Precision.HIGHEST,
                preferred_element_type=F32,
            )
            small_mine[row : row + 1, :] = line[0:1, 0:LANES]
            small_mine[row + 1 : row + 2, :] = line[0:1, LANES:]

        def to_dp(src, dst, k, index):
            return remote(src, dst, small_send.at[k], small_recv.at[k], index)

        copies = [to_dp(small_mine, small_c.at[1], 0, high * 4 + low * 2 + (1 - core))]
        copies[0].start()
        context_pair.wait_recv()
        for k in range(seg_len // tile):
            at = slice(k * tile, (k + 1) * tile)
            segment_out[0, at] = (
                residual_grad[at, :] + own_rows(k) + context_land[at, :].astype(F32)
            ).astype(BF16)
        copies[0].wait_recv()
        small_c[0] = small_mine[...] + small_c[1]
        copies.append(to_dp(small_c.at[0], small_y.at[1], 1, high * 4 + (1 - low) * 2 + core))
        copies[1].start()
        scatter.tick(10)
        copies[1].wait_recv()
        small_y[0] = small_c[0] + small_y[1]
        along = []
        for k in range(1, nhi):
            to = lax.rem(high + k, nhi) * 4 + low * 2 + core
            along.append(to_dp(small_y.at[0], small_z.at[k], 2 + k, to))
        for copy in along:
            copy.start()
        scatter.tick(11)
        for copy in along:
            copy.wait_recv()
        line = small_y[0]
        for k in range(1, nhi):
            line = line + small_z[k]
        small_z[0] = line
        last = pltpu.make_async_remote_copy(
            src_ref=small_z.at[0],
            dst_ref=small_x,
            send_sem=small_send.at[2],
            recv_sem=small_recv.at[2],
            device_id={"head": 1 - x},
            device_id_type=MESH,
        )
        last.start()
        scatter.tick(12)
        branch_pair.wait_recv()
        load_own.wait()
        for k in range(seg_len // tile):
            at = slice(k * tile, (k + 1) * tile)
            result_out[0, at] = (own_rows_sum[at, :] + branch_land[at, :].astype(F32)).astype(BF16)
        for b in range(2):
            out_pairs[b].wait_recv()
            out_out[:, b * LANES : (b + 1) * LANES] = out_keep[b] + out_land[b].astype(F32)
        last.wait_recv()
        line = lax.broadcasted_iota(jnp.int32, (SMALL, LANES), 0)
        small_out[...] = small_z[0] + jnp.where(line < 8, small_x[...], 0.0)
        for copy in [context_pair, branch_pair, *out_pairs, *copies, *along, last]:
            copy.wait_send()
        for c in range(count):
            scatter.close(c)


def attention_backward(
    n, dout, kv, q, wide, near, place_keys, xhat_t, mats, table_t, gain, shift, segment,
    residual_grad, small_in, own_sum, branch, down, out,
):
    _, seg_len, width = segment.shape
    context = kv.shape[2]
    past = context - seg_len
    rows = width // n
    nhi = n // 4
    half_rows = rows // 2
    seq = lambda t: 1 - t // 4
    head = lambda t: lax.rem(t, 4)
    by_both = lambda t: (head(t), seq(t), 0, 0)
    single = pl.Buffered(1)
    any_spec = pl.BlockSpec(memory_space=pl.ANY)
    dma = pltpu.SemaphoreType.DMA
    f32 = lambda *shape: jax.ShapeDtypeStruct(shape, F32)
    lead = (nhi, 2, 2)
    full = lambda shape: pl.BlockSpec(shape, lambda t: (0,) * len(shape), pipeline_mode=single)
    outs = (
        jax.ShapeDtypeStruct((1, seg_len, width), BF16),
        jax.ShapeDtypeStruct((1, seg_len, width), BF16),
        f32(rows, LANES),
        f32(rows, LANES),
        f32(rows, LANES),
        f32(rows, LANES),
        f32(half_rows, width),
        f32(2 * rows, width),
        f32(SMALL, LANES),
    )
    return pl.pallas_call(
        functools.partial(backward_kernel, n, past, seg_len),
        grid=(8,),
        out_shape=outs,
        in_specs=[
            pl.BlockSpec((1, seg_len, 128), lambda t: (seq(t), 0, head(t))),
            pl.BlockSpec((1, 1, context, 256), by_both),
            pl.BlockSpec((1, 1, seg_len, 256), by_both),
            pl.BlockSpec((1, 1, HALF, past + HALF), by_both),
            pl.BlockSpec((1, 1, HALF, seg_len), by_both),
            pl.BlockSpec((1, past + HALF, 128), lambda t: (head(t), 0, 0)),
            pl.BlockSpec((1, width, context), lambda t: (seq(t), 0, 0), pipeline_mode=single),
            *[pl.BlockSpec((width, 128), lambda t: (0, head(t)))] * 3,
            full(table_t.shape),
            full((1, width)),
            full((width, 1)),
            full((width, 1)),
            pl.BlockSpec((1, seg_len, width), lambda t: (seq(t), 0, 0), pipeline_mode=single),
            full((seg_len, width)),
            full((SMALL, LANES)),
            any_spec,
            any_spec,
            any_spec,
            any_spec,
        ],
        out_specs=tuple(full(o.shape) for o in outs),
        scratch_shapes=[
            pltpu.VMEM((width, 384), BF16),
            pltpu.VMEM((4, width, 384), F32),
            pltpu.VMEM((4, 8, 384), F32),
            pltpu.VMEM((4, 128, past + HALF), BF16),
            pltpu.VMEM((seg_len, width), F32),
            pltpu.VMEM((256, context), BF16),
            pltpu.VMEM((width, 128), F32),
            pltpu.VMEM((width, 128), F32),
            pltpu.VMEM((4,) + lead + (rows, LANES), BF16),
            pltpu.VMEM((seg_len, width), BF16),
            pltpu.VMEM((seg_len, width), BF16),
            pltpu.VMEM((seg_len, width), BF16),
            pltpu.VMEM((seg_len, width), F32),
            dma(()),
            pltpu.VMEM((2, half_rows, LANES), F32),
            pltpu.VMEM((2, half_rows, LANES), BF16),
            pltpu.VMEM((2, half_rows, LANES), BF16),
            pltpu.VMEM((SMALL, LANES), F32),
            pltpu.VMEM((2, SMALL, LANES), F32),
            pltpu.VMEM((2, SMALL, LANES), F32),
            pltpu.VMEM((nhi, SMALL, LANES), F32),
            pltpu.VMEM((SMALL, LANES), F32),
            dma((4,)),
            dma((4,)),
            dma((2 + nhi,)),
            dma((2 + nhi,)),
        ]
        + Scatter.scratch(10, nhi, rows),
        compiler_params=pltpu.CompilerParams(
            vmem_limit_bytes=VMEM_LIMIT,
            dimension_semantics=("arbitrary",),
            collective_id=1,
            has_side_effects=True,
        ),
        name="attention_backward",
    )(
        dout, kv, q, wide, near, place_keys, xhat_t, *mats, table_t,
        gain.reshape(1, width), gain.reshape(width, 1), shift.reshape(width, 1), segment,
        residual_grad, small_in, own_sum, branch, down, out,
    )


def body(
    n,
    segment,
    memory,
    compressed,
    doc_lengths,
    memory_valid,
    query_weight,
    key_weight,
    value_weight,
    position_weight,
    content_bias,
    position_bias,
    output_weight,
    up_weight,
    down_weight,
    compress_weight,
    norm_gain,
    norm_shift,
    post_gain,
    post_shift,
    cotangent,
    compress_cotangent,
):
    x = lax.axis_index("head")
    dp = lax.axis_index("dp")
    first = x == 0
    nhi = n // 4
    width = segment.shape[2]
    seg_len = segment.shape[1]
    past = memory.shape[1] + compressed.shape[1]
    context = past + seg_len
    rows = query_weight.shape[0]
    half_rows = output_weight.shape[0]
    new_count = compress_cotangent.shape[1]
    comp_rows = compress_weight.shape[0]

    def swap(a):
        return lax.ppermute(a, "head", [(0, 1), (1, 0)])

    def pick(a, index):
        return jnp.where(index == 0, a[0], a[1])

    def in_order(own, got, axis):
        return jnp.where(
            first,
            jnp.concatenate([own, got], axis=axis),
            jnp.concatenate([got, own], axis=axis),
        )

    ffr = down_weight.shape[0]
    up_parts = (
        up_weight.reshape(half_rows, 4, n // 4, 2, ffr)
        .transpose(3, 1, 0, 2, 4)
        .reshape(2, 4, half_rows, LANES)
    )
    lane = jnp.arange(width, dtype=jnp.int32)

    def spread(vector, index, size):
        return jnp.where(lane // size == index, jnp.tile(vector, width // size), 0).reshape(2, LANES)

    bias_lane = jnp.arange(LANES, dtype=jnp.int32) % 128
    per = content_bias.shape[1]

    def spread_bias(bias):
        tiled = jnp.tile(bias, (1, n)).reshape(1, LANES)
        return jnp.where((bias_lane // per == dp), tiled, 0)

    small = jnp.concatenate(
        [
            spread(v, dp * 2 + x, half_rows)
            for v in (norm_gain, norm_shift, post_gain, post_shift)
        ]
        + [
            spread_bias(content_bias),
            spread_bias(position_bias),
            jnp.zeros((SMALL - 10, LANES), BF16),
        ]
    ).astype(BF16)

    end_one = doc_lengths[:, 0]
    end_two = end_one + doc_lengths[:, 1]
    docs = jnp.stack([end_one, end_two, end_two + doc_lengths[:, 2], memory_valid], axis=1)
    table = position_rows(context, width, past + HALF)

    (
        att, seg_other, cot_other, params, kv, q, wide, near, place_keys, xhat_t,
        query_whole, key_whole, value_whole, _, out_whole, up_whole, down_whole, comp_whole, *_,
    ) = attention_forward(
        n, docs, compressed, memory, segment, cotangent,
        (query_weight, key_weight, value_weight, position_weight),
        output_weight, up_parts, down_weight, compress_weight, small, jnp.asarray(table),
    )
    mats = [w.reshape(width, LANES) for w in (query_whole, key_whole, value_whole)]
    out_mat = out_whole.reshape(width, width)
    comp_mat = comp_whole.reshape(3 * width, LANES)
    gain_one, shift_one = (params[2 * i : 2 * i + 2].reshape(1, width) for i in range(2))
    segment_both = jnp.concatenate([segment, seg_other[None]])
    comp_cot = in_order(compress_cotangent, swap(compress_cotangent), 0)
    windows = memory[:, : 3 * new_count].reshape(-1, 3 * width)
    made_half = dot(windows, comp_mat).astype(BF16).reshape(2, new_count, LANES)
    made = in_order(pick(made_half, x), swap(pick(made_half, 1 - x)), 1)
    comp_cot_half = pick(comp_cot.reshape(-1, 2, LANES).transpose(1, 0, 2), x)
    comp_grads = dot_tn(windows, comp_cot_half).astype(BF16)

    lead = (nhi, 2, 2)
    own_sum, branch, residual_grad, dout, out_grads, down_grads, small_in, comp_done, up_done = feed_forward(
        n, att, segment, seg_other, cotangent, cot_other, out_mat,
        up_whole.reshape(4, width, LANES), down_whole.reshape(4 * LANES, width), params,
        comp_grads.reshape(lead + (3 * rows, LANES)),
    )

    (
        result, segment_grad, query_done, key_done, value_done, place_done,
        out_done, down_done, small_done,
    ) = attention_backward(
        n, dout, kv, q, wide, near, place_keys, xhat_t, mats, jnp.asarray(table.T.copy()),
        gain_one, shift_one, segment_both, residual_grad, small_in, own_sum, branch,
        down_grads.reshape(lead + (2 * rows, 2 * LANES)),
        out_grads.reshape(lead + (rows, 2 * LANES)),
    )

    up_final = (
        up_done.reshape(2, 4, half_rows, n // 4, ffr)
        .transpose(2, 1, 3, 0, 4)
        .reshape(half_rows, -1)
    )
    vectors = lax.dynamic_slice_in_dim(
        small_done[0:8].reshape(4, width), (dp * 2 + x) * half_rows, half_rows, 1
    )
    biases = lax.dynamic_slice_in_dim(small_done[8:10].reshape(2, 4, 128), dp * per, per, 2)
    return (
        result,
        made[None],
        segment_grad,
        query_done,
        key_done,
        value_done,
        place_done,
        biases[0],
        biases[1],
        out_done,
        up_final,
        down_done,
        comp_done,
        vectors[0],
        vectors[1],
        vectors[2],
        vectors[3],
    )


def solution(mesh):
    split = P(("dp", "head"))
    wide = P(("dp", "head"), None)
    deep = P(("dp", "head"), None, None)
    return jax.shard_map(
        functools.partial(body, mesh.shape["dp"]),
        mesh=mesh,
        in_specs=(
            deep,
            P("dp", None, None),
            P("dp", None, None),
            P("dp", None),
            P("dp"),
            P("dp", "head"),
            P("dp", "head"),
            P("dp", "head"),
            P("dp", "head"),
            P("head", "dp"),
            P("head", "dp"),
            wide,
            wide,
            wide,
            wide,
            split,
            split,
            split,
            split,
            deep,
            deep,
        ),
        out_specs=(
            deep,
            deep,
            deep,
            P("dp", "head"),
            P("dp", "head"),
            P("dp", "head"),
            P("dp", "head"),
            P("head", "dp"),
            P("head", "dp"),
            wide,
            wide,
            wide,
            wide,
            split,
            split,
            split,
            split,
        ),
        check_vma=False,
    )
```

```python
import functools
import math

import jax
import jax.numpy as jnp
import numpy as np
from jax import lax
from jax.experimental import pallas as pl
from jax.experimental.pallas import tpu as pltpu
from jax.sharding import PartitionSpec as P

F32 = jnp.float32
BF16 = jnp.bfloat16
MESH = pl.DeviceIdType.MESH
VMEM_LIMIT = 62 * 1024 * 1024
HALF = 256
LANES = 512
SMALL = 16


def dot(a, b):
    return lax.dot_general(a, b, (((1,), (0,)), ((), ())), preferred_element_type=F32)


def dot_nt(a, b):
    return lax.dot_general(a, b, (((1,), (1,)), ((), ())), preferred_element_type=F32)


def dot_tn(a, b):
    return lax.dot_general(a, b, (((0,), (0,)), ((), ())), preferred_element_type=F32)


def position_rows(context, width, used):
    distance = np.arange(context, dtype=np.float32)[:, None]
    frequency = np.exp(
        np.arange(width // 2, dtype=np.float32) * np.float32(-2.0 * math.log(10000.0) / width)
    )
    phases = distance * frequency[None, :].astype(np.float32)
    table = np.concatenate([np.sin(phases), np.cos(phases)], axis=1)
    return table[::-1][context - used :].astype(jnp.bfloat16)


def place(n):
    me = lax.axis_index("dp")
    core = lax.rem(me, 2)
    low = lax.rem(me // 2, 2)
    high = me // 4
    return core, low, high, n // 4


def meet(core, low, high, nhi, more=0):
    barrier = pltpu.get_barrier_semaphore()

    def tell(index):
        pl.semaphore_signal(barrier, inc=1, device_id={"dp": index}, device_id_type=MESH)

    for k in range(1, nhi):
        tell(lax.rem(high + k, nhi) * 4 + low * 2 + core)
    tell(high * 4 + (1 - low) * 2 + core)
    tell(high * 4 + low * 2 + (1 - core))
    pl.semaphore_wait(barrier, nhi + 1 + more)


def remote(src, dst, send, recv, index):
    return pltpu.make_async_remote_copy(
        src_ref=src,
        dst_ref=dst,
        send_sem=send,
        recv_sem=recv,
        device_id={"dp": index},
        device_id_type=MESH,
    )


class Gather:
    def __init__(self, n, pairs, sems):
        self.core, self.low, self.high, self.nhi = place(n)
        self.pairs = pairs
        (self.zs, self.zr, self.ys, self.yr, self.cs, self.cr, self.own) = sems
        order = sorted(range(1, self.nhi), key=lambda k: (min(k, self.nhi - k), k))
        self.order = order

    def z_copy(self, c, k):
        shard, whole = self.pairs[c]
        return remote(
            shard,
            whole.at[self.high, self.low, self.core],
            self.zs.at[c, k],
            self.zr.at[c, k],
            lax.rem(self.high + k, self.nhi) * 4 + self.low * 2 + self.core,
        )

    def own_copy(self, c):
        shard, whole = self.pairs[c]
        return pltpu.make_async_copy(
            shard, whole.at[self.high, self.low, self.core], self.own.at[c]
        )

    def y_copy(self, c, k):
        shard, whole = self.pairs[c]
        at = whole.at[lax.rem(self.high + k, self.nhi), self.low, self.core]
        return remote(
            shard if k == 0 else at,
            at,
            self.ys.at[c, k],
            self.yr.at[c, k],
            self.high * 4 + (1 - self.low) * 2 + self.core,
        )

    def c_copy(self, c):
        _, whole = self.pairs[c]
        part = whole.at[:, :, self.core]
        return remote(
            part,
            part,
            self.cs.at[c],
            self.cr.at[c],
            self.high * 4 + self.low * 2 + (1 - self.core),
        )

    def start(self, c):
        for k in self.order:
            self.z_copy(c, k).start()
        self.y_copy(c, 0).start()
        self.own_copy(c).start()

    def pass_y(self, c):
        for k in self.order:
            self.z_copy(c, self.nhi - k).wait_recv()
            self.y_copy(c, k).start()

    def pass_core(self, c):
        self.own_copy(c).wait()
        for k in range(self.nhi):
            self.y_copy(c, k).wait_recv()
        self.c_copy(c).start()

    def arrive(self, c):
        self.c_copy(c).wait_recv()

    def close(self, c):
        for k in self.order:
            self.z_copy(c, k).wait_send()
        for k in range(self.nhi):
            self.y_copy(c, k).wait_send()
        self.c_copy(c).wait_send()

    @staticmethod
    def semaphores(count, nhi):
        dma = pltpu.SemaphoreType.DMA
        return [dma((count, nhi))] * 4 + [dma((count,))] * 3


class Scatter:
    def __init__(self, n, items, mine, mine_sem, sems):
        self.core, self.low, self.high, self.nhi = place(n)
        self.items = items
        self.mine, self.mine_sem = mine, mine_sem
        (self.cs, self.cr, self.ys, self.yr, self.zs, self.zr) = sems

    def c_copy(self, c):
        return remote(
            self.items[c][0].at[:, :, 1 - self.core],
            self.items[c][2],
            self.cs.at[c],
            self.cr.at[c],
            self.high * 4 + self.low * 2 + (1 - self.core),
        )

    def mine_copy(self, c):
        slot = c % 2
        return pltpu.make_async_copy(
            self.items[c][0].at[:, :, self.core], self.mine.at[slot], self.mine_sem.at[slot]
        )

    def y_copy(self, c):
        return remote(
            self.items[c][2].at[:, 1 - self.low],
            self.items[c][3],
            self.ys.at[c],
            self.yr.at[c],
            self.high * 4 + (1 - self.low) * 2 + self.core,
        )

    def z_copies(self, c):
        return [
            remote(
                self.items[c][3].at[lax.rem(self.high + k, self.nhi)],
                self.items[c][4].at[k - 1],
                self.zs.at[c, k - 1],
                self.zr.at[c, k - 1],
                lax.rem(self.high + k, self.nhi) * 4 + self.low * 2 + self.core,
            )
            for k in range(1, self.nhi)
        ]

    def start(self, c):
        self.c_copy(c).start()
        if not self.items[c][1]:
            self.mine_copy(c).start()

    def add_core(self, c):
        here = self.items[c][1]
        if not here:
            self.mine_copy(c).wait()
        self.c_copy(c).wait_recv()
        land = self.items[c][2]

        def body(i, carry):
            for j in range(2):
                own = self.items[c][0][i, j, self.core] if here else self.mine[c % 2, i, j]
                land[i, j] = land[i, j] + own
            return carry

        lax.fori_loop(0, self.nhi, body, 0)
        self.y_copy(c).start()

    def add_y(self, c):
        self.y_copy(c).wait_recv()
        src, land = self.items[c][2], self.items[c][3]

        def body(i, carry):
            land[i] = land[i] + src[i, self.low]
            return carry

        lax.fori_loop(0, self.nhi, body, 0)
        for copy in self.z_copies(c):
            copy.start()

    def add_z(self, c):
        for copy in self.z_copies(c):
            copy.wait_recv()
        land, last, done = self.items[c][3:]
        total = land[self.high].astype(F32)
        for k in range(self.nhi - 1):
            total = total + last[k].astype(F32)
        done(total)

    def tick(self, t):
        count = len(self.items)
        if 0 <= t - 1 < count:
            self.add_core(t - 1)
        if t < count:
            self.start(t)
        if 0 <= t - 2 < count:
            self.add_y(t - 2)
        if 0 <= t - 3 < count:
            self.add_z(t - 3)

    def close(self, c):
        self.c_copy(c).wait_send()
        self.y_copy(c).wait_send()
        for copy in self.z_copies(c):
            copy.wait_send()

    @staticmethod
    def scratch(count, nhi, rows):
        dma = pltpu.SemaphoreType.DMA
        return [
            pltpu.VMEM((count, nhi, 2, rows, LANES), BF16),
            pltpu.VMEM((count, nhi, rows, LANES), BF16),
            pltpu.VMEM((count, nhi - 1, rows, LANES), BF16),
            pltpu.VMEM((2, nhi, 2, rows, LANES), BF16),
            dma((2,)),
            dma((count,)),
            dma((count,)),
            dma((count,)),
            dma((count,)),
            dma((count, nhi - 1)),
            dma((count, nhi - 1)),
        ]


def norm_rows(values):
    mean = jnp.mean(values, axis=-1, keepdims=True)
    centred = values - mean
    variance = jnp.mean(centred * centred, axis=-1, keepdims=True)
    return centred * lax.rsqrt(variance + 1e-05)


def attend_rows(query_content, query_place, keys, place_keys, first_seen, last_seen, scale):
    width = keys.shape[0]
    content = dot_nt(query_content, keys)
    by_place = pltpu.roll(
        dot_nt(query_place, place_keys), width - (HALF - 1), 1, stride=1, stride_axis=0
    )
    column = lax.broadcasted_iota(jnp.int32, (HALF, width), 1)
    seen = (column >= first_seen) & (column <= last_seen)
    scores = jnp.where(seen, (content + by_place) * (scale * math.log2(math.e)), -1e30)
    top = jnp.max(scores, axis=1, keepdims=True)
    expo = jnp.exp2(scores - top)
    return expo * (1.0 / jnp.sum(expo, axis=1, keepdims=True))


def forward_kernel(
    n,
    past,
    seg_len,
    docs,
    valid,
    compressed,
    memory,
    segment,
    cotangent,
    comp_cot,
    query_w,
    key_w,
    value_w,
    place_w,
    out_w,
    up_parts,
    down_w,
    comp_w,
    small,
    table,
    attended,
    seg_both,
    cot_other,
    xhat_hbm,
    windows_hbm,
    comp_grads_hbm,
    params,
    kv_out,
    q_out,
    wide_out,
    near_out,
    place_out,
    query_whole,
    key_whole,
    value_whole,
    place_whole,
    out_whole,
    up_whole,
    down_whole,
    small_whole,
    out_shard,
    up_shard,
    comp_shard,
    small_shard,
    normed,
    xhat_out,
    memory_f,
    windows,
    comp_rows_cot,
    comp_grads,
    past_rows,
    seg_rows,
    flat,
    small_rows,
    att,
    load_sem,
    flat_sem,
    own_sem,
    store_sem,
    pair_send,
    pair_recv,
    att_own,
    att_send,
    att_recv,
    *sems,
):
    step = pl.program_id(0)
    x = lax.axis_index("head")
    core, low, high, nhi = place(n)
    tile = 256
    width = normed.shape[2]
    context = past + seg_len
    head = jnp.maximum(step - 2, 0) // 2
    half = comp_w.shape[1] // 2

    items = [(small_shard, small_whole)]
    items += [(query_w, query_whole), (key_w, key_whole), (value_w, value_whole), (place_w, place_whole)]
    for b in range(2):
        to = pl.ds(b * LANES, LANES)
        items.append((out_shard.at[:, :, to], out_whole.at[:, :, :, :, :, to]))
    items += [(up_shard.at[f], up_whole.at[f]) for f in range(4)]
    mid = down_w.shape[0] // 2
    for part in range(2):
        for b in range(2):
            at, to = pl.ds(part * mid, mid), pl.ds(b * LANES, LANES)
            items.append((down_w.at[at, to], down_whole.at[:, :, :, at, to]))
    gather = Gather(n, items, sems)
    count = len(items)
    needs = {5: 1, 7: 2}
    pad_rows = comp_cot.shape[0]

    def pair(src, dst, k):
        return pltpu.make_async_remote_copy(
            src_ref=src,
            dst_ref=dst,
            send_sem=pair_send.at[k],
            recv_sem=pair_recv.at[k],
            device_id={"head": 1 - x},
            device_id_type=MESH,
        )

    mine_at = pl.ds(pl.multiple_of(x * half, half), half)
    other_at = pl.ds(pl.multiple_of((1 - x) * half, half), half)
    pairs = [
        pair(small, small_shard.at[x], 0),
        pair(out_w, out_shard.at[x], 1),
        pair(up_parts.at[1 - x], up_shard.at[:, x], 2),
        pair(comp_w.at[:, other_at], comp_shard.at[x], 3),
        pair(segment.at[0], seg_both.at[1], 4),
        pair(cotangent.at[0], cot_other, 5),
        pair(comp_cot.at[:, other_at], comp_rows_cot.at[1], 6),
    ]
    owns = [
        pltpu.make_async_copy(small, small_shard.at[x], own_sem.at[0]),
        pltpu.make_async_copy(out_w, out_shard.at[x], own_sem.at[1]),
        pltpu.make_async_copy(up_parts.at[x], up_shard.at[:, x], own_sem.at[2]),
        pltpu.make_async_copy(comp_w.at[:, mine_at], comp_shard.at[x], own_sem.at[3]),
        pltpu.make_async_copy(segment.at[0], seg_both.at[0], own_sem.at[4]),
        pltpu.make_async_copy(comp_cot.at[:, mine_at], comp_rows_cot.at[0], own_sem.at[5]),
    ]
    loads = []
    for i in range(2):
        s = lax.rem(x + i, 2)
        loads.append(pltpu.make_async_copy(compressed.at[s], past_rows.at[i, 0], load_sem.at[i, 0]))
        loads.append(pltpu.make_async_copy(memory.at[s], past_rows.at[i, 1], load_sem.at[i, 1]))
    loads.append(pltpu.make_async_copy(segment.at[0], seg_rows.at[0], load_sem.at[0, 2]))
    load_other = pltpu.make_async_copy(seg_both.at[1], seg_rows.at[1], load_sem.at[1, 2])
    store_xhat = pltpu.make_async_copy(xhat_out, xhat_hbm, store_sem.at[0])
    store_windows = pltpu.make_async_copy(windows, windows_hbm, store_sem.at[1])
    store_grads = pltpu.make_async_copy(comp_grads, comp_grads_hbm, store_sem.at[2])

    joined = set()

    def join(k):
        if k not in joined:
            joined.add(k)
            owns[k].wait()
            pairs[k].wait_recv()

    def tick(t):
        lead = t + 3
        if lead < count:
            if lead in needs:
                join(needs[lead])
            gather.start(lead)
        if t < count:
            gather.pass_y(t)
        if 0 <= t - 1 < count:
            gather.pass_core(t - 1)
        if 0 <= t - 2 < count:
            gather.arrive(t - 2)

    def flat_copies(h, slot):
        at = pl.ds(h * 128, 128)
        return [
            pltpu.make_async_copy(
                whole.at[:, :, :, :, at],
                flat.at[slot, :, :, :, :, pl.ds(j * 128, 128)],
                flat_sem.at[slot, j],
            )
            for j, whole in enumerate((query_whole, key_whole, value_whole, place_whole))
        ]

    def norm_into(i, values, at):
        eye = (
            lax.broadcasted_iota(jnp.int32, (tile, tile), 0)
            == lax.broadcasted_iota(jnp.int32, (tile, tile), 1)
        ).astype(BF16)
        gain = jnp.concatenate([params[0:1, :], params[1:2, :]], axis=1)
        shift = jnp.concatenate([params[2:3, :], params[3:4, :]], axis=1)
        xhat = norm_rows(values.astype(F32))
        normed[i, pl.ds(at, tile)] = (xhat * gain + shift).astype(BF16)
        xhat = xhat.astype(BF16)
        for b in range(width // tile):
            xhat_out[i, b * tile : (b + 1) * tile, pl.ds(at, tile)] = dot_nt(
                eye, xhat[:, b * tile : (b + 1) * tile]
            ).astype(BF16)

    def norm_past(i):
        per = past // 2 // tile

        def one(k, carry):
            at = pl.multiple_of(k * tile, tile)
            inner = pl.multiple_of(lax.rem(k, per) * tile, tile)
            norm_into(i, past_rows[i, k // per, pl.ds(inner, tile)], at)
            return carry

        lax.fori_loop(0, past // tile, one, 0)

    def norm_segment(i):
        def one(k, carry):
            at = pl.multiple_of(k * tile, tile)
            norm_into(i, seg_rows[i, pl.ds(at, tile)], past + at)
            return carry

        lax.fori_loop(0, seg_len // tile, one, 0)

    @pl.when(step == 0)
    def _():
        barrier = pltpu.get_barrier_semaphore()
        pl.semaphore_signal(
            barrier, inc=1, device_id={"head": 1 - x}, device_id_type=MESH
        )
        meet(core, low, high, nhi, 1)
        for k in (0, 1, 2, 6, 4, 3, 5):
            pairs[k].start()
        for copy in owns:
            copy.start()
        for copy in loads:
            copy.start()
        gather.start(1)
        join(0)
        gather.start(0)
        gather.start(2)
        tick(0)
        tick(1)
        tick(2)
        summed = pltpu.make_async_copy(small_whole, small_rows, load_sem.at[0, 3])
        summed.start()
        summed.wait()
        both = jnp.sum(small_rows[...].reshape(n, 2, SMALL, LANES).astype(F32), axis=0)
        row = lax.broadcasted_iota(jnp.int32, (SMALL, LANES), 0)
        by_head = jnp.where(x == 0, both[0], both[1])
        params[...] = jnp.where(row < 8, both[0] + both[1], by_head)
        for copy in (loads[0], loads[1], loads[4]):
            copy.wait()
        norm_past(0)
        tick(3)
        norm_segment(0)
        tick(4)

    @pl.when(step == 1)
    def _():
        for copy in loads[2:4]:
            copy.wait()
        norm_past(1)
        tick(5)
        memory_f[:, past // 2 :, :] = jnp.zeros((width // 128, 16, 128), F32)
        for i in range(2):
            for b in range(width // 128):
                at = slice(b * 128, (b + 1) * 128)
                memory_f[b, 0 : past // 2, :] = past_rows[i, 1, :, at].astype(F32)
                for tap in range(3):
                    windows[tap, i * pad_rows : (i + 1) * pad_rows, at] = memory_f[
                        b, pl.ds(tap, pad_rows, stride=3), :
                    ].astype(BF16)
        store_windows.start()
        owns[5].wait()
        pairs[6].wait_recv()
        tick(6)
        for copy in flat_copies(0, 0):
            copy.start()
        comp_rows_both = comp_rows_cot[...].reshape(2 * pad_rows, LANES)
        for tap in range(3):
            for k in range(width // tile):
                at = slice(k * tile, (k + 1) * tile)
                comp_grads[tap * width + k * tile : tap * width + (k + 1) * tile, :] = dot_tn(
                    windows[tap, :, at], comp_rows_both
                ).astype(BF16)
        store_grads.start()

    for k in range(2, 10):

        @pl.when(step == k)
        def _(k=k):
            tick(k + 5)
            h, slot = (k - 2) // 2, ((k - 2) // 2) % 2
            if k % 2 == 0:
                for copy in flat_copies(h, slot):
                    copy.wait()
                if h < 3:
                    for copy in flat_copies(h + 1, 1 - slot):
                        copy.start()
            if k == 3:
                pairs[4].wait_recv()
                load_other.start()
                load_other.wait()
                norm_segment(1)
                store_xhat.start()

    def att_pair(h, i):
        at = pl.ds(pl.multiple_of(x * LANES + h * 128, 128), 128)
        return pltpu.make_async_remote_copy(
            src_ref=att.at[h, i],
            dst_ref=attended.at[1 - i, :, at],
            send_sem=att_send.at[h, i],
            recv_sem=att_recv.at[h, i],
            device_id={"head": 1 - x},
            device_id_type=MESH,
        )

    def att_local(h, i):
        at = pl.ds(pl.multiple_of(x * LANES + h * 128, 128), 128)
        return pltpu.make_async_copy(att.at[h, i], attended.at[i, :, at], att_own.at[h, i])

    @pl.when(step >= 2)
    def _():
        i = lax.rem(step, 2)
        s = lax.rem(x + i, 2)
        slot = lax.rem(head, 2)

        def weights(a, b):
            return flat[slot, :, :, :, :, a:b].reshape(width, b - a)

        @pl.when(i == 0)
        def _():
            mat = weights(384, 512)
            for k in range(table.shape[0] // tile):
                place_out[0, k * tile : (k + 1) * tile] = dot(
                    table[k * tile : (k + 1) * tile], mat
                ).astype(BF16)

        mat = weights(128, 384)
        for k in range(context // tile):
            kv_out[0, 0, k * tile : (k + 1) * tile] = dot(
                normed[i, pl.ds(k * tile, tile)], mat
            ).astype(BF16)
        mat = weights(0, 128)
        bias_at = pl.ds(pl.multiple_of(head * 128, 128), 128)
        for k in range(seg_len // tile):
            queries = dot(normed[i, pl.ds(past + k * tile, tile)], mat)
            at = slice(k * tile, (k + 1) * tile)
            q_out[0, 0, at, 0:128] = (queries + params[8:9, bias_at]).astype(BF16)
            q_out[0, 0, at, 128:256] = (queries + params[9:10, bias_at]).astype(BF16)

        scale = 1.0 / math.sqrt(128)
        for part, out, key_start, key_count, place_start in (
            (0, wide_out, 0, past + HALF, 0),
            (1, near_out, past, seg_len, past - HALF),
        ):
            token = lax.broadcasted_iota(jnp.int32, (HALF, 1), 0) + part * HALF
            end, first = 0, past - valid[s]
            for doc in range(3):
                end = end + docs[s, doc]
                first = jnp.where(token >= end, past + end, first)
            at = slice(part * HALF, (part + 1) * HALF)
            weights_low = attend_rows(
                q_out[0, 0, at, 0:128],
                q_out[0, 0, at, 128:256],
                kv_out[0, 0, key_start : key_start + key_count, 0:128],
                place_out[0, place_start : place_start + key_count],
                first - key_start,
                token + (past - key_start),
                scale,
            ).astype(BF16)
            out[0, 0] = weights_low
            att[head, i, at] = dot(
                weights_low, kv_out[0, 0, key_start : key_start + key_count, 128:256]
            ).astype(BF16)
        att_pair(head, i).start()
        att_local(head, i).start()

    @pl.when(step == pl.num_programs(0) - 1)
    def _():
        for t in range(15, count + 2):
            tick(t)
        owns[3].wait()
        owns[4].wait()
        pairs[3].wait_recv()
        for copy in (store_xhat, store_windows, store_grads):
            copy.wait()
        for h in range(4):
            for i in range(2):
                att_local(h, i).wait()
                att_pair(h, i).wait()
        for copy in pairs:
            copy.wait_send()
        pairs[5].wait_recv()
        for c in range(count):
            gather.close(c)


def attention_forward(
    n, docs, valid, compressed, memory, segment, cotangent, comp_cot, mats, out_w, up_parts, down_w,
    comp_w, small, table,
):
    _, seg_len, width = segment.shape
    past = compressed.shape[1] + memory.shape[1]
    context = past + seg_len
    nhi = n // 4
    lead = (nhi, 2, 2)
    half_rows = out_w.shape[0]
    comp_rows = comp_w.shape[0]
    pad_rows = comp_cot.shape[0]
    any_spec = pl.BlockSpec(memory_space=pl.ANY)
    smem = pl.BlockSpec(memory_space=pltpu.SMEM)
    single = pl.Buffered(1)
    bf = lambda *shape: jax.ShapeDtypeStruct(shape, BF16)
    head = lambda t: jnp.maximum(t - 2, 0) // 2
    which = lambda t: lax.rem(jnp.maximum(t, 2), 2)
    by_both = lambda t: (head(t), which(t), 0, 0)
    dma = pltpu.SemaphoreType.DMA
    count = 15
    return pl.pallas_call(
        functools.partial(forward_kernel, n, past, seg_len),
        grid=(10,),
        out_shape=(
            bf(2, seg_len, width),
            bf(2, seg_len, width),
            bf(seg_len, width),
            bf(2, width, context),
            bf(3, 2 * pad_rows, width),
            bf(3 * width, LANES),
            jax.ShapeDtypeStruct((SMALL, LANES), F32),
            bf(4, 2, context, 256),
            bf(4, 2, seg_len, 256),
            bf(4, 2, HALF, past + HALF),
            bf(4, 2, HALF, seg_len),
            bf(4, past + HALF, 128),
            *[bf(*lead, *w.shape) for w in mats],
            bf(*lead, 2, half_rows, width),
            bf(4, *lead, 2, half_rows, LANES),
            bf(*lead, *down_w.shape),
            bf(*lead, 2, SMALL, LANES),
            bf(2, half_rows, width),
            bf(4, 2, half_rows, LANES),
            bf(2, comp_rows, LANES),
            bf(2, SMALL, LANES),
        ),
        in_specs=[smem, smem]
        + [any_spec] * 14
        + [pl.BlockSpec(table.shape, lambda t: (0, 0), pipeline_mode=single)],
        out_specs=(
            *[any_spec] * 6,
            pl.BlockSpec((SMALL, LANES), lambda t: (0, 0)),
            pl.BlockSpec((1, 1, context, 256), by_both),
            pl.BlockSpec((1, 1, seg_len, 256), by_both),
            pl.BlockSpec((1, 1, HALF, past + HALF), by_both),
            pl.BlockSpec((1, 1, HALF, seg_len), by_both),
            pl.BlockSpec((1, past + HALF, 128), lambda t: (head(t), 0, 0)),
            *[any_spec] * 12,
        ),
        scratch_shapes=[
            pltpu.VMEM((2, context, width), BF16),
            pltpu.VMEM((2, width, context), BF16),
            pltpu.VMEM((width // 128, past // 2 + 16, 128), F32),
            pltpu.VMEM((3, 2 * pad_rows, width), BF16),
            pltpu.VMEM((2, pad_rows, LANES), BF16),
            pltpu.VMEM((3 * width, LANES), BF16),
            pltpu.VMEM((2, 2, past // 2, width), BF16),
            pltpu.VMEM((2, seg_len, width), BF16),
            pltpu.VMEM((2,) + lead + (mats[0].shape[0], LANES), BF16),
            pltpu.VMEM(lead + (2, SMALL, LANES), BF16),
            pltpu.VMEM((4, 2, seg_len, 128), BF16),
            dma((2, 4)),
            dma((2, 4)),
            dma((6,)),
            dma((3,)),
            dma((7,)),
            dma((7,)),
            dma((4, 2)),
            dma((4, 2)),
            dma((4, 2)),
        ]
        + Gather.semaphores(count, nhi),
        compiler_params=pltpu.CompilerParams(
            vmem_limit_bytes=VMEM_LIMIT,
            dimension_semantics=("arbitrary",),
            collective_id=0,
            has_side_effects=True,
        ),
        name="attention_forward",
    )(
        docs, valid, compressed, memory, segment, cotangent, comp_cot, *mats, out_w, up_parts, down_w,
        comp_w, small, table,
    )


def gelu_parts(v):
    c = math.sqrt(2.0 / math.pi)
    square = v * v
    t = jnp.tanh(c * (v + 0.044715 * square * v))
    half = 0.5 * (1.0 + t)
    value = v * half
    return value, half + value * (1.0 - half) * (2 * c + (6 * 0.044715 * c) * square)


def feed_kernel(
    n,
    att_in,
    seg_in,
    cotangent,
    cot_other,
    out_in,
    up_in,
    down_in,
    params,
    comp,
    comp_shard,
    own_out,
    branch_out,
    residual_out,
    dout,
    out_grads,
    down_grads,
    small_out,
    comp_out,
    up_out,
    comp_whole,
    att,
    seg,
    cot,
    out_w,
    up,
    down,
    residual,
    low,
    low_t,
    act,
    pre,
    branch,
    terms,
    terms_land,
    cast,
    up_grads,
    mixed,
    stage,
    up_send,
    up_land,
    comp_stage,
    comp_send,
    comp_land,
    load_sem,
    store_sem,
    stage_sem,
    pair_send,
    pair_recv,
    land_c,
    land_y,
    land_z,
    mine,
    mine_sem,
    *sems,
):
    sems, gather_sems = sems[:6], sems[6:]
    x = lax.axis_index("head")
    core, low_y, high, nhi = place(n)
    tile = 256
    _, seg_len, width = att.shape
    rows = width // n
    half_rows = rows // 2
    comp_rows = comp_send.shape[0]

    def pair(src, dst, k):
        return pltpu.make_async_remote_copy(
            src_ref=src,
            dst_ref=dst,
            send_sem=pair_send.at[k],
            recv_sem=pair_recv.at[k],
            device_id={"head": 1 - x},
            device_id_type=MESH,
        )

    terms_pair = pair(cast.at[0], terms_land, 0)
    mixed_pair = pair(mixed.at[1 - x], dout.at[1], 1)
    comp_pair = pair(comp_send, comp_land, 2)
    up_pairs = [pair(up_send.at[f], up_land.at[f], 3 + f) for f in range(4)]
    scatter = Scatter(
        n,
        [
            (part, here, land_c.at[c], land_y.at[c], land_z.at[c], done)
            for c, (part, here, done) in enumerate(
                [
                    (
                        comp.at[:, :, :, pl.ds(m * rows, rows)],
                        False,
                        comp_block(m, x, rows, comp_stage, comp_out, comp_send, comp_pair),
                    )
                    for m in range(3)
                ]
                + [
                    (up_grads.at[f], True, up_block(f, x, up_out, up_send, up_pairs[f]))
                    for f in range(4)
                ]
            )
        ],
        mine,
        mine_sem,
        sems,
    )

    third = comp_rows // 3
    gather = Gather(
        n,
        [
            (
                comp_shard.at[:, pl.ds(m * third, third)],
                comp_whole.at[:, :, :, :, pl.ds(m * third, third)],
            )
            for m in range(3)
        ],
        gather_sems,
    )

    def load(src, dst, k):
        return pltpu.make_async_copy(src, dst, load_sem.at[k])

    loads = {
        "att1": load(att_in.at[1], att.at[1], 0),
        "out": load(out_in, out_w, 1),
        "seg1": load(seg_in.at[1], seg.at[1], 2),
        "cot1": load(cot_other, cot.at[1], 3),
        "up": load(up_in, up, 4),
        "down": load(down_in, down, 5),
        "att0": load(att_in.at[0], att.at[0], 6),
        "seg0": load(seg_in.at[0], seg.at[0], 7),
        "cot0": load(cotangent.at[0], cot.at[0], 8),
    }
    for copy in loads.values():
        copy.start()
    barrier = pltpu.get_barrier_semaphore()
    pl.semaphore_signal(barrier, inc=1, device_id={"head": 1 - x}, device_id_type=MESH)
    meet(core, low_y, high, nhi, 1)
    scatter.start(0)
    scatter.start(1)
    gather.start(0)

    eye = (
        lax.broadcasted_iota(jnp.int32, (tile, tile), 0)
        == lax.broadcasted_iota(jnp.int32, (tile, tile), 1)
    ).astype(BF16)
    gain = jnp.concatenate([params[4:5, :], params[5:6, :]], axis=1)
    shift = jnp.concatenate([params[6:7, :], params[7:8, :]], axis=1)

    def project(i):
        for k in range(seg_len // tile):
            at = slice(k * tile, (k + 1) * tile)
            whole_at = slice(i * seg_len + k * tile, i * seg_len + (k + 1) * tile)
            value = seg[i, at].astype(F32) + dot(att[i, at], out_w[...])
            residual[at, :] = value
            value = (norm_rows(value) * gain + shift).astype(BF16)
            low[whole_at, :] = value
            for b in range(width // tile):
                low_t[b * tile : (b + 1) * tile, whole_at] = dot_nt(
                    eye, value[:, b * tile : (b + 1) * tile]
                ).astype(BF16)

    def hidden(i, between):
        whole_at = slice(i * seg_len, (i + 1) * seg_len)
        branch[...] = jnp.zeros_like(branch)
        terms[...] = jnp.zeros_like(terms)

        def one(f, carry):
            down_at = pl.ds(pl.multiple_of(f * LANES, LANES), LANES)
            value, slope = gelu_parts(dot(low[whole_at, :], up[f]))
            value = value.astype(BF16)
            act[f, whole_at, :] = value
            back = dot_nt(cot[i], down[down_at, :]).astype(BF16).astype(F32)
            back = (back * slope).astype(BF16)
            pre[f, whole_at, :] = back
            branch[...] += dot(value, down[down_at, :])
            terms[...] += dot_nt(back, up[f])
            for k, steps in enumerate(between):

                @pl.when(f == k)
                def _(steps=steps):
                    for run, c in steps:
                        run(c)

            return carry

        lax.fori_loop(0, 4, one, 0)

    for name in ("att1", "out", "seg1"):
        loads[name].wait()
    project(1)
    scatter.add_core(0)
    scatter.start(2)
    gather.pass_y(0)
    gather.start(1)
    for name in ("cot1", "up", "down"):
        loads[name].wait()
    hidden(
        1,
        (
            ((scatter.add_core, 1), (scatter.add_y, 0)),
            ((gather.pass_y, 1), (gather.start, 2), (gather.pass_core, 0)),
            ((scatter.add_core, 2), (scatter.add_y, 1), (scatter.add_z, 0)),
            ((gather.pass_y, 2), (gather.pass_core, 1)),
        ),
    )
    cast[0] = terms[...].astype(BF16)
    terms_pair.start()
    cast[1] = branch[...].astype(BF16)
    store_branch = pltpu.make_async_copy(cast.at[1], branch_out, store_sem.at[0])
    store_branch.start()
    for name in ("att0", "seg0", "cot0"):
        loads[name].wait()
    project(0)
    scatter.add_y(2)
    scatter.add_z(1)
    hidden(0, (((gather.pass_core, 2),), ((scatter.add_z, 2),)))
    branch[...] += residual[...]
    store_own = pltpu.make_async_copy(branch, own_out, store_sem.at[1])
    store_own.start()

    block = tile // (4 * rows)

    def up_grad(f):
        for k in range(width // tile):
            grad = dot(low_t[k * tile : (k + 1) * tile, :], pre[f]).astype(BF16)
            up_grads[f, k * block : (k + 1) * block] = grad.reshape(block, 2, 2, rows, LANES)
        scatter.start(3 + f)

    up_grad(0)
    up_grad(1)
    scatter.add_core(3)
    up_grad(2)
    scatter.add_core(4)
    up_grad(3)
    scatter.add_core(5)
    scatter.add_y(3)
    for m in range(3):
        gather.arrive(m)

    terms_pair.wait_recv()
    gain_grad = jnp.zeros((1, width), F32)
    shift_grad = jnp.zeros((1, width), F32)
    terms_pair.wait_send()
    for k in range(seg_len // tile):
        at = slice(k * tile, (k + 1) * tile)
        grad = terms[at, :] + terms_land[at, :].astype(F32)
        value = residual[at, :]
        mean = jnp.mean(value, axis=-1, keepdims=True)
        centred = value - mean
        rstd = lax.rsqrt(jnp.mean(centred * centred, axis=-1, keepdims=True) + 1e-05)
        xhat = centred * rstd
        gain_grad += jnp.sum(grad * xhat, axis=0, keepdims=True)
        shift_grad += jnp.sum(grad, axis=0, keepdims=True)
        grad = cot[0, at].astype(F32) + norm_back(xhat, rstd, grad * gain)
        residual[at, :] = grad
        grad = grad.astype(BF16)
        cast[0, at, :] = grad
        back = dot_nt(grad, out_w[...]).astype(BF16)
        mixed[0, at, :] = back[:, 0:LANES]
        mixed[1, at, :] = back[:, LANES:]
    mixed_pair.start()
    store_dout = pltpu.make_async_copy(mixed.at[x], dout.at[0], store_sem.at[2])
    store_dout.start()
    store_residual = pltpu.make_async_copy(residual, residual_out, store_sem.at[3])
    store_residual.start()
    small_out[...] = jnp.zeros_like(small_out)
    small_out[4:5, :] = gain_grad[:, 0:LANES]
    small_out[5:6, :] = gain_grad[:, LANES:]
    small_out[6:7, :] = shift_grad[:, 0:LANES]
    small_out[7:8, :] = shift_grad[:, LANES:]
    scatter.add_core(6)
    scatter.add_y(4)
    scatter.add_z(3)

    staged = [None, None]
    jobs = [(out_grads, k * tile, None, k) for k in range(width // tile)]
    jobs += [
        (down_grads, f * LANES + k * tile, f, k) for f in range(4) for k in range(LANES // tile)
    ]
    for j, (target, start, f, k) in enumerate(jobs):
        slot = j % 2
        at = slice(k * tile, (k + 1) * tile)
        if f is None:
            grad = dot_tn(att[0, :, at], cast[0])
        else:
            grad = dot_tn(act[f, 0:seg_len, at], cot[0]) + dot_tn(act[f, seg_len:, at], cot[1])
        if staged[slot] is not None:
            staged[slot].wait()
        stage[slot] = grad.astype(BF16)
        staged[slot] = pltpu.make_async_copy(
            stage.at[slot], target.at[pl.ds(start, tile)], stage_sem.at[slot]
        )
        staged[slot].start()
        if j == 3:
            scatter.add_y(5)
            scatter.add_z(4)
        if j == 10:
            scatter.add_y(6)
            scatter.add_z(5)
    scatter.add_z(6)
    comp_pair.wait_recv()
    to = pl.ds(pl.multiple_of((1 - x) * LANES, LANES), LANES)
    comp_out[:, to] = comp_land[...].astype(F32)
    for f in range(4):
        up_pairs[f].wait_recv()
        up_out[1 - x, f] = up_land[f].astype(F32)
    mixed_pair.wait_recv()
    for copy in [mixed_pair, comp_pair, *up_pairs]:
        copy.wait_send()
    for copy in [*staged, store_branch, store_own, store_dout, store_residual]:
        copy.wait()
    for c in range(7):
        scatter.close(c)
    for m in range(3):
        gather.close(m)


def comp_block(m, x, rows, stage, out, send, pair):
    def done(total):
        stage[m * rows : (m + 1) * rows, :] = total
        if m == 2:
            half = send.shape[0]
            upper, lower = stage[0:half, :], stage[half:, :]
            to = pl.ds(pl.multiple_of(x * LANES, LANES), LANES)
            out[:, to] = jnp.where(x == 0, upper, lower)
            send[...] = jnp.where(x == 0, lower, upper).astype(BF16)
            pair.start()

    return done


def up_block(f, x, out, send, pair):
    def done(total):
        half = send.shape[1]
        upper, lower = total[0:half], total[half:]
        out[x, f] = jnp.where(x == 0, upper, lower)
        send[f] = jnp.where(x == 0, lower, upper).astype(BF16)
        pair.start()

    return done


def feed_forward(
    n, att, seg_both, cotangent, cot_other, out_w, up, down, params, comp, comp_shard
):
    _, seg_len, width = att.shape
    rows = width // n
    half_rows = rows // 2
    nhi = n // 4
    comp_rows = comp.shape[3] // 2
    total = 2 * seg_len
    any_spec = pl.BlockSpec(memory_space=pl.ANY)
    vmem = pl.BlockSpec(memory_space=pltpu.VMEM)
    dma = pltpu.SemaphoreType.DMA
    f32 = lambda *shape: jax.ShapeDtypeStruct(shape, F32)
    bf = lambda *shape: jax.ShapeDtypeStruct(shape, BF16)
    return pl.pallas_call(
        functools.partial(feed_kernel, n),
        out_shape=(
            f32(seg_len, width),
            bf(seg_len, width),
            f32(seg_len, width),
            bf(2, seg_len, LANES),
            bf(width, width),
            bf(4 * LANES, width),
            f32(SMALL, LANES),
            f32(comp_rows, width),
            f32(2, 4, half_rows, LANES),
            bf(nhi, 2, 2, *comp_shard.shape),
        ),
        in_specs=[any_spec] * 7 + [vmem, any_spec, any_spec],
        out_specs=(any_spec,) * 6 + (vmem,) * 3 + (any_spec,),
        scratch_shapes=[
            pltpu.VMEM((2, seg_len, width), BF16),
            pltpu.VMEM((2, seg_len, width), BF16),
            pltpu.VMEM((2, seg_len, width), BF16),
            pltpu.VMEM((width, width), BF16),
            pltpu.VMEM((4, width, LANES), BF16),
            pltpu.VMEM((4 * LANES, width), BF16),
            pltpu.VMEM((seg_len, width), F32),
            pltpu.VMEM((total, width), BF16),
            pltpu.VMEM((width, total), BF16),
            pltpu.VMEM((4, total, LANES), BF16),
            pltpu.VMEM((4, total, LANES), BF16),
            pltpu.VMEM((seg_len, width), F32),
            pltpu.VMEM((seg_len, width), F32),
            pltpu.VMEM((seg_len, width), BF16),
            pltpu.VMEM((2, seg_len, width), BF16),
            pltpu.VMEM((4, nhi, 2, 2, rows, LANES), BF16),
            pltpu.VMEM((2, seg_len, LANES), BF16),
            pltpu.VMEM((2, 256, width), BF16),
            pltpu.VMEM((4, half_rows, LANES), BF16),
            pltpu.VMEM((4, half_rows, LANES), BF16),
            pltpu.VMEM((3 * rows, LANES), F32),
            pltpu.VMEM((comp_rows, LANES), BF16),
            pltpu.VMEM((comp_rows, LANES), BF16),
            dma((9,)),
            dma((4,)),
            dma((2,)),
            dma((7,)),
            dma((7,)),
        ]
        + Scatter.scratch(7, nhi, rows)
        + Gather.semaphores(3, nhi),
        compiler_params=pltpu.CompilerParams(
            vmem_limit_bytes=VMEM_LIMIT, collective_id=2, has_side_effects=True
        ),
        name="feed_forward",
    )(att, seg_both, cotangent, cot_other, out_w, up, down, params, comp, comp_shard)


def norm_back(xhat, rstd, grad):
    a = jnp.mean(grad, axis=-1, keepdims=True)
    b = jnp.mean(grad * xhat, axis=-1, keepdims=True)
    return rstd * (grad - a - xhat * b)


def backward_kernel(
    n,
    past,
    seg_len,
    dout,
    kv,
    q,
    wide,
    near,
    place_keys,
    xhat_t,
    query_w,
    key_w,
    value_w,
    table_t,
    params,
    segment,
    residual_grad,
    small_in,
    own_sum,
    branch,
    down,
    out,
    result_out,
    segment_out,
    query_out,
    key_out,
    value_out,
    place_out,
    out_out,
    down_out,
    small_out,
    flat,
    raw,
    sums,
    place_sum,
    input_grad,
    dkv,
    columns,
    gain_sum,
    shift_sum,
    head_grads,
    context_land,
    context_send,
    branch_land,
    own_rows_sum,
    own_sem,
    out_keep,
    out_send,
    out_land,
    small_mine,
    small_c,
    small_y,
    small_z,
    small_x,
    pair_send,
    pair_recv,
    small_send,
    small_recv,
    land_c,
    land_y,
    land_z,
    mine,
    mine_sem,
    *sems,
):
    step = pl.program_id(0)
    x = lax.axis_index("head")
    core, low, high, nhi = place(n)
    head = lax.rem(step, 4)
    tile = 256
    context = past + seg_len
    width = flat.shape[0]
    rows = width // n
    half_rows = rows // 2
    scale = 1.0 / math.sqrt(128)
    flip = (
        lax.broadcasted_iota(jnp.int32, (HALF, HALF), 0)
        + lax.broadcasted_iota(jnp.int32, (HALF, HALF), 1)
        == HALF - 1
    ).astype(BF16)

    def pair(src, dst, k):
        return pltpu.make_async_remote_copy(
            src_ref=src,
            dst_ref=dst,
            send_sem=pair_send.at[k],
            recv_sem=pair_recv.at[k],
            device_id={"head": 1 - x},
            device_id_type=MESH,
        )

    context_pair = pair(context_send, context_land, 0)
    branch_pair = pair(branch, branch_land, 1)
    out_pairs = [pair(out_send.at[b], out_land.at[b], 2 + b) for b in range(2)]
    load_own = pltpu.make_async_copy(own_sum, own_rows_sum, own_sem)

    def down_done(a, b):
        def done(total):
            down_out[a * rows : (a + 1) * rows, b * LANES : (b + 1) * LANES] = total

        return done

    def out_done(b):
        def done(total):
            upper, lower = total[0:half_rows], total[half_rows:]
            out_keep[b] = jnp.where(x == 0, upper, lower)
            out_send[b] = jnp.where(x == 0, lower, upper).astype(BF16)
            out_pairs[b].start()

        return done

    def head_done(h):
        def done(total):
            for j, ref in enumerate((query_out, key_out, value_out, place_out)):
                ref[:, h * 128 : (h + 1) * 128] = total[:, j * 128 : (j + 1) * 128]

        return done

    parts = []
    for a in range(2):
        for b in range(2):
            at, to = pl.ds(a * rows, rows), pl.ds(b * LANES, LANES)
            parts.append((down.at[:, :, :, at, to], False, down_done(a, b)))
    parts += [
        (out.at[:, :, :, :, pl.ds(b * LANES, LANES)], False, out_done(b)) for b in range(2)
    ]
    parts += [(head_grads.at[h], True, head_done(h)) for h in range(4)]
    scatter = Scatter(
        n,
        [
            (part, here, land_c.at[c], land_y.at[c], land_z.at[c], done)
            for c, (part, here, done) in enumerate(parts)
        ],
        mine,
        mine_sem,
        sems,
    )
    count = len(parts)

    @pl.when(step == 0)
    def _():
        barrier = pltpu.get_barrier_semaphore()
        pl.semaphore_signal(barrier, inc=1, device_id={"head": 1 - x}, device_id_type=MESH)
        meet(core, low, high, nhi, 1)
        load_own.start()
        branch_pair.start()
        for j in range(2):
            line = jnp.concatenate([params[2 * j : 2 * j + 1, :], params[2 * j + 1 : 2 * j + 2, :]], axis=1)
            columns[j] = jnp.broadcast_to(line, (128, width)).T
        raw[...] = jnp.zeros_like(raw)
        sums[...] = jnp.zeros_like(sums)
        place_sum[...] = jnp.zeros_like(place_sum)
        gain_sum[...] = jnp.zeros_like(gain_sum)
        shift_sum[...] = jnp.zeros_like(shift_sum)
        small_mine[...] = small_in[...]

    @pl.when(head == 0)
    def _():
        input_grad[...] = jnp.zeros_like(input_grad)

    start, add_core, add_y, add_z = scatter.start, scatter.add_core, scatter.add_y, scatter.add_z
    before = {
        0: ((start, 0), (start, 1)),
        1: ((add_core, 1), (start, 2), (add_y, 0)),
        2: ((add_core, 2), (start, 3), (add_y, 1), (add_z, 0)),
        3: ((add_core, 3), (start, 4), (add_y, 2), (add_z, 1)),
        4: ((add_core, 4), (start, 5), (add_y, 3), (add_z, 2)),
        5: ((add_core, 5), (start, 6), (add_y, 4), (add_z, 3)),
        6: ((start, 7), (add_y, 5), (add_z, 4)),
        7: ((start, 8), (add_y, 6), (add_z, 5)),
    }
    within = {0: ((add_core, 0),), 5: ((add_core, 6),), 6: ((add_core, 7),), 7: ((add_core, 8),)}

    def run(table):
        for k, steps in table.items():

            @pl.when(step == k)
            def _(steps=steps):
                for do, c in steps:
                    do(c)

    run(before)

    for j, mat in enumerate((query_w, key_w, value_w)):
        flat[:, j * 128 : (j + 1) * 128] = mat[...]

    query_grads = []
    key_rows = []
    value_rows = []
    place_rows = []
    bias_at = pl.ds(pl.multiple_of(head * 128, 128), 128)
    for part, weights_ref, key_start, key_count, place_start in (
        (0, wide, 0, past + HALF, 0),
        (1, near, past, seg_len, past - HALF),
    ):
        at = slice(part * HALF, (part + 1) * HALF)
        keys_at = slice(key_start, key_start + key_count)
        attn = weights_ref[0, 0]
        grad = dout[0, at]
        value_rows.append(dot_tn(grad, attn))
        weights_grad = dot_nt(grad, kv[0, 0, keys_at, 128:256])
        attn = attn.astype(F32)
        row = jnp.sum(weights_grad * attn, axis=1, keepdims=True)
        scores_grad = (attn * (weights_grad - row) * scale).astype(BF16)
        content_grad = dot(scores_grad, kv[0, 0, keys_at, 0:128]).astype(BF16)
        key_rows.append(dot_tn(q[0, 0, at, 0:128], scores_grad))
        by_place = pltpu.roll(dot(flip, scores_grad), 0, 1, stride=1, stride_axis=0).astype(BF16)
        place_grad = dot(by_place, place_keys[0, place_start : place_start + key_count])
        place_grad = dot(flip, place_grad.astype(BF16)).astype(BF16)
        flipped_q = dot(flip, q[0, 0, at, 128:256]).astype(BF16)
        place_rows.append(dot_tn(flipped_q, by_place))
        content_f = content_grad.astype(F32)
        place_f = place_grad.astype(F32)
        small_mine[8:9, bias_at] += jnp.sum(content_f, axis=0, keepdims=True)
        small_mine[9:10, bias_at] += jnp.sum(place_f, axis=0, keepdims=True)
        query_grads.append((content_f + place_f).astype(BF16))

    for j, (wide_rows, near_rows) in enumerate((key_rows, value_rows)):
        at = slice(j * 128, (j + 1) * 128)
        dkv[at, 0:past] = wide_rows[:, 0:past].astype(BF16)
        dkv[at, past : past + HALF] = (wide_rows[:, past:] + near_rows[:, 0:HALF]).astype(BF16)
        dkv[at, past + HALF :] = near_rows[:, HALF:].astype(BF16)
    split = past - HALF
    for at, rows_grad in (
        (slice(0, split), place_rows[0][:, 0:split]),
        (slice(split, None), place_rows[0][:, split:] + place_rows[1]),
    ):
        place_sum[head, :, at] = (
            place_sum[head, :, at].astype(F32) + rows_grad.astype(BF16).astype(F32)
        ).astype(BF16)
    dq = jnp.concatenate(query_grads, axis=0)
    stacked = jnp.concatenate([dq, dkv[:, past:].astype(F32).T.astype(BF16)], axis=1)

    run(within)

    ones = jnp.ones((8, context), BF16)
    sums[head, :, 0:128] += dot(ones[:, 0:seg_len], dq)
    sums[head, :, 128:384] += dot_nt(ones, dkv[...])
    for k in range(width // tile):
        at = slice(k * tile, (k + 1) * tile)
        raw[head, at, 0:128] += dot(xhat_t[0, at, past:], dq)
        raw[head, at, 128:384] += dot_nt(xhat_t[0, at, :], dkv[...])
        input_grad[:, at] += dot_nt(stacked, flat[at, 0:384])

    @pl.when(step >= 4)
    def _():
        place_low = place_sum[head]
        block = tile // (4 * rows)
        total = sums[head, 0:1, :]
        for k in range(width // tile):
            at = slice(k * tile, (k + 1) * tile)
            to = slice(k * block, (k + 1) * block)
            got = raw[head, at, :]
            mats = flat[at, 0:384].astype(F32)
            for acc, term in ((gain_sum, mats * got), (shift_sum, mats * total)):
                acc[at, :] += term[:, 0:128] + term[:, 128:256] + term[:, 256:384]
            grad = (columns[0, at, 0:1] * got + columns[1, at, 0:1] * total).astype(BF16)
            head_grads[head, to, :, :, :, 0:384] = grad.reshape(block, 2, 2, rows, 384)
            grad = dot_nt(table_t[at, :], place_low).astype(BF16)
            head_grads[head, to, :, :, :, 384:512] = grad.reshape(block, 2, 2, rows, 128)

    def own_rows(k):
        gain = jnp.concatenate([params[0:1, :], params[1:2, :]], axis=1)
        at = slice(k * tile, (k + 1) * tile)
        values = segment[0, at].astype(F32)
        mean = jnp.mean(values, axis=-1, keepdims=True)
        centred = values - mean
        rstd = lax.rsqrt(jnp.mean(centred * centred, axis=-1, keepdims=True) + 1e-05)
        return norm_back(centred * rstd, rstd, input_grad[at, :] * gain)

    @pl.when(step == 3)
    def _():
        for k in range(seg_len // tile):
            context_send[k * tile : (k + 1) * tile, :] = own_rows(k).astype(BF16)
        context_pair.start()

    @pl.when(step == 5)
    def _():
        branch_pair.wait_recv()
        load_own.wait()
        for k in range(seg_len // tile):
            at = slice(k * tile, (k + 1) * tile)
            result_out[0, at] = (own_rows_sum[at, :] + branch_land[at, :].astype(F32)).astype(BF16)

    @pl.when(step == 7)
    def _():
        start(9)
        one = jnp.ones((8, 128), F32)
        for acc, row in ((gain_sum, 0), (shift_sum, 2)):
            line = lax.dot_general(
                one,
                acc[...],
                (((1,), (1,)), ((), ())),
                precision=lax.Precision.HIGHEST,
                preferred_element_type=F32,
            )
            small_mine[row : row + 1, :] = line[0:1, 0:LANES]
            small_mine[row + 1 : row + 2, :] = line[0:1, LANES:]

        def to_dp(src, dst, k, index):
            return remote(src, dst, small_send.at[k], small_recv.at[k], index)

        copies = [to_dp(small_mine, small_c.at[1], 0, high * 4 + low * 2 + (1 - core))]
        copies[0].start()
        add_core(9)
        context_pair.wait_recv()
        for k in range(seg_len // tile):
            at = slice(k * tile, (k + 1) * tile)
            segment_out[0, at] = (
                residual_grad[at, :] + own_rows(k) + context_land[at, :].astype(F32)
            ).astype(BF16)
        copies[0].wait_recv()
        small_c[0] = small_mine[...] + small_c[1]
        copies.append(to_dp(small_c.at[0], small_y.at[1], 1, high * 4 + (1 - low) * 2 + core))
        copies[1].start()
        add_y(7)
        add_z(6)
        copies[1].wait_recv()
        small_y[0] = small_c[0] + small_y[1]
        along = []
        for k in range(1, nhi):
            to = lax.rem(high + k, nhi) * 4 + low * 2 + core
            along.append(to_dp(small_y.at[0], small_z.at[k], 2 + k, to))
        for copy in along:
            copy.start()
        add_y(8)
        add_z(7)
        add_y(9)
        for copy in along:
            copy.wait_recv()
        line = small_y[0]
        for k in range(1, nhi):
            line = line + small_z[k]
        small_z[0] = line
        last = pltpu.make_async_remote_copy(
            src_ref=small_z.at[0],
            dst_ref=small_x,
            send_sem=small_send.at[2],
            recv_sem=small_recv.at[2],
            device_id={"head": 1 - x},
            device_id_type=MESH,
        )
        last.start()
        add_z(8)
        add_z(9)
        for b in range(2):
            out_pairs[b].wait_recv()
            out_out[:, b * LANES : (b + 1) * LANES] = out_keep[b] + out_land[b].astype(F32)
        last.wait_recv()
        line = lax.broadcasted_iota(jnp.int32, (SMALL, LANES), 0)
        small_out[...] = small_z[0] + jnp.where(line < 8, small_x[...], 0.0)
        for copy in [context_pair, branch_pair, *out_pairs, *copies, *along, last]:
            copy.wait_send()
        for c in range(count):
            scatter.close(c)


def attention_backward(
    n, dout, kv, q, wide, near, place_keys, xhat_t, mats, table_t, params, segment,
    residual_grad, small_in, own_sum, branch, down, out,
):
    _, seg_len, width = segment.shape
    context = kv.shape[2]
    past = context - seg_len
    rows = width // n
    nhi = n // 4
    half_rows = rows // 2
    seq = lambda t: 1 - t // 4
    head = lambda t: lax.rem(t, 4)
    by_both = lambda t: (head(t), seq(t), 0, 0)
    single = pl.Buffered(1)
    any_spec = pl.BlockSpec(memory_space=pl.ANY)
    dma = pltpu.SemaphoreType.DMA
    f32 = lambda *shape: jax.ShapeDtypeStruct(shape, F32)
    lead = (nhi, 2, 2)
    full = lambda shape: pl.BlockSpec(shape, lambda t: (0,) * len(shape), pipeline_mode=single)
    outs = (
        jax.ShapeDtypeStruct((1, seg_len, width), BF16),
        jax.ShapeDtypeStruct((1, seg_len, width), BF16),
        f32(rows, LANES),
        f32(rows, LANES),
        f32(rows, LANES),
        f32(rows, LANES),
        f32(half_rows, width),
        f32(2 * rows, width),
        f32(SMALL, LANES),
    )
    return pl.pallas_call(
        functools.partial(backward_kernel, n, past, seg_len),
        grid=(8,),
        out_shape=outs,
        in_specs=[
            pl.BlockSpec((1, seg_len, 128), lambda t: (seq(t), 0, head(t))),
            pl.BlockSpec((1, 1, context, 256), by_both),
            pl.BlockSpec((1, 1, seg_len, 256), by_both),
            pl.BlockSpec((1, 1, HALF, past + HALF), by_both),
            pl.BlockSpec((1, 1, HALF, seg_len), by_both),
            pl.BlockSpec((1, past + HALF, 128), lambda t: (head(t), 0, 0)),
            pl.BlockSpec((1, width, context), lambda t: (seq(t), 0, 0), pipeline_mode=single),
            *[pl.BlockSpec((width, 128), lambda t: (0, head(t)))] * 3,
            full(table_t.shape),
            full((SMALL, LANES)),
            pl.BlockSpec((1, seg_len, width), lambda t: (seq(t), 0, 0), pipeline_mode=single),
            full((seg_len, width)),
            full((SMALL, LANES)),
            any_spec,
            any_spec,
            any_spec,
            any_spec,
        ],
        out_specs=tuple(full(o.shape) for o in outs),
        scratch_shapes=[
            pltpu.VMEM((width, 384), BF16),
            pltpu.VMEM((4, width, 384), F32),
            pltpu.VMEM((4, 8, 384), F32),
            pltpu.VMEM((4, 128, past + HALF), BF16),
            pltpu.VMEM((seg_len, width), F32),
            pltpu.VMEM((256, context), BF16),
            pltpu.VMEM((2, width, 128), F32),
            pltpu.VMEM((width, 128), F32),
            pltpu.VMEM((width, 128), F32),
            pltpu.VMEM((4,) + lead + (rows, LANES), BF16),
            pltpu.VMEM((seg_len, width), BF16),
            pltpu.VMEM((seg_len, width), BF16),
            pltpu.VMEM((seg_len, width), BF16),
            pltpu.VMEM((seg_len, width), F32),
            dma(()),
            pltpu.VMEM((2, half_rows, LANES), F32),
            pltpu.VMEM((2, half_rows, LANES), BF16),
            pltpu.VMEM((2, half_rows, LANES), BF16),
            pltpu.VMEM((SMALL, LANES), F32),
            pltpu.VMEM((2, SMALL, LANES), F32),
            pltpu.VMEM((2, SMALL, LANES), F32),
            pltpu.VMEM((nhi, SMALL, LANES), F32),
            pltpu.VMEM((SMALL, LANES), F32),
            dma((4,)),
            dma((4,)),
            dma((2 + nhi,)),
            dma((2 + nhi,)),
        ]
        + Scatter.scratch(10, nhi, rows),
        compiler_params=pltpu.CompilerParams(
            vmem_limit_bytes=VMEM_LIMIT,
            dimension_semantics=("arbitrary",),
            collective_id=1,
            has_side_effects=True,
        ),
        name="attention_backward",
    )(
        dout, kv, q, wide, near, place_keys, xhat_t, *mats, table_t,
        params, segment,
        residual_grad, small_in, own_sum, branch, down, out,
    )


def finish_kernel(n, *refs):
    count = len(refs) // 2
    up, up_out = refs[0], refs[count]
    _, _, half_rows, _ = up.shape
    size = LANES // (n // 4)
    for f in range(4):
        for j in range(n // 4):
            for half in range(2):
                to = ((f * (n // 4) + j) * 2 + half) * size
                up_out[:, to : to + size] = up[half, f, :, j * size : (j + 1) * size]
    for src, dst in zip(refs[1:count], refs[count + 1 :]):
        dst[...] = src[...]


def finish(n, up, others):
    vmem = pl.BlockSpec(memory_space=pltpu.VMEM)
    same = [jax.ShapeDtypeStruct(a.shape, a.dtype) for a in others]
    out = jax.ShapeDtypeStruct((up.shape[2], 8 * LANES), F32)
    return pl.pallas_call(
        functools.partial(finish_kernel, n),
        out_shape=(out, *same),
        in_specs=[vmem] * (1 + len(others)),
        out_specs=(vmem,) * (1 + len(others)),
        compiler_params=pltpu.CompilerParams(vmem_limit_bytes=VMEM_LIMIT),
        name="finish",
    )(up, *others)


def body(
    n,
    segment,
    memory,
    compressed,
    doc_lengths,
    memory_valid,
    query_weight,
    key_weight,
    value_weight,
    position_weight,
    content_bias,
    position_bias,
    output_weight,
    up_weight,
    down_weight,
    compress_weight,
    norm_gain,
    norm_shift,
    post_gain,
    post_shift,
    cotangent,
    compress_cotangent,
):
    x = lax.axis_index("head")
    dp = lax.axis_index("dp")
    first = x == 0
    nhi = n // 4
    width = segment.shape[2]
    seg_len = segment.shape[1]
    past = memory.shape[1] + compressed.shape[1]
    context = past + seg_len
    rows = query_weight.shape[0]
    half_rows = output_weight.shape[0]
    new_count = compress_cotangent.shape[1]
    comp_rows = compress_weight.shape[0]

    def swap(a):
        return lax.ppermute(a, "head", [(0, 1), (1, 0)])

    def pick(a, index):
        return jnp.where(index == 0, a[0], a[1])

    def in_order(own, got, axis):
        return jnp.where(
            first,
            jnp.concatenate([own, got], axis=axis),
            jnp.concatenate([got, own], axis=axis),
        )

    ffr = down_weight.shape[0]
    up_parts = (
        up_weight.reshape(half_rows, 4, n // 4, 2, ffr)
        .transpose(3, 1, 0, 2, 4)
        .reshape(2, 4, half_rows, LANES)
    )
    per = content_bias.shape[1]
    vectors = jnp.stack([norm_gain, norm_shift, post_gain, post_shift])
    here = jnp.arange(2 * n, dtype=jnp.int32)[None, :, None] == dp * 2 + x
    norms = jnp.where(here, vectors[:, None, :], 0).reshape(8, LANES)
    here = jnp.arange(n, dtype=jnp.int32)[None, None, :, None] == dp
    bias = jnp.stack([content_bias, position_bias])[:, :, None, :]
    bias = jnp.where(here, bias, 0).reshape(2, LANES)
    small = jnp.concatenate([norms, bias, jnp.zeros((SMALL - 10, LANES), BF16)])
    pad_rows = -(-new_count // 16) * 16
    comp_cot = jnp.pad(compress_cotangent[0], ((0, pad_rows - new_count), (0, 0)))
    table = position_rows(context, width, past + HALF)

    (
        att, seg_both, cot_other, xhat_t, windows, comp_grads, params, kv, q, wide, near, place_keys,
        query_whole, key_whole, value_whole, _, out_whole, up_whole, down_whole, _, _, _, comp_shard, _,
    ) = attention_forward(
        n, doc_lengths, memory_valid, compressed, memory, segment, cotangent, comp_cot,
        (query_weight, key_weight, value_weight, position_weight),
        output_weight, up_parts, down_weight, compress_weight, small, jnp.asarray(table),
    )

    lead = (nhi, 2, 2)
    (
        own_sum, branch, residual_grad, dout, out_grads, down_grads, small_in, comp_done, up_done,
        comp_whole,
    ) = feed_forward(
        n, att, seg_both, cotangent, cot_other, out_whole.reshape(width, width),
        up_whole.reshape(4, width, LANES), down_whole.reshape(4 * LANES, width), params,
        comp_grads.reshape(lead + (3 * rows, LANES)), comp_shard,
    )

    made = jnp.einsum(
        "kic,kcd->id", windows, comp_whole.reshape(3, width, LANES), preferred_element_type=F32
    ).astype(BF16)
    made = in_order(made[:new_count], swap(made[pad_rows : pad_rows + new_count]), 1)

    mats = [w.reshape(width, LANES) for w in (query_whole, key_whole, value_whole)]
    result, segment_grad, *matrices, small_done = attention_backward(
        n, dout, kv, q, wide, near, place_keys, xhat_t, mats, jnp.asarray(table.T.copy()),
        params, seg_both, residual_grad, small_in, own_sum, branch,
        down_grads.reshape(lead + (2 * rows, 2 * LANES)),
        out_grads.reshape(lead + (rows, 2 * LANES)),
    )

    up_final, result, segment_grad, *matrices, comp_final = finish(
        n, up_done, (result, segment_grad, *matrices, comp_done)
    )
    query_final, key_final, value_final, place_final, out_final, down_final = matrices
    vectors = lax.dynamic_slice_in_dim(
        small_done[0:8].reshape(4, width), (dp * 2 + x) * half_rows, half_rows, 1
    )
    biases = lax.dynamic_slice_in_dim(small_done[8:10].reshape(2, 4, 128), dp * per, per, 2)
    return (
        result,
        made[None],
        segment_grad,
        query_final,
        key_final,
        value_final,
        place_final,
        biases[0],
        biases[1],
        out_final,
        up_final,
        down_final,
        comp_final,
        vectors[0],
        vectors[1],
        vectors[2],
        vectors[3],
    )


def solution(mesh):
    split = P(("dp", "head"))
    wide = P(("dp", "head"), None)
    deep = P(("dp", "head"), None, None)
    return jax.shard_map(
        functools.partial(body, mesh.shape["dp"]),
        mesh=mesh,
        in_specs=(
            deep,
            P("dp", None, None),
            P("dp", None, None),
            P("dp", None),
            P("dp"),
            P("dp", "head"),
            P("dp", "head"),
            P("dp", "head"),
            P("dp", "head"),
            P("head", "dp"),
            P("head", "dp"),
            wide,
            wide,
            wide,
            wide,
            split,
            split,
            split,
            split,
            deep,
            deep,
        ),
        out_specs=(
            deep,
            deep,
            deep,
            P("dp", "head"),
            P("dp", "head"),
            P("dp", "head"),
            P("dp", "head"),
            P("head", "dp"),
            P("head", "dp"),
            wide,
            wide,
            wide,
            wide,
            split,
            split,
            split,
            split,
        ),
        check_vma=False,
    )
```

```python
import functools
import math

import jax
import jax.numpy as jnp
import numpy as np
from jax import lax
from jax.experimental import pallas as pl
from jax.experimental.pallas import tpu as pltpu
from jax.sharding import PartitionSpec as P

F32 = jnp.float32
BF16 = jnp.bfloat16
MESH = pl.DeviceIdType.MESH
VMEM_LIMIT = 62 * 1024 * 1024
HALF = 256
LANES = 512
SMALL = 16


def dot(a, b):
    return lax.dot_general(a, b, (((1,), (0,)), ((), ())), preferred_element_type=F32)


def dot_nt(a, b):
    return lax.dot_general(a, b, (((1,), (1,)), ((), ())), preferred_element_type=F32)


def dot_tn(a, b):
    return lax.dot_general(a, b, (((0,), (0,)), ((), ())), preferred_element_type=F32)


def position_rows(context, width, used):
    distance = np.arange(context, dtype=np.float32)[:, None]
    frequency = np.exp(
        np.arange(width // 2, dtype=np.float32) * np.float32(-2.0 * math.log(10000.0) / width)
    )
    phases = distance * frequency[None, :].astype(np.float32)
    table = np.concatenate([np.sin(phases), np.cos(phases)], axis=1)
    return table[::-1][context - used :].astype(jnp.bfloat16)


def place(n):
    me = lax.axis_index("dp")
    core = lax.rem(me, 2)
    low = lax.rem(me // 2, 2)
    high = me // 4
    return core, low, high, n // 4


def meet(core, low, high, nhi, more=0):
    barrier = pltpu.get_barrier_semaphore()

    def tell(index):
        pl.semaphore_signal(barrier, inc=1, device_id={"dp": index}, device_id_type=MESH)

    for k in range(1, nhi):
        tell(lax.rem(high + k, nhi) * 4 + low * 2 + core)
    tell(high * 4 + (1 - low) * 2 + core)
    tell(high * 4 + low * 2 + (1 - core))
    pl.semaphore_wait(barrier, nhi + 1 + more)


def remote(src, dst, send, recv, index):
    return pltpu.make_async_remote_copy(
        src_ref=src,
        dst_ref=dst,
        send_sem=send,
        recv_sem=recv,
        device_id={"dp": index},
        device_id_type=MESH,
    )


class Gather:
    def __init__(self, n, pairs, sems):
        self.core, self.low, self.high, self.nhi = place(n)
        self.pairs = pairs
        (self.zs, self.zr, self.ys, self.yr, self.cs, self.cr, self.own) = sems
        order = sorted(range(1, self.nhi), key=lambda k: (min(k, self.nhi - k), k))
        self.order = order

    def z_copy(self, c, k):
        shard, whole = self.pairs[c]
        return remote(
            shard,
            whole.at[self.high, self.low, self.core],
            self.zs.at[c, k],
            self.zr.at[c, k],
            lax.rem(self.high + k, self.nhi) * 4 + self.low * 2 + self.core,
        )

    def own_copy(self, c):
        shard, whole = self.pairs[c]
        return pltpu.make_async_copy(
            shard, whole.at[self.high, self.low, self.core], self.own.at[c]
        )

    def y_copy(self, c, k):
        shard, whole = self.pairs[c]
        at = whole.at[lax.rem(self.high + k, self.nhi), self.low, self.core]
        return remote(
            shard if k == 0 else at,
            at,
            self.ys.at[c, k],
            self.yr.at[c, k],
            self.high * 4 + (1 - self.low) * 2 + self.core,
        )

    def c_copy(self, c):
        _, whole = self.pairs[c]
        part = whole.at[:, :, self.core]
        return remote(
            part,
            part,
            self.cs.at[c],
            self.cr.at[c],
            self.high * 4 + self.low * 2 + (1 - self.core),
        )

    def start(self, c):
        for k in self.order:
            self.z_copy(c, k).start()
        self.y_copy(c, 0).start()
        self.own_copy(c).start()

    def pass_y(self, c):
        for k in self.order:
            self.z_copy(c, self.nhi - k).wait_recv()
            self.y_copy(c, k).start()

    def pass_core(self, c):
        self.own_copy(c).wait()
        for k in range(self.nhi):
            self.y_copy(c, k).wait_recv()
        self.c_copy(c).start()

    def arrive(self, c):
        self.c_copy(c).wait_recv()

    def close(self, c):
        for k in self.order:
            self.z_copy(c, k).wait_send()
        for k in range(self.nhi):
            self.y_copy(c, k).wait_send()
        self.c_copy(c).wait_send()

    @staticmethod
    def semaphores(count, nhi):
        dma = pltpu.SemaphoreType.DMA
        return [dma((count, nhi))] * 4 + [dma((count,))] * 3


class Scatter:
    def __init__(self, n, items, mine, mine_sem, sems):
        self.core, self.low, self.high, self.nhi = place(n)
        self.items = items
        self.mine, self.mine_sem = mine, mine_sem
        (self.cs, self.cr, self.ys, self.yr, self.zs, self.zr) = sems

    def c_copy(self, c):
        return remote(
            self.items[c][0].at[:, :, 1 - self.core],
            self.items[c][2],
            self.cs.at[c],
            self.cr.at[c],
            self.high * 4 + self.low * 2 + (1 - self.core),
        )

    def mine_copy(self, c):
        slot = c % 2
        return pltpu.make_async_copy(
            self.items[c][0].at[:, :, self.core], self.mine.at[slot], self.mine_sem.at[slot]
        )

    def y_copy(self, c):
        return remote(
            self.items[c][2].at[:, 1 - self.low],
            self.items[c][3],
            self.ys.at[c],
            self.yr.at[c],
            self.high * 4 + (1 - self.low) * 2 + self.core,
        )

    def z_copies(self, c):
        return [
            remote(
                self.items[c][3].at[lax.rem(self.high + k, self.nhi)],
                self.items[c][4].at[k - 1],
                self.zs.at[c, k - 1],
                self.zr.at[c, k - 1],
                lax.rem(self.high + k, self.nhi) * 4 + self.low * 2 + self.core,
            )
            for k in range(1, self.nhi)
        ]

    def start(self, c):
        self.c_copy(c).start()
        if not self.items[c][1]:
            self.mine_copy(c).start()

    def add_core(self, c):
        here = self.items[c][1]
        if not here:
            self.mine_copy(c).wait()
        self.c_copy(c).wait_recv()
        land = self.items[c][2]

        def body(i, carry):
            for j in range(2):
                own = self.items[c][0][i, j, self.core] if here else self.mine[c % 2, i, j]
                land[i, j] = land[i, j] + own
            return carry

        lax.fori_loop(0, self.nhi, body, 0)
        self.y_copy(c).start()

    def add_y(self, c):
        self.y_copy(c).wait_recv()
        src, land = self.items[c][2], self.items[c][3]

        def body(i, carry):
            land[i] = land[i] + src[i, self.low]
            return carry

        lax.fori_loop(0, self.nhi, body, 0)
        for copy in self.z_copies(c):
            copy.start()

    def add_z(self, c):
        for copy in self.z_copies(c):
            copy.wait_recv()
        land, last, done = self.items[c][3:]
        total = land[self.high].astype(F32)
        for k in range(self.nhi - 1):
            total = total + last[k].astype(F32)
        done(total)

    def tick(self, t):
        count = len(self.items)
        if 0 <= t - 1 < count:
            self.add_core(t - 1)
        if t < count:
            self.start(t)
        if 0 <= t - 2 < count:
            self.add_y(t - 2)
        if 0 <= t - 3 < count:
            self.add_z(t - 3)

    def close(self, c):
        self.c_copy(c).wait_send()
        self.y_copy(c).wait_send()
        for copy in self.z_copies(c):
            copy.wait_send()

    @staticmethod
    def scratch(count, nhi, rows):
        dma = pltpu.SemaphoreType.DMA
        return [
            pltpu.VMEM((count, nhi, 2, rows, LANES), BF16),
            pltpu.VMEM((count, nhi, rows, LANES), BF16),
            pltpu.VMEM((count, nhi - 1, rows, LANES), BF16),
            pltpu.VMEM((2, nhi, 2, rows, LANES), BF16),
            dma((2,)),
            dma((count,)),
            dma((count,)),
            dma((count,)),
            dma((count,)),
            dma((count, nhi - 1)),
            dma((count, nhi - 1)),
        ]


def norm_rows(values):
    mean = jnp.mean(values, axis=-1, keepdims=True)
    centred = values - mean
    variance = jnp.mean(centred * centred, axis=-1, keepdims=True)
    return centred * lax.rsqrt(variance + 1e-05)


def attend_rows(query_content, query_place, keys, place_keys, first_seen, last_seen, scale):
    width = keys.shape[0]
    content = dot_nt(query_content, keys)
    by_place = pltpu.roll(
        dot_nt(query_place, place_keys), width - (HALF - 1), 1, stride=1, stride_axis=0
    )
    column = lax.broadcasted_iota(jnp.int32, (HALF, width), 1)
    seen = (column >= first_seen) & (column <= last_seen)
    scores = jnp.where(seen, (content + by_place) * (scale * math.log2(math.e)), -1e30)
    top = jnp.max(scores, axis=1, keepdims=True)
    expo = jnp.exp2(scores - top)
    return expo * (1.0 / jnp.sum(expo, axis=1, keepdims=True))


def forward_kernel(
    n,
    past,
    seg_len,
    docs,
    valid,
    compressed,
    memory,
    segment,
    cotangent,
    comp_cot,
    query_w,
    key_w,
    value_w,
    place_w,
    out_w,
    up_parts,
    down_w,
    comp_w,
    small,
    table,
    attended,
    seg_other,
    cot_other,
    xhat_hbm,
    windows_hbm,
    comp_grads_hbm,
    comp_shard_hbm,
    params,
    kv_out,
    q_out,
    wide_out,
    near_out,
    place_out,
    query_whole,
    key_whole,
    value_whole,
    place_whole,
    out_whole,
    up_whole,
    down_whole,
    small_whole,
    out_shard,
    up_shard,
    comp_shard,
    small_shard,
    normed,
    xhat_out,
    memory_f,
    windows,
    comp_rows_cot,
    comp_grads,
    past_rows,
    seg_rows,
    flat,
    small_rows,
    att,
    load_sem,
    flat_sem,
    own_sem,
    store_sem,
    pair_send,
    pair_recv,
    att_own,
    att_send,
    att_recv,
    *sems,
):
    step = pl.program_id(0)
    x = lax.axis_index("head")
    core, low, high, nhi = place(n)
    tile = 256
    width = normed.shape[2]
    context = past + seg_len
    head = jnp.maximum(step - 2, 0) // 2
    half = comp_w.shape[1] // 2

    items = [(small_shard, small_whole)]
    items += [(query_w, query_whole), (key_w, key_whole), (value_w, value_whole), (place_w, place_whole)]
    for b in range(2):
        to = pl.ds(b * LANES, LANES)
        items.append((out_shard.at[:, :, to], out_whole.at[:, :, :, :, :, to]))
    items += [(up_shard.at[f], up_whole.at[f]) for f in range(4)]
    mid = down_w.shape[0] // 2
    for part in range(2):
        for b in range(2):
            at, to = pl.ds(part * mid, mid), pl.ds(b * LANES, LANES)
            items.append((down_w.at[at, to], down_whole.at[:, :, :, at, to]))
    gather = Gather(n, items, sems)
    count = len(items)
    needs = {5: 1, 7: 2}
    pad_rows = comp_cot.shape[0]

    def pair(src, dst, k):
        return pltpu.make_async_remote_copy(
            src_ref=src,
            dst_ref=dst,
            send_sem=pair_send.at[k],
            recv_sem=pair_recv.at[k],
            device_id={"head": 1 - x},
            device_id_type=MESH,
        )

    mine_at = pl.ds(pl.multiple_of(x * half, half), half)
    other_at = pl.ds(pl.multiple_of((1 - x) * half, half), half)
    pairs = [
        pair(small, small_shard.at[x], 0),
        pair(out_w, out_shard.at[x], 1),
        pair(up_parts.at[1 - x], up_shard.at[:, x], 2),
        pair(comp_w.at[:, other_at], comp_shard.at[x], 3),
        pair(segment.at[0], seg_other, 4),
        pair(cotangent.at[0], cot_other, 5),
        pair(comp_cot.at[:, other_at], comp_rows_cot.at[1], 6),
    ]
    owns = [
        pltpu.make_async_copy(small, small_shard.at[x], own_sem.at[0]),
        pltpu.make_async_copy(out_w, out_shard.at[x], own_sem.at[1]),
        pltpu.make_async_copy(up_parts.at[x], up_shard.at[:, x], own_sem.at[2]),
        pltpu.make_async_copy(comp_w.at[:, mine_at], comp_shard.at[x], own_sem.at[3]),
        pltpu.make_async_copy(comp_cot.at[:, mine_at], comp_rows_cot.at[0], own_sem.at[4]),
    ]
    loads = []
    for i in range(2):
        s = lax.rem(x + i, 2)
        loads.append(pltpu.make_async_copy(compressed.at[s], past_rows.at[i, 0], load_sem.at[i, 0]))
        loads.append(pltpu.make_async_copy(memory.at[s], past_rows.at[i, 1], load_sem.at[i, 1]))
    loads.append(pltpu.make_async_copy(segment.at[0], seg_rows.at[0], load_sem.at[0, 2]))
    load_other = pltpu.make_async_copy(seg_other, seg_rows.at[1], load_sem.at[1, 2])
    store_xhat = pltpu.make_async_copy(xhat_out, xhat_hbm, store_sem.at[0])
    store_windows = pltpu.make_async_copy(windows, windows_hbm, store_sem.at[1])
    store_grads = pltpu.make_async_copy(comp_grads, comp_grads_hbm, store_sem.at[2])
    store_shard = pltpu.make_async_copy(comp_shard, comp_shard_hbm, store_sem.at[3])

    joined = set()

    def join(k):
        if k not in joined:
            joined.add(k)
            owns[k].wait()
            pairs[k].wait_recv()

    def tick(t):
        lead = t + 3
        if lead < count:
            if lead in needs:
                join(needs[lead])
            gather.start(lead)
        if t < count:
            gather.pass_y(t)
        if 0 <= t - 1 < count:
            gather.pass_core(t - 1)
        if 0 <= t - 2 < count:
            gather.arrive(t - 2)

    def flat_copies(h, slot):
        at = pl.ds(h * 128, 128)
        return [
            pltpu.make_async_copy(
                whole.at[:, :, :, :, at],
                flat.at[slot, :, :, :, :, pl.ds(j * 128, 128)],
                flat_sem.at[slot, j],
            )
            for j, whole in enumerate((query_whole, key_whole, value_whole, place_whole))
        ]

    def norm_into(i, values, at):
        eye = (
            lax.broadcasted_iota(jnp.int32, (tile, tile), 0)
            == lax.broadcasted_iota(jnp.int32, (tile, tile), 1)
        ).astype(BF16)
        gain = jnp.concatenate([params[0:1, :], params[1:2, :]], axis=1)
        shift = jnp.concatenate([params[2:3, :], params[3:4, :]], axis=1)
        xhat = norm_rows(values.astype(F32))
        normed[i, pl.ds(at, tile)] = (xhat * gain + shift).astype(BF16)
        xhat = xhat.astype(BF16)
        for b in range(width // tile):
            xhat_out[i, b * tile : (b + 1) * tile, pl.ds(at, tile)] = dot_nt(
                eye, xhat[:, b * tile : (b + 1) * tile]
            ).astype(BF16)

    def norm_past(i):
        per = past // 2 // tile

        def one(k, carry):
            at = pl.multiple_of(k * tile, tile)
            inner = pl.multiple_of(lax.rem(k, per) * tile, tile)
            norm_into(i, past_rows[i, k // per, pl.ds(inner, tile)], at)
            return carry

        lax.fori_loop(0, past // tile, one, 0)

    def norm_segment(i):
        def one(k, carry):
            at = pl.multiple_of(k * tile, tile)
            norm_into(i, seg_rows[i, pl.ds(at, tile)], past + at)
            return carry

        lax.fori_loop(0, seg_len // tile, one, 0)

    @pl.when(step == 0)
    def _():
        barrier = pltpu.get_barrier_semaphore()
        pl.semaphore_signal(
            barrier, inc=1, device_id={"head": 1 - x}, device_id_type=MESH
        )
        meet(core, low, high, nhi, 1)
        for k in (0, 1, 2, 6, 3, 4, 5):
            pairs[k].start()
        for copy in owns:
            copy.start()
        for copy in loads:
            copy.start()
        gather.start(1)
        join(0)
        gather.start(0)
        gather.start(2)
        tick(0)
        tick(1)
        tick(2)
        summed = pltpu.make_async_copy(small_whole, small_rows, load_sem.at[0, 3])
        summed.start()
        summed.wait()
        both = jnp.sum(small_rows[...].reshape(n, 2, SMALL, LANES).astype(F32), axis=0)
        row = lax.broadcasted_iota(jnp.int32, (SMALL, LANES), 0)
        by_head = jnp.where(x == 0, both[0], both[1])
        params[...] = jnp.where(row < 8, both[0] + both[1], by_head)
        for copy in (loads[0], loads[1], loads[4]):
            copy.wait()
        norm_past(0)
        tick(3)
        norm_segment(0)
        tick(4)

    @pl.when(step == 1)
    def _():
        for copy in loads[2:4]:
            copy.wait()
        norm_past(1)
        tick(5)
        memory_f[:, past // 2 :, :] = jnp.zeros((width // 128, 16, 128), F32)
        for i in range(2):
            for b in range(width // 128):
                at = slice(b * 128, (b + 1) * 128)
                memory_f[b, 0 : past // 2, :] = past_rows[i, 1, :, at].astype(F32)
                for tap in range(3):
                    windows[tap, i * pad_rows : (i + 1) * pad_rows, at] = memory_f[
                        b, pl.ds(tap, pad_rows, stride=3), :
                    ].astype(BF16)
        store_windows.start()
        owns[4].wait()
        pairs[6].wait_recv()
        tick(6)
        for copy in flat_copies(0, 0):
            copy.start()
        comp_rows_both = comp_rows_cot[...].reshape(2 * pad_rows, LANES)
        for tap in range(3):
            for k in range(width // tile):
                at = slice(k * tile, (k + 1) * tile)
                comp_grads[tap * width + k * tile : tap * width + (k + 1) * tile, :] = dot_tn(
                    windows[tap, :, at], comp_rows_both
                ).astype(BF16)
        store_grads.start()

    for k in range(2, 10):

        @pl.when(step == k)
        def _(k=k):
            tick(k + 5)
            h, slot = (k - 2) // 2, ((k - 2) // 2) % 2
            if k % 2 == 0:
                for copy in flat_copies(h, slot):
                    copy.wait()
                if h < 3:
                    for copy in flat_copies(h + 1, 1 - slot):
                        copy.start()
            if k == 3:
                pairs[4].wait_recv()
                load_other.start()
                load_other.wait()
                norm_segment(1)
                store_xhat.start()
                join(3)
                store_shard.start()

    def att_pair(h, i):
        at = pl.ds(pl.multiple_of(x * LANES + h * 128, 128), 128)
        return pltpu.make_async_remote_copy(
            src_ref=att.at[h, i],
            dst_ref=attended.at[1 - i, :, at],
            send_sem=att_send.at[h, i],
            recv_sem=att_recv.at[h, i],
            device_id={"head": 1 - x},
            device_id_type=MESH,
        )

    def att_local(h, i):
        at = pl.ds(pl.multiple_of(x * LANES + h * 128, 128), 128)
        return pltpu.make_async_copy(att.at[h, i], attended.at[i, :, at], att_own.at[h, i])

    @pl.when(step >= 2)
    def _():
        i = lax.rem(step, 2)
        s = lax.rem(x + i, 2)
        slot = lax.rem(head, 2)

        def weights(a, b):
            return flat[slot, :, :, :, :, a:b].reshape(width, b - a)

        @pl.when(i == 0)
        def _():
            mat = weights(384, 512)
            for k in range(table.shape[0] // tile):
                place_out[0, k * tile : (k + 1) * tile] = dot(
                    table[k * tile : (k + 1) * tile], mat
                ).astype(BF16)

        mat = weights(128, 384)
        for k in range(context // tile):
            kv_out[0, 0, k * tile : (k + 1) * tile] = dot(
                normed[i, pl.ds(k * tile, tile)], mat
            ).astype(BF16)
        mat = weights(0, 128)
        bias_at = pl.ds(pl.multiple_of(head * 128, 128), 128)
        for k in range(seg_len // tile):
            queries = dot(normed[i, pl.ds(past + k * tile, tile)], mat)
            at = slice(k * tile, (k + 1) * tile)
            q_out[0, 0, at, 0:128] = (queries + params[8:9, bias_at]).astype(BF16)
            q_out[0, 0, at, 128:256] = (queries + params[9:10, bias_at]).astype(BF16)

        scale = 1.0 / math.sqrt(128)
        for part, out, key_start, key_count, place_start in (
            (0, wide_out, 0, past + HALF, 0),
            (1, near_out, past, seg_len, past - HALF),
        ):
            token = lax.broadcasted_iota(jnp.int32, (HALF, 1), 0) + part * HALF
            end, first = 0, past - valid[s]
            for doc in range(3):
                end = end + docs[s, doc]
                first = jnp.where(token >= end, past + end, first)
            at = slice(part * HALF, (part + 1) * HALF)
            weights_low = attend_rows(
                q_out[0, 0, at, 0:128],
                q_out[0, 0, at, 128:256],
                kv_out[0, 0, key_start : key_start + key_count, 0:128],
                place_out[0, place_start : place_start + key_count],
                first - key_start,
                token + (past - key_start),
                scale,
            ).astype(BF16)
            out[0, 0] = weights_low
            att[head, i, at] = dot(
                weights_low, kv_out[0, 0, key_start : key_start + key_count, 128:256]
            ).astype(BF16)
        att_pair(head, i).start()
        att_local(head, i).start()

    @pl.when(step == pl.num_programs(0) - 1)
    def _():
        for t in range(15, count + 2):
            tick(t)
        for copy in (store_xhat, store_windows, store_grads, store_shard):
            copy.wait()
        for h in range(4):
            for i in range(2):
                att_local(h, i).wait()
                att_pair(h, i).wait()
        for copy in pairs:
            copy.wait_send()
        pairs[5].wait_recv()
        for c in range(count):
            gather.close(c)


def attention_forward(
    n, docs, valid, compressed, memory, segment, cotangent, comp_cot, mats, out_w, up_parts, down_w,
    comp_w, small, table,
):
    _, seg_len, width = segment.shape
    past = compressed.shape[1] + memory.shape[1]
    context = past + seg_len
    nhi = n // 4
    lead = (nhi, 2, 2)
    half_rows = out_w.shape[0]
    comp_rows = comp_w.shape[0]
    pad_rows = comp_cot.shape[0]
    any_spec = pl.BlockSpec(memory_space=pl.ANY)
    smem = pl.BlockSpec(memory_space=pltpu.SMEM)
    single = pl.Buffered(1)
    bf = lambda *shape: jax.ShapeDtypeStruct(shape, BF16)
    head = lambda t: jnp.maximum(t - 2, 0) // 2
    which = lambda t: lax.rem(jnp.maximum(t, 2), 2)
    by_both = lambda t: (head(t), which(t), 0, 0)
    dma = pltpu.SemaphoreType.DMA
    full = lambda shape: pl.BlockSpec(shape, lambda t: (0,) * len(shape), pipeline_mode=single)
    count = 15
    return pl.pallas_call(
        functools.partial(forward_kernel, n, past, seg_len),
        grid=(10,),
        out_shape=(
            bf(2, seg_len, width),
            bf(seg_len, width),
            bf(seg_len, width),
            bf(2, width, context),
            bf(3, 2 * pad_rows, width),
            bf(3 * width, LANES),
            bf(2, comp_rows, LANES),
            jax.ShapeDtypeStruct((SMALL, LANES), F32),
            bf(4, 2, context, 256),
            bf(4, 2, seg_len, 256),
            bf(4, 2, HALF, past + HALF),
            bf(4, 2, HALF, seg_len),
            bf(4, past + HALF, 128),
            *[bf(*lead, *w.shape) for w in mats],
            bf(*lead, 2, half_rows, width),
            bf(4, *lead, 2, half_rows, LANES),
            bf(*lead, *down_w.shape),
            bf(*lead, 2, SMALL, LANES),
        ),
        in_specs=[smem, smem]
        + [any_spec] * 5
        + [full(a.shape) for a in (*mats, out_w, up_parts, down_w, comp_w, small)]
        + [pl.BlockSpec(table.shape, lambda t: (0, 0), pipeline_mode=single)],
        out_specs=(
            *[any_spec] * 6,
            any_spec,
            pl.BlockSpec((SMALL, LANES), lambda t: (0, 0)),
            pl.BlockSpec((1, 1, context, 256), by_both),
            pl.BlockSpec((1, 1, seg_len, 256), by_both),
            pl.BlockSpec((1, 1, HALF, past + HALF), by_both),
            pl.BlockSpec((1, 1, HALF, seg_len), by_both),
            pl.BlockSpec((1, past + HALF, 128), lambda t: (head(t), 0, 0)),
            *[any_spec] * 8,
        ),
        scratch_shapes=[
            pltpu.VMEM((2, half_rows, width), BF16),
            pltpu.VMEM((4, 2, half_rows, LANES), BF16),
            pltpu.VMEM((2, comp_rows, LANES), BF16),
            pltpu.VMEM((2, SMALL, LANES), BF16),
            pltpu.VMEM((2, context, width), BF16),
            pltpu.VMEM((2, width, context), BF16),
            pltpu.VMEM((width // 128, past // 2 + 16, 128), F32),
            pltpu.VMEM((3, 2 * pad_rows, width), BF16),
            pltpu.VMEM((2, pad_rows, LANES), BF16),
            pltpu.VMEM((3 * width, LANES), BF16),
            pltpu.VMEM((2, 2, past // 2, width), BF16),
            pltpu.VMEM((2, seg_len, width), BF16),
            pltpu.VMEM((2,) + lead + (mats[0].shape[0], LANES), BF16),
            pltpu.VMEM(lead + (2, SMALL, LANES), BF16),
            pltpu.VMEM((4, 2, seg_len, 128), BF16),
            dma((2, 4)),
            dma((2, 4)),
            dma((6,)),
            dma((4,)),
            dma((7,)),
            dma((7,)),
            dma((4, 2)),
            dma((4, 2)),
            dma((4, 2)),
        ]
        + Gather.semaphores(count, nhi),
        compiler_params=pltpu.CompilerParams(
            vmem_limit_bytes=VMEM_LIMIT,
            dimension_semantics=("arbitrary",),
            collective_id=0,
            has_side_effects=True,
        ),
        name="attention_forward",
    )(
        docs, valid, compressed, memory, segment, cotangent, comp_cot, *mats, out_w, up_parts, down_w,
        comp_w, small, table,
    )


def gelu_parts(v):
    c = math.sqrt(2.0 / math.pi)
    square = v * v
    t = jnp.tanh(c * (v + 0.044715 * square * v))
    half = 0.5 * (1.0 + t)
    value = v * half
    return value, half + value * (1.0 - half) * (2 * c + (6 * 0.044715 * c) * square)


def feed_kernel(
    n,
    att_in,
    segment,
    seg_other,
    cotangent,
    cot_other,
    out_in,
    up_in,
    down_in,
    params,
    comp,
    comp_shard,
    own_out,
    branch_out,
    residual_out,
    dout,
    out_grads,
    down_grads,
    small_out,
    comp_out,
    up_out,
    comp_whole,
    att,
    seg,
    cot,
    out_w,
    up,
    down,
    residual,
    low,
    low_t,
    act,
    pre,
    branch,
    terms,
    terms_land,
    cast,
    up_grads,
    mixed,
    stage,
    up_send,
    up_land,
    comp_stage,
    comp_send,
    comp_land,
    load_sem,
    store_sem,
    stage_sem,
    pair_send,
    pair_recv,
    land_c,
    land_y,
    land_z,
    mine,
    mine_sem,
    *sems,
):
    sems, gather_sems = sems[:6], sems[6:]
    x = lax.axis_index("head")
    core, low_y, high, nhi = place(n)
    tile = 256
    _, seg_len, width = att.shape
    rows = width // n
    half_rows = rows // 2
    comp_rows = comp_send.shape[0]

    def pair(src, dst, k):
        return pltpu.make_async_remote_copy(
            src_ref=src,
            dst_ref=dst,
            send_sem=pair_send.at[k],
            recv_sem=pair_recv.at[k],
            device_id={"head": 1 - x},
            device_id_type=MESH,
        )

    terms_pair = pair(cast.at[0], terms_land, 0)
    mixed_pair = pair(mixed.at[1 - x], dout.at[1], 1)
    comp_pair = pair(comp_send, comp_land, 2)
    up_pairs = [pair(up_send.at[f], up_land.at[f], 3 + f) for f in range(4)]
    scatter = Scatter(
        n,
        [
            (part, here, land_c.at[c], land_y.at[c], land_z.at[c], done)
            for c, (part, here, done) in enumerate(
                [
                    (
                        comp.at[:, :, :, pl.ds(m * rows, rows)],
                        False,
                        comp_block(m, x, rows, comp_stage, comp_out, comp_send, comp_pair),
                    )
                    for m in range(3)
                ]
                + [
                    (up_grads.at[f], True, up_block(f, x, up_out, up_send, up_pairs[f]))
                    for f in range(4)
                ]
            )
        ],
        mine,
        mine_sem,
        sems,
    )

    third = comp_rows // 3
    gather = Gather(
        n,
        [
            (
                comp_shard.at[:, pl.ds(m * third, third)],
                comp_whole.at[:, :, :, :, pl.ds(m * third, third)],
            )
            for m in range(3)
        ],
        gather_sems,
    )

    def load(src, dst, k):
        return pltpu.make_async_copy(src, dst, load_sem.at[k])

    loads = {
        "att1": load(att_in.at[1], att.at[1], 0),
        "out": load(out_in, out_w, 1),
        "seg1": load(seg_other, seg.at[1], 2),
        "cot1": load(cot_other, cot.at[1], 3),
        "up": load(up_in, up, 4),
        "down": load(down_in, down, 5),
        "att0": load(att_in.at[0], att.at[0], 6),
        "seg0": load(segment.at[0], seg.at[0], 7),
        "cot0": load(cotangent.at[0], cot.at[0], 8),
    }
    for copy in loads.values():
        copy.start()
    barrier = pltpu.get_barrier_semaphore()
    pl.semaphore_signal(barrier, inc=1, device_id={"head": 1 - x}, device_id_type=MESH)
    meet(core, low_y, high, nhi, 1)
    scatter.start(0)
    scatter.start(1)
    gather.start(0)

    eye = (
        lax.broadcasted_iota(jnp.int32, (tile, tile), 0)
        == lax.broadcasted_iota(jnp.int32, (tile, tile), 1)
    ).astype(BF16)
    gain = jnp.concatenate([params[4:5, :], params[5:6, :]], axis=1)
    shift = jnp.concatenate([params[6:7, :], params[7:8, :]], axis=1)

    def project(i):
        for k in range(seg_len // tile):
            at = slice(k * tile, (k + 1) * tile)
            whole_at = slice(i * seg_len + k * tile, i * seg_len + (k + 1) * tile)
            value = seg[i, at].astype(F32) + dot(att[i, at], out_w[...])
            residual[at, :] = value
            value = (norm_rows(value) * gain + shift).astype(BF16)
            low[whole_at, :] = value
            for b in range(width // tile):
                low_t[b * tile : (b + 1) * tile, whole_at] = dot_nt(
                    eye, value[:, b * tile : (b + 1) * tile]
                ).astype(BF16)

    def hidden(i, between):
        whole_at = slice(i * seg_len, (i + 1) * seg_len)
        branch[...] = jnp.zeros_like(branch)
        terms[...] = jnp.zeros_like(terms)

        def one(f, carry):
            down_at = pl.ds(pl.multiple_of(f * LANES, LANES), LANES)
            value, slope = gelu_parts(dot(low[whole_at, :], up[f]))
            value = value.astype(BF16)
            act[f, whole_at, :] = value
            back = dot_nt(cot[i], down[down_at, :]).astype(BF16).astype(F32)
            back = (back * slope).astype(BF16)
            pre[f, whole_at, :] = back
            branch[...] += dot(value, down[down_at, :])
            terms[...] += dot_nt(back, up[f])
            for k, steps in enumerate(between):

                @pl.when(f == k)
                def _(steps=steps):
                    for run, c in steps:
                        run(c)

            return carry

        lax.fori_loop(0, 4, one, 0)

    for name in ("att1", "out", "seg1"):
        loads[name].wait()
    project(1)
    scatter.add_core(0)
    scatter.start(2)
    gather.start(1)
    for name in ("cot1", "up", "down"):
        loads[name].wait()
    hidden(
        1,
        (
            ((scatter.add_core, 1), (gather.pass_y, 0)),
            ((scatter.add_core, 2), (scatter.add_y, 0), (gather.start, 2)),
            ((gather.pass_y, 1),),
            ((scatter.add_y, 1),),
        ),
    )
    cast[0] = terms[...].astype(BF16)
    terms_pair.start()
    cast[1] = branch[...].astype(BF16)
    store_branch = pltpu.make_async_copy(cast.at[1], branch_out, store_sem.at[0])
    store_branch.start()
    for name in ("att0", "seg0", "cot0"):
        loads[name].wait()
    project(0)
    scatter.add_z(0)
    hidden(
        0,
        (
            ((gather.pass_core, 0),),
            ((gather.pass_y, 2),),
            ((scatter.add_y, 2),),
            ((scatter.add_z, 1),),
        ),
    )
    branch[...] += residual[...]
    store_own = pltpu.make_async_copy(branch, own_out, store_sem.at[1])
    store_own.start()

    block = tile // (4 * rows)

    def up_grad(f):
        for k in range(width // tile):
            grad = dot(low_t[k * tile : (k + 1) * tile, :], pre[f]).astype(BF16)
            up_grads[f, k * block : (k + 1) * block] = grad.reshape(block, 2, 2, rows, LANES)
        scatter.start(3 + f)

    up_grad(0)
    gather.pass_core(1)
    up_grad(1)
    scatter.add_core(3)
    scatter.add_z(2)
    up_grad(2)
    scatter.add_core(4)
    up_grad(3)
    scatter.add_core(5)

    terms_pair.wait_recv()
    gain_grad = jnp.zeros((1, width), F32)
    shift_grad = jnp.zeros((1, width), F32)
    terms_pair.wait_send()
    for k in range(seg_len // tile):
        at = slice(k * tile, (k + 1) * tile)
        grad = terms[at, :] + terms_land[at, :].astype(F32)
        value = residual[at, :]
        mean = jnp.mean(value, axis=-1, keepdims=True)
        centred = value - mean
        rstd = lax.rsqrt(jnp.mean(centred * centred, axis=-1, keepdims=True) + 1e-05)
        xhat = centred * rstd
        gain_grad += jnp.sum(grad * xhat, axis=0, keepdims=True)
        shift_grad += jnp.sum(grad, axis=0, keepdims=True)
        grad = cot[0, at].astype(F32) + norm_back(xhat, rstd, grad * gain)
        residual[at, :] = grad
        grad = grad.astype(BF16)
        cast[0, at, :] = grad
        back = dot_nt(grad, out_w[...]).astype(BF16)
        mixed[0, at, :] = back[:, 0:LANES]
        mixed[1, at, :] = back[:, LANES:]
    mixed_pair.start()
    store_dout = pltpu.make_async_copy(mixed.at[x], dout.at[0], store_sem.at[2])
    store_dout.start()
    store_residual = pltpu.make_async_copy(residual, residual_out, store_sem.at[3])
    store_residual.start()
    small_out[...] = jnp.zeros_like(small_out)
    small_out[4:5, :] = gain_grad[:, 0:LANES]
    small_out[5:6, :] = gain_grad[:, LANES:]
    small_out[6:7, :] = shift_grad[:, 0:LANES]
    small_out[7:8, :] = shift_grad[:, LANES:]
    scatter.add_core(6)
    gather.pass_core(2)

    staged = [None, None]
    jobs = [(out_grads, k * tile, None, k) for k in range(width // tile)]
    jobs += [
        (down_grads, f * LANES + k * tile, f, k) for f in range(4) for k in range(LANES // tile)
    ]
    for j, (target, start, f, k) in enumerate(jobs):
        slot = j % 2
        at = slice(k * tile, (k + 1) * tile)
        if f is None:
            grad = dot_tn(att[0, :, at], cast[0])
        else:
            grad = dot_tn(act[f, 0:seg_len, at], cot[0]) + dot_tn(act[f, seg_len:, at], cot[1])
        if staged[slot] is not None:
            staged[slot].wait()
        stage[slot] = grad.astype(BF16)
        staged[slot] = pltpu.make_async_copy(
            stage.at[slot], target.at[pl.ds(start, tile)], stage_sem.at[slot]
        )
        staged[slot].start()
        if j == 3:
            scatter.add_y(3)
        if j == 10:
            scatter.add_y(4)
            scatter.add_z(3)
    scatter.add_y(5)
    scatter.add_z(4)
    scatter.add_y(6)
    scatter.add_z(5)
    scatter.add_z(6)
    for m in range(3):
        gather.arrive(m)
    comp_pair.wait_recv()
    to = pl.ds(pl.multiple_of((1 - x) * LANES, LANES), LANES)
    comp_out[:, to] = comp_land[...].astype(F32)
    for f in range(4):
        up_pairs[f].wait_recv()
        up_out[1 - x, f] = up_land[f].astype(F32)
    mixed_pair.wait_recv()
    for copy in [mixed_pair, comp_pair, *up_pairs]:
        copy.wait_send()
    for copy in [*staged, store_branch, store_own, store_dout, store_residual]:
        copy.wait()
    for c in range(7):
        scatter.close(c)
    for m in range(3):
        gather.close(m)


def comp_block(m, x, rows, stage, out, send, pair):
    def done(total):
        stage[m * rows : (m + 1) * rows, :] = total
        if m == 2:
            half = send.shape[0]
            upper, lower = stage[0:half, :], stage[half:, :]
            to = pl.ds(pl.multiple_of(x * LANES, LANES), LANES)
            out[:, to] = jnp.where(x == 0, upper, lower)
            send[...] = jnp.where(x == 0, lower, upper).astype(BF16)
            pair.start()

    return done


def up_block(f, x, out, send, pair):
    def done(total):
        half = send.shape[1]
        upper, lower = total[0:half], total[half:]
        out[x, f] = jnp.where(x == 0, upper, lower)
        send[f] = jnp.where(x == 0, lower, upper).astype(BF16)
        pair.start()

    return done


def feed_forward(
    n, att, segment, seg_other, cotangent, cot_other, out_w, up, down, params, comp, comp_shard
):
    _, seg_len, width = att.shape
    rows = width // n
    half_rows = rows // 2
    nhi = n // 4
    comp_rows = comp.shape[3] // 2
    total = 2 * seg_len
    any_spec = pl.BlockSpec(memory_space=pl.ANY)
    vmem = pl.BlockSpec(memory_space=pltpu.VMEM)
    dma = pltpu.SemaphoreType.DMA
    f32 = lambda *shape: jax.ShapeDtypeStruct(shape, F32)
    bf = lambda *shape: jax.ShapeDtypeStruct(shape, BF16)
    return pl.pallas_call(
        functools.partial(feed_kernel, n),
        out_shape=(
            f32(seg_len, width),
            bf(seg_len, width),
            f32(seg_len, width),
            bf(2, seg_len, LANES),
            bf(width, width),
            bf(4 * LANES, width),
            f32(SMALL, LANES),
            f32(comp_rows, width),
            f32(2, 4, half_rows, LANES),
            bf(nhi, 2, 2, *comp_shard.shape),
        ),
        in_specs=[any_spec] * 8 + [vmem, any_spec, vmem],
        out_specs=(any_spec,) * 6 + (vmem,) * 3 + (any_spec,),
        scratch_shapes=[
            pltpu.VMEM((2, seg_len, width), BF16),
            pltpu.VMEM((2, seg_len, width), BF16),
            pltpu.VMEM((2, seg_len, width), BF16),
            pltpu.VMEM((width, width), BF16),
            pltpu.VMEM((4, width, LANES), BF16),
            pltpu.VMEM((4 * LANES, width), BF16),
            pltpu.VMEM((seg_len, width), F32),
            pltpu.VMEM((total, width), BF16),
            pltpu.VMEM((width, total), BF16),
            pltpu.VMEM((4, total, LANES), BF16),
            pltpu.VMEM((4, total, LANES), BF16),
            pltpu.VMEM((seg_len, width), F32),
            pltpu.VMEM((seg_len, width), F32),
            pltpu.VMEM((seg_len, width), BF16),
            pltpu.VMEM((2, seg_len, width), BF16),
            pltpu.VMEM((4, nhi, 2, 2, rows, LANES), BF16),
            pltpu.VMEM((2, seg_len, LANES), BF16),
            pltpu.VMEM((2, 256, width), BF16),
            pltpu.VMEM((4, half_rows, LANES), BF16),
            pltpu.VMEM((4, half_rows, LANES), BF16),
            pltpu.VMEM((3 * rows, LANES), F32),
            pltpu.VMEM((comp_rows, LANES), BF16),
            pltpu.VMEM((comp_rows, LANES), BF16),
            dma((9,)),
            dma((4,)),
            dma((2,)),
            dma((7,)),
            dma((7,)),
        ]
        + Scatter.scratch(7, nhi, rows)
        + Gather.semaphores(3, nhi),
        compiler_params=pltpu.CompilerParams(
            vmem_limit_bytes=VMEM_LIMIT, collective_id=2, has_side_effects=True
        ),
        name="feed_forward",
    )(att, segment, seg_other, cotangent, cot_other, out_w, up, down, params, comp, comp_shard)


def norm_back(xhat, rstd, grad):
    a = jnp.mean(grad, axis=-1, keepdims=True)
    b = jnp.mean(grad * xhat, axis=-1, keepdims=True)
    return rstd * (grad - a - xhat * b)


def backward_kernel(
    n,
    past,
    seg_len,
    dout,
    kv,
    q,
    wide,
    near,
    place_keys,
    xhat_t,
    query_w,
    key_w,
    value_w,
    table_t,
    params,
    segment,
    seg_other,
    residual_grad,
    small_in,
    own_sum,
    branch,
    down,
    out,
    result_out,
    segment_out,
    query_out,
    key_out,
    value_out,
    place_out,
    out_out,
    down_out,
    small_out,
    flat,
    raw,
    sums,
    place_sum,
    input_grad,
    dkv,
    columns,
    gain_sum,
    shift_sum,
    head_grads,
    context_land,
    context_send,
    branch_land,
    own_rows_sum,
    own_sem,
    seg_rows,
    seg_sem,
    out_keep,
    out_send,
    out_land,
    small_mine,
    small_c,
    small_y,
    small_z,
    small_x,
    pair_send,
    pair_recv,
    small_send,
    small_recv,
    land_c,
    land_y,
    land_z,
    mine,
    mine_sem,
    *sems,
):
    step = pl.program_id(0)
    x = lax.axis_index("head")
    core, low, high, nhi = place(n)
    head = lax.rem(step, 4)
    tile = 256
    context = past + seg_len
    width = flat.shape[0]
    rows = width // n
    half_rows = rows // 2
    scale = 1.0 / math.sqrt(128)
    flip = (
        lax.broadcasted_iota(jnp.int32, (HALF, HALF), 0)
        + lax.broadcasted_iota(jnp.int32, (HALF, HALF), 1)
        == HALF - 1
    ).astype(BF16)

    def pair(src, dst, k):
        return pltpu.make_async_remote_copy(
            src_ref=src,
            dst_ref=dst,
            send_sem=pair_send.at[k],
            recv_sem=pair_recv.at[k],
            device_id={"head": 1 - x},
            device_id_type=MESH,
        )

    context_pair = pair(context_send, context_land, 0)
    branch_pair = pair(branch, branch_land, 1)
    out_pairs = [pair(out_send.at[b], out_land.at[b], 2 + b) for b in range(2)]
    load_own = pltpu.make_async_copy(own_sum, own_rows_sum, own_sem)
    load_other = pltpu.make_async_copy(seg_other, seg_rows, seg_sem)
    load_segment = pltpu.make_async_copy(segment.at[0], seg_rows, seg_sem)

    def down_done(a, b):
        def done(total):
            down_out[a * rows : (a + 1) * rows, b * LANES : (b + 1) * LANES] = total

        return done

    def out_done(b):
        def done(total):
            upper, lower = total[0:half_rows], total[half_rows:]
            out_keep[b] = jnp.where(x == 0, upper, lower)
            out_send[b] = jnp.where(x == 0, lower, upper).astype(BF16)
            out_pairs[b].start()

        return done

    def head_done(h):
        def done(total):
            for j, ref in enumerate((query_out, key_out, value_out, place_out)):
                ref[:, h * 128 : (h + 1) * 128] = total[:, j * 128 : (j + 1) * 128]

        return done

    parts = []
    for a in range(2):
        for b in range(2):
            at, to = pl.ds(a * rows, rows), pl.ds(b * LANES, LANES)
            parts.append((down.at[:, :, :, at, to], False, down_done(a, b)))
    parts += [
        (out.at[:, :, :, :, pl.ds(b * LANES, LANES)], False, out_done(b)) for b in range(2)
    ]
    parts += [(head_grads.at[h], True, head_done(h)) for h in range(4)]
    scatter = Scatter(
        n,
        [
            (part, here, land_c.at[c], land_y.at[c], land_z.at[c], done)
            for c, (part, here, done) in enumerate(parts)
        ],
        mine,
        mine_sem,
        sems,
    )
    count = len(parts)

    @pl.when(step == 0)
    def _():
        barrier = pltpu.get_barrier_semaphore()
        pl.semaphore_signal(barrier, inc=1, device_id={"head": 1 - x}, device_id_type=MESH)
        meet(core, low, high, nhi, 1)
        load_own.start()
        load_other.start()
        branch_pair.start()
        for j in range(2):
            line = jnp.concatenate([params[2 * j : 2 * j + 1, :], params[2 * j + 1 : 2 * j + 2, :]], axis=1)
            columns[j] = jnp.broadcast_to(line, (128, width)).T
        raw[...] = jnp.zeros_like(raw)
        sums[...] = jnp.zeros_like(sums)
        place_sum[...] = jnp.zeros_like(place_sum)
        gain_sum[...] = jnp.zeros_like(gain_sum)
        shift_sum[...] = jnp.zeros_like(shift_sum)
        small_mine[...] = small_in[...]

    @pl.when(head == 0)
    def _():
        input_grad[...] = jnp.zeros_like(input_grad)

    start, add_core, add_y, add_z = scatter.start, scatter.add_core, scatter.add_y, scatter.add_z
    before = {
        0: ((start, 0), (start, 1)),
        1: ((add_core, 1), (start, 3)),
        2: ((add_core, 3), (start, 5)),
        3: ((add_y, 2), (add_core, 4)),
        4: ((add_y, 3),),
        5: ((start, 6), (add_z, 3)),
        6: ((add_z, 4), (start, 7)),
        7: ((start, 8),),
    }
    within = {
        0: ((add_core, 0), (start, 2)),
        1: ((add_y, 0), (add_core, 2), (start, 4)),
        2: ((add_y, 1), (add_z, 0)),
        3: ((add_z, 1), (add_core, 5)),
        4: ((add_y, 4), (add_z, 2)),
        5: ((add_core, 6), (add_y, 5)),
        6: ((add_core, 7), (add_y, 6), (add_z, 5)),
        7: ((add_core, 8), (add_y, 7), (add_z, 6)),
    }

    def run(table):
        for k, steps in table.items():

            @pl.when(step == k)
            def _(steps=steps):
                for do, c in steps:
                    do(c)

    run(before)

    for j, mat in enumerate((query_w, key_w, value_w)):
        flat[:, j * 128 : (j + 1) * 128] = mat[...]

    query_grads = []
    key_rows = []
    value_rows = []
    place_rows = []
    bias_at = pl.ds(pl.multiple_of(head * 128, 128), 128)
    for part, weights_ref, key_start, key_count, place_start in (
        (0, wide, 0, past + HALF, 0),
        (1, near, past, seg_len, past - HALF),
    ):
        at = slice(part * HALF, (part + 1) * HALF)
        keys_at = slice(key_start, key_start + key_count)
        attn = weights_ref[0, 0]
        grad = dout[0, at]
        value_rows.append(dot_tn(grad, attn))
        weights_grad = dot_nt(grad, kv[0, 0, keys_at, 128:256])
        attn = attn.astype(F32)
        row = jnp.sum(weights_grad * attn, axis=1, keepdims=True)
        scores_grad = (attn * (weights_grad - row) * scale).astype(BF16)
        content_grad = dot(scores_grad, kv[0, 0, keys_at, 0:128]).astype(BF16)
        key_rows.append(dot_tn(q[0, 0, at, 0:128], scores_grad))
        by_place = pltpu.roll(dot(flip, scores_grad), 0, 1, stride=1, stride_axis=0).astype(BF16)
        place_grad = dot(by_place, place_keys[0, place_start : place_start + key_count])
        place_grad = dot(flip, place_grad.astype(BF16)).astype(BF16)
        flipped_q = dot(flip, q[0, 0, at, 128:256]).astype(BF16)
        place_rows.append(dot_tn(flipped_q, by_place))
        content_f = content_grad.astype(F32)
        place_f = place_grad.astype(F32)
        small_mine[8:9, bias_at] += jnp.sum(content_f, axis=0, keepdims=True)
        small_mine[9:10, bias_at] += jnp.sum(place_f, axis=0, keepdims=True)
        query_grads.append((content_f + place_f).astype(BF16))

    for j, (wide_rows, near_rows) in enumerate((key_rows, value_rows)):
        at = slice(j * 128, (j + 1) * 128)
        dkv[at, 0:past] = wide_rows[:, 0:past].astype(BF16)
        dkv[at, past : past + HALF] = (wide_rows[:, past:] + near_rows[:, 0:HALF]).astype(BF16)
        dkv[at, past + HALF :] = near_rows[:, HALF:].astype(BF16)
    split = past - HALF
    for at, rows_grad in (
        (slice(0, split), place_rows[0][:, 0:split]),
        (slice(split, None), place_rows[0][:, split:] + place_rows[1]),
    ):
        place_sum[head, :, at] = (
            place_sum[head, :, at].astype(F32) + rows_grad.astype(BF16).astype(F32)
        ).astype(BF16)
    dq = jnp.concatenate(query_grads, axis=0)
    stacked = jnp.concatenate([dq, dkv[:, past:].astype(F32).T.astype(BF16)], axis=1)

    run(within)

    ones = jnp.ones((8, context), BF16)
    sums[head, :, 0:128] += dot(ones[:, 0:seg_len], dq)
    sums[head, :, 128:384] += dot_nt(ones, dkv[...])
    for k in range(width // tile):
        at = slice(k * tile, (k + 1) * tile)
        raw[head, at, 0:128] += dot(xhat_t[0, at, past:], dq)
        raw[head, at, 128:384] += dot_nt(xhat_t[0, at, :], dkv[...])
        input_grad[:, at] += dot_nt(stacked, flat[at, 0:384])

    @pl.when(step >= 4)
    def _():
        place_low = place_sum[head]
        block = tile // (4 * rows)
        total = sums[head, 0:1, :]
        for k in range(width // tile):
            at = slice(k * tile, (k + 1) * tile)
            to = slice(k * block, (k + 1) * block)
            got = raw[head, at, :]
            mats = flat[at, 0:384].astype(F32)
            for acc, term in ((gain_sum, mats * got), (shift_sum, mats * total)):
                acc[at, :] += term[:, 0:128] + term[:, 128:256] + term[:, 256:384]
            grad = (columns[0, at, 0:1] * got + columns[1, at, 0:1] * total).astype(BF16)
            head_grads[head, to, :, :, :, 0:384] = grad.reshape(block, 2, 2, rows, 384)
            grad = dot_nt(table_t[at, :], place_low).astype(BF16)
            head_grads[head, to, :, :, :, 384:512] = grad.reshape(block, 2, 2, rows, 128)

    def own_rows(k):
        gain = jnp.concatenate([params[0:1, :], params[1:2, :]], axis=1)
        at = slice(k * tile, (k + 1) * tile)
        values = seg_rows[at, :].astype(F32)
        mean = jnp.mean(values, axis=-1, keepdims=True)
        centred = values - mean
        rstd = lax.rsqrt(jnp.mean(centred * centred, axis=-1, keepdims=True) + 1e-05)
        return norm_back(centred * rstd, rstd, input_grad[at, :] * gain)

    @pl.when(step == 4)
    def _():
        load_segment.start()

    @pl.when(step == 3)
    def _():
        load_other.wait()
        for k in range(seg_len // tile):
            context_send[k * tile : (k + 1) * tile, :] = own_rows(k).astype(BF16)
        context_pair.start()

    @pl.when(step == 5)
    def _():
        branch_pair.wait_recv()
        load_own.wait()
        for k in range(seg_len // tile):
            at = slice(k * tile, (k + 1) * tile)
            result_out[0, at] = (own_rows_sum[at, :] + branch_land[at, :].astype(F32)).astype(BF16)

    @pl.when(step == 7)
    def _():
        start(9)
        one = jnp.ones((8, 128), F32)
        for acc, row in ((gain_sum, 0), (shift_sum, 2)):
            line = lax.dot_general(
                one,
                acc[...],
                (((1,), (1,)), ((), ())),
                precision=lax.Precision.HIGHEST,
                preferred_element_type=F32,
            )
            small_mine[row : row + 1, :] = line[0:1, 0:LANES]
            small_mine[row + 1 : row + 2, :] = line[0:1, LANES:]

        def to_dp(src, dst, k, index):
            return remote(src, dst, small_send.at[k], small_recv.at[k], index)

        copies = [to_dp(small_mine, small_c.at[1], 0, high * 4 + low * 2 + (1 - core))]
        copies[0].start()
        add_core(9)
        load_segment.wait()
        context_pair.wait_recv()
        for k in range(seg_len // tile):
            at = slice(k * tile, (k + 1) * tile)
            segment_out[0, at] = (
                residual_grad[at, :] + own_rows(k) + context_land[at, :].astype(F32)
            ).astype(BF16)
        add_z(7)
        add_y(8)
        copies[0].wait_recv()
        small_c[0] = small_mine[...] + small_c[1]
        copies.append(to_dp(small_c.at[0], small_y.at[1], 1, high * 4 + (1 - low) * 2 + core))
        copies[1].start()
        copies[1].wait_recv()
        small_y[0] = small_c[0] + small_y[1]
        along = []
        for k in range(1, nhi):
            to = lax.rem(high + k, nhi) * 4 + low * 2 + core
            along.append(to_dp(small_y.at[0], small_z.at[k], 2 + k, to))
        for copy in along:
            copy.start()
        add_y(9)
        add_z(8)
        for copy in along:
            copy.wait_recv()
        line = small_y[0]
        for k in range(1, nhi):
            line = line + small_z[k]
        small_z[0] = line
        last = pltpu.make_async_remote_copy(
            src_ref=small_z.at[0],
            dst_ref=small_x,
            send_sem=small_send.at[2],
            recv_sem=small_recv.at[2],
            device_id={"head": 1 - x},
            device_id_type=MESH,
        )
        last.start()
        add_z(9)
        for b in range(2):
            out_pairs[b].wait_recv()
            out_out[:, b * LANES : (b + 1) * LANES] = out_keep[b] + out_land[b].astype(F32)
        last.wait_recv()
        line = lax.broadcasted_iota(jnp.int32, (SMALL, LANES), 0)
        small_out[...] = small_z[0] + jnp.where(line < 8, small_x[...], 0.0)
        for copy in [context_pair, branch_pair, *out_pairs, *copies, *along, last]:
            copy.wait_send()
        for c in range(count):
            scatter.close(c)


def attention_backward(
    n, dout, kv, q, wide, near, place_keys, xhat_t, mats, table_t, params, segment,
    seg_other, residual_grad, small_in, own_sum, branch, down, out,
):
    _, seg_len, width = segment.shape
    context = kv.shape[2]
    past = context - seg_len
    rows = width // n
    nhi = n // 4
    half_rows = rows // 2
    seq = lambda t: 1 - t // 4
    head = lambda t: lax.rem(t, 4)
    by_both = lambda t: (head(t), seq(t), 0, 0)
    single = pl.Buffered(1)
    any_spec = pl.BlockSpec(memory_space=pl.ANY)
    dma = pltpu.SemaphoreType.DMA
    f32 = lambda *shape: jax.ShapeDtypeStruct(shape, F32)
    lead = (nhi, 2, 2)
    full = lambda shape: pl.BlockSpec(shape, lambda t: (0,) * len(shape), pipeline_mode=single)
    outs = (
        jax.ShapeDtypeStruct((1, seg_len, width), BF16),
        jax.ShapeDtypeStruct((1, seg_len, width), BF16),
        f32(rows, LANES),
        f32(rows, LANES),
        f32(rows, LANES),
        f32(rows, LANES),
        f32(half_rows, width),
        f32(2 * rows, width),
        f32(SMALL, LANES),
    )
    return pl.pallas_call(
        functools.partial(backward_kernel, n, past, seg_len),
        grid=(8,),
        out_shape=outs,
        in_specs=[
            pl.BlockSpec((1, seg_len, 128), lambda t: (seq(t), 0, head(t))),
            pl.BlockSpec((1, 1, context, 256), by_both),
            pl.BlockSpec((1, 1, seg_len, 256), by_both),
            pl.BlockSpec((1, 1, HALF, past + HALF), by_both),
            pl.BlockSpec((1, 1, HALF, seg_len), by_both),
            pl.BlockSpec((1, past + HALF, 128), lambda t: (head(t), 0, 0)),
            pl.BlockSpec((1, width, context), lambda t: (seq(t), 0, 0), pipeline_mode=single),
            *[pl.BlockSpec((width, 128), lambda t: (0, head(t)))] * 3,
            full(table_t.shape),
            full((SMALL, LANES)),
            any_spec,
            any_spec,
            full((seg_len, width)),
            full((SMALL, LANES)),
            any_spec,
            any_spec,
            any_spec,
            any_spec,
        ],
        out_specs=tuple(full(o.shape) for o in outs),
        scratch_shapes=[
            pltpu.VMEM((width, 384), BF16),
            pltpu.VMEM((4, width, 384), F32),
            pltpu.VMEM((4, 8, 384), F32),
            pltpu.VMEM((4, 128, past + HALF), BF16),
            pltpu.VMEM((seg_len, width), F32),
            pltpu.VMEM((256, context), BF16),
            pltpu.VMEM((2, width, 128), F32),
            pltpu.VMEM((width, 128), F32),
            pltpu.VMEM((width, 128), F32),
            pltpu.VMEM((4,) + lead + (rows, LANES), BF16),
            pltpu.VMEM((seg_len, width), BF16),
            pltpu.VMEM((seg_len, width), BF16),
            pltpu.VMEM((seg_len, width), BF16),
            pltpu.VMEM((seg_len, width), F32),
            dma(()),
            pltpu.VMEM((seg_len, width), BF16),
            dma(()),
            pltpu.VMEM((2, half_rows, LANES), F32),
            pltpu.VMEM((2, half_rows, LANES), BF16),
            pltpu.VMEM((2, half_rows, LANES), BF16),
            pltpu.VMEM((SMALL, LANES), F32),
            pltpu.VMEM((2, SMALL, LANES), F32),
            pltpu.VMEM((2, SMALL, LANES), F32),
            pltpu.VMEM((nhi, SMALL, LANES), F32),
            pltpu.VMEM((SMALL, LANES), F32),
            dma((4,)),
            dma((4,)),
            dma((2 + nhi,)),
            dma((2 + nhi,)),
        ]
        + Scatter.scratch(10, nhi, rows),
        compiler_params=pltpu.CompilerParams(
            vmem_limit_bytes=VMEM_LIMIT,
            dimension_semantics=("arbitrary",),
            collective_id=1,
            has_side_effects=True,
        ),
        name="attention_backward",
    )(
        dout, kv, q, wide, near, place_keys, xhat_t, *mats, table_t,
        params, segment, seg_other,
        residual_grad, small_in, own_sum, branch, down, out,
    )


def finish_kernel(n, *refs):
    count = len(refs) // 2
    up, up_out = refs[0], refs[count]
    _, _, half_rows, _ = up.shape
    size = LANES // (n // 4)
    for f in range(4):
        for j in range(n // 4):
            for half in range(2):
                to = ((f * (n // 4) + j) * 2 + half) * size
                up_out[:, to : to + size] = up[half, f, :, j * size : (j + 1) * size]
    for src, dst in zip(refs[1:count], refs[count + 1 :]):
        dst[...] = src[...]


def finish(n, up, others):
    vmem = pl.BlockSpec(memory_space=pltpu.VMEM)
    same = [jax.ShapeDtypeStruct(a.shape, a.dtype) for a in others]
    out = jax.ShapeDtypeStruct((up.shape[2], 8 * LANES), F32)
    return pl.pallas_call(
        functools.partial(finish_kernel, n),
        out_shape=(out, *same),
        in_specs=[vmem] * (1 + len(others)),
        out_specs=(vmem,) * (1 + len(others)),
        compiler_params=pltpu.CompilerParams(vmem_limit_bytes=VMEM_LIMIT),
        name="finish",
    )(up, *others)


def body(
    n,
    segment,
    memory,
    compressed,
    doc_lengths,
    memory_valid,
    query_weight,
    key_weight,
    value_weight,
    position_weight,
    content_bias,
    position_bias,
    output_weight,
    up_weight,
    down_weight,
    compress_weight,
    norm_gain,
    norm_shift,
    post_gain,
    post_shift,
    cotangent,
    compress_cotangent,
):
    x = lax.axis_index("head")
    dp = lax.axis_index("dp")
    first = x == 0
    nhi = n // 4
    width = segment.shape[2]
    seg_len = segment.shape[1]
    past = memory.shape[1] + compressed.shape[1]
    context = past + seg_len
    rows = query_weight.shape[0]
    half_rows = output_weight.shape[0]
    new_count = compress_cotangent.shape[1]
    comp_rows = compress_weight.shape[0]

    def swap(a):
        return lax.ppermute(a, "head", [(0, 1), (1, 0)])

    def pick(a, index):
        return jnp.where(index == 0, a[0], a[1])

    def in_order(own, got, axis):
        return jnp.where(
            first,
            jnp.concatenate([own, got], axis=axis),
            jnp.concatenate([got, own], axis=axis),
        )

    ffr = down_weight.shape[0]
    up_parts = (
        up_weight.reshape(half_rows, 4, n // 4, 2, ffr)
        .transpose(3, 1, 0, 2, 4)
        .reshape(2, 4, half_rows, LANES)
    )
    per = content_bias.shape[1]
    vectors = jnp.stack([norm_gain, norm_shift, post_gain, post_shift])
    here = jnp.arange(2 * n, dtype=jnp.int32)[None, :, None] == dp * 2 + x
    norms = jnp.where(here, vectors[:, None, :], 0).reshape(8, LANES)
    here = jnp.arange(n, dtype=jnp.int32)[None, None, :, None] == dp
    bias = jnp.stack([content_bias, position_bias])[:, :, None, :]
    bias = jnp.where(here, bias, 0).reshape(2, LANES)
    small = jnp.concatenate([norms, bias, jnp.zeros((SMALL - 10, LANES), BF16)])
    pad_rows = -(-new_count // 16) * 16
    comp_cot = jnp.pad(compress_cotangent[0], ((0, pad_rows - new_count), (0, 0)))
    table = position_rows(context, width, past + HALF)

    (
        att, seg_other, cot_other, xhat_t, windows, comp_grads, comp_shard, params, kv, q, wide, near,
        place_keys, query_whole, key_whole, value_whole, _, out_whole, up_whole, down_whole, _,
    ) = attention_forward(
        n, doc_lengths, memory_valid, compressed, memory, segment, cotangent, comp_cot,
        (query_weight, key_weight, value_weight, position_weight),
        output_weight, up_parts, down_weight, compress_weight, small, jnp.asarray(table),
    )

    lead = (nhi, 2, 2)
    (
        own_sum, branch, residual_grad, dout, out_grads, down_grads, small_in, comp_done, up_done,
        comp_whole,
    ) = feed_forward(
        n, att, segment, seg_other, cotangent, cot_other, out_whole.reshape(width, width),
        up_whole.reshape(4, width, LANES), down_whole.reshape(4 * LANES, width), params,
        comp_grads.reshape(lead + (3 * rows, LANES)), comp_shard,
    )

    made = jnp.einsum(
        "kic,kcd->id", windows, comp_whole.reshape(3, width, LANES), preferred_element_type=F32
    ).astype(BF16)
    made = in_order(made[:new_count], swap(made[pad_rows : pad_rows + new_count]), 1)

    mats = [w.reshape(width, LANES) for w in (query_whole, key_whole, value_whole)]
    result, segment_grad, *matrices, small_done = attention_backward(
        n, dout, kv, q, wide, near, place_keys, xhat_t, mats, jnp.asarray(table.T.copy()),
        params, segment, seg_other, residual_grad, small_in, own_sum, branch,
        down_grads.reshape(lead + (2 * rows, 2 * LANES)),
        out_grads.reshape(lead + (rows, 2 * LANES)),
    )

    up_final, result, segment_grad, *matrices, comp_final = finish(
        n, up_done, (result, segment_grad, *matrices, comp_done)
    )
    query_final, key_final, value_final, place_final, out_final, down_final = matrices
    vectors = lax.dynamic_slice_in_dim(
        small_done[0:8].reshape(4, width), (dp * 2 + x) * half_rows, half_rows, 1
    )
    biases = lax.dynamic_slice_in_dim(small_done[8:10].reshape(2, 4, 128), dp * per, per, 2)
    return (
        result,
        made[None],
        segment_grad,
        query_final,
        key_final,
        value_final,
        place_final,
        biases[0],
        biases[1],
        out_final,
        up_final,
        down_final,
        comp_final,
        vectors[0],
        vectors[1],
        vectors[2],
        vectors[3],
    )


def solution(mesh):
    split = P(("dp", "head"))
    wide = P(("dp", "head"), None)
    deep = P(("dp", "head"), None, None)
    return jax.shard_map(
        functools.partial(body, mesh.shape["dp"]),
        mesh=mesh,
        in_specs=(
            deep,
            P("dp", None, None),
            P("dp", None, None),
            P("dp", None),
            P("dp"),
            P("dp", "head"),
            P("dp", "head"),
            P("dp", "head"),
            P("dp", "head"),
            P("head", "dp"),
            P("head", "dp"),
            wide,
            wide,
            wide,
            wide,
            split,
            split,
            split,
            split,
            deep,
            deep,
        ),
        out_specs=(
            deep,
            deep,
            deep,
            P("dp", "head"),
            P("dp", "head"),
            P("dp", "head"),
            P("dp", "head"),
            P("head", "dp"),
            P("head", "dp"),
            wide,
            wide,
            wide,
            wide,
            split,
            split,
            split,
            split,
        ),
        check_vma=False,
    )
```

```python
import functools
import math

import jax
import jax.numpy as jnp
import numpy as np
from jax import lax
from jax.experimental import pallas as pl
from jax.experimental.pallas import tpu as pltpu
from jax.sharding import PartitionSpec as P

F32 = jnp.float32
BF16 = jnp.bfloat16
MESH = pl.DeviceIdType.MESH
VMEM_LIMIT = 62 * 1024 * 1024
HALF = 256
LANES = 512
SMALL = 16


def dot(a, b):
    return lax.dot_general(a, b, (((1,), (0,)), ((), ())), preferred_element_type=F32)


def dot_nt(a, b):
    return lax.dot_general(a, b, (((1,), (1,)), ((), ())), preferred_element_type=F32)


def dot_tn(a, b):
    return lax.dot_general(a, b, (((0,), (0,)), ((), ())), preferred_element_type=F32)


def position_rows(context, width, used):
    distance = np.arange(context, dtype=np.float32)[:, None]
    frequency = np.exp(
        np.arange(width // 2, dtype=np.float32) * np.float32(-2.0 * math.log(10000.0) / width)
    )
    phases = distance * frequency[None, :].astype(np.float32)
    table = np.concatenate([np.sin(phases), np.cos(phases)], axis=1)
    return table[::-1][context - used :].astype(jnp.bfloat16)


def place(n):
    me = lax.axis_index("dp")
    core = lax.rem(me, 2)
    low = lax.rem(me // 2, 2)
    high = me // 4
    return core, low, high, n // 4


def meet(core, low, high, nhi, more=0):
    barrier = pltpu.get_barrier_semaphore()

    def tell(index):
        pl.semaphore_signal(barrier, inc=1, device_id={"dp": index}, device_id_type=MESH)

    for k in range(1, nhi):
        tell(lax.rem(high + k, nhi) * 4 + low * 2 + core)
    tell(high * 4 + (1 - low) * 2 + core)
    tell(high * 4 + low * 2 + (1 - core))
    pl.semaphore_wait(barrier, nhi + 1 + more)


def remote(src, dst, send, recv, index):
    return pltpu.make_async_remote_copy(
        src_ref=src,
        dst_ref=dst,
        send_sem=send,
        recv_sem=recv,
        device_id={"dp": index},
        device_id_type=MESH,
    )


class Gather:
    def __init__(self, n, pairs, sems):
        self.core, self.low, self.high, self.nhi = place(n)
        self.pairs = pairs
        (self.zs, self.zr, self.ys, self.yr, self.cs, self.cr, self.own) = sems
        order = sorted(range(1, self.nhi), key=lambda k: (min(k, self.nhi - k), k))
        self.order = order

    def z_copy(self, c, k):
        shard, whole = self.pairs[c]
        return remote(
            shard,
            whole.at[self.high, self.low, self.core],
            self.zs.at[c, k],
            self.zr.at[c, k],
            lax.rem(self.high + k, self.nhi) * 4 + self.low * 2 + self.core,
        )

    def own_copy(self, c):
        shard, whole = self.pairs[c]
        return pltpu.make_async_copy(
            shard, whole.at[self.high, self.low, self.core], self.own.at[c]
        )

    def y_copy(self, c, k):
        shard, whole = self.pairs[c]
        at = whole.at[lax.rem(self.high + k, self.nhi), self.low, self.core]
        return remote(
            shard if k == 0 else at,
            at,
            self.ys.at[c, k],
            self.yr.at[c, k],
            self.high * 4 + (1 - self.low) * 2 + self.core,
        )

    def c_copy(self, c):
        _, whole = self.pairs[c]
        part = whole.at[:, :, self.core]
        return remote(
            part,
            part,
            self.cs.at[c],
            self.cr.at[c],
            self.high * 4 + self.low * 2 + (1 - self.core),
        )

    def start(self, c):
        for k in self.order:
            self.z_copy(c, k).start()
        self.y_copy(c, 0).start()
        self.own_copy(c).start()

    def pass_y(self, c):
        for k in self.order:
            self.z_copy(c, self.nhi - k).wait_recv()
            self.y_copy(c, k).start()

    def pass_core(self, c):
        self.own_copy(c).wait()
        for k in range(self.nhi):
            self.y_copy(c, k).wait_recv()
        self.c_copy(c).start()

    def arrive(self, c):
        self.c_copy(c).wait_recv()

    def close(self, c):
        for k in self.order:
            self.z_copy(c, k).wait_send()
        for k in range(self.nhi):
            self.y_copy(c, k).wait_send()
        self.c_copy(c).wait_send()

    @staticmethod
    def semaphores(count, nhi):
        dma = pltpu.SemaphoreType.DMA
        return [dma((count, nhi))] * 4 + [dma((count,))] * 3


class Scatter:
    def __init__(self, n, items, mine, mine_sem, sems):
        self.core, self.low, self.high, self.nhi = place(n)
        self.items = items
        self.mine, self.mine_sem = mine, mine_sem
        (self.cs, self.cr, self.ys, self.yr, self.zs, self.zr) = sems

    def c_copy(self, c):
        return remote(
            self.items[c][0].at[:, :, 1 - self.core],
            self.items[c][2],
            self.cs.at[c],
            self.cr.at[c],
            self.high * 4 + self.low * 2 + (1 - self.core),
        )

    def mine_copy(self, c):
        slot = c % 2
        return pltpu.make_async_copy(
            self.items[c][0].at[:, :, self.core], self.mine.at[slot], self.mine_sem.at[slot]
        )

    def y_copy(self, c):
        return remote(
            self.items[c][2].at[:, 1 - self.low],
            self.items[c][3],
            self.ys.at[c],
            self.yr.at[c],
            self.high * 4 + (1 - self.low) * 2 + self.core,
        )

    def z_copies(self, c):
        return [
            remote(
                self.items[c][3].at[lax.rem(self.high + k, self.nhi)],
                self.items[c][4].at[k - 1],
                self.zs.at[c, k - 1],
                self.zr.at[c, k - 1],
                lax.rem(self.high + k, self.nhi) * 4 + self.low * 2 + self.core,
            )
            for k in range(1, self.nhi)
        ]

    def start(self, c):
        self.c_copy(c).start()
        if not self.items[c][1]:
            self.mine_copy(c).start()

    def add_core(self, c):
        here = self.items[c][1]
        if not here:
            self.mine_copy(c).wait()
        self.c_copy(c).wait_recv()
        land = self.items[c][2]

        def body(i, carry):
            for j in range(2):
                own = self.items[c][0][i, j, self.core] if here else self.mine[c % 2, i, j]
                land[i, j] = land[i, j] + own
            return carry

        lax.fori_loop(0, self.nhi, body, 0)
        self.y_copy(c).start()

    def add_y(self, c):
        self.y_copy(c).wait_recv()
        src, land = self.items[c][2], self.items[c][3]

        def body(i, carry):
            land[i] = land[i] + src[i, self.low]
            return carry

        lax.fori_loop(0, self.nhi, body, 0)
        for copy in self.z_copies(c):
            copy.start()

    def add_z(self, c):
        for copy in self.z_copies(c):
            copy.wait_recv()
        land, last, done = self.items[c][3:]
        total = land[self.high].astype(F32)
        for k in range(self.nhi - 1):
            total = total + last[k].astype(F32)
        done(total)

    def tick(self, t):
        count = len(self.items)
        if 0 <= t - 1 < count:
            self.add_core(t - 1)
        if t < count:
            self.start(t)
        if 0 <= t - 2 < count:
            self.add_y(t - 2)
        if 0 <= t - 3 < count:
            self.add_z(t - 3)

    def close(self, c):
        self.c_copy(c).wait_send()
        self.y_copy(c).wait_send()
        for copy in self.z_copies(c):
            copy.wait_send()

    @staticmethod
    def scratch(count, nhi, rows):
        dma = pltpu.SemaphoreType.DMA
        return [
            pltpu.VMEM((count, nhi, 2, rows, LANES), BF16),
            pltpu.VMEM((count, nhi, rows, LANES), BF16),
            pltpu.VMEM((count, nhi - 1, rows, LANES), BF16),
            pltpu.VMEM((2, nhi, 2, rows, LANES), BF16),
            dma((2,)),
            dma((count,)),
            dma((count,)),
            dma((count,)),
            dma((count,)),
            dma((count, nhi - 1)),
            dma((count, nhi - 1)),
        ]


def norm_rows(values):
    mean = jnp.mean(values, axis=-1, keepdims=True)
    centred = values - mean
    variance = jnp.mean(centred * centred, axis=-1, keepdims=True)
    return centred * lax.rsqrt(variance + 1e-05)


def attend_rows(query_content, query_place, keys, place_keys, first_seen, last_seen, scale):
    width = keys.shape[0]
    content = dot_nt(query_content, keys)
    by_place = pltpu.roll(
        dot_nt(query_place, place_keys), width - (HALF - 1), 1, stride=1, stride_axis=0
    )
    column = lax.broadcasted_iota(jnp.int32, (HALF, width), 1)
    seen = (column >= first_seen) & (column <= last_seen)
    scores = jnp.where(seen, (content + by_place) * (scale * math.log2(math.e)), -1e30)
    top = jnp.max(scores, axis=1, keepdims=True)
    expo = jnp.exp2(scores - top)
    return expo * (1.0 / jnp.sum(expo, axis=1, keepdims=True))


def forward_kernel(
    n,
    past,
    seg_len,
    docs,
    valid,
    compressed,
    memory,
    segment,
    cotangent,
    comp_cot,
    query_w,
    key_w,
    value_w,
    place_w,
    out_w,
    up_parts,
    down_w,
    comp_w,
    small,
    table,
    attended,
    seg_other,
    cot_other,
    xhat_hbm,
    windows_hbm,
    comp_grads_hbm,
    comp_shard_hbm,
    params,
    kv_out,
    q_out,
    wide_out,
    near_out,
    place_out,
    query_whole,
    key_whole,
    value_whole,
    place_whole,
    out_whole,
    up_whole,
    down_whole,
    small_whole,
    out_shard,
    up_shard,
    comp_shard,
    small_shard,
    normed,
    xhat_out,
    memory_f,
    windows,
    comp_rows_cot,
    comp_grads,
    past_rows,
    seg_rows,
    flat,
    small_rows,
    att,
    load_sem,
    flat_sem,
    own_sem,
    store_sem,
    pair_send,
    pair_recv,
    att_own,
    att_send,
    att_recv,
    *sems,
):
    step = pl.program_id(0)
    x = lax.axis_index("head")
    core, low, high, nhi = place(n)
    tile = 256
    width = normed.shape[2]
    context = past + seg_len
    head = jnp.maximum(step - 2, 0) // 2
    half = comp_w.shape[1] // 2

    items = [(small_shard, small_whole)]
    items += [(query_w, query_whole), (key_w, key_whole), (value_w, value_whole), (place_w, place_whole)]
    for b in range(2):
        to = pl.ds(b * LANES, LANES)
        items.append((out_shard.at[:, :, to], out_whole.at[:, :, :, :, :, to]))
    items += [(up_shard.at[f], up_whole.at[f]) for f in range(4)]
    mid = down_w.shape[0] // 2
    for part in range(2):
        for b in range(2):
            at, to = pl.ds(part * mid, mid), pl.ds(b * LANES, LANES)
            items.append((down_w.at[at, to], down_whole.at[:, :, :, at, to]))
    gather = Gather(n, items, sems)
    count = len(items)
    needs = {5: 1, 7: 2}
    pad_rows = comp_cot.shape[0]

    def pair(src, dst, k):
        return pltpu.make_async_remote_copy(
            src_ref=src,
            dst_ref=dst,
            send_sem=pair_send.at[k],
            recv_sem=pair_recv.at[k],
            device_id={"head": 1 - x},
            device_id_type=MESH,
        )

    mine_at = pl.ds(pl.multiple_of(x * half, half), half)
    other_at = pl.ds(pl.multiple_of((1 - x) * half, half), half)
    pairs = [
        pair(small, small_shard.at[x], 0),
        pair(out_w, out_shard.at[x], 1),
        pair(up_parts.at[1 - x], up_shard.at[:, x], 2),
        pair(comp_w.at[:, other_at], comp_shard.at[x], 3),
        pair(segment.at[0], seg_other, 4),
        pair(cotangent.at[0], cot_other, 5),
        pair(comp_cot.at[:, other_at], comp_rows_cot.at[1], 6),
    ]
    owns = [
        pltpu.make_async_copy(small, small_shard.at[x], own_sem.at[0]),
        pltpu.make_async_copy(out_w, out_shard.at[x], own_sem.at[1]),
        pltpu.make_async_copy(up_parts.at[x], up_shard.at[:, x], own_sem.at[2]),
        pltpu.make_async_copy(comp_w.at[:, mine_at], comp_shard.at[x], own_sem.at[3]),
        pltpu.make_async_copy(comp_cot.at[:, mine_at], comp_rows_cot.at[0], own_sem.at[4]),
    ]
    loads = []
    for i in range(2):
        s = lax.rem(x + i, 2)
        loads.append(pltpu.make_async_copy(compressed.at[s], past_rows.at[i, 0], load_sem.at[i, 0]))
        loads.append(pltpu.make_async_copy(memory.at[s], past_rows.at[i, 1], load_sem.at[i, 1]))
    loads.append(pltpu.make_async_copy(segment.at[0], seg_rows.at[0], load_sem.at[0, 2]))
    load_other = pltpu.make_async_copy(seg_other, seg_rows.at[1], load_sem.at[1, 2])
    store_xhat = pltpu.make_async_copy(xhat_out, xhat_hbm, store_sem.at[0])
    store_windows = pltpu.make_async_copy(windows, windows_hbm, store_sem.at[1])
    store_grads = pltpu.make_async_copy(comp_grads, comp_grads_hbm, store_sem.at[2])
    store_shard = pltpu.make_async_copy(comp_shard, comp_shard_hbm, store_sem.at[3])

    joined = set()

    def join(k):
        if k not in joined:
            joined.add(k)
            owns[k].wait()
            pairs[k].wait_recv()

    def tick(t):
        lead = t + 3
        if lead < count:
            if lead in needs:
                join(needs[lead])
            gather.start(lead)
        if t < count:
            gather.pass_y(t)
        if 0 <= t - 1 < count:
            gather.pass_core(t - 1)
        if 0 <= t - 2 < count:
            gather.arrive(t - 2)

    def flat_copies(h, slot):
        at = pl.ds(h * 128, 128)
        return [
            pltpu.make_async_copy(
                whole.at[:, :, :, :, at],
                flat.at[slot, :, :, :, :, pl.ds(j * 128, 128)],
                flat_sem.at[slot, j],
            )
            for j, whole in enumerate((query_whole, key_whole, value_whole, place_whole))
        ]

    def norm_into(i, values, at):
        eye = (
            lax.broadcasted_iota(jnp.int32, (tile, tile), 0)
            == lax.broadcasted_iota(jnp.int32, (tile, tile), 1)
        ).astype(BF16)
        gain = jnp.concatenate([params[0:1, :], params[1:2, :]], axis=1)
        shift = jnp.concatenate([params[2:3, :], params[3:4, :]], axis=1)
        xhat = norm_rows(values.astype(F32))
        normed[i, pl.ds(at, tile)] = (xhat * gain + shift).astype(BF16)
        xhat = xhat.astype(BF16)
        for b in range(width // tile):
            xhat_out[i, b * tile : (b + 1) * tile, pl.ds(at, tile)] = dot_nt(
                eye, xhat[:, b * tile : (b + 1) * tile]
            ).astype(BF16)

    def norm_past(i):
        per = past // 2 // tile

        def one(k, carry):
            at = pl.multiple_of(k * tile, tile)
            inner = pl.multiple_of(lax.rem(k, per) * tile, tile)
            norm_into(i, past_rows[i, k // per, pl.ds(inner, tile)], at)
            return carry

        lax.fori_loop(0, past // tile, one, 0)

    def norm_segment(i):
        def one(k, carry):
            at = pl.multiple_of(k * tile, tile)
            norm_into(i, seg_rows[i, pl.ds(at, tile)], past + at)
            return carry

        lax.fori_loop(0, seg_len // tile, one, 0)

    @pl.when(step == 0)
    def _():
        barrier = pltpu.get_barrier_semaphore()
        pl.semaphore_signal(
            barrier, inc=1, device_id={"head": 1 - x}, device_id_type=MESH
        )
        meet(core, low, high, nhi, 1)
        for k in (0, 1, 2, 6, 3, 4, 5):
            pairs[k].start()
        for copy in owns:
            copy.start()
        for copy in loads:
            copy.start()
        gather.start(1)
        join(0)
        gather.start(0)
        gather.start(2)
        tick(0)
        tick(1)
        tick(2)
        summed = pltpu.make_async_copy(small_whole, small_rows, load_sem.at[0, 3])
        summed.start()
        summed.wait()
        both = jnp.sum(small_rows[...].reshape(n, 2, SMALL, LANES).astype(F32), axis=0)
        row = lax.broadcasted_iota(jnp.int32, (SMALL, LANES), 0)
        by_head = jnp.where(x == 0, both[0], both[1])
        params[...] = jnp.where(row < 8, both[0] + both[1], by_head)
        for copy in (loads[0], loads[1], loads[4]):
            copy.wait()
        norm_past(0)
        tick(3)
        norm_segment(0)
        tick(4)

    @pl.when(step == 1)
    def _():
        for copy in loads[2:4]:
            copy.wait()
        norm_past(1)
        tick(5)
        memory_f[:, past // 2 :, :] = jnp.zeros((width // 128, 16, 128), F32)
        for i in range(2):
            for b in range(width // 128):
                at = slice(b * 128, (b + 1) * 128)
                memory_f[b, 0 : past // 2, :] = past_rows[i, 1, :, at].astype(F32)
                for tap in range(3):
                    windows[tap, i * pad_rows : (i + 1) * pad_rows, at] = memory_f[
                        b, pl.ds(tap, pad_rows, stride=3), :
                    ].astype(BF16)
        store_windows.start()
        owns[4].wait()
        pairs[6].wait_recv()
        tick(6)
        for copy in flat_copies(0, 0):
            copy.start()
        comp_rows_both = comp_rows_cot[...].reshape(2 * pad_rows, LANES)
        for tap in range(3):
            for k in range(width // tile):
                at = slice(k * tile, (k + 1) * tile)
                comp_grads[tap * width + k * tile : tap * width + (k + 1) * tile, :] = dot_tn(
                    windows[tap, :, at], comp_rows_both
                ).astype(BF16)
        store_grads.start()

    for k in range(2, 10):

        @pl.when(step == k)
        def _(k=k):
            tick(k + 5)
            h, slot = (k - 2) // 2, ((k - 2) // 2) % 2
            if k % 2 == 0:
                for copy in flat_copies(h, slot):
                    copy.wait()
                if h < 3:
                    for copy in flat_copies(h + 1, 1 - slot):
                        copy.start()
            if k == 3:
                pairs[4].wait_recv()
                load_other.start()
                load_other.wait()
                norm_segment(1)
                store_xhat.start()
                join(3)
                store_shard.start()

    def att_pair(h, i):
        at = pl.ds(pl.multiple_of(x * LANES + h * 128, 128), 128)
        return pltpu.make_async_remote_copy(
            src_ref=att.at[h, i],
            dst_ref=attended.at[1 - i, :, at],
            send_sem=att_send.at[h, i],
            recv_sem=att_recv.at[h, i],
            device_id={"head": 1 - x},
            device_id_type=MESH,
        )

    def att_local(h, i):
        at = pl.ds(pl.multiple_of(x * LANES + h * 128, 128), 128)
        return pltpu.make_async_copy(att.at[h, i], attended.at[i, :, at], att_own.at[h, i])

    @pl.when(step >= 2)
    def _():
        i = lax.rem(step, 2)
        s = lax.rem(x + i, 2)
        slot = lax.rem(head, 2)

        def weights(a, b):
            return flat[slot, :, :, :, :, a:b].reshape(width, b - a)

        @pl.when(i == 0)
        def _():
            mat = weights(384, 512)
            for k in range(table.shape[0] // tile):
                place_out[0, k * tile : (k + 1) * tile] = dot(
                    table[k * tile : (k + 1) * tile], mat
                ).astype(BF16)

        mat = weights(128, 384)
        for k in range(context // tile):
            kv_out[0, 0, k * tile : (k + 1) * tile] = dot(
                normed[i, pl.ds(k * tile, tile)], mat
            ).astype(BF16)
        mat = weights(0, 128)
        bias_at = pl.ds(pl.multiple_of(head * 128, 128), 128)
        for k in range(seg_len // tile):
            queries = dot(normed[i, pl.ds(past + k * tile, tile)], mat)
            at = slice(k * tile, (k + 1) * tile)
            q_out[0, 0, at, 0:128] = (queries + params[8:9, bias_at]).astype(BF16)
            q_out[0, 0, at, 128:256] = (queries + params[9:10, bias_at]).astype(BF16)

        scale = 1.0 / math.sqrt(128)
        for part, out, key_start, key_count, place_start in (
            (0, wide_out, 0, past + HALF, 0),
            (1, near_out, past, seg_len, past - HALF),
        ):
            token = lax.broadcasted_iota(jnp.int32, (HALF, 1), 0) + part * HALF
            end, first = 0, past - valid[s]
            for doc in range(3):
                end = end + docs[s, doc]
                first = jnp.where(token >= end, past + end, first)
            at = slice(part * HALF, (part + 1) * HALF)
            weights_low = attend_rows(
                q_out[0, 0, at, 0:128],
                q_out[0, 0, at, 128:256],
                kv_out[0, 0, key_start : key_start + key_count, 0:128],
                place_out[0, place_start : place_start + key_count],
                first - key_start,
                token + (past - key_start),
                scale,
            ).astype(BF16)
            out[0, 0] = weights_low
            att[head, i, at] = dot(
                weights_low, kv_out[0, 0, key_start : key_start + key_count, 128:256]
            ).astype(BF16)
        att_pair(head, i).start()
        att_local(head, i).start()

    @pl.when(step == pl.num_programs(0) - 1)
    def _():
        for t in range(15, count + 2):
            tick(t)
        for copy in (store_xhat, store_windows, store_grads, store_shard):
            copy.wait()
        for h in range(4):
            for i in range(2):
                att_local(h, i).wait()
                att_pair(h, i).wait()
        for copy in pairs:
            copy.wait_send()
        pairs[5].wait_recv()
        for c in range(count):
            gather.close(c)


def attention_forward(
    n, docs, valid, compressed, memory, segment, cotangent, comp_cot, mats, out_w, up_parts, down_w,
    comp_w, small, table,
):
    _, seg_len, width = segment.shape
    past = compressed.shape[1] + memory.shape[1]
    context = past + seg_len
    nhi = n // 4
    lead = (nhi, 2, 2)
    half_rows = out_w.shape[0]
    comp_rows = comp_w.shape[0]
    pad_rows = comp_cot.shape[0]
    any_spec = pl.BlockSpec(memory_space=pl.ANY)
    smem = pl.BlockSpec(memory_space=pltpu.SMEM)
    single = pl.Buffered(1)
    bf = lambda *shape: jax.ShapeDtypeStruct(shape, BF16)
    head = lambda t: jnp.maximum(t - 2, 0) // 2
    which = lambda t: lax.rem(jnp.maximum(t, 2), 2)
    by_both = lambda t: (head(t), which(t), 0, 0)
    dma = pltpu.SemaphoreType.DMA
    full = lambda shape: pl.BlockSpec(shape, lambda t: (0,) * len(shape), pipeline_mode=single)
    count = 15
    return pl.pallas_call(
        functools.partial(forward_kernel, n, past, seg_len),
        grid=(10,),
        out_shape=(
            bf(2, seg_len, width),
            bf(seg_len, width),
            bf(seg_len, width),
            bf(2, width, context),
            bf(3, 2 * pad_rows, width),
            bf(3 * width, LANES),
            bf(2, comp_rows, LANES),
            jax.ShapeDtypeStruct((SMALL, LANES), F32),
            bf(4, 2, context, 256),
            bf(4, 2, seg_len, 256),
            bf(4, 2, HALF, past + HALF),
            bf(4, 2, HALF, seg_len),
            bf(4, past + HALF, 128),
            *[bf(*lead, *w.shape) for w in mats],
            bf(*lead, 2, half_rows, width),
            bf(4, *lead, 2, half_rows, LANES),
            bf(*lead, *down_w.shape),
            bf(*lead, 2, SMALL, LANES),
        ),
        in_specs=[smem, smem]
        + [any_spec] * 5
        + [full(a.shape) for a in (*mats, out_w, up_parts, down_w, comp_w, small)]
        + [pl.BlockSpec(table.shape, lambda t: (0, 0), pipeline_mode=single)],
        out_specs=(
            *[any_spec] * 6,
            any_spec,
            pl.BlockSpec((SMALL, LANES), lambda t: (0, 0)),
            pl.BlockSpec((1, 1, context, 256), by_both),
            pl.BlockSpec((1, 1, seg_len, 256), by_both),
            pl.BlockSpec((1, 1, HALF, past + HALF), by_both),
            pl.BlockSpec((1, 1, HALF, seg_len), by_both),
            pl.BlockSpec((1, past + HALF, 128), lambda t: (head(t), 0, 0)),
            *[any_spec] * 8,
        ),
        scratch_shapes=[
            pltpu.VMEM((2, half_rows, width), BF16),
            pltpu.VMEM((4, 2, half_rows, LANES), BF16),
            pltpu.VMEM((2, comp_rows, LANES), BF16),
            pltpu.VMEM((2, SMALL, LANES), BF16),
            pltpu.VMEM((2, context, width), BF16),
            pltpu.VMEM((2, width, context), BF16),
            pltpu.VMEM((width // 128, past // 2 + 16, 128), F32),
            pltpu.VMEM((3, 2 * pad_rows, width), BF16),
            pltpu.VMEM((2, pad_rows, LANES), BF16),
            pltpu.VMEM((3 * width, LANES), BF16),
            pltpu.VMEM((2, 2, past // 2, width), BF16),
            pltpu.VMEM((2, seg_len, width), BF16),
            pltpu.VMEM((2,) + lead + (mats[0].shape[0], LANES), BF16),
            pltpu.VMEM(lead + (2, SMALL, LANES), BF16),
            pltpu.VMEM((4, 2, seg_len, 128), BF16),
            dma((2, 4)),
            dma((2, 4)),
            dma((6,)),
            dma((4,)),
            dma((7,)),
            dma((7,)),
            dma((4, 2)),
            dma((4, 2)),
            dma((4, 2)),
        ]
        + Gather.semaphores(count, nhi),
        compiler_params=pltpu.CompilerParams(
            vmem_limit_bytes=VMEM_LIMIT,
            dimension_semantics=("arbitrary",),
            collective_id=0,
            has_side_effects=True,
        ),
        name="attention_forward",
    )(
        docs, valid, compressed, memory, segment, cotangent, comp_cot, *mats, out_w, up_parts, down_w,
        comp_w, small, table,
    )


def gelu_parts(v):
    c = math.sqrt(2.0 / math.pi)
    square = v * v
    t = jnp.tanh(c * (v + 0.044715 * square * v))
    half = 0.5 * (1.0 + t)
    value = v * half
    return value, half + value * (1.0 - half) * (2 * c + (6 * 0.044715 * c) * square)


def feed_kernel(
    n,
    att_in,
    segment,
    seg_other,
    cotangent,
    cot_other,
    out_in,
    up_in,
    down_in,
    params,
    comp,
    comp_shard,
    own_out,
    branch_out,
    residual_out,
    dout,
    out_grads,
    down_grads,
    up_rest,
    small_out,
    comp_out,
    up_out,
    comp_whole,
    att,
    seg,
    cot,
    out_w,
    up,
    down,
    residual,
    low,
    low_t,
    act,
    pre,
    branch,
    terms,
    terms_land,
    cast,
    up_grads,
    mixed,
    stage,
    up_send,
    up_land,
    comp_stage,
    comp_send,
    comp_land,
    load_sem,
    store_sem,
    stage_sem,
    pair_send,
    pair_recv,
    land_c,
    land_y,
    land_z,
    mine,
    mine_sem,
    *sems,
):
    sems, gather_sems = sems[:6], sems[6:]
    x = lax.axis_index("head")
    core, low_y, high, nhi = place(n)
    tile = 256
    _, seg_len, width = att.shape
    rows = width // n
    half_rows = rows // 2
    comp_rows = comp_send.shape[0]

    def pair(src, dst, k):
        return pltpu.make_async_remote_copy(
            src_ref=src,
            dst_ref=dst,
            send_sem=pair_send.at[k],
            recv_sem=pair_recv.at[k],
            device_id={"head": 1 - x},
            device_id_type=MESH,
        )

    terms_pair = pair(cast.at[0], terms_land, 0)
    mixed_pair = pair(mixed.at[1 - x], dout.at[1], 1)
    comp_pair = pair(comp_send, comp_land, 2)
    up_pairs = [pair(up_send.at[f], up_land.at[f], 3 + f) for f in range(2)]
    scatter = Scatter(
        n,
        [
            (part, here, land_c.at[c], land_y.at[c], land_z.at[c], done)
            for c, (part, here, done) in enumerate(
                [
                    (
                        comp.at[:, :, :, pl.ds(m * rows, rows)],
                        False,
                        comp_block(m, x, rows, comp_stage, comp_out, comp_send, comp_pair),
                    )
                    for m in range(3)
                ]
                + [
                    (up_grads.at[f], True, up_block(f, x, up_out, up_send, up_pairs[f]))
                    for f in range(2)
                ]
            )
        ],
        mine,
        mine_sem,
        sems,
    )

    third = comp_rows // 3
    gather = Gather(
        n,
        [
            (
                comp_shard.at[:, pl.ds(m * third, third)],
                comp_whole.at[:, :, :, :, pl.ds(m * third, third)],
            )
            for m in range(3)
        ],
        gather_sems,
    )

    def load(src, dst, k):
        return pltpu.make_async_copy(src, dst, load_sem.at[k])

    loads = {
        "att1": load(att_in.at[1], att.at[1], 0),
        "out": load(out_in, out_w, 1),
        "seg1": load(seg_other, seg.at[1], 2),
        "cot1": load(cot_other, cot.at[1], 3),
        "up": load(up_in, up, 4),
        "down": load(down_in, down, 5),
        "att0": load(att_in.at[0], att.at[0], 6),
        "seg0": load(segment.at[0], seg.at[0], 7),
        "cot0": load(cotangent.at[0], cot.at[0], 8),
    }
    for copy in loads.values():
        copy.start()
    barrier = pltpu.get_barrier_semaphore()
    pl.semaphore_signal(barrier, inc=1, device_id={"head": 1 - x}, device_id_type=MESH)
    meet(core, low_y, high, nhi, 1)
    scatter.start(0)
    scatter.start(1)
    gather.start(0)

    eye = (
        lax.broadcasted_iota(jnp.int32, (tile, tile), 0)
        == lax.broadcasted_iota(jnp.int32, (tile, tile), 1)
    ).astype(BF16)
    gain = jnp.concatenate([params[4:5, :], params[5:6, :]], axis=1)
    shift = jnp.concatenate([params[6:7, :], params[7:8, :]], axis=1)

    def project(i):
        for k in range(seg_len // tile):
            at = slice(k * tile, (k + 1) * tile)
            whole_at = slice(i * seg_len + k * tile, i * seg_len + (k + 1) * tile)
            value = seg[i, at].astype(F32) + dot(att[i, at], out_w[...])
            residual[at, :] = value
            value = (norm_rows(value) * gain + shift).astype(BF16)
            low[whole_at, :] = value
            for b in range(width // tile):
                low_t[b * tile : (b + 1) * tile, whole_at] = dot_nt(
                    eye, value[:, b * tile : (b + 1) * tile]
                ).astype(BF16)

    def hidden(i, between):
        whole_at = slice(i * seg_len, (i + 1) * seg_len)
        branch[...] = jnp.zeros_like(branch)
        terms[...] = jnp.zeros_like(terms)

        def one(f, carry):
            down_at = pl.ds(pl.multiple_of(f * LANES, LANES), LANES)
            value, slope = gelu_parts(dot(low[whole_at, :], up[f]))
            value = value.astype(BF16)
            act[f, whole_at, :] = value
            back = dot_nt(cot[i], down[down_at, :]).astype(BF16).astype(F32)
            back = (back * slope).astype(BF16)
            pre[f, whole_at, :] = back
            branch[...] += dot(value, down[down_at, :])
            terms[...] += dot_nt(back, up[f])
            for k, steps in enumerate(between):

                @pl.when(f == k)
                def _(steps=steps):
                    for run, c in steps:
                        run(c)

            return carry

        lax.fori_loop(0, 4, one, 0)

    for name in ("att1", "out", "seg1"):
        loads[name].wait()
    project(1)
    scatter.add_core(0)
    scatter.start(2)
    gather.start(1)
    for name in ("cot1", "up", "down"):
        loads[name].wait()
    hidden(
        1,
        (
            ((scatter.add_core, 1), (gather.pass_y, 0)),
            ((scatter.add_core, 2), (scatter.add_y, 0), (gather.start, 2)),
            ((gather.pass_y, 1),),
            ((scatter.add_y, 1),),
        ),
    )
    cast[0] = terms[...].astype(BF16)
    terms_pair.start()
    cast[1] = branch[...].astype(BF16)
    store_branch = pltpu.make_async_copy(cast.at[1], branch_out, store_sem.at[0])
    store_branch.start()
    for name in ("att0", "seg0", "cot0"):
        loads[name].wait()
    project(0)
    scatter.add_z(0)
    hidden(
        0,
        (
            ((gather.pass_core, 0),),
            ((gather.pass_y, 2),),
            ((scatter.add_y, 2),),
            ((scatter.add_z, 1),),
        ),
    )
    branch[...] += residual[...]
    store_own = pltpu.make_async_copy(branch, own_out, store_sem.at[1])
    store_own.start()

    block = tile // (4 * rows)

    def up_grad(f):
        for k in range(width // tile):
            grad = dot(low_t[k * tile : (k + 1) * tile, :], pre[f]).astype(BF16)
            up_grads[f, k * block : (k + 1) * block] = grad.reshape(block, 2, 2, rows, LANES)
        if f < 2:
            scatter.start(3 + f)

    up_grad(0)
    gather.pass_core(1)
    up_grad(1)
    scatter.add_core(3)
    scatter.add_z(2)
    up_grad(2)
    scatter.add_core(4)
    up_grad(3)
    store_rest = pltpu.make_async_copy(up_grads.at[pl.ds(2, 2)], up_rest, store_sem.at[4])
    store_rest.start()

    terms_pair.wait_recv()
    gain_grad = jnp.zeros((1, width), F32)
    shift_grad = jnp.zeros((1, width), F32)
    terms_pair.wait_send()
    for k in range(seg_len // tile):
        at = slice(k * tile, (k + 1) * tile)
        grad = terms[at, :] + terms_land[at, :].astype(F32)
        value = residual[at, :]
        mean = jnp.mean(value, axis=-1, keepdims=True)
        centred = value - mean
        rstd = lax.rsqrt(jnp.mean(centred * centred, axis=-1, keepdims=True) + 1e-05)
        xhat = centred * rstd
        gain_grad += jnp.sum(grad * xhat, axis=0, keepdims=True)
        shift_grad += jnp.sum(grad, axis=0, keepdims=True)
        grad = cot[0, at].astype(F32) + norm_back(xhat, rstd, grad * gain)
        residual[at, :] = grad
        grad = grad.astype(BF16)
        cast[0, at, :] = grad
        back = dot_nt(grad, out_w[...]).astype(BF16)
        mixed[0, at, :] = back[:, 0:LANES]
        mixed[1, at, :] = back[:, LANES:]
    mixed_pair.start()
    store_dout = pltpu.make_async_copy(mixed.at[x], dout.at[0], store_sem.at[2])
    store_dout.start()
    store_residual = pltpu.make_async_copy(residual, residual_out, store_sem.at[3])
    store_residual.start()
    small_out[...] = jnp.zeros_like(small_out)
    small_out[4:5, :] = gain_grad[:, 0:LANES]
    small_out[5:6, :] = gain_grad[:, LANES:]
    small_out[6:7, :] = shift_grad[:, 0:LANES]
    small_out[7:8, :] = shift_grad[:, LANES:]
    gather.pass_core(2)

    staged = [None, None]
    jobs = [(out_grads, k * tile, None, k) for k in range(width // tile)]
    jobs += [
        (down_grads, f * LANES + k * tile, f, k) for f in range(4) for k in range(LANES // tile)
    ]
    for j, (target, start, f, k) in enumerate(jobs):
        slot = j % 2
        at = slice(k * tile, (k + 1) * tile)
        if f is None:
            grad = dot_tn(att[0, :, at], cast[0])
        else:
            grad = dot_tn(act[f, 0:seg_len, at], cot[0]) + dot_tn(act[f, seg_len:, at], cot[1])
        if staged[slot] is not None:
            staged[slot].wait()
        stage[slot] = grad.astype(BF16)
        staged[slot] = pltpu.make_async_copy(
            stage.at[slot], target.at[pl.ds(start, tile)], stage_sem.at[slot]
        )
        staged[slot].start()
        if j == 3:
            scatter.add_y(3)
        if j == 10:
            scatter.add_y(4)
            scatter.add_z(3)
    scatter.add_z(4)
    for m in range(3):
        gather.arrive(m)
    comp_pair.wait_recv()
    to = pl.ds(pl.multiple_of((1 - x) * LANES, LANES), LANES)
    comp_out[:, to] = comp_land[...].astype(F32)
    for f in range(2):
        up_pairs[f].wait_recv()
        up_out[1 - x, f] = up_land[f].astype(F32)
    mixed_pair.wait_recv()
    for copy in [mixed_pair, comp_pair, *up_pairs]:
        copy.wait_send()
    for copy in [*staged, store_branch, store_own, store_dout, store_residual, store_rest]:
        copy.wait()
    for c in range(5):
        scatter.close(c)
    for m in range(3):
        gather.close(m)


def comp_block(m, x, rows, stage, out, send, pair):
    def done(total):
        stage[m * rows : (m + 1) * rows, :] = total
        if m == 2:
            half = send.shape[0]
            upper, lower = stage[0:half, :], stage[half:, :]
            to = pl.ds(pl.multiple_of(x * LANES, LANES), LANES)
            out[:, to] = jnp.where(x == 0, upper, lower)
            send[...] = jnp.where(x == 0, lower, upper).astype(BF16)
            pair.start()

    return done


def up_block(f, x, out, send, pair):
    def done(total):
        half = send.shape[1]
        upper, lower = total[0:half], total[half:]
        out[x, f] = jnp.where(x == 0, upper, lower)
        send[f] = jnp.where(x == 0, lower, upper).astype(BF16)
        pair.start()

    return done


def feed_forward(
    n, att, segment, seg_other, cotangent, cot_other, out_w, up, down, params, comp, comp_shard
):
    _, seg_len, width = att.shape
    rows = width // n
    half_rows = rows // 2
    nhi = n // 4
    comp_rows = comp.shape[3] // 2
    total = 2 * seg_len
    any_spec = pl.BlockSpec(memory_space=pl.ANY)
    vmem = pl.BlockSpec(memory_space=pltpu.VMEM)
    dma = pltpu.SemaphoreType.DMA
    f32 = lambda *shape: jax.ShapeDtypeStruct(shape, F32)
    bf = lambda *shape: jax.ShapeDtypeStruct(shape, BF16)
    return pl.pallas_call(
        functools.partial(feed_kernel, n),
        out_shape=(
            f32(seg_len, width),
            bf(seg_len, width),
            f32(seg_len, width),
            bf(2, seg_len, LANES),
            bf(width, width),
            bf(4 * LANES, width),
            bf(2, nhi, 2, 2, rows, LANES),
            f32(SMALL, LANES),
            f32(comp_rows, width),
            f32(2, 2, half_rows, LANES),
            bf(nhi, 2, 2, *comp_shard.shape),
        ),
        in_specs=[any_spec] * 8 + [vmem, any_spec, vmem],
        out_specs=(any_spec,) * 7 + (vmem,) * 3 + (any_spec,),
        scratch_shapes=[
            pltpu.VMEM((2, seg_len, width), BF16),
            pltpu.VMEM((2, seg_len, width), BF16),
            pltpu.VMEM((2, seg_len, width), BF16),
            pltpu.VMEM((width, width), BF16),
            pltpu.VMEM((4, width, LANES), BF16),
            pltpu.VMEM((4 * LANES, width), BF16),
            pltpu.VMEM((seg_len, width), F32),
            pltpu.VMEM((total, width), BF16),
            pltpu.VMEM((width, total), BF16),
            pltpu.VMEM((4, total, LANES), BF16),
            pltpu.VMEM((4, total, LANES), BF16),
            pltpu.VMEM((seg_len, width), F32),
            pltpu.VMEM((seg_len, width), F32),
            pltpu.VMEM((seg_len, width), BF16),
            pltpu.VMEM((2, seg_len, width), BF16),
            pltpu.VMEM((4, nhi, 2, 2, rows, LANES), BF16),
            pltpu.VMEM((2, seg_len, LANES), BF16),
            pltpu.VMEM((2, 256, width), BF16),
            pltpu.VMEM((2, half_rows, LANES), BF16),
            pltpu.VMEM((2, half_rows, LANES), BF16),
            pltpu.VMEM((3 * rows, LANES), F32),
            pltpu.VMEM((comp_rows, LANES), BF16),
            pltpu.VMEM((comp_rows, LANES), BF16),
            dma((9,)),
            dma((5,)),
            dma((2,)),
            dma((5,)),
            dma((5,)),
        ]
        + Scatter.scratch(5, nhi, rows)
        + Gather.semaphores(3, nhi),
        compiler_params=pltpu.CompilerParams(
            vmem_limit_bytes=VMEM_LIMIT, collective_id=2, has_side_effects=True
        ),
        name="feed_forward",
    )(att, segment, seg_other, cotangent, cot_other, out_w, up, down, params, comp, comp_shard)


def norm_back(xhat, rstd, grad):
    a = jnp.mean(grad, axis=-1, keepdims=True)
    b = jnp.mean(grad * xhat, axis=-1, keepdims=True)
    return rstd * (grad - a - xhat * b)


def backward_kernel(
    n,
    past,
    seg_len,
    dout,
    kv,
    q,
    wide,
    near,
    place_keys,
    xhat_hbm,
    query_w,
    key_w,
    value_w,
    table_hbm,
    params,
    segment,
    seg_other,
    residual_hbm,
    small_in,
    own_sum,
    branch,
    up,
    down,
    out,
    result_out,
    segment_out,
    query_out,
    key_out,
    value_out,
    place_out,
    out_out,
    down_out,
    up_out,
    small_out,
    xhat_t,
    table_t,
    residual_grad,
    load_sem,
    up_send,
    up_land,
    flat,
    raw,
    sums,
    place_sum,
    input_grad,
    dkv,
    columns,
    gain_sum,
    shift_sum,
    head_grads,
    context_land,
    context_send,
    branch_land,
    own_rows_sum,
    own_sem,
    seg_rows,
    seg_sem,
    out_keep,
    out_send,
    out_land,
    small_mine,
    small_c,
    small_y,
    small_z,
    small_x,
    pair_send,
    pair_recv,
    small_send,
    small_recv,
    land_c,
    land_y,
    land_z,
    mine,
    mine_sem,
    *sems,
):
    step = pl.program_id(0)
    x = lax.axis_index("head")
    core, low, high, nhi = place(n)
    head = lax.rem(step, 4)
    tile = 256
    context = past + seg_len
    width = flat.shape[0]
    rows = width // n
    half_rows = rows // 2
    scale = 1.0 / math.sqrt(128)
    flip = (
        lax.broadcasted_iota(jnp.int32, (HALF, HALF), 0)
        + lax.broadcasted_iota(jnp.int32, (HALF, HALF), 1)
        == HALF - 1
    ).astype(BF16)

    def pair(src, dst, k):
        return pltpu.make_async_remote_copy(
            src_ref=src,
            dst_ref=dst,
            send_sem=pair_send.at[k],
            recv_sem=pair_recv.at[k],
            device_id={"head": 1 - x},
            device_id_type=MESH,
        )

    context_pair = pair(context_send, context_land, 0)
    branch_pair = pair(branch, branch_land, 1)
    out_pairs = [pair(out_send.at[b], out_land.at[b], 2 + b) for b in range(2)]
    load_own = pltpu.make_async_copy(own_sum, own_rows_sum, own_sem)
    up_pairs = [pair(up_send.at[f], up_land.at[f], 4 + f) for f in range(2)]
    load_xhat = [
        pltpu.make_async_copy(xhat_hbm.at[1 - i], xhat_t, load_sem.at[0]) for i in range(2)
    ]
    load_table = pltpu.make_async_copy(table_hbm, table_t, load_sem.at[1])
    load_residual = pltpu.make_async_copy(residual_hbm, residual_grad, load_sem.at[2])
    load_other = pltpu.make_async_copy(seg_other, seg_rows, seg_sem)
    load_segment = pltpu.make_async_copy(segment.at[0], seg_rows, seg_sem)

    def down_done(a, b):
        def done(total):
            down_out[a * rows : (a + 1) * rows, b * LANES : (b + 1) * LANES] = total

        return done

    def out_done(b):
        def done(total):
            upper, lower = total[0:half_rows], total[half_rows:]
            out_keep[b] = jnp.where(x == 0, upper, lower)
            out_send[b] = jnp.where(x == 0, lower, upper).astype(BF16)
            out_pairs[b].start()

        return done

    def head_done(h):
        def done(total):
            for j, ref in enumerate((query_out, key_out, value_out, place_out)):
                ref[:, h * 128 : (h + 1) * 128] = total[:, j * 128 : (j + 1) * 128]

        return done

    parts = [(up.at[f], False, up_block(f, x, up_out, up_send, up_pairs[f])) for f in range(2)]
    for a in range(2):
        for b in range(2):
            at, to = pl.ds(a * rows, rows), pl.ds(b * LANES, LANES)
            parts.append((down.at[:, :, :, at, to], False, down_done(a, b)))
    parts += [
        (out.at[:, :, :, :, pl.ds(b * LANES, LANES)], False, out_done(b)) for b in range(2)
    ]
    parts += [(head_grads.at[h], True, head_done(h)) for h in range(4)]
    scatter = Scatter(
        n,
        [
            (part, here, land_c.at[c], land_y.at[c], land_z.at[c], done)
            for c, (part, here, done) in enumerate(parts)
        ],
        mine,
        mine_sem,
        sems,
    )
    count = len(parts)

    @pl.when(step == 0)
    def _():
        barrier = pltpu.get_barrier_semaphore()
        pl.semaphore_signal(barrier, inc=1, device_id={"head": 1 - x}, device_id_type=MESH)
        meet(core, low, high, nhi, 1)
        load_xhat[0].start()
        load_other.start()
        load_own.start()
        load_table.start()
        load_residual.start()
        branch_pair.start()
        for j in range(2):
            line = jnp.concatenate([params[2 * j : 2 * j + 1, :], params[2 * j + 1 : 2 * j + 2, :]], axis=1)
            columns[j] = jnp.broadcast_to(line, (128, width)).T
        raw[...] = jnp.zeros_like(raw)
        sums[...] = jnp.zeros_like(sums)
        place_sum[...] = jnp.zeros_like(place_sum)
        gain_sum[...] = jnp.zeros_like(gain_sum)
        shift_sum[...] = jnp.zeros_like(shift_sum)
        small_mine[...] = small_in[...]

    @pl.when(head == 0)
    def _():
        input_grad[...] = jnp.zeros_like(input_grad)

    start, add_core, add_y, add_z = scatter.start, scatter.add_core, scatter.add_y, scatter.add_z
    before = {
        0: ((start, 0), (start, 1)),
        1: ((add_core, 1), (start, 3)),
        2: ((add_core, 3), (start, 5)),
        3: ((add_y, 2), (add_core, 5), (start, 7)),
        4: ((add_y, 3),),
        5: ((start, 8), (add_z, 3), (add_core, 7)),
        6: ((add_z, 4), (start, 9)),
        7: ((add_y, 7), (start, 10)),
    }
    within = {
        0: ((add_core, 0), (start, 2)),
        1: ((add_y, 0), (add_core, 2), (start, 4)),
        2: ((add_y, 1), (add_z, 0), (add_core, 4), (start, 6)),
        3: ((add_z, 1), (add_core, 6)),
        4: ((add_y, 4), (add_z, 2)),
        5: ((add_y, 5), (add_core, 8)),
        6: ((add_y, 6), (add_z, 5), (add_core, 9)),
        7: ((add_core, 10), (add_z, 6)),
    }

    def run(table):
        for k, steps in table.items():

            @pl.when(step == k)
            def _(steps=steps):
                for do, c in steps:
                    do(c)

    run(before)

    for j, mat in enumerate((query_w, key_w, value_w)):
        flat[:, j * 128 : (j + 1) * 128] = mat[...]

    query_grads = []
    key_rows = []
    value_rows = []
    place_rows = []
    bias_at = pl.ds(pl.multiple_of(head * 128, 128), 128)
    for part, weights_ref, key_start, key_count, place_start in (
        (0, wide, 0, past + HALF, 0),
        (1, near, past, seg_len, past - HALF),
    ):
        at = slice(part * HALF, (part + 1) * HALF)
        keys_at = slice(key_start, key_start + key_count)
        attn = weights_ref[0, 0]
        grad = dout[0, at]
        value_rows.append(dot_tn(grad, attn))
        weights_grad = dot_nt(grad, kv[0, 0, keys_at, 128:256])
        attn = attn.astype(F32)
        row = jnp.sum(weights_grad * attn, axis=1, keepdims=True)
        scores_grad = (attn * (weights_grad - row) * scale).astype(BF16)
        content_grad = dot(scores_grad, kv[0, 0, keys_at, 0:128]).astype(BF16)
        key_rows.append(dot_tn(q[0, 0, at, 0:128], scores_grad))
        by_place = pltpu.roll(dot(flip, scores_grad), 0, 1, stride=1, stride_axis=0).astype(BF16)
        place_grad = dot(by_place, place_keys[0, place_start : place_start + key_count])
        place_grad = dot(flip, place_grad.astype(BF16)).astype(BF16)
        flipped_q = dot(flip, q[0, 0, at, 128:256]).astype(BF16)
        place_rows.append(dot_tn(flipped_q, by_place))
        content_f = content_grad.astype(F32)
        place_f = place_grad.astype(F32)
        small_mine[8:9, bias_at] += jnp.sum(content_f, axis=0, keepdims=True)
        small_mine[9:10, bias_at] += jnp.sum(place_f, axis=0, keepdims=True)
        query_grads.append((content_f + place_f).astype(BF16))

    for j, (wide_rows, near_rows) in enumerate((key_rows, value_rows)):
        at = slice(j * 128, (j + 1) * 128)
        dkv[at, 0:past] = wide_rows[:, 0:past].astype(BF16)
        dkv[at, past : past + HALF] = (wide_rows[:, past:] + near_rows[:, 0:HALF]).astype(BF16)
        dkv[at, past + HALF :] = near_rows[:, HALF:].astype(BF16)
    split = past - HALF
    for at, rows_grad in (
        (slice(0, split), place_rows[0][:, 0:split]),
        (slice(split, None), place_rows[0][:, split:] + place_rows[1]),
    ):
        place_sum[head, :, at] = (
            place_sum[head, :, at].astype(F32) + rows_grad.astype(BF16).astype(F32)
        ).astype(BF16)
    dq = jnp.concatenate(query_grads, axis=0)
    stacked = jnp.concatenate([dq, dkv[:, past:].astype(F32).T.astype(BF16)], axis=1)

    run(within)

    @pl.when(step == 0)
    def _():
        load_xhat[0].wait()

    @pl.when(step == 4)
    def _():
        load_xhat[1].wait()
        load_table.wait()

    ones = jnp.ones((8, context), BF16)
    sums[head, :, 0:128] += dot(ones[:, 0:seg_len], dq)
    sums[head, :, 128:384] += dot_nt(ones, dkv[...])
    for k in range(width // tile):
        at = slice(k * tile, (k + 1) * tile)
        raw[head, at, 0:128] += dot(xhat_t[at, past:], dq)
        raw[head, at, 128:384] += dot_nt(xhat_t[at, :], dkv[...])
        input_grad[:, at] += dot_nt(stacked, flat[at, 0:384])

    @pl.when(step >= 4)
    def _():
        place_low = place_sum[head]
        block = tile // (4 * rows)
        total = sums[head, 0:1, :]
        for k in range(width // tile):
            at = slice(k * tile, (k + 1) * tile)
            to = slice(k * block, (k + 1) * block)
            got = raw[head, at, :]
            mats = flat[at, 0:384].astype(F32)
            for acc, term in ((gain_sum, mats * got), (shift_sum, mats * total)):
                acc[at, :] += term[:, 0:128] + term[:, 128:256] + term[:, 256:384]
            grad = (columns[0, at, 0:1] * got + columns[1, at, 0:1] * total).astype(BF16)
            head_grads[head, to, :, :, :, 0:384] = grad.reshape(block, 2, 2, rows, 384)
            grad = dot_nt(table_t[at, :], place_low).astype(BF16)
            head_grads[head, to, :, :, :, 384:512] = grad.reshape(block, 2, 2, rows, 128)

    def own_rows(k):
        gain = jnp.concatenate([params[0:1, :], params[1:2, :]], axis=1)
        at = slice(k * tile, (k + 1) * tile)
        values = seg_rows[at, :].astype(F32)
        mean = jnp.mean(values, axis=-1, keepdims=True)
        centred = values - mean
        rstd = lax.rsqrt(jnp.mean(centred * centred, axis=-1, keepdims=True) + 1e-05)
        return norm_back(centred * rstd, rstd, input_grad[at, :] * gain)

    @pl.when(step == 4)
    def _():
        load_segment.start()

    @pl.when(step == 3)
    def _():
        load_xhat[1].start()
        load_other.wait()
        for k in range(seg_len // tile):
            context_send[k * tile : (k + 1) * tile, :] = own_rows(k).astype(BF16)
        context_pair.start()

    @pl.when(step == 5)
    def _():
        branch_pair.wait_recv()
        load_own.wait()
        for k in range(seg_len // tile):
            at = slice(k * tile, (k + 1) * tile)
            result_out[0, at] = (own_rows_sum[at, :] + branch_land[at, :].astype(F32)).astype(BF16)

    @pl.when(step == 7)
    def _():
        start(11)
        one = jnp.ones((8, 128), F32)
        for acc, row in ((gain_sum, 0), (shift_sum, 2)):
            line = lax.dot_general(
                one,
                acc[...],
                (((1,), (1,)), ((), ())),
                precision=lax.Precision.HIGHEST,
                preferred_element_type=F32,
            )
            small_mine[row : row + 1, :] = line[0:1, 0:LANES]
            small_mine[row + 1 : row + 2, :] = line[0:1, LANES:]

        def to_dp(src, dst, k, index):
            return remote(src, dst, small_send.at[k], small_recv.at[k], index)

        copies = [to_dp(small_mine, small_c.at[1], 0, high * 4 + low * 2 + (1 - core))]
        copies[0].start()
        add_core(11)
        load_segment.wait()
        load_residual.wait()
        context_pair.wait_recv()
        for k in range(seg_len // tile):
            at = slice(k * tile, (k + 1) * tile)
            segment_out[0, at] = (
                residual_grad[at, :] + own_rows(k) + context_land[at, :].astype(F32)
            ).astype(BF16)
        add_y(8)
        add_z(7)
        copies[0].wait_recv()
        small_c[0] = small_mine[...] + small_c[1]
        copies.append(to_dp(small_c.at[0], small_y.at[1], 1, high * 4 + (1 - low) * 2 + core))
        copies[1].start()
        add_y(9)
        add_z(8)
        copies[1].wait_recv()
        small_y[0] = small_c[0] + small_y[1]
        along = []
        for k in range(1, nhi):
            to = lax.rem(high + k, nhi) * 4 + low * 2 + core
            along.append(to_dp(small_y.at[0], small_z.at[k], 2 + k, to))
        for copy in along:
            copy.start()
        add_y(10)
        add_z(9)
        for copy in along:
            copy.wait_recv()
        line = small_y[0]
        for k in range(1, nhi):
            line = line + small_z[k]
        small_z[0] = line
        last = pltpu.make_async_remote_copy(
            src_ref=small_z.at[0],
            dst_ref=small_x,
            send_sem=small_send.at[2],
            recv_sem=small_recv.at[2],
            device_id={"head": 1 - x},
            device_id_type=MESH,
        )
        last.start()
        add_y(11)
        add_z(10)
        add_z(11)
        for f in range(2):
            up_pairs[f].wait_recv()
            up_out[1 - x, f] = up_land[f].astype(F32)
        for b in range(2):
            out_pairs[b].wait_recv()
            out_out[:, b * LANES : (b + 1) * LANES] = out_keep[b] + out_land[b].astype(F32)
        last.wait_recv()
        line = lax.broadcasted_iota(jnp.int32, (SMALL, LANES), 0)
        small_out[...] = small_z[0] + jnp.where(line < 8, small_x[...], 0.0)
        for copy in [context_pair, branch_pair, *up_pairs, *out_pairs, *copies, *along, last]:
            copy.wait_send()
        for c in range(count):
            scatter.close(c)


def attention_backward(
    n, dout, kv, q, wide, near, place_keys, xhat_t, mats, table_t, params, segment,
    seg_other, residual_grad, small_in, own_sum, branch, up, down, out,
):
    _, seg_len, width = segment.shape
    context = kv.shape[2]
    past = context - seg_len
    rows = width // n
    nhi = n // 4
    half_rows = rows // 2
    seq = lambda t: 1 - t // 4
    head = lambda t: lax.rem(t, 4)
    by_both = lambda t: (head(t), seq(t), 0, 0)
    single = pl.Buffered(1)
    any_spec = pl.BlockSpec(memory_space=pl.ANY)
    dma = pltpu.SemaphoreType.DMA
    f32 = lambda *shape: jax.ShapeDtypeStruct(shape, F32)
    lead = (nhi, 2, 2)
    full = lambda shape: pl.BlockSpec(shape, lambda t: (0,) * len(shape), pipeline_mode=single)
    outs = (
        jax.ShapeDtypeStruct((1, seg_len, width), BF16),
        jax.ShapeDtypeStruct((1, seg_len, width), BF16),
        f32(rows, LANES),
        f32(rows, LANES),
        f32(rows, LANES),
        f32(rows, LANES),
        f32(half_rows, width),
        f32(2 * rows, width),
        f32(2, 2, half_rows, LANES),
        f32(SMALL, LANES),
    )
    return pl.pallas_call(
        functools.partial(backward_kernel, n, past, seg_len),
        grid=(8,),
        out_shape=outs,
        in_specs=[
            pl.BlockSpec((1, seg_len, 128), lambda t: (seq(t), 0, head(t))),
            pl.BlockSpec((1, 1, context, 256), by_both),
            pl.BlockSpec((1, 1, seg_len, 256), by_both),
            pl.BlockSpec((1, 1, HALF, past + HALF), by_both),
            pl.BlockSpec((1, 1, HALF, seg_len), by_both),
            pl.BlockSpec((1, past + HALF, 128), lambda t: (head(t), 0, 0)),
            any_spec,
            *[pl.BlockSpec((width, 128), lambda t: (0, head(t)))] * 3,
            any_spec,
            full((SMALL, LANES)),
            any_spec,
            any_spec,
            any_spec,
            full((SMALL, LANES)),
            any_spec,
            any_spec,
            any_spec,
            any_spec,
            any_spec,
        ],
        out_specs=tuple(full(o.shape) for o in outs),
        scratch_shapes=[
            pltpu.VMEM((width, context), BF16),
            pltpu.VMEM(table_t.shape, BF16),
            pltpu.VMEM((seg_len, width), F32),
            dma((3,)),
            pltpu.VMEM((2, half_rows, LANES), BF16),
            pltpu.VMEM((2, half_rows, LANES), BF16),
            pltpu.VMEM((width, 384), BF16),
            pltpu.VMEM((4, width, 384), F32),
            pltpu.VMEM((4, 8, 384), F32),
            pltpu.VMEM((4, 128, past + HALF), BF16),
            pltpu.VMEM((seg_len, width), F32),
            pltpu.VMEM((256, context), BF16),
            pltpu.VMEM((2, width, 128), F32),
            pltpu.VMEM((width, 128), F32),
            pltpu.VMEM((width, 128), F32),
            pltpu.VMEM((4,) + lead + (rows, LANES), BF16),
            pltpu.VMEM((seg_len, width), BF16),
            pltpu.VMEM((seg_len, width), BF16),
            pltpu.VMEM((seg_len, width), BF16),
            pltpu.VMEM((seg_len, width), F32),
            dma(()),
            pltpu.VMEM((seg_len, width), BF16),
            dma(()),
            pltpu.VMEM((2, half_rows, LANES), F32),
            pltpu.VMEM((2, half_rows, LANES), BF16),
            pltpu.VMEM((2, half_rows, LANES), BF16),
            pltpu.VMEM((SMALL, LANES), F32),
            pltpu.VMEM((2, SMALL, LANES), F32),
            pltpu.VMEM((2, SMALL, LANES), F32),
            pltpu.VMEM((nhi, SMALL, LANES), F32),
            pltpu.VMEM((SMALL, LANES), F32),
            dma((6,)),
            dma((6,)),
            dma((2 + nhi,)),
            dma((2 + nhi,)),
        ]
        + Scatter.scratch(12, nhi, rows),
        compiler_params=pltpu.CompilerParams(
            vmem_limit_bytes=VMEM_LIMIT,
            dimension_semantics=("arbitrary",),
            collective_id=1,
            has_side_effects=True,
        ),
        name="attention_backward",
    )(
        dout, kv, q, wide, near, place_keys, xhat_t, *mats, table_t,
        params, segment, seg_other,
        residual_grad, small_in, own_sum, branch, up, down, out,
    )


def finish_kernel(n, *refs):
    count = (len(refs) - 1) // 2
    ups, refs = refs[:2], refs[1:]
    up_out = refs[count]
    size = LANES // (n // 4)
    for f in range(4):
        for j in range(n // 4):
            for half in range(2):
                to = ((f * (n // 4) + j) * 2 + half) * size
                up_out[:, to : to + size] = ups[f // 2][
                    half, f % 2, :, j * size : (j + 1) * size
                ]
    for src, dst in zip(refs[1:count], refs[count + 1 :]):
        dst[...] = src[...]


def finish(n, ups, others):
    vmem = pl.BlockSpec(memory_space=pltpu.VMEM)
    same = [jax.ShapeDtypeStruct(a.shape, a.dtype) for a in others]
    out = jax.ShapeDtypeStruct((ups[0].shape[2], 8 * LANES), F32)
    return pl.pallas_call(
        functools.partial(finish_kernel, n),
        out_shape=(out, *same),
        in_specs=[vmem] * (2 + len(others)),
        out_specs=(vmem,) * (1 + len(others)),
        compiler_params=pltpu.CompilerParams(vmem_limit_bytes=VMEM_LIMIT),
        name="finish",
    )(*ups, *others)


def body(
    n,
    segment,
    memory,
    compressed,
    doc_lengths,
    memory_valid,
    query_weight,
    key_weight,
    value_weight,
    position_weight,
    content_bias,
    position_bias,
    output_weight,
    up_weight,
    down_weight,
    compress_weight,
    norm_gain,
    norm_shift,
    post_gain,
    post_shift,
    cotangent,
    compress_cotangent,
):
    x = lax.axis_index("head")
    dp = lax.axis_index("dp")
    first = x == 0
    nhi = n // 4
    width = segment.shape[2]
    seg_len = segment.shape[1]
    past = memory.shape[1] + compressed.shape[1]
    context = past + seg_len
    rows = query_weight.shape[0]
    half_rows = output_weight.shape[0]
    new_count = compress_cotangent.shape[1]
    comp_rows = compress_weight.shape[0]

    def swap(a):
        return lax.ppermute(a, "head", [(0, 1), (1, 0)])

    def pick(a, index):
        return jnp.where(index == 0, a[0], a[1])

    def in_order(own, got, axis):
        return jnp.where(
            first,
            jnp.concatenate([own, got], axis=axis),
            jnp.concatenate([got, own], axis=axis),
        )

    ffr = down_weight.shape[0]
    up_parts = (
        up_weight.reshape(half_rows, 4, n // 4, 2, ffr)
        .transpose(3, 1, 0, 2, 4)
        .reshape(2, 4, half_rows, LANES)
    )
    per = content_bias.shape[1]
    vectors = jnp.stack([norm_gain, norm_shift, post_gain, post_shift])
    here = jnp.arange(2 * n, dtype=jnp.int32)[None, :, None] == dp * 2 + x
    norms = jnp.where(here, vectors[:, None, :], 0).reshape(8, LANES)
    here = jnp.arange(n, dtype=jnp.int32)[None, None, :, None] == dp
    bias = jnp.stack([content_bias, position_bias])[:, :, None, :]
    bias = jnp.where(here, bias, 0).reshape(2, LANES)
    small = jnp.concatenate([norms, bias, jnp.zeros((SMALL - 10, LANES), BF16)])
    pad_rows = -(-new_count // 16) * 16
    comp_cot = jnp.pad(compress_cotangent[0], ((0, pad_rows - new_count), (0, 0)))
    table = position_rows(context, width, past + HALF)

    (
        att, seg_other, cot_other, xhat_t, windows, comp_grads, comp_shard, params, kv, q, wide, near,
        place_keys, query_whole, key_whole, value_whole, _, out_whole, up_whole, down_whole, _,
    ) = attention_forward(
        n, doc_lengths, memory_valid, compressed, memory, segment, cotangent, comp_cot,
        (query_weight, key_weight, value_weight, position_weight),
        output_weight, up_parts, down_weight, compress_weight, small, jnp.asarray(table),
    )

    lead = (nhi, 2, 2)
    (
        own_sum, branch, residual_grad, dout, out_grads, down_grads, up_rest, small_in, comp_done,
        up_first, comp_whole,
    ) = feed_forward(
        n, att, segment, seg_other, cotangent, cot_other, out_whole.reshape(width, width),
        up_whole.reshape(4, width, LANES), down_whole.reshape(4 * LANES, width), params,
        comp_grads.reshape(lead + (3 * rows, LANES)), comp_shard,
    )

    made = jnp.einsum(
        "kic,kcd->id", windows, comp_whole.reshape(3, width, LANES), preferred_element_type=F32
    ).astype(BF16)
    made = in_order(made[:new_count], swap(made[pad_rows : pad_rows + new_count]), 1)

    mats = [w.reshape(width, LANES) for w in (query_whole, key_whole, value_whole)]
    result, segment_grad, *matrices, up_last, small_done = attention_backward(
        n, dout, kv, q, wide, near, place_keys, xhat_t, mats, jnp.asarray(table.T.copy()),
        params, segment, seg_other, residual_grad, small_in, own_sum, branch,
        up_rest,
        down_grads.reshape(lead + (2 * rows, 2 * LANES)),
        out_grads.reshape(lead + (rows, 2 * LANES)),
    )

    up_final, result, segment_grad, *matrices, comp_final = finish(
        n, (up_first, up_last), (result, segment_grad, *matrices, comp_done)
    )
    query_final, key_final, value_final, place_final, out_final, down_final = matrices
    vectors = lax.dynamic_slice_in_dim(
        small_done[0:8].reshape(4, width), (dp * 2 + x) * half_rows, half_rows, 1
    )
    biases = lax.dynamic_slice_in_dim(small_done[8:10].reshape(2, 4, 128), dp * per, per, 2)
    return (
        result,
        made[None],
        segment_grad,
        query_final,
        key_final,
        value_final,
        place_final,
        biases[0],
        biases[1],
        out_final,
        up_final,
        down_final,
        comp_final,
        vectors[0],
        vectors[1],
        vectors[2],
        vectors[3],
    )


def solution(mesh):
    split = P(("dp", "head"))
    wide = P(("dp", "head"), None)
    deep = P(("dp", "head"), None, None)
    return jax.shard_map(
        functools.partial(body, mesh.shape["dp"]),
        mesh=mesh,
        in_specs=(
            deep,
            P("dp", None, None),
            P("dp", None, None),
            P("dp", None),
            P("dp"),
            P("dp", "head"),
            P("dp", "head"),
            P("dp", "head"),
            P("dp", "head"),
            P("head", "dp"),
            P("head", "dp"),
            wide,
            wide,
            wide,
            wide,
            split,
            split,
            split,
            split,
            deep,
            deep,
        ),
        out_specs=(
            deep,
            deep,
            deep,
            P("dp", "head"),
            P("dp", "head"),
            P("dp", "head"),
            P("dp", "head"),
            P("head", "dp"),
            P("head", "dp"),
            wide,
            wide,
            wide,
            wide,
            split,
            split,
            split,
            split,
        ),
        check_vma=False,
    )
```

```python
import functools
import math

import jax
import jax.numpy as jnp
import numpy as np
from jax import lax
from jax.experimental import pallas as pl
from jax.experimental.pallas import tpu as pltpu
from jax.sharding import PartitionSpec as P

F32 = jnp.float32
BF16 = jnp.bfloat16
MESH = pl.DeviceIdType.MESH
VMEM_LIMIT = 62 * 1024 * 1024
HALF = 256
LANES = 512
SMALL = 16


def dot(a, b):
    return lax.dot_general(a, b, (((1,), (0,)), ((), ())), preferred_element_type=F32)


def dot_nt(a, b):
    return lax.dot_general(a, b, (((1,), (1,)), ((), ())), preferred_element_type=F32)


def dot_tn(a, b):
    return lax.dot_general(a, b, (((0,), (0,)), ((), ())), preferred_element_type=F32)


def position_rows(context, width, used):
    distance = np.arange(context, dtype=np.float32)[:, None]
    frequency = np.exp(
        np.arange(width // 2, dtype=np.float32) * np.float32(-2.0 * math.log(10000.0) / width)
    )
    phases = distance * frequency[None, :].astype(np.float32)
    table = np.concatenate([np.sin(phases), np.cos(phases)], axis=1)
    return table[::-1][context - used :].astype(jnp.bfloat16)


def place(n):
    me = lax.axis_index("dp")
    core = lax.rem(me, 2)
    low = lax.rem(me // 2, 2)
    high = me // 4
    return core, low, high, n // 4


def meet(core, low, high, nhi, more=0):
    barrier = pltpu.get_barrier_semaphore()

    def tell(index):
        pl.semaphore_signal(barrier, inc=1, device_id={"dp": index}, device_id_type=MESH)

    for k in range(1, nhi):
        tell(lax.rem(high + k, nhi) * 4 + low * 2 + core)
    tell(high * 4 + (1 - low) * 2 + core)
    tell(high * 4 + low * 2 + (1 - core))
    pl.semaphore_wait(barrier, nhi + 1 + more)


def remote(src, dst, send, recv, index):
    return pltpu.make_async_remote_copy(
        src_ref=src,
        dst_ref=dst,
        send_sem=send,
        recv_sem=recv,
        device_id={"dp": index},
        device_id_type=MESH,
    )


class Gather:
    def __init__(self, n, pairs, sems):
        self.core, self.low, self.high, self.nhi = place(n)
        self.pairs = pairs
        (self.zs, self.zr, self.ys, self.yr, self.cs, self.cr, self.own) = sems
        order = sorted(range(1, self.nhi), key=lambda k: (min(k, self.nhi - k), k))
        self.order = order

    def z_copy(self, c, k):
        shard, whole = self.pairs[c]
        return remote(
            shard,
            whole.at[self.high, self.low, self.core],
            self.zs.at[c, k],
            self.zr.at[c, k],
            lax.rem(self.high + k, self.nhi) * 4 + self.low * 2 + self.core,
        )

    def own_copy(self, c):
        shard, whole = self.pairs[c]
        return pltpu.make_async_copy(
            shard, whole.at[self.high, self.low, self.core], self.own.at[c]
        )

    def y_copy(self, c, k):
        shard, whole = self.pairs[c]
        at = whole.at[lax.rem(self.high + k, self.nhi), self.low, self.core]
        return remote(
            shard if k == 0 else at,
            at,
            self.ys.at[c, k],
            self.yr.at[c, k],
            self.high * 4 + (1 - self.low) * 2 + self.core,
        )

    def c_copy(self, c):
        _, whole = self.pairs[c]
        part = whole.at[:, :, self.core]
        return remote(
            part,
            part,
            self.cs.at[c],
            self.cr.at[c],
            self.high * 4 + self.low * 2 + (1 - self.core),
        )

    def start(self, c):
        for k in self.order:
            self.z_copy(c, k).start()
        self.y_copy(c, 0).start()
        self.own_copy(c).start()

    def pass_y(self, c):
        for k in self.order:
            self.z_copy(c, self.nhi - k).wait_recv()
            self.y_copy(c, k).start()

    def pass_core(self, c):
        self.own_copy(c).wait()
        for k in range(self.nhi):
            self.y_copy(c, k).wait_recv()
        self.c_copy(c).start()

    def arrive(self, c):
        self.c_copy(c).wait_recv()

    def close(self, c):
        for k in self.order:
            self.z_copy(c, k).wait_send()
        for k in range(self.nhi):
            self.y_copy(c, k).wait_send()
        self.c_copy(c).wait_send()

    @staticmethod
    def semaphores(count, nhi):
        dma = pltpu.SemaphoreType.DMA
        return [dma((count, nhi))] * 4 + [dma((count,))] * 3


class Scatter:
    def __init__(self, n, items, mine, mine_sem, sems):
        self.core, self.low, self.high, self.nhi = place(n)
        self.items = items
        self.mine, self.mine_sem = mine, mine_sem
        (self.cs, self.cr, self.ys, self.yr, self.zs, self.zr) = sems

    def c_copy(self, c):
        return remote(
            self.items[c][0].at[:, :, 1 - self.core],
            self.items[c][2],
            self.cs.at[c],
            self.cr.at[c],
            self.high * 4 + self.low * 2 + (1 - self.core),
        )

    def mine_copy(self, c):
        slot = c % 2
        return pltpu.make_async_copy(
            self.items[c][0].at[:, :, self.core], self.mine.at[slot], self.mine_sem.at[slot]
        )

    def y_copy(self, c):
        return remote(
            self.items[c][2].at[:, 1 - self.low],
            self.items[c][3],
            self.ys.at[c],
            self.yr.at[c],
            self.high * 4 + (1 - self.low) * 2 + self.core,
        )

    def z_copies(self, c):
        return [
            remote(
                self.items[c][3].at[lax.rem(self.high + k, self.nhi)],
                self.items[c][4].at[k - 1],
                self.zs.at[c, k - 1],
                self.zr.at[c, k - 1],
                lax.rem(self.high + k, self.nhi) * 4 + self.low * 2 + self.core,
            )
            for k in range(1, self.nhi)
        ]

    def start(self, c):
        self.c_copy(c).start()
        if not self.items[c][1]:
            self.mine_copy(c).start()

    def add_core(self, c):
        here = self.items[c][1]
        if not here:
            self.mine_copy(c).wait()
        self.c_copy(c).wait_recv()
        land = self.items[c][2]

        def body(i, carry):
            for j in range(2):
                own = self.items[c][0][i, j, self.core] if here else self.mine[c % 2, i, j]
                land[i, j] = land[i, j] + own
            return carry

        lax.fori_loop(0, self.nhi, body, 0)
        self.y_copy(c).start()

    def add_y(self, c):
        self.y_copy(c).wait_recv()
        src, land = self.items[c][2], self.items[c][3]

        def body(i, carry):
            land[i] = land[i] + src[i, self.low]
            return carry

        lax.fori_loop(0, self.nhi, body, 0)
        for copy in self.z_copies(c):
            copy.start()

    def add_z(self, c):
        for copy in self.z_copies(c):
            copy.wait_recv()
        land, last, done = self.items[c][3:]
        total = land[self.high].astype(F32)
        for k in range(self.nhi - 1):
            total = total + last[k].astype(F32)
        done(total)

    def tick(self, t):
        count = len(self.items)
        if 0 <= t - 1 < count:
            self.add_core(t - 1)
        if t < count:
            self.start(t)
        if 0 <= t - 2 < count:
            self.add_y(t - 2)
        if 0 <= t - 3 < count:
            self.add_z(t - 3)

    def close(self, c):
        self.c_copy(c).wait_send()
        self.y_copy(c).wait_send()
        for copy in self.z_copies(c):
            copy.wait_send()

    @staticmethod
    def scratch(count, nhi, rows):
        dma = pltpu.SemaphoreType.DMA
        return [
            pltpu.VMEM((count, nhi, 2, rows, LANES), BF16),
            pltpu.VMEM((count, nhi, rows, LANES), BF16),
            pltpu.VMEM((count, nhi - 1, rows, LANES), BF16),
            pltpu.VMEM((2, nhi, 2, rows, LANES), BF16),
            dma((2,)),
            dma((count,)),
            dma((count,)),
            dma((count,)),
            dma((count,)),
            dma((count, nhi - 1)),
            dma((count, nhi - 1)),
        ]


def norm_rows(values):
    mean = jnp.mean(values, axis=-1, keepdims=True)
    centred = values - mean
    variance = jnp.mean(centred * centred, axis=-1, keepdims=True)
    return centred * lax.rsqrt(variance + 1e-05)


def attend_rows(query_content, query_place, keys, place_keys, first_seen, last_seen, scale):
    width = keys.shape[0]
    content = dot_nt(query_content, keys)
    by_place = pltpu.roll(
        dot_nt(query_place, place_keys), width - (HALF - 1), 1, stride=1, stride_axis=0
    )
    column = lax.broadcasted_iota(jnp.int32, (HALF, width), 1)
    seen = (column >= first_seen) & (column <= last_seen)
    scores = jnp.where(seen, (content + by_place) * (scale * math.log2(math.e)), -1e30)
    top = jnp.max(scores, axis=1, keepdims=True)
    expo = jnp.exp2(scores - top)
    return expo * (1.0 / jnp.sum(expo, axis=1, keepdims=True))


def forward_kernel(
    n,
    past,
    seg_len,
    docs,
    valid,
    compressed,
    memory,
    segment,
    cotangent,
    comp_cot,
    query_w,
    key_w,
    value_w,
    place_w,
    out_w,
    up_w,
    down_w,
    comp_w,
    small,
    table,
    attended,
    seg_other,
    cot_other,
    xhat_hbm,
    windows_hbm,
    comp_grads_hbm,
    comp_shard_hbm,
    params,
    kv_out,
    q_out,
    wide_out,
    near_out,
    place_out,
    query_whole,
    key_whole,
    value_whole,
    place_whole,
    out_whole,
    up_whole,
    down_whole,
    small_whole,
    out_shard,
    up_parts,
    up_shard,
    comp_shard,
    small_shard,
    normed,
    xhat_out,
    memory_f,
    windows,
    comp_rows_cot,
    comp_grads,
    past_rows,
    seg_rows,
    flat,
    small_rows,
    att,
    load_sem,
    flat_sem,
    own_sem,
    store_sem,
    pair_send,
    pair_recv,
    att_own,
    att_send,
    att_recv,
    *sems,
):
    step = pl.program_id(0)
    x = lax.axis_index("head")
    core, low, high, nhi = place(n)
    tile = 256
    width = normed.shape[2]
    context = past + seg_len
    head = jnp.maximum(step - 2, 0) // 2
    half = comp_w.shape[1] // 2

    items = [(small_shard, small_whole)]
    items += [(query_w, query_whole), (key_w, key_whole), (value_w, value_whole), (place_w, place_whole)]
    for b in range(2):
        to = pl.ds(b * LANES, LANES)
        items.append((out_shard.at[:, :, to], out_whole.at[:, :, :, :, :, to]))
    items += [(up_shard.at[f], up_whole.at[f]) for f in range(4)]
    mid = down_w.shape[0] // 2
    for part in range(2):
        for b in range(2):
            at, to = pl.ds(part * mid, mid), pl.ds(b * LANES, LANES)
            items.append((down_w.at[at, to], down_whole.at[:, :, :, at, to]))
    gather = Gather(n, items, sems)
    count = len(items)
    needs = {5: 1, 7: 2}
    pad_rows = comp_cot.shape[0]

    def pair(src, dst, k):
        return pltpu.make_async_remote_copy(
            src_ref=src,
            dst_ref=dst,
            send_sem=pair_send.at[k],
            recv_sem=pair_recv.at[k],
            device_id={"head": 1 - x},
            device_id_type=MESH,
        )

    mine_at = pl.ds(pl.multiple_of(x * half, half), half)
    other_at = pl.ds(pl.multiple_of((1 - x) * half, half), half)
    pairs = [
        pair(small, small_shard.at[x], 0),
        pair(out_w, out_shard.at[x], 1),
        pair(up_parts.at[1 - x], up_shard.at[:, x], 2),
        pair(comp_w.at[:, other_at], comp_shard.at[x], 3),
        pair(segment.at[0], seg_other, 4),
        pair(cotangent.at[0], cot_other, 5),
        pair(comp_cot.at[:, other_at], comp_rows_cot.at[1], 6),
    ]
    owns = [
        pltpu.make_async_copy(small, small_shard.at[x], own_sem.at[0]),
        pltpu.make_async_copy(out_w, out_shard.at[x], own_sem.at[1]),
        pltpu.make_async_copy(up_parts.at[x], up_shard.at[:, x], own_sem.at[2]),
        pltpu.make_async_copy(comp_w.at[:, mine_at], comp_shard.at[x], own_sem.at[3]),
        pltpu.make_async_copy(comp_cot.at[:, mine_at], comp_rows_cot.at[0], own_sem.at[4]),
    ]
    loads = []
    for i in range(2):
        s = lax.rem(x + i, 2)
        loads.append(pltpu.make_async_copy(compressed.at[s], past_rows.at[i, 0], load_sem.at[i, 0]))
        loads.append(pltpu.make_async_copy(memory.at[s], past_rows.at[i, 1], load_sem.at[i, 1]))
    loads.append(pltpu.make_async_copy(segment.at[0], seg_rows.at[0], load_sem.at[0, 2]))
    load_other = pltpu.make_async_copy(seg_other, seg_rows.at[1], load_sem.at[1, 2])
    store_xhat = pltpu.make_async_copy(xhat_out, xhat_hbm, store_sem.at[0])
    store_windows = pltpu.make_async_copy(windows, windows_hbm, store_sem.at[1])
    store_grads = pltpu.make_async_copy(comp_grads, comp_grads_hbm, store_sem.at[2])
    store_shard = pltpu.make_async_copy(comp_shard, comp_shard_hbm, store_sem.at[3])

    joined = set()

    def join(k):
        if k not in joined:
            joined.add(k)
            owns[k].wait()
            pairs[k].wait_recv()

    def tick(t):
        lead = t + 3
        if lead < count:
            if lead in needs:
                join(needs[lead])
            gather.start(lead)
        if t < count:
            gather.pass_y(t)
        if 0 <= t - 1 < count:
            gather.pass_core(t - 1)
        if 0 <= t - 2 < count and t != 6:
            gather.arrive(t - 2)

    def flat_copies(h, slot):
        at = pl.ds(h * 128, 128)
        return [
            pltpu.make_async_copy(
                whole.at[:, :, :, :, at],
                flat.at[slot, :, :, :, :, pl.ds(j * 128, 128)],
                flat_sem.at[slot, j],
            )
            for j, whole in enumerate((query_whole, key_whole, value_whole, place_whole))
        ]

    def norm_into(i, values, at):
        eye = (
            lax.broadcasted_iota(jnp.int32, (tile, tile), 0)
            == lax.broadcasted_iota(jnp.int32, (tile, tile), 1)
        ).astype(BF16)
        gain = jnp.concatenate([params[0:1, :], params[1:2, :]], axis=1)
        shift = jnp.concatenate([params[2:3, :], params[3:4, :]], axis=1)
        xhat = norm_rows(values.astype(F32))
        normed[i, pl.ds(at, tile)] = (xhat * gain + shift).astype(BF16)
        xhat = xhat.astype(BF16)
        for b in range(width // tile):
            xhat_out[i, b * tile : (b + 1) * tile, pl.ds(at, tile)] = dot_nt(
                eye, xhat[:, b * tile : (b + 1) * tile]
            ).astype(BF16)

    def norm_past(i):
        per = past // 2 // tile

        def one(k, carry):
            at = pl.multiple_of(k * tile, tile)
            inner = pl.multiple_of(lax.rem(k, per) * tile, tile)
            norm_into(i, past_rows[i, k // per, pl.ds(inner, tile)], at)
            return carry

        lax.fori_loop(0, past // tile, one, 0)

    def norm_segment(i):
        def one(k, carry):
            at = pl.multiple_of(k * tile, tile)
            norm_into(i, seg_rows[i, pl.ds(at, tile)], past + at)
            return carry

        lax.fori_loop(0, seg_len // tile, one, 0)

    @pl.when(step == 0)
    def _():
        barrier = pltpu.get_barrier_semaphore()
        pl.semaphore_signal(
            barrier, inc=1, device_id={"head": 1 - x}, device_id_type=MESH
        )
        meet(core, low, high, nhi, 1)
        for k in (0, 1):
            pairs[k].start()
            owns[k].start()
        gather.start(1)
        size = LANES // (n // 4)
        for half_at in range(2):
            for f in range(4):
                for j in range(n // 4):
                    at = ((f * (n // 4) + j) * 2 + half_at) * size
                    up_parts[half_at, f, :, j * size : (j + 1) * size] = up_w[:, at : at + size]
        for k in (2, 6, 3, 4, 5):
            pairs[k].start()
        for copy in owns[2:]:
            copy.start()
        for copy in loads:
            copy.start()
        join(0)
        gather.start(0)
        gather.start(2)
        tick(0)
        tick(1)
        tick(2)
        summed = pltpu.make_async_copy(small_whole, small_rows, load_sem.at[0, 3])
        summed.start()
        summed.wait()
        both = jnp.sum(small_rows[...].reshape(n, 2, SMALL, LANES).astype(F32), axis=0)
        row = lax.broadcasted_iota(jnp.int32, (SMALL, LANES), 0)
        by_head = jnp.where(x == 0, both[0], both[1])
        params[...] = jnp.where(row < 8, both[0] + both[1], by_head)
        for copy in (loads[0], loads[1], loads[4]):
            copy.wait()
        norm_past(0)
        tick(3)
        norm_segment(0)
        tick(4)

    @pl.when(step == 1)
    def _():
        for copy in loads[2:4]:
            copy.wait()
        norm_past(1)
        memory_f[:, past // 2 :, :] = jnp.zeros((width // 128, 16, 128), F32)
        for i in range(2):
            for b in range(width // 128):
                at = slice(b * 128, (b + 1) * 128)
                memory_f[b, 0 : past // 2, :] = past_rows[i, 1, :, at].astype(F32)
                for tap in range(3):
                    windows[tap, i * pad_rows : (i + 1) * pad_rows, at] = memory_f[
                        b, pl.ds(tap, pad_rows, stride=3), :
                    ].astype(BF16)
        store_windows.start()
        owns[4].wait()
        pairs[6].wait_recv()
        comp_rows_both = comp_rows_cot[...].reshape(2 * pad_rows, LANES)
        for tap in range(3):
            for k in range(width // tile):
                at = slice(k * tile, (k + 1) * tile)
                comp_grads[tap * width + k * tile : tap * width + (k + 1) * tile, :] = dot_tn(
                    windows[tap, :, at], comp_rows_both
                ).astype(BF16)
        store_grads.start()
        tick(5)
        gather.arrive(4)
        for copy in flat_copies(0, 0):
            copy.start()

    for k in range(2, 10):

        @pl.when(step == k)
        def _(k=k):
            h, slot = (k - 2) // 2, ((k - 2) // 2) % 2
            if k % 2 == 0:
                for copy in flat_copies(h, slot):
                    copy.wait()
                if h < 3:
                    for copy in flat_copies(h + 1, 1 - slot):
                        copy.start()
            if k == 3:
                pairs[4].wait_recv()
                load_other.start()
                load_other.wait()
                norm_segment(1)
                store_xhat.start()
                join(3)
                store_shard.start()

    def att_pair(h, i):
        at = pl.ds(pl.multiple_of(x * LANES + h * 128, 128), 128)
        return pltpu.make_async_remote_copy(
            src_ref=att.at[h, i],
            dst_ref=attended.at[1 - i, :, at],
            send_sem=att_send.at[h, i],
            recv_sem=att_recv.at[h, i],
            device_id={"head": 1 - x},
            device_id_type=MESH,
        )

    def att_local(h, i):
        at = pl.ds(pl.multiple_of(x * LANES + h * 128, 128), 128)
        return pltpu.make_async_copy(att.at[h, i], attended.at[i, :, at], att_own.at[h, i])

    @pl.when(step >= 2)
    def _():
        i = lax.rem(step, 2)
        s = lax.rem(x + i, 2)
        slot = lax.rem(head, 2)

        def weights(a, b):
            return flat[slot, :, :, :, :, a:b].reshape(width, b - a)

        @pl.when(i == 0)
        def _():
            mat = weights(384, 512)
            for k in range(table.shape[0] // tile):
                place_out[0, k * tile : (k + 1) * tile] = dot(
                    table[k * tile : (k + 1) * tile], mat
                ).astype(BF16)

        mat = weights(128, 384)
        for k in range(context // tile):
            kv_out[0, 0, k * tile : (k + 1) * tile] = dot(
                normed[i, pl.ds(k * tile, tile)], mat
            ).astype(BF16)
        mat = weights(0, 128)
        bias_at = pl.ds(pl.multiple_of(head * 128, 128), 128)
        for k in range(seg_len // tile):
            queries = dot(normed[i, pl.ds(past + k * tile, tile)], mat)
            at = slice(k * tile, (k + 1) * tile)
            q_out[0, 0, at, 0:128] = (queries + params[8:9, bias_at]).astype(BF16)
            q_out[0, 0, at, 128:256] = (queries + params[9:10, bias_at]).astype(BF16)

        flip = (
            lax.broadcasted_iota(jnp.int32, (HALF, HALF), 0)
            + lax.broadcasted_iota(jnp.int32, (HALF, HALF), 1)
            == HALF - 1
        ).astype(BF16)
        scale = 1.0 / math.sqrt(128)
        for part, out, key_start, key_count, place_start in (
            (0, wide_out, 0, past + HALF, 0),
            (1, near_out, past, seg_len, past - HALF),
        ):
            token = lax.broadcasted_iota(jnp.int32, (HALF, 1), 0) + part * HALF
            end, first = 0, past - valid[s]
            for doc in range(3):
                end = end + docs[s, doc]
                first = jnp.where(token >= end, past + end, first)
            at = slice(part * HALF, (part + 1) * HALF)
            weights_low = attend_rows(
                q_out[0, 0, at, 0:128],
                q_out[0, 0, at, 128:256],
                kv_out[0, 0, key_start : key_start + key_count, 0:128],
                place_out[0, place_start : place_start + key_count],
                first - key_start,
                token + (past - key_start),
                scale,
            ).astype(BF16)
            out[0, 0] = dot(flip, weights_low).astype(BF16)
            q_out[0, 0, at] = dot(flip, q_out[0, 0, at]).astype(BF16)
            att[head, i, at] = dot(
                weights_low, kv_out[0, 0, key_start : key_start + key_count, 128:256]
            ).astype(BF16)
        att_pair(head, i).start()
        att_local(head, i).start()

    for k in range(2, 10):
        pl.when(step == k)(functools.partial(tick, k + 4))

    @pl.when(step == pl.num_programs(0) - 1)
    def _():
        for t in range(14, count + 2):
            tick(t)
        for copy in (store_xhat, store_windows, store_grads, store_shard):
            copy.wait()
        for h in range(4):
            for i in range(2):
                att_local(h, i).wait()
                att_pair(h, i).wait()
        for copy in pairs:
            copy.wait_send()
        pairs[5].wait_recv()
        for c in range(count):
            gather.close(c)


def attention_forward(
    n, docs, valid, compressed, memory, segment, cotangent, comp_cot, mats, out_w, up_w, down_w,
    comp_w, small, table,
):
    _, seg_len, width = segment.shape
    past = compressed.shape[1] + memory.shape[1]
    context = past + seg_len
    nhi = n // 4
    lead = (nhi, 2, 2)
    half_rows = out_w.shape[0]
    comp_rows = comp_w.shape[0]
    pad_rows = comp_cot.shape[0]
    any_spec = pl.BlockSpec(memory_space=pl.ANY)
    smem = pl.BlockSpec(memory_space=pltpu.SMEM)
    single = pl.Buffered(1)
    bf = lambda *shape: jax.ShapeDtypeStruct(shape, BF16)
    head = lambda t: jnp.maximum(t - 2, 0) // 2
    which = lambda t: lax.rem(jnp.maximum(t, 2), 2)
    by_both = lambda t: (head(t), which(t), 0, 0)
    dma = pltpu.SemaphoreType.DMA
    full = lambda shape: pl.BlockSpec(shape, lambda t: (0,) * len(shape), pipeline_mode=single)
    count = 15
    return pl.pallas_call(
        functools.partial(forward_kernel, n, past, seg_len),
        grid=(10,),
        out_shape=(
            bf(2, seg_len, width),
            bf(seg_len, width),
            bf(seg_len, width),
            bf(2, width, context),
            bf(3, 2 * pad_rows, width),
            bf(3 * width, LANES),
            bf(2, comp_rows, LANES),
            jax.ShapeDtypeStruct((SMALL, LANES), F32),
            bf(4, 2, context, 256),
            bf(4, 2, seg_len, 256),
            bf(4, 2, HALF, past + HALF),
            bf(4, 2, HALF, seg_len),
            bf(4, past + HALF, 128),
            *[bf(*lead, *w.shape) for w in mats],
            bf(*lead, 2, half_rows, width),
            bf(4, *lead, 2, half_rows, LANES),
            bf(*lead, *down_w.shape),
            bf(*lead, 2, SMALL, LANES),
        ),
        in_specs=[smem, smem]
        + [any_spec] * 5
        + [full(a.shape) for a in (*mats, out_w, up_w, down_w, comp_w, small)]
        + [pl.BlockSpec(table.shape, lambda t: (0, 0), pipeline_mode=single)],
        out_specs=(
            *[any_spec] * 6,
            any_spec,
            pl.BlockSpec((SMALL, LANES), lambda t: (0, 0)),
            pl.BlockSpec((1, 1, context, 256), by_both),
            pl.BlockSpec((1, 1, seg_len, 256), by_both),
            pl.BlockSpec((1, 1, HALF, past + HALF), by_both),
            pl.BlockSpec((1, 1, HALF, seg_len), by_both),
            pl.BlockSpec((1, past + HALF, 128), lambda t: (head(t), 0, 0)),
            *[any_spec] * 8,
        ),
        scratch_shapes=[
            pltpu.VMEM((2, half_rows, width), BF16),
            pltpu.VMEM((2, 4, half_rows, LANES), BF16),
            pltpu.VMEM((4, 2, half_rows, LANES), BF16),
            pltpu.VMEM((2, comp_rows, LANES), BF16),
            pltpu.VMEM((2, SMALL, LANES), BF16),
            pltpu.VMEM((2, context, width), BF16),
            pltpu.VMEM((2, width, context), BF16),
            pltpu.VMEM((width // 128, past // 2 + 16, 128), F32),
            pltpu.VMEM((3, 2 * pad_rows, width), BF16),
            pltpu.VMEM((2, pad_rows, LANES), BF16),
            pltpu.VMEM((3 * width, LANES), BF16),
            pltpu.VMEM((2, 2, past // 2, width), BF16),
            pltpu.VMEM((2, seg_len, width), BF16),
            pltpu.VMEM((2,) + lead + (mats[0].shape[0], LANES), BF16),
            pltpu.VMEM(lead + (2, SMALL, LANES), BF16),
            pltpu.VMEM((4, 2, seg_len, 128), BF16),
            dma((2, 4)),
            dma((2, 4)),
            dma((6,)),
            dma((4,)),
            dma((7,)),
            dma((7,)),
            dma((4, 2)),
            dma((4, 2)),
            dma((4, 2)),
        ]
        + Gather.semaphores(count, nhi),
        compiler_params=pltpu.CompilerParams(
            vmem_limit_bytes=VMEM_LIMIT,
            dimension_semantics=("arbitrary",),
            collective_id=0,
            has_side_effects=True,
        ),
        name="attention_forward",
    )(
        docs, valid, compressed, memory, segment, cotangent, comp_cot, *mats, out_w, up_w, down_w,
        comp_w, small, table,
    )


def gelu_parts(v):
    c = math.sqrt(2.0 / math.pi)
    square = v * v
    t = jnp.tanh(c * (v + 0.044715 * square * v))
    half = 0.5 * (1.0 + t)
    value = v * half
    return value, half + value * (1.0 - half) * (2 * c + (6 * 0.044715 * c) * square)


def feed_kernel(
    n,
    att_in,
    segment,
    seg_other,
    cotangent,
    cot_other,
    out_in,
    up_in,
    down_in,
    params,
    comp,
    comp_shard,
    own_out,
    branch_out,
    residual_out,
    dout,
    out_grads,
    down_grads,
    up_rest,
    small_out,
    comp_out,
    up_out,
    comp_whole,
    att,
    seg,
    cot,
    out_w,
    up,
    down,
    residual,
    low,
    low_t,
    act,
    pre,
    branch,
    terms,
    terms_land,
    cast,
    up_grads,
    mixed,
    stage,
    up_send,
    up_land,
    comp_stage,
    comp_send,
    comp_land,
    load_sem,
    store_sem,
    stage_sem,
    pair_send,
    pair_recv,
    land_c,
    land_y,
    land_z,
    mine,
    mine_sem,
    *sems,
):
    sems, gather_sems = sems[:6], sems[6:]
    x = lax.axis_index("head")
    core, low_y, high, nhi = place(n)
    tile = 256
    _, seg_len, width = att.shape
    rows = width // n
    half_rows = rows // 2
    comp_rows = comp_send.shape[0]

    def pair(src, dst, k):
        return pltpu.make_async_remote_copy(
            src_ref=src,
            dst_ref=dst,
            send_sem=pair_send.at[k],
            recv_sem=pair_recv.at[k],
            device_id={"head": 1 - x},
            device_id_type=MESH,
        )

    terms_pair = pair(cast.at[0], terms_land, 0)
    mixed_pair = pair(mixed.at[1 - x], dout.at[1], 1)
    comp_pair = pair(comp_send, comp_land, 2)
    up_pairs = [pair(up_send.at[f], up_land.at[f], 3 + f) for f in range(2)]
    scatter = Scatter(
        n,
        [
            (part, here, land_c.at[c], land_y.at[c], land_z.at[c], done)
            for c, (part, here, done) in enumerate(
                [
                    (
                        comp.at[:, :, :, pl.ds(m * rows, rows)],
                        False,
                        comp_block(m, x, rows, comp_stage, comp_out, comp_send, comp_pair),
                    )
                    for m in range(3)
                ]
                + [
                    (up_grads.at[f], True, up_block(f, x, up_out, up_send, up_pairs[f]))
                    for f in range(2)
                ]
            )
        ],
        mine,
        mine_sem,
        sems,
    )

    third = comp_rows // 3
    gather = Gather(
        n,
        [
            (
                comp_shard.at[:, pl.ds(m * third, third)],
                comp_whole.at[:, :, :, :, pl.ds(m * third, third)],
            )
            for m in range(3)
        ],
        gather_sems,
    )

    def load(src, dst, k):
        return pltpu.make_async_copy(src, dst, load_sem.at[k])

    loads = {
        "att1": load(att_in.at[1], att.at[1], 0),
        "out": load(out_in, out_w, 1),
        "seg1": load(seg_other, seg.at[1], 2),
        "cot1": load(cot_other, cot.at[1], 3),
        "up": load(up_in, up, 4),
        "down": load(down_in, down, 5),
        "att0": load(att_in.at[0], att.at[0], 6),
        "seg0": load(segment.at[0], seg.at[0], 7),
        "cot0": load(cotangent.at[0], cot.at[0], 8),
    }
    for copy in loads.values():
        copy.start()
    barrier = pltpu.get_barrier_semaphore()
    pl.semaphore_signal(barrier, inc=1, device_id={"head": 1 - x}, device_id_type=MESH)
    meet(core, low_y, high, nhi, 1)
    scatter.start(0)
    scatter.start(1)
    gather.start(0)

    eye = (
        lax.broadcasted_iota(jnp.int32, (tile, tile), 0)
        == lax.broadcasted_iota(jnp.int32, (tile, tile), 1)
    ).astype(BF16)
    gain = jnp.concatenate([params[4:5, :], params[5:6, :]], axis=1)
    shift = jnp.concatenate([params[6:7, :], params[7:8, :]], axis=1)

    def project(i):
        for k in range(seg_len // tile):
            at = slice(k * tile, (k + 1) * tile)
            whole_at = slice(i * seg_len + k * tile, i * seg_len + (k + 1) * tile)
            value = seg[i, at].astype(F32) + dot(att[i, at], out_w[...])
            residual[at, :] = value
            value = (norm_rows(value) * gain + shift).astype(BF16)
            low[whole_at, :] = value
            for b in range(width // tile):
                low_t[b * tile : (b + 1) * tile, whole_at] = dot_nt(
                    eye, value[:, b * tile : (b + 1) * tile]
                ).astype(BF16)

    def hidden(i, between):
        whole_at = slice(i * seg_len, (i + 1) * seg_len)
        branch[...] = jnp.zeros_like(branch)
        terms[...] = jnp.zeros_like(terms)

        def one(f, carry):
            down_at = pl.ds(pl.multiple_of(f * LANES, LANES), LANES)
            value, slope = gelu_parts(dot(low[whole_at, :], up[f]))
            value = value.astype(BF16)
            act[f, whole_at, :] = value
            back = dot_nt(cot[i], down[down_at, :]).astype(BF16).astype(F32)
            back = (back * slope).astype(BF16)
            pre[f, whole_at, :] = back
            branch[...] += dot(value, down[down_at, :])
            terms[...] += dot_nt(back, up[f])
            for k, steps in enumerate(between):

                @pl.when(f == k)
                def _(steps=steps):
                    for run, c in steps:
                        run(c)

            return carry

        lax.fori_loop(0, 4, one, 0)

    for name in ("att1", "out", "seg1"):
        loads[name].wait()
    project(1)
    scatter.add_core(0)
    scatter.start(2)
    gather.start(1)
    for name in ("cot1", "up", "down"):
        loads[name].wait()
    hidden(
        1,
        (
            ((scatter.add_core, 1), (gather.pass_y, 0)),
            ((scatter.add_core, 2), (scatter.add_y, 0), (gather.start, 2)),
            ((gather.pass_y, 1),),
            ((scatter.add_y, 1),),
        ),
    )
    cast[0] = terms[...].astype(BF16)
    terms_pair.start()
    cast[1] = branch[...].astype(BF16)
    store_branch = pltpu.make_async_copy(cast.at[1], branch_out, store_sem.at[0])
    store_branch.start()
    for name in ("att0", "seg0", "cot0"):
        loads[name].wait()
    project(0)
    scatter.add_z(0)
    hidden(
        0,
        (
            ((gather.pass_core, 0),),
            ((gather.pass_y, 2),),
            ((scatter.add_y, 2),),
            ((scatter.add_z, 1),),
        ),
    )
    branch[...] += residual[...]
    store_own = pltpu.make_async_copy(branch, own_out, store_sem.at[1])
    store_own.start()

    block = tile // (4 * rows)

    def up_grad(f):
        for k in range(width // tile):
            grad = dot(low_t[k * tile : (k + 1) * tile, :], pre[f]).astype(BF16)
            up_grads[f, k * block : (k + 1) * block] = grad.reshape(block, 2, 2, rows, LANES)
        if f < 2:
            scatter.start(3 + f)

    up_grad(0)
    gather.pass_core(1)
    up_grad(1)
    scatter.add_core(3)
    scatter.add_z(2)
    up_grad(2)
    scatter.add_core(4)
    up_grad(3)
    store_rest = pltpu.make_async_copy(up_grads.at[pl.ds(2, 2)], up_rest, store_sem.at[4])
    store_rest.start()

    terms_pair.wait_recv()
    gain_grad = jnp.zeros((1, width), F32)
    shift_grad = jnp.zeros((1, width), F32)
    terms_pair.wait_send()
    for k in range(seg_len // tile):
        at = slice(k * tile, (k + 1) * tile)
        grad = terms[at, :] + terms_land[at, :].astype(F32)
        value = residual[at, :]
        mean = jnp.mean(value, axis=-1, keepdims=True)
        centred = value - mean
        rstd = lax.rsqrt(jnp.mean(centred * centred, axis=-1, keepdims=True) + 1e-05)
        xhat = centred * rstd
        gain_grad += jnp.sum(grad * xhat, axis=0, keepdims=True)
        shift_grad += jnp.sum(grad, axis=0, keepdims=True)
        grad = cot[0, at].astype(F32) + norm_back(xhat, rstd, grad * gain)
        residual[at, :] = grad
        grad = grad.astype(BF16)
        cast[0, at, :] = grad
        back = dot_nt(grad, out_w[...]).astype(BF16)
        mixed[0, at, :] = back[:, 0:LANES]
        mixed[1, at, :] = back[:, LANES:]
    mixed_pair.start()
    store_dout = pltpu.make_async_copy(mixed.at[x], dout.at[0], store_sem.at[2])
    store_dout.start()
    store_residual = pltpu.make_async_copy(residual, residual_out, store_sem.at[3])
    store_residual.start()
    small_out[...] = jnp.zeros_like(small_out)
    small_out[4:5, :] = gain_grad[:, 0:LANES]
    small_out[5:6, :] = gain_grad[:, LANES:]
    small_out[6:7, :] = shift_grad[:, 0:LANES]
    small_out[7:8, :] = shift_grad[:, LANES:]
    gather.pass_core(2)

    staged = [None, None]
    jobs = [(out_grads, k * tile, None, k) for k in range(width // tile)]
    jobs += [
        (down_grads, f * LANES + k * tile, f, k) for f in range(4) for k in range(LANES // tile)
    ]
    for j, (target, start, f, k) in enumerate(jobs):
        slot = j % 2
        at = slice(k * tile, (k + 1) * tile)
        if f is None:
            grad = dot_tn(att[0, :, at], cast[0])
        else:
            grad = dot_tn(act[f, 0:seg_len, at], cot[0]) + dot_tn(act[f, seg_len:, at], cot[1])
        if staged[slot] is not None:
            staged[slot].wait()
        stage[slot] = grad.astype(BF16)
        staged[slot] = pltpu.make_async_copy(
            stage.at[slot], target.at[pl.ds(start, tile)], stage_sem.at[slot]
        )
        staged[slot].start()
        if j == 3:
            scatter.add_y(3)
        if j == 10:
            scatter.add_y(4)
            scatter.add_z(3)
    scatter.add_z(4)
    for m in range(3):
        gather.arrive(m)
    comp_pair.wait_recv()
    to = pl.ds(pl.multiple_of((1 - x) * LANES, LANES), LANES)
    comp_out[:, to] = comp_land[...].astype(F32)
    for f in range(2):
        up_pairs[f].wait_recv()
        up_out[1 - x, f] = up_land[f].astype(F32)
    mixed_pair.wait_recv()
    for copy in [mixed_pair, comp_pair, *up_pairs]:
        copy.wait_send()
    for copy in [*staged, store_branch, store_own, store_dout, store_residual, store_rest]:
        copy.wait()
    for c in range(5):
        scatter.close(c)
    for m in range(3):
        gather.close(m)


def comp_block(m, x, rows, stage, out, send, pair):
    def done(total):
        stage[m * rows : (m + 1) * rows, :] = total
        if m == 2:
            half = send.shape[0]
            upper, lower = stage[0:half, :], stage[half:, :]
            to = pl.ds(pl.multiple_of(x * LANES, LANES), LANES)
            out[:, to] = jnp.where(x == 0, upper, lower)
            send[...] = jnp.where(x == 0, lower, upper).astype(BF16)
            pair.start()

    return done


def up_block(f, x, out, send, pair):
    def done(total):
        half = send.shape[1]
        upper, lower = total[0:half], total[half:]
        out[x, f] = jnp.where(x == 0, upper, lower)
        send[f] = jnp.where(x == 0, lower, upper).astype(BF16)
        pair.start()

    return done


def feed_forward(
    n, att, segment, seg_other, cotangent, cot_other, out_w, up, down, params, comp, comp_shard
):
    _, seg_len, width = att.shape
    rows = width // n
    half_rows = rows // 2
    nhi = n // 4
    comp_rows = comp.shape[3] // 2
    total = 2 * seg_len
    any_spec = pl.BlockSpec(memory_space=pl.ANY)
    vmem = pl.BlockSpec(memory_space=pltpu.VMEM)
    dma = pltpu.SemaphoreType.DMA
    f32 = lambda *shape: jax.ShapeDtypeStruct(shape, F32)
    bf = lambda *shape: jax.ShapeDtypeStruct(shape, BF16)
    return pl.pallas_call(
        functools.partial(feed_kernel, n),
        out_shape=(
            f32(seg_len, width),
            bf(seg_len, width),
            f32(seg_len, width),
            bf(2, seg_len, LANES),
            bf(width, width),
            bf(4 * LANES, width),
            bf(2, nhi, 2, 2, rows, LANES),
            f32(SMALL, LANES),
            f32(comp_rows, width),
            f32(2, 2, half_rows, LANES),
            bf(nhi, 2, 2, *comp_shard.shape),
        ),
        in_specs=[any_spec] * 8 + [vmem, any_spec, vmem],
        out_specs=(any_spec,) * 7 + (vmem,) * 3 + (any_spec,),
        scratch_shapes=[
            pltpu.VMEM((2, seg_len, width), BF16),
            pltpu.VMEM((2, seg_len, width), BF16),
            pltpu.VMEM((2, seg_len, width), BF16),
            pltpu.VMEM((width, width), BF16),
            pltpu.VMEM((4, width, LANES), BF16),
            pltpu.VMEM((4 * LANES, width), BF16),
            pltpu.VMEM((seg_len, width), F32),
            pltpu.VMEM((total, width), BF16),
            pltpu.VMEM((width, total), BF16),
            pltpu.VMEM((4, total, LANES), BF16),
            pltpu.VMEM((4, total, LANES), BF16),
            pltpu.VMEM((seg_len, width), F32),
            pltpu.VMEM((seg_len, width), F32),
            pltpu.VMEM((seg_len, width), BF16),
            pltpu.VMEM((2, seg_len, width), BF16),
            pltpu.VMEM((4, nhi, 2, 2, rows, LANES), BF16),
            pltpu.VMEM((2, seg_len, LANES), BF16),
            pltpu.VMEM((2, 256, width), BF16),
            pltpu.VMEM((2, half_rows, LANES), BF16),
            pltpu.VMEM((2, half_rows, LANES), BF16),
            pltpu.VMEM((3 * rows, LANES), F32),
            pltpu.VMEM((comp_rows, LANES), BF16),
            pltpu.VMEM((comp_rows, LANES), BF16),
            dma((9,)),
            dma((5,)),
            dma((2,)),
            dma((5,)),
            dma((5,)),
        ]
        + Scatter.scratch(5, nhi, rows)
        + Gather.semaphores(3, nhi),
        compiler_params=pltpu.CompilerParams(
            vmem_limit_bytes=VMEM_LIMIT, collective_id=2, has_side_effects=True
        ),
        name="feed_forward",
    )(att, segment, seg_other, cotangent, cot_other, out_w, up, down, params, comp, comp_shard)


def norm_back(xhat, rstd, grad):
    a = jnp.mean(grad, axis=-1, keepdims=True)
    b = jnp.mean(grad * xhat, axis=-1, keepdims=True)
    return rstd * (grad - a - xhat * b)


def backward_kernel(
    n,
    past,
    seg_len,
    dout,
    kv,
    q,
    wide,
    near,
    place_keys,
    xhat_hbm,
    query_w,
    key_w,
    value_w,
    table_hbm,
    params,
    segment,
    seg_other,
    residual_hbm,
    small_in,
    own_sum,
    branch,
    up,
    down,
    out,
    result_out,
    segment_out,
    query_out,
    key_out,
    value_out,
    place_out,
    out_out,
    down_out,
    up_out,
    small_out,
    xhat_t,
    table_t,
    residual_grad,
    load_sem,
    up_send,
    up_land,
    flat,
    raw,
    sums,
    place_sum,
    input_grad,
    dkv,
    columns,
    gain_sum,
    shift_sum,
    head_grads,
    context_land,
    context_send,
    branch_land,
    own_rows_sum,
    own_sem,
    seg_rows,
    seg_sem,
    out_keep,
    out_send,
    out_land,
    small_mine,
    small_c,
    small_y,
    small_z,
    small_x,
    pair_send,
    pair_recv,
    small_send,
    small_recv,
    land_c,
    land_y,
    land_z,
    mine,
    mine_sem,
    *sems,
):
    step = pl.program_id(0)
    x = lax.axis_index("head")
    core, low, high, nhi = place(n)
    head = lax.rem(step, 4)
    tile = 256
    context = past + seg_len
    width = flat.shape[0]
    rows = width // n
    half_rows = rows // 2
    scale = 1.0 / math.sqrt(128)
    flip = (
        lax.broadcasted_iota(jnp.int32, (HALF, HALF), 0)
        + lax.broadcasted_iota(jnp.int32, (HALF, HALF), 1)
        == HALF - 1
    ).astype(BF16)

    def pair(src, dst, k):
        return pltpu.make_async_remote_copy(
            src_ref=src,
            dst_ref=dst,
            send_sem=pair_send.at[k],
            recv_sem=pair_recv.at[k],
            device_id={"head": 1 - x},
            device_id_type=MESH,
        )

    context_pair = pair(context_send, context_land, 0)
    branch_pair = pair(branch, branch_land, 1)
    out_pairs = [pair(out_send.at[b], out_land.at[b], 2 + b) for b in range(2)]
    load_own = pltpu.make_async_copy(own_sum, own_rows_sum, own_sem)
    up_pairs = [pair(up_send.at[f], up_land.at[f], 4 + f) for f in range(2)]
    load_xhat = [
        pltpu.make_async_copy(xhat_hbm.at[1 - i], xhat_t, load_sem.at[0]) for i in range(2)
    ]
    load_table = pltpu.make_async_copy(table_hbm, table_t, load_sem.at[1])
    load_residual = pltpu.make_async_copy(residual_hbm, residual_grad, load_sem.at[2])
    load_other = pltpu.make_async_copy(seg_other, seg_rows, seg_sem)
    load_segment = pltpu.make_async_copy(segment.at[0], seg_rows, seg_sem)

    def down_done(a, b):
        def done(total):
            down_out[a * rows : (a + 1) * rows, b * LANES : (b + 1) * LANES] = total

        return done

    def out_done(b):
        def done(total):
            upper, lower = total[0:half_rows], total[half_rows:]
            out_keep[b] = jnp.where(x == 0, upper, lower)
            out_send[b] = jnp.where(x == 0, lower, upper).astype(BF16)
            out_pairs[b].start()

        return done

    def head_done(h):
        def done(total):
            for j, ref in enumerate((query_out, key_out, value_out, place_out)):
                ref[:, h * 128 : (h + 1) * 128] = total[:, j * 128 : (j + 1) * 128]

        return done

    parts = [(up.at[f], False, up_block(f, x, up_out, up_send, up_pairs[f])) for f in range(2)]
    for a in range(2):
        for b in range(2):
            at, to = pl.ds(a * rows, rows), pl.ds(b * LANES, LANES)
            parts.append((down.at[:, :, :, at, to], False, down_done(a, b)))
    parts += [
        (out.at[:, :, :, :, pl.ds(b * LANES, LANES)], False, out_done(b)) for b in range(2)
    ]
    parts += [(head_grads.at[h], True, head_done(h)) for h in range(4)]
    scatter = Scatter(
        n,
        [
            (part, here, land_c.at[c], land_y.at[c], land_z.at[c], done)
            for c, (part, here, done) in enumerate(parts)
        ],
        mine,
        mine_sem,
        sems,
    )
    count = len(parts)

    @pl.when(step == 0)
    def _():
        barrier = pltpu.get_barrier_semaphore()
        pl.semaphore_signal(barrier, inc=1, device_id={"head": 1 - x}, device_id_type=MESH)
        meet(core, low, high, nhi, 1)
        load_xhat[0].start()
        load_other.start()
        load_own.start()
        load_table.start()
        load_residual.start()
        branch_pair.start()
        for j in range(2):
            line = jnp.concatenate([params[2 * j : 2 * j + 1, :], params[2 * j + 1 : 2 * j + 2, :]], axis=1)
            columns[j] = jnp.broadcast_to(line, (128, width)).T
        raw[...] = jnp.zeros_like(raw)
        sums[...] = jnp.zeros_like(sums)
        place_sum[...] = jnp.zeros_like(place_sum)
        gain_sum[...] = jnp.zeros_like(gain_sum)
        shift_sum[...] = jnp.zeros_like(shift_sum)
        small_mine[...] = small_in[...]

    @pl.when(head == 0)
    def _():
        input_grad[...] = jnp.zeros_like(input_grad)

    start, add_core, add_y, add_z = scatter.start, scatter.add_core, scatter.add_y, scatter.add_z
    before = {
        0: ((start, 0), (start, 1)),
        1: ((add_core, 1), (start, 3)),
        2: ((add_core, 3), (start, 5)),
        3: ((add_y, 2), (add_core, 5), (start, 7)),
        4: ((add_y, 3),),
        5: ((start, 8), (add_z, 3), (add_core, 7)),
        6: ((add_z, 4), (start, 9)),
        7: ((add_y, 7), (start, 10)),
    }
    within = {
        0: ((add_core, 0), (start, 2)),
        1: ((add_y, 0), (add_core, 2), (start, 4)),
        2: ((add_y, 1), (add_z, 0), (add_core, 4), (start, 6)),
        3: ((add_z, 1), (add_core, 6)),
        4: ((add_y, 4), (add_z, 2)),
        5: ((add_y, 5), (add_core, 8)),
        6: ((add_y, 6), (add_z, 5), (add_core, 9)),
        7: ((add_core, 10), (add_z, 6)),
    }

    def run(table):
        for k, steps in table.items():

            @pl.when(step == k)
            def _(steps=steps):
                for do, c in steps:
                    do(c)

    run(before)

    for j, mat in enumerate((query_w, key_w, value_w)):
        flat[:, j * 128 : (j + 1) * 128] = mat[...]

    query_grads = []
    key_rows = []
    value_rows = []
    place_rows = []
    bias_at = pl.ds(pl.multiple_of(head * 128, 128), 128)
    for part, weights_ref, key_start, key_count, place_start in (
        (0, wide, 0, past + HALF, 0),
        (1, near, past, seg_len, past - HALF),
    ):
        at = slice(part * HALF, (part + 1) * HALF)
        keys_at = slice(key_start, key_start + key_count)
        attn = weights_ref[0, 0]
        grad = dot(flip, dout[0, at]).astype(BF16)
        value_rows.append(dot_tn(grad, attn))
        weights_grad = dot_nt(grad, kv[0, 0, keys_at, 128:256])
        attn = attn.astype(F32)
        row = jnp.sum(weights_grad * attn, axis=1, keepdims=True)
        scores_f = attn * (weights_grad - row) * scale
        scores_grad = scores_f.astype(BF16)
        content_grad = dot(scores_grad, kv[0, 0, keys_at, 0:128]).astype(BF16)
        key_rows.append(dot_tn(q[0, 0, at, 0:128], scores_grad))
        by_place = pltpu.roll(scores_f, 0, 1, stride=1, stride_axis=0).astype(BF16)
        place_grad = dot(by_place, place_keys[0, place_start : place_start + key_count])
        place_grad = place_grad.astype(BF16)
        place_rows.append(dot_tn(q[0, 0, at, 128:256], by_place))
        content_f = content_grad.astype(F32)
        place_f = place_grad.astype(F32)
        small_mine[8:9, bias_at] += jnp.sum(content_f, axis=0, keepdims=True)
        small_mine[9:10, bias_at] += jnp.sum(place_f, axis=0, keepdims=True)
        query_grads.append(dot(flip, (content_f + place_f).astype(BF16)).astype(BF16))

    for j, (wide_rows, near_rows) in enumerate((key_rows, value_rows)):
        at = slice(j * 128, (j + 1) * 128)
        dkv[at, 0:past] = wide_rows[:, 0:past].astype(BF16)
        dkv[at, past : past + HALF] = (wide_rows[:, past:] + near_rows[:, 0:HALF]).astype(BF16)
        dkv[at, past + HALF :] = near_rows[:, HALF:].astype(BF16)
    split = past - HALF
    for at, rows_grad in (
        (slice(0, split), place_rows[0][:, 0:split]),
        (slice(split, None), place_rows[0][:, split:] + place_rows[1]),
    ):
        place_sum[head, :, at] = (
            place_sum[head, :, at].astype(F32) + rows_grad.astype(BF16).astype(F32)
        ).astype(BF16)
    dq = jnp.concatenate(query_grads, axis=0)
    stacked = jnp.concatenate([dq, dkv[:, past:].astype(F32).T.astype(BF16)], axis=1)

    run(within)

    @pl.when(step == 0)
    def _():
        load_xhat[0].wait()

    @pl.when(step == 4)
    def _():
        load_xhat[1].wait()
        load_table.wait()

    ones = jnp.ones((8, context), BF16)
    sums[head, :, 0:128] += dot(ones[:, 0:seg_len], dq)
    sums[head, :, 128:384] += dot_nt(ones, dkv[...])
    for k in range(width // tile):
        at = slice(k * tile, (k + 1) * tile)
        raw[head, at, 0:128] += dot(xhat_t[at, past:], dq)
        raw[head, at, 128:384] += dot_nt(xhat_t[at, :], dkv[...])
        input_grad[:, at] += dot_nt(stacked, flat[at, 0:384])

    @pl.when(step >= 4)
    def _():
        place_low = place_sum[head]
        block = tile // (4 * rows)
        total = sums[head, 0:1, :]
        for k in range(width // tile):
            at = slice(k * tile, (k + 1) * tile)
            to = slice(k * block, (k + 1) * block)
            got = raw[head, at, :]
            mats = flat[at, 0:384].astype(F32)
            for acc, term in ((gain_sum, mats * got), (shift_sum, mats * total)):
                acc[at, :] += term[:, 0:128] + term[:, 128:256] + term[:, 256:384]
            grad = (columns[0, at, 0:1] * got + columns[1, at, 0:1] * total).astype(BF16)
            head_grads[head, to, :, :, :, 0:384] = grad.reshape(block, 2, 2, rows, 384)
            grad = dot_nt(table_t[at, :], place_low).astype(BF16)
            head_grads[head, to, :, :, :, 384:512] = grad.reshape(block, 2, 2, rows, 128)

    def own_rows(k):
        gain = jnp.concatenate([params[0:1, :], params[1:2, :]], axis=1)
        at = slice(k * tile, (k + 1) * tile)
        values = seg_rows[at, :].astype(F32)
        mean = jnp.mean(values, axis=-1, keepdims=True)
        centred = values - mean
        rstd = lax.rsqrt(jnp.mean(centred * centred, axis=-1, keepdims=True) + 1e-05)
        return norm_back(centred * rstd, rstd, input_grad[at, :] * gain)

    @pl.when(step == 4)
    def _():
        load_segment.start()

    @pl.when(step == 3)
    def _():
        load_xhat[1].start()
        load_other.wait()
        for k in range(seg_len // tile):
            context_send[k * tile : (k + 1) * tile, :] = own_rows(k).astype(BF16)
        context_pair.start()

    @pl.when(step == 5)
    def _():
        branch_pair.wait_recv()
        load_own.wait()
        for k in range(seg_len // tile):
            at = slice(k * tile, (k + 1) * tile)
            result_out[0, at] = (own_rows_sum[at, :] + branch_land[at, :].astype(F32)).astype(BF16)

    @pl.when(step == 7)
    def _():
        start(11)
        one = jnp.ones((8, 128), F32)
        for acc, row in ((gain_sum, 0), (shift_sum, 2)):
            line = lax.dot_general(
                one,
                acc[...],
                (((1,), (1,)), ((), ())),
                precision=lax.Precision.HIGHEST,
                preferred_element_type=F32,
            )
            small_mine[row : row + 1, :] = line[0:1, 0:LANES]
            small_mine[row + 1 : row + 2, :] = line[0:1, LANES:]

        def to_dp(src, dst, k, index):
            return remote(src, dst, small_send.at[k], small_recv.at[k], index)

        copies = [to_dp(small_mine, small_c.at[1], 0, high * 4 + low * 2 + (1 - core))]
        copies[0].start()
        add_core(11)
        load_segment.wait()
        load_residual.wait()
        context_pair.wait_recv()
        for k in range(seg_len // tile):
            at = slice(k * tile, (k + 1) * tile)
            segment_out[0, at] = (
                residual_grad[at, :] + own_rows(k) + context_land[at, :].astype(F32)
            ).astype(BF16)
        add_y(8)
        add_z(7)
        copies[0].wait_recv()
        small_c[0] = small_mine[...] + small_c[1]
        copies.append(to_dp(small_c.at[0], small_y.at[1], 1, high * 4 + (1 - low) * 2 + core))
        copies[1].start()
        add_y(9)
        add_z(8)
        copies[1].wait_recv()
        small_y[0] = small_c[0] + small_y[1]
        along = []
        for k in range(1, nhi):
            to = lax.rem(high + k, nhi) * 4 + low * 2 + core
            along.append(to_dp(small_y.at[0], small_z.at[k], 2 + k, to))
        for copy in along:
            copy.start()
        add_y(10)
        add_z(9)
        for copy in along:
            copy.wait_recv()
        line = small_y[0]
        for k in range(1, nhi):
            line = line + small_z[k]
        small_z[0] = line
        last = pltpu.make_async_remote_copy(
            src_ref=small_z.at[0],
            dst_ref=small_x,
            send_sem=small_send.at[2],
            recv_sem=small_recv.at[2],
            device_id={"head": 1 - x},
            device_id_type=MESH,
        )
        last.start()
        add_y(11)
        add_z(10)
        add_z(11)
        for f in range(2):
            up_pairs[f].wait_recv()
            up_out[1 - x, f] = up_land[f].astype(F32)
        for b in range(2):
            out_pairs[b].wait_recv()
            out_out[:, b * LANES : (b + 1) * LANES] = out_keep[b] + out_land[b].astype(F32)
        last.wait_recv()
        line = lax.broadcasted_iota(jnp.int32, (SMALL, LANES), 0)
        small_out[...] = small_z[0] + jnp.where(line < 8, small_x[...], 0.0)
        for copy in [context_pair, branch_pair, *up_pairs, *out_pairs, *copies, *along, last]:
            copy.wait_send()
        for c in range(count):
            scatter.close(c)


def attention_backward(
    n, dout, kv, q, wide, near, place_keys, xhat_t, mats, table_t, params, segment,
    seg_other, residual_grad, small_in, own_sum, branch, up, down, out,
):
    _, seg_len, width = segment.shape
    context = kv.shape[2]
    past = context - seg_len
    rows = width // n
    nhi = n // 4
    half_rows = rows // 2
    seq = lambda t: 1 - t // 4
    head = lambda t: lax.rem(t, 4)
    by_both = lambda t: (head(t), seq(t), 0, 0)
    single = pl.Buffered(1)
    any_spec = pl.BlockSpec(memory_space=pl.ANY)
    dma = pltpu.SemaphoreType.DMA
    f32 = lambda *shape: jax.ShapeDtypeStruct(shape, F32)
    lead = (nhi, 2, 2)
    full = lambda shape: pl.BlockSpec(shape, lambda t: (0,) * len(shape), pipeline_mode=single)
    outs = (
        jax.ShapeDtypeStruct((1, seg_len, width), BF16),
        jax.ShapeDtypeStruct((1, seg_len, width), BF16),
        f32(rows, LANES),
        f32(rows, LANES),
        f32(rows, LANES),
        f32(rows, LANES),
        f32(half_rows, width),
        f32(2 * rows, width),
        f32(2, 2, half_rows, LANES),
        f32(SMALL, LANES),
    )
    return pl.pallas_call(
        functools.partial(backward_kernel, n, past, seg_len),
        grid=(8,),
        out_shape=outs,
        in_specs=[
            pl.BlockSpec((1, seg_len, 128), lambda t: (seq(t), 0, head(t))),
            pl.BlockSpec((1, 1, context, 256), by_both),
            pl.BlockSpec((1, 1, seg_len, 256), by_both),
            pl.BlockSpec((1, 1, HALF, past + HALF), by_both),
            pl.BlockSpec((1, 1, HALF, seg_len), by_both),
            pl.BlockSpec((1, past + HALF, 128), lambda t: (head(t), 0, 0)),
            any_spec,
            *[pl.BlockSpec((width, 128), lambda t: (0, head(t)))] * 3,
            any_spec,
            full((SMALL, LANES)),
            any_spec,
            any_spec,
            any_spec,
            full((SMALL, LANES)),
            any_spec,
            any_spec,
            any_spec,
            any_spec,
            any_spec,
        ],
        out_specs=tuple(full(o.shape) for o in outs),
        scratch_shapes=[
            pltpu.VMEM((width, context), BF16),
            pltpu.VMEM(table_t.shape, BF16),
            pltpu.VMEM((seg_len, width), F32),
            dma((3,)),
            pltpu.VMEM((2, half_rows, LANES), BF16),
            pltpu.VMEM((2, half_rows, LANES), BF16),
            pltpu.VMEM((width, 384), BF16),
            pltpu.VMEM((4, width, 384), F32),
            pltpu.VMEM((4, 8, 384), F32),
            pltpu.VMEM((4, 128, past + HALF), BF16),
            pltpu.VMEM((seg_len, width), F32),
            pltpu.VMEM((256, context), BF16),
            pltpu.VMEM((2, width, 128), F32),
            pltpu.VMEM((width, 128), F32),
            pltpu.VMEM((width, 128), F32),
            pltpu.VMEM((4,) + lead + (rows, LANES), BF16),
            pltpu.VMEM((seg_len, width), BF16),
            pltpu.VMEM((seg_len, width), BF16),
            pltpu.VMEM((seg_len, width), BF16),
            pltpu.VMEM((seg_len, width), F32),
            dma(()),
            pltpu.VMEM((seg_len, width), BF16),
            dma(()),
            pltpu.VMEM((2, half_rows, LANES), F32),
            pltpu.VMEM((2, half_rows, LANES), BF16),
            pltpu.VMEM((2, half_rows, LANES), BF16),
            pltpu.VMEM((SMALL, LANES), F32),
            pltpu.VMEM((2, SMALL, LANES), F32),
            pltpu.VMEM((2, SMALL, LANES), F32),
            pltpu.VMEM((nhi, SMALL, LANES), F32),
            pltpu.VMEM((SMALL, LANES), F32),
            dma((6,)),
            dma((6,)),
            dma((2 + nhi,)),
            dma((2 + nhi,)),
        ]
        + Scatter.scratch(12, nhi, rows),
        compiler_params=pltpu.CompilerParams(
            vmem_limit_bytes=VMEM_LIMIT,
            dimension_semantics=("arbitrary",),
            collective_id=1,
            has_side_effects=True,
        ),
        name="attention_backward",
    )(
        dout, kv, q, wide, near, place_keys, xhat_t, *mats, table_t,
        params, segment, seg_other,
        residual_grad, small_in, own_sum, branch, up, down, out,
    )


def finish_kernel(n, *refs):
    count = (len(refs) - 1) // 2
    ups, refs = refs[:2], refs[1:]
    up_out = refs[count]
    size = LANES // (n // 4)
    for f in range(4):
        for j in range(n // 4):
            for half in range(2):
                to = ((f * (n // 4) + j) * 2 + half) * size
                up_out[:, to : to + size] = ups[f // 2][
                    half, f % 2, :, j * size : (j + 1) * size
                ]
    for src, dst in zip(refs[1:count], refs[count + 1 :]):
        dst[...] = src[...]


def finish(n, ups, others):
    vmem = pl.BlockSpec(memory_space=pltpu.VMEM)
    same = [jax.ShapeDtypeStruct(a.shape, a.dtype) for a in others]
    out = jax.ShapeDtypeStruct((ups[0].shape[2], 8 * LANES), F32)
    return pl.pallas_call(
        functools.partial(finish_kernel, n),
        out_shape=(out, *same),
        in_specs=[vmem] * (2 + len(others)),
        out_specs=(vmem,) * (1 + len(others)),
        compiler_params=pltpu.CompilerParams(vmem_limit_bytes=VMEM_LIMIT),
        name="finish",
    )(*ups, *others)


def body(
    n,
    segment,
    memory,
    compressed,
    doc_lengths,
    memory_valid,
    query_weight,
    key_weight,
    value_weight,
    position_weight,
    content_bias,
    position_bias,
    output_weight,
    up_weight,
    down_weight,
    compress_weight,
    norm_gain,
    norm_shift,
    post_gain,
    post_shift,
    cotangent,
    compress_cotangent,
):
    x = lax.axis_index("head")
    dp = lax.axis_index("dp")
    first = x == 0
    nhi = n // 4
    width = segment.shape[2]
    seg_len = segment.shape[1]
    past = memory.shape[1] + compressed.shape[1]
    context = past + seg_len
    rows = query_weight.shape[0]
    half_rows = output_weight.shape[0]
    new_count = compress_cotangent.shape[1]
    comp_rows = compress_weight.shape[0]

    def swap(a):
        return lax.ppermute(a, "head", [(0, 1), (1, 0)])

    def pick(a, index):
        return jnp.where(index == 0, a[0], a[1])

    def in_order(own, got, axis):
        return jnp.where(
            first,
            jnp.concatenate([own, got], axis=axis),
            jnp.concatenate([got, own], axis=axis),
        )

    per = content_bias.shape[1]
    vectors = jnp.stack([norm_gain, norm_shift, post_gain, post_shift])
    here = jnp.arange(2 * n, dtype=jnp.int32)[None, :, None] == dp * 2 + x
    norms = jnp.where(here, vectors[:, None, :], 0).reshape(8, LANES)
    here = jnp.arange(n, dtype=jnp.int32)[None, None, :, None] == dp
    bias = jnp.stack([content_bias, position_bias])[:, :, None, :]
    bias = jnp.where(here, bias, 0).reshape(2, LANES)
    small = jnp.concatenate([norms, bias, jnp.zeros((SMALL - 10, LANES), BF16)])
    pad_rows = -(-new_count // 16) * 16
    comp_cot = jnp.pad(compress_cotangent[0], ((0, pad_rows - new_count), (0, 0)))
    table = position_rows(context, width, past + HALF)

    (
        att, seg_other, cot_other, xhat_t, windows, comp_grads, comp_shard, params, kv, q, wide, near,
        place_keys, query_whole, key_whole, value_whole, _, out_whole, up_whole, down_whole, _,
    ) = attention_forward(
        n, doc_lengths, memory_valid, compressed, memory, segment, cotangent, comp_cot,
        (query_weight, key_weight, value_weight, position_weight),
        output_weight, up_weight, down_weight, compress_weight, small, jnp.asarray(table),
    )

    lead = (nhi, 2, 2)
    (
        own_sum, branch, residual_grad, dout, out_grads, down_grads, up_rest, small_in, comp_done,
        up_first, comp_whole,
    ) = feed_forward(
        n, att, segment, seg_other, cotangent, cot_other, out_whole.reshape(width, width),
        up_whole.reshape(4, width, LANES), down_whole.reshape(4 * LANES, width), params,
        comp_grads.reshape(lead + (3 * rows, LANES)), comp_shard,
    )

    made = jnp.einsum(
        "kic,kcd->id", windows, comp_whole.reshape(3, width, LANES), preferred_element_type=F32
    ).astype(BF16)
    made = in_order(made[:new_count], swap(made[pad_rows : pad_rows + new_count]), 1)

    mats = [w.reshape(width, LANES) for w in (query_whole, key_whole, value_whole)]
    result, segment_grad, *matrices, up_last, small_done = attention_backward(
        n, dout, kv, q, wide, near, place_keys, xhat_t, mats, jnp.asarray(table.T.copy()),
        params, segment, seg_other, residual_grad, small_in, own_sum, branch,
        up_rest,
        down_grads.reshape(lead + (2 * rows, 2 * LANES)),
        out_grads.reshape(lead + (rows, 2 * LANES)),
    )

    up_final, result, segment_grad, *matrices, comp_final = finish(
        n, (up_first, up_last), (result, segment_grad, *matrices, comp_done)
    )
    query_final, key_final, value_final, place_final, out_final, down_final = matrices
    vectors = lax.dynamic_slice_in_dim(
        small_done[0:8].reshape(4, width), (dp * 2 + x) * half_rows, half_rows, 1
    )
    biases = lax.dynamic_slice_in_dim(small_done[8:10].reshape(2, 4, 128), dp * per, per, 2)
    return (
        result,
        made[None],
        segment_grad,
        query_final,
        key_final,
        value_final,
        place_final,
        biases[0],
        biases[1],
        out_final,
        up_final,
        down_final,
        comp_final,
        vectors[0],
        vectors[1],
        vectors[2],
        vectors[3],
    )


def solution(mesh):
    split = P(("dp", "head"))
    wide = P(("dp", "head"), None)
    deep = P(("dp", "head"), None, None)
    return jax.shard_map(
        functools.partial(body, mesh.shape["dp"]),
        mesh=mesh,
        in_specs=(
            deep,
            P("dp", None, None),
            P("dp", None, None),
            P("dp", None),
            P("dp"),
            P("dp", "head"),
            P("dp", "head"),
            P("dp", "head"),
            P("dp", "head"),
            P("head", "dp"),
            P("head", "dp"),
            wide,
            wide,
            wide,
            wide,
            split,
            split,
            split,
            split,
            deep,
            deep,
        ),
        out_specs=(
            deep,
            deep,
            deep,
            P("dp", "head"),
            P("dp", "head"),
            P("dp", "head"),
            P("dp", "head"),
            P("head", "dp"),
            P("head", "dp"),
            wide,
            wide,
            wide,
            wide,
            split,
            split,
            split,
            split,
        ),
        check_vma=False,
    )
```

```python
import functools
import math

import jax
import jax.numpy as jnp
import numpy as np
from jax import lax
from jax.experimental import pallas as pl
from jax.experimental.pallas import tpu as pltpu
from jax.sharding import PartitionSpec as P

F32 = jnp.float32
BF16 = jnp.bfloat16
MESH = pl.DeviceIdType.MESH
VMEM_LIMIT = 62 * 1024 * 1024
HALF = 256
LANES = 512
SMALL = 16


def dot(a, b):
    return lax.dot_general(a, b, (((1,), (0,)), ((), ())), preferred_element_type=F32)


def dot_nt(a, b):
    return lax.dot_general(a, b, (((1,), (1,)), ((), ())), preferred_element_type=F32)


def dot_tn(a, b):
    return lax.dot_general(a, b, (((0,), (0,)), ((), ())), preferred_element_type=F32)


def position_rows(context, width, used):
    distance = np.arange(context, dtype=np.float32)[:, None]
    frequency = np.exp(
        np.arange(width // 2, dtype=np.float32) * np.float32(-2.0 * math.log(10000.0) / width)
    )
    phases = distance * frequency[None, :].astype(np.float32)
    table = np.concatenate([np.sin(phases), np.cos(phases)], axis=1)
    return table[::-1][context - used :].astype(jnp.bfloat16)


def place(n):
    me = lax.axis_index("dp")
    core = lax.rem(me, 2)
    low = lax.rem(me // 2, 2)
    high = me // 4
    return core, low, high, n // 4


def meet(core, low, high, nhi, more=0):
    barrier = pltpu.get_barrier_semaphore()

    def tell(index):
        pl.semaphore_signal(barrier, inc=1, device_id={"dp": index}, device_id_type=MESH)

    for k in range(1, nhi):
        tell(lax.rem(high + k, nhi) * 4 + low * 2 + core)
    tell(high * 4 + (1 - low) * 2 + core)
    tell(high * 4 + low * 2 + (1 - core))
    pl.semaphore_wait(barrier, nhi + 1 + more)


def remote(src, dst, send, recv, index):
    return pltpu.make_async_remote_copy(
        src_ref=src,
        dst_ref=dst,
        send_sem=send,
        recv_sem=recv,
        device_id={"dp": index},
        device_id_type=MESH,
    )


class Gather:
    def __init__(self, n, pairs, sems):
        self.core, self.low, self.high, self.nhi = place(n)
        self.pairs = pairs
        (self.zs, self.zr, self.ys, self.yr, self.cs, self.cr, self.own) = sems
        order = sorted(range(1, self.nhi), key=lambda k: (min(k, self.nhi - k), k))
        self.order = order

    def z_copy(self, c, k):
        shard, whole = self.pairs[c]
        return remote(
            shard,
            whole.at[self.high, self.low, self.core],
            self.zs.at[c, k],
            self.zr.at[c, k],
            lax.rem(self.high + k, self.nhi) * 4 + self.low * 2 + self.core,
        )

    def own_copy(self, c):
        shard, whole = self.pairs[c]
        return pltpu.make_async_copy(
            shard, whole.at[self.high, self.low, self.core], self.own.at[c]
        )

    def y_copy(self, c, k):
        shard, whole = self.pairs[c]
        at = whole.at[lax.rem(self.high + k, self.nhi), self.low, self.core]
        return remote(
            shard if k == 0 else at,
            at,
            self.ys.at[c, k],
            self.yr.at[c, k],
            self.high * 4 + (1 - self.low) * 2 + self.core,
        )

    def c_copy(self, c):
        _, whole = self.pairs[c]
        part = whole.at[:, :, self.core]
        return remote(
            part,
            part,
            self.cs.at[c],
            self.cr.at[c],
            self.high * 4 + self.low * 2 + (1 - self.core),
        )

    def start(self, c):
        for k in self.order:
            self.z_copy(c, k).start()
        self.y_copy(c, 0).start()
        self.own_copy(c).start()

    def pass_y(self, c):
        for k in self.order:
            self.z_copy(c, self.nhi - k).wait_recv()
            self.y_copy(c, k).start()

    def pass_core(self, c):
        self.own_copy(c).wait()
        for k in range(self.nhi):
            self.y_copy(c, k).wait_recv()
        self.c_copy(c).start()

    def arrive(self, c):
        self.c_copy(c).wait_recv()

    def close(self, c):
        for k in self.order:
            self.z_copy(c, k).wait_send()
        for k in range(self.nhi):
            self.y_copy(c, k).wait_send()
        self.c_copy(c).wait_send()

    @staticmethod
    def semaphores(count, nhi):
        dma = pltpu.SemaphoreType.DMA
        return [dma((count, nhi))] * 4 + [dma((count,))] * 3


class Scatter:
    def __init__(self, n, items, mine, mine_sem, sems):
        self.core, self.low, self.high, self.nhi = place(n)
        self.items = items
        self.mine, self.mine_sem = mine, mine_sem
        (self.cs, self.cr, self.ys, self.yr, self.zs, self.zr) = sems

    def c_copy(self, c):
        return remote(
            self.items[c][0].at[:, :, 1 - self.core],
            self.items[c][2],
            self.cs.at[c],
            self.cr.at[c],
            self.high * 4 + self.low * 2 + (1 - self.core),
        )

    def mine_copy(self, c):
        slot = c % 2
        return pltpu.make_async_copy(
            self.items[c][0].at[:, :, self.core], self.mine.at[slot], self.mine_sem.at[slot]
        )

    def y_copy(self, c):
        return remote(
            self.items[c][2].at[:, 1 - self.low],
            self.items[c][3],
            self.ys.at[c],
            self.yr.at[c],
            self.high * 4 + (1 - self.low) * 2 + self.core,
        )

    def z_copies(self, c):
        return [
            remote(
                self.items[c][3].at[lax.rem(self.high + k, self.nhi)],
                self.items[c][4].at[k - 1],
                self.zs.at[c, k - 1],
                self.zr.at[c, k - 1],
                lax.rem(self.high + k, self.nhi) * 4 + self.low * 2 + self.core,
            )
            for k in range(1, self.nhi)
        ]

    def start(self, c):
        self.c_copy(c).start()
        if not self.items[c][1]:
            self.mine_copy(c).start()

    def add_core(self, c):
        here = self.items[c][1]
        if not here:
            self.mine_copy(c).wait()
        self.c_copy(c).wait_recv()
        land = self.items[c][2]

        def body(i, carry):
            for j in range(2):
                own = self.items[c][0][i, j, self.core] if here else self.mine[c % 2, i, j]
                land[i, j] = land[i, j] + own
            return carry

        lax.fori_loop(0, self.nhi, body, 0)
        self.y_copy(c).start()

    def add_y(self, c):
        self.y_copy(c).wait_recv()
        src, land = self.items[c][2], self.items[c][3]

        def body(i, carry):
            land[i] = land[i] + src[i, self.low]
            return carry

        lax.fori_loop(0, self.nhi, body, 0)
        for copy in self.z_copies(c):
            copy.start()

    def add_z(self, c):
        for copy in self.z_copies(c):
            copy.wait_recv()
        land, last, done = self.items[c][3:]
        total = land[self.high].astype(F32)
        for k in range(self.nhi - 1):
            total = total + last[k].astype(F32)
        done(total)

    def tick(self, t):
        count = len(self.items)
        if 0 <= t - 1 < count:
            self.add_core(t - 1)
        if t < count:
            self.start(t)
        if 0 <= t - 2 < count:
            self.add_y(t - 2)
        if 0 <= t - 3 < count:
            self.add_z(t - 3)

    def close(self, c):
        self.c_copy(c).wait_send()
        self.y_copy(c).wait_send()
        for copy in self.z_copies(c):
            copy.wait_send()

    @staticmethod
    def scratch(count, nhi, rows):
        dma = pltpu.SemaphoreType.DMA
        return [
            pltpu.VMEM((count, nhi, 2, rows, LANES), BF16),
            pltpu.VMEM((count, nhi, rows, LANES), BF16),
            pltpu.VMEM((count, nhi - 1, rows, LANES), BF16),
            pltpu.VMEM((2, nhi, 2, rows, LANES), BF16),
            dma((2,)),
            dma((count,)),
            dma((count,)),
            dma((count,)),
            dma((count,)),
            dma((count, nhi - 1)),
            dma((count, nhi - 1)),
        ]


def norm_rows(values):
    mean = jnp.mean(values, axis=-1, keepdims=True)
    centred = values - mean
    variance = jnp.mean(centred * centred, axis=-1, keepdims=True)
    return centred * lax.rsqrt(variance + 1e-05)


def attend_rows(query_content, query_place, keys, place_keys, first_seen, last_seen, scale):
    width = keys.shape[0]
    content = dot_nt(query_content, keys)
    by_place = pltpu.roll(
        dot_nt(query_place, place_keys), width - (HALF - 1), 1, stride=1, stride_axis=0
    )
    column = lax.broadcasted_iota(jnp.int32, (HALF, width), 1)
    seen = (column >= first_seen) & (column <= last_seen)
    scores = jnp.where(seen, (content + by_place) * (scale * math.log2(math.e)), -1e30)
    top = jnp.max(scores, axis=1, keepdims=True)
    expo = jnp.exp2(scores - top)
    return expo * (1.0 / jnp.sum(expo, axis=1, keepdims=True))


def forward_kernel(
    n,
    past,
    seg_len,
    docs,
    valid,
    compressed,
    memory,
    segment,
    cotangent,
    comp_cot,
    query_w,
    key_w,
    value_w,
    place_w,
    out_w,
    up_w,
    down_w,
    comp_w,
    small,
    table,
    attended,
    seg_other,
    cot_other,
    xhat_hbm,
    windows_hbm,
    comp_grads_hbm,
    comp_shard_hbm,
    params,
    kv_out,
    q_out,
    wide_out,
    near_out,
    place_out,
    query_whole,
    key_whole,
    value_whole,
    place_whole,
    out_whole,
    up_whole,
    down_whole,
    small_whole,
    out_shard,
    up_parts,
    up_shard,
    comp_shard,
    small_shard,
    normed,
    xhat_out,
    memory_f,
    windows,
    comp_rows_cot,
    comp_grads,
    past_rows,
    seg_rows,
    flat,
    small_rows,
    att,
    load_sem,
    flat_sem,
    own_sem,
    store_sem,
    pair_send,
    pair_recv,
    att_own,
    att_send,
    att_recv,
    *sems,
):
    step = pl.program_id(0)
    x = lax.axis_index("head")
    core, low, high, nhi = place(n)
    tile = 256
    width = normed.shape[2]
    context = past + seg_len
    head = jnp.maximum(step - 2, 0) // 2
    half = comp_w.shape[1] // 2

    items = [(small_shard, small_whole)]
    items += [(query_w, query_whole), (key_w, key_whole), (value_w, value_whole), (place_w, place_whole)]
    for b in range(2):
        to = pl.ds(b * LANES, LANES)
        items.append((out_shard.at[:, :, to], out_whole.at[:, :, :, :, :, to]))
    items += [(up_shard.at[f], up_whole.at[f]) for f in range(4)]
    mid = down_w.shape[0] // 2
    for part in range(2):
        for b in range(2):
            at, to = pl.ds(part * mid, mid), pl.ds(b * LANES, LANES)
            items.append((down_w.at[at, to], down_whole.at[:, :, :, at, to]))
    gather = Gather(n, items, sems)
    count = len(items)
    needs = {5: 1, 7: 2}
    pad_rows = comp_cot.shape[0]

    def pair(src, dst, k):
        return pltpu.make_async_remote_copy(
            src_ref=src,
            dst_ref=dst,
            send_sem=pair_send.at[k],
            recv_sem=pair_recv.at[k],
            device_id={"head": 1 - x},
            device_id_type=MESH,
        )

    mine_at = pl.ds(pl.multiple_of(x * half, half), half)
    other_at = pl.ds(pl.multiple_of((1 - x) * half, half), half)
    pairs = [
        pair(small, small_shard.at[x], 0),
        pair(out_w, out_shard.at[x], 1),
        pair(up_parts.at[1 - x], up_shard.at[:, x], 2),
        pair(comp_w.at[:, other_at], comp_shard.at[x], 3),
        pair(segment.at[0], seg_other, 4),
        pair(cotangent.at[0], cot_other, 5),
        pair(comp_cot.at[:, other_at], comp_rows_cot.at[1], 6),
    ]
    owns = [
        pltpu.make_async_copy(small, small_shard.at[x], own_sem.at[0]),
        pltpu.make_async_copy(out_w, out_shard.at[x], own_sem.at[1]),
        pltpu.make_async_copy(up_parts.at[x], up_shard.at[:, x], own_sem.at[2]),
        pltpu.make_async_copy(comp_w.at[:, mine_at], comp_shard.at[x], own_sem.at[3]),
        pltpu.make_async_copy(comp_cot.at[:, mine_at], comp_rows_cot.at[0], own_sem.at[4]),
    ]
    loads = []
    for i in range(2):
        s = lax.rem(x + i, 2)
        loads.append(pltpu.make_async_copy(compressed.at[s], past_rows.at[i, 0], load_sem.at[i, 0]))
        loads.append(pltpu.make_async_copy(memory.at[s], past_rows.at[i, 1], load_sem.at[i, 1]))
    loads.append(pltpu.make_async_copy(segment.at[0], seg_rows.at[0], load_sem.at[0, 2]))
    load_other = pltpu.make_async_copy(seg_other, seg_rows.at[1], load_sem.at[1, 2])
    store_xhat = pltpu.make_async_copy(xhat_out, xhat_hbm, store_sem.at[0])
    store_windows = pltpu.make_async_copy(windows, windows_hbm, store_sem.at[1])
    store_grads = pltpu.make_async_copy(comp_grads, comp_grads_hbm, store_sem.at[2])
    store_shard = pltpu.make_async_copy(comp_shard, comp_shard_hbm, store_sem.at[3])

    joined = set()

    def join(k):
        if k not in joined:
            joined.add(k)
            owns[k].wait()
            pairs[k].wait_recv()

    def tick(t):
        lead = t + 3
        if lead < count:
            if lead in needs:
                join(needs[lead])
            gather.start(lead)
        if t < count:
            gather.pass_y(t)
        if 0 <= t - 1 < count:
            gather.pass_core(t - 1)
        if 0 <= t - 2 < count and t != 6:
            gather.arrive(t - 2)

    def flat_copies(h, slot):
        at = pl.ds(h * 128, 128)
        return [
            pltpu.make_async_copy(
                whole.at[:, :, :, :, at],
                flat.at[slot, :, :, :, :, pl.ds(j * 128, 128)],
                flat_sem.at[slot, j],
            )
            for j, whole in enumerate((query_whole, key_whole, value_whole, place_whole))
        ]

    def norm_into(i, values, at):
        eye = (
            lax.broadcasted_iota(jnp.int32, (tile, tile), 0)
            == lax.broadcasted_iota(jnp.int32, (tile, tile), 1)
        ).astype(BF16)
        gain = jnp.concatenate([params[0:1, :], params[1:2, :]], axis=1)
        shift = jnp.concatenate([params[2:3, :], params[3:4, :]], axis=1)
        xhat = norm_rows(values.astype(F32))
        normed[i, pl.ds(at, tile)] = (xhat * gain + shift).astype(BF16)
        xhat = xhat.astype(BF16)
        for b in range(width // tile):
            xhat_out[i, b * tile : (b + 1) * tile, pl.ds(at, tile)] = dot_nt(
                eye, xhat[:, b * tile : (b + 1) * tile]
            ).astype(BF16)

    def norm_past(i):
        per = past // 2 // tile

        def one(k, carry):
            at = pl.multiple_of(k * tile, tile)
            inner = pl.multiple_of(lax.rem(k, per) * tile, tile)
            norm_into(i, past_rows[i, k // per, pl.ds(inner, tile)], at)
            return carry

        lax.fori_loop(0, past // tile, one, 0)

    def norm_segment(i):
        def one(k, carry):
            at = pl.multiple_of(k * tile, tile)
            norm_into(i, seg_rows[i, pl.ds(at, tile)], past + at)
            return carry

        lax.fori_loop(0, seg_len // tile, one, 0)

    @pl.when(step == 0)
    def _():
        barrier = pltpu.get_barrier_semaphore()
        pl.semaphore_signal(
            barrier, inc=1, device_id={"head": 1 - x}, device_id_type=MESH
        )
        meet(core, low, high, nhi, 1)
        for k in (0, 1):
            pairs[k].start()
            owns[k].start()
        gather.start(1)
        size = LANES // (n // 4)
        for half_at in range(2):
            for f in range(4):
                for j in range(n // 4):
                    at = ((f * (n // 4) + j) * 2 + half_at) * size
                    up_parts[half_at, f, :, j * size : (j + 1) * size] = up_w[:, at : at + size]
        for k in (2, 6, 3, 4, 5):
            pairs[k].start()
        for copy in owns[2:]:
            copy.start()
        for copy in loads:
            copy.start()
        join(0)
        gather.start(0)
        gather.start(2)
        tick(0)
        tick(1)
        tick(2)
        summed = pltpu.make_async_copy(small_whole, small_rows, load_sem.at[0, 3])
        summed.start()
        summed.wait()
        both = jnp.sum(small_rows[...].reshape(n, 2, SMALL, LANES).astype(F32), axis=0)
        row = lax.broadcasted_iota(jnp.int32, (SMALL, LANES), 0)
        by_head = jnp.where(x == 0, both[0], both[1])
        params[...] = jnp.where(row < 8, both[0] + both[1], by_head)
        for copy in (loads[0], loads[1], loads[4]):
            copy.wait()
        norm_past(0)
        tick(3)
        norm_segment(0)

    @pl.when(step == 1)
    def _():
        for copy in loads[2:4]:
            copy.wait()
        norm_past(1)
        tick(4)
        tick(5)
        gather.arrive(4)
        for copy in flat_copies(0, 0):
            copy.start()

    for k in range(2, 10):

        @pl.when(step == k)
        def _(k=k):
            h, slot = (k - 2) // 2, ((k - 2) // 2) % 2
            if k % 2 == 0:
                for copy in flat_copies(h, slot):
                    copy.wait()
                if h < 3:
                    for copy in flat_copies(h + 1, 1 - slot):
                        copy.start()
            if k == 3:
                pairs[4].wait_recv()
                load_other.start()
                load_other.wait()
                norm_segment(1)
                store_xhat.start()
                join(3)
                store_shard.start()

    def att_pair(h, i):
        at = pl.ds(pl.multiple_of(x * LANES + h * 128, 128), 128)
        return pltpu.make_async_remote_copy(
            src_ref=att.at[h, i],
            dst_ref=attended.at[1 - i, :, at],
            send_sem=att_send.at[h, i],
            recv_sem=att_recv.at[h, i],
            device_id={"head": 1 - x},
            device_id_type=MESH,
        )

    def att_local(h, i):
        at = pl.ds(pl.multiple_of(x * LANES + h * 128, 128), 128)
        return pltpu.make_async_copy(att.at[h, i], attended.at[i, :, at], att_own.at[h, i])

    @pl.when(step >= 2)
    def _():
        i = lax.rem(step, 2)
        s = lax.rem(x + i, 2)
        slot = lax.rem(head, 2)

        def weights(a, b):
            return flat[slot, :, :, :, :, a:b].reshape(width, b - a)

        @pl.when(i == 0)
        def _():
            mat = weights(384, 512)
            for k in range(table.shape[0] // tile):
                place_out[0, k * tile : (k + 1) * tile] = dot(
                    table[k * tile : (k + 1) * tile], mat
                ).astype(BF16)

        mat = weights(128, 384)
        for k in range(context // tile):
            kv_out[0, 0, k * tile : (k + 1) * tile] = dot(
                normed[i, pl.ds(k * tile, tile)], mat
            ).astype(BF16)
        mat = weights(0, 128)
        bias_at = pl.ds(pl.multiple_of(head * 128, 128), 128)
        for k in range(seg_len // tile):
            queries = dot(normed[i, pl.ds(past + k * tile, tile)], mat)
            at = slice(k * tile, (k + 1) * tile)
            q_out[0, 0, at, 0:128] = (queries + params[8:9, bias_at]).astype(BF16)
            q_out[0, 0, at, 128:256] = (queries + params[9:10, bias_at]).astype(BF16)

        flip = (
            lax.broadcasted_iota(jnp.int32, (HALF, HALF), 0)
            + lax.broadcasted_iota(jnp.int32, (HALF, HALF), 1)
            == HALF - 1
        ).astype(BF16)
        scale = 1.0 / math.sqrt(128)
        for part, out, key_start, key_count, place_start in (
            (0, wide_out, 0, past + HALF, 0),
            (1, near_out, past, seg_len, past - HALF),
        ):
            token = lax.broadcasted_iota(jnp.int32, (HALF, 1), 0) + part * HALF
            end, first = 0, past - valid[s]
            for doc in range(3):
                end = end + docs[s, doc]
                first = jnp.where(token >= end, past + end, first)
            at = slice(part * HALF, (part + 1) * HALF)
            weights_low = attend_rows(
                q_out[0, 0, at, 0:128],
                q_out[0, 0, at, 128:256],
                kv_out[0, 0, key_start : key_start + key_count, 0:128],
                place_out[0, place_start : place_start + key_count],
                first - key_start,
                token + (past - key_start),
                scale,
            ).astype(BF16)
            out[0, 0] = dot(flip, weights_low).astype(BF16)
            q_out[0, 0, at] = dot(flip, q_out[0, 0, at]).astype(BF16)
            att[head, i, at] = dot(
                weights_low, kv_out[0, 0, key_start : key_start + key_count, 128:256]
            ).astype(BF16)
        att_pair(head, i).start()
        att_local(head, i).start()

    for k in range(2, 10):
        pl.when(step == k)(functools.partial(tick, k + 4))

    @pl.when(step == pl.num_programs(0) - 1)
    def _():
        memory_f[:, past // 2 :, :] = jnp.zeros((width // 128, 16, 128), F32)
        for i in range(2):
            for b in range(width // 128):
                at = slice(b * 128, (b + 1) * 128)
                memory_f[b, 0 : past // 2, :] = past_rows[i, 1, :, at].astype(F32)
                for tap in range(3):
                    windows[tap, i * pad_rows : (i + 1) * pad_rows, at] = memory_f[
                        b, pl.ds(tap, pad_rows, stride=3), :
                    ].astype(BF16)
        store_windows.start()
        owns[4].wait()
        pairs[6].wait_recv()
        tick(14)
        comp_rows_both = comp_rows_cot[...].reshape(2 * pad_rows, LANES)
        for tap in range(3):
            for k in range(width // tile):
                at = slice(k * tile, (k + 1) * tile)
                comp_grads[tap * width + k * tile : tap * width + (k + 1) * tile, :] = dot_tn(
                    windows[tap, :, at], comp_rows_both
                ).astype(BF16)
        store_grads.start()
        for t in range(15, count + 2):
            tick(t)
        for copy in (store_xhat, store_windows, store_grads, store_shard):
            copy.wait()
        for h in range(4):
            for i in range(2):
                att_local(h, i).wait()
                att_pair(h, i).wait()
        for copy in pairs:
            copy.wait_send()
        pairs[5].wait_recv()
        for c in range(count):
            gather.close(c)


def attention_forward(
    n, docs, valid, compressed, memory, segment, cotangent, comp_cot, mats, out_w, up_w, down_w,
    comp_w, small, table,
):
    _, seg_len, width = segment.shape
    past = compressed.shape[1] + memory.shape[1]
    context = past + seg_len
    nhi = n // 4
    lead = (nhi, 2, 2)
    half_rows = out_w.shape[0]
    comp_rows = comp_w.shape[0]
    pad_rows = comp_cot.shape[0]
    any_spec = pl.BlockSpec(memory_space=pl.ANY)
    smem = pl.BlockSpec(memory_space=pltpu.SMEM)
    single = pl.Buffered(1)
    bf = lambda *shape: jax.ShapeDtypeStruct(shape, BF16)
    head = lambda t: jnp.maximum(t - 2, 0) // 2
    which = lambda t: lax.rem(jnp.maximum(t, 2), 2)
    by_both = lambda t: (head(t), which(t), 0, 0)
    dma = pltpu.SemaphoreType.DMA
    full = lambda shape: pl.BlockSpec(shape, lambda t: (0,) * len(shape), pipeline_mode=single)
    count = 15
    return pl.pallas_call(
        functools.partial(forward_kernel, n, past, seg_len),
        grid=(10,),
        out_shape=(
            bf(2, seg_len, width),
            bf(seg_len, width),
            bf(seg_len, width),
            bf(2, width, context),
            bf(3, 2 * pad_rows, width),
            bf(3 * width, LANES),
            bf(2, comp_rows, LANES),
            jax.ShapeDtypeStruct((SMALL, LANES), F32),
            bf(4, 2, context, 256),
            bf(4, 2, seg_len, 256),
            bf(4, 2, HALF, past + HALF),
            bf(4, 2, HALF, seg_len),
            bf(4, past + HALF, 128),
            *[bf(*lead, *w.shape) for w in mats],
            bf(*lead, 2, half_rows, width),
            bf(4, *lead, 2, half_rows, LANES),
            bf(*lead, *down_w.shape),
            bf(*lead, 2, SMALL, LANES),
        ),
        in_specs=[smem, smem]
        + [any_spec] * 5
        + [full(a.shape) for a in (*mats, out_w, up_w, down_w, comp_w, small)]
        + [pl.BlockSpec(table.shape, lambda t: (0, 0), pipeline_mode=single)],
        out_specs=(
            *[any_spec] * 6,
            any_spec,
            pl.BlockSpec((SMALL, LANES), lambda t: (0, 0)),
            pl.BlockSpec((1, 1, context, 256), by_both),
            pl.BlockSpec((1, 1, seg_len, 256), by_both),
            pl.BlockSpec((1, 1, HALF, past + HALF), by_both),
            pl.BlockSpec((1, 1, HALF, seg_len), by_both),
            pl.BlockSpec((1, past + HALF, 128), lambda t: (head(t), 0, 0)),
            *[any_spec] * 8,
        ),
        scratch_shapes=[
            pltpu.VMEM((2, half_rows, width), BF16),
            pltpu.VMEM((2, 4, half_rows, LANES), BF16),
            pltpu.VMEM((4, 2, half_rows, LANES), BF16),
            pltpu.VMEM((2, comp_rows, LANES), BF16),
            pltpu.VMEM((2, SMALL, LANES), BF16),
            pltpu.VMEM((2, context, width), BF16),
            pltpu.VMEM((2, width, context), BF16),
            pltpu.VMEM((width // 128, past // 2 + 16, 128), F32),
            pltpu.VMEM((3, 2 * pad_rows, width), BF16),
            pltpu.VMEM((2, pad_rows, LANES), BF16),
            pltpu.VMEM((3 * width, LANES), BF16),
            pltpu.VMEM((2, 2, past // 2, width), BF16),
            pltpu.VMEM((2, seg_len, width), BF16),
            pltpu.VMEM((2,) + lead + (mats[0].shape[0], LANES), BF16),
            pltpu.VMEM(lead + (2, SMALL, LANES), BF16),
            pltpu.VMEM((4, 2, seg_len, 128), BF16),
            dma((2, 4)),
            dma((2, 4)),
            dma((6,)),
            dma((4,)),
            dma((7,)),
            dma((7,)),
            dma((4, 2)),
            dma((4, 2)),
            dma((4, 2)),
        ]
        + Gather.semaphores(count, nhi),
        compiler_params=pltpu.CompilerParams(
            vmem_limit_bytes=VMEM_LIMIT,
            dimension_semantics=("arbitrary",),
            collective_id=0,
            has_side_effects=True,
        ),
        name="attention_forward",
    )(
        docs, valid, compressed, memory, segment, cotangent, comp_cot, *mats, out_w, up_w, down_w,
        comp_w, small, table,
    )


def gelu_parts(v):
    c = math.sqrt(2.0 / math.pi)
    square = v * v
    t = jnp.tanh(c * (v + 0.044715 * square * v))
    half = 0.5 * (1.0 + t)
    value = v * half
    return value, half + value * (1.0 - half) * (2 * c + (6 * 0.044715 * c) * square)


def feed_kernel(
    n,
    att_in,
    segment,
    seg_other,
    cotangent,
    cot_other,
    out_in,
    up_in,
    down_in,
    params,
    comp,
    comp_shard,
    windows,
    own_out,
    branch_out,
    residual_out,
    dout,
    out_grads,
    down_grads,
    up_rest,
    small_out,
    comp_out,
    up_out,
    made_out,
    comp_whole,
    att,
    seg,
    cot,
    out_w,
    up,
    down,
    residual,
    low,
    low_t,
    act,
    pre,
    branch,
    terms,
    terms_land,
    cast,
    up_grads,
    mixed,
    stage,
    up_send,
    up_land,
    comp_stage,
    comp_send,
    comp_land,
    made_own,
    made_send,
    made_land,
    made_sem,
    load_sem,
    store_sem,
    stage_sem,
    pair_send,
    pair_recv,
    land_c,
    land_y,
    land_z,
    mine,
    mine_sem,
    *sems,
):
    sems, gather_sems = sems[:6], sems[6:]
    x = lax.axis_index("head")
    core, low_y, high, nhi = place(n)
    tile = 256
    _, seg_len, width = att.shape
    rows = width // n
    half_rows = rows // 2
    comp_rows = comp_send.shape[0]

    def pair(src, dst, k):
        return pltpu.make_async_remote_copy(
            src_ref=src,
            dst_ref=dst,
            send_sem=pair_send.at[k],
            recv_sem=pair_recv.at[k],
            device_id={"head": 1 - x},
            device_id_type=MESH,
        )

    terms_pair = pair(cast.at[0], terms_land, 0)
    mixed_pair = pair(mixed.at[1 - x], dout.at[1], 1)
    comp_pair = pair(comp_send, comp_land, 2)
    up_pairs = [pair(up_send.at[f], up_land.at[f], 3 + f) for f in range(2)]
    made_pair = pair(made_send, made_land, 5)
    scatter = Scatter(
        n,
        [
            (part, here, land_c.at[c], land_y.at[c], land_z.at[c], done)
            for c, (part, here, done) in enumerate(
                [
                    (
                        comp.at[:, :, :, pl.ds(m * rows, rows)],
                        False,
                        comp_block(m, x, rows, comp_stage, comp_out, comp_send, comp_pair),
                    )
                    for m in range(3)
                ]
                + [
                    (up_grads.at[f], True, up_block(f, x, up_out, up_send, up_pairs[f]))
                    for f in range(2)
                ]
            )
        ],
        mine,
        mine_sem,
        sems,
    )

    third = comp_rows // 3
    gather = Gather(
        n,
        [
            (
                comp_shard.at[:, pl.ds(m * third, third)],
                comp_whole.at[:, :, :, :, pl.ds(m * third, third)],
            )
            for m in range(3)
        ],
        gather_sems,
    )

    def load(src, dst, k):
        return pltpu.make_async_copy(src, dst, load_sem.at[k])

    loads = {
        "att1": load(att_in.at[1], att.at[1], 0),
        "out": load(out_in, out_w, 1),
        "seg1": load(seg_other, seg.at[1], 2),
        "cot1": load(cot_other, cot.at[1], 3),
        "up": load(up_in, up, 4),
        "down": load(down_in, down, 5),
        "att0": load(att_in.at[0], att.at[0], 6),
        "seg0": load(segment.at[0], seg.at[0], 7),
        "cot0": load(cotangent.at[0], cot.at[0], 8),
    }
    for copy in loads.values():
        copy.start()
    barrier = pltpu.get_barrier_semaphore()
    pl.semaphore_signal(barrier, inc=1, device_id={"head": 1 - x}, device_id_type=MESH)
    meet(core, low_y, high, nhi, 1)
    scatter.start(0)
    scatter.start(1)
    gather.start(0)

    eye = (
        lax.broadcasted_iota(jnp.int32, (tile, tile), 0)
        == lax.broadcasted_iota(jnp.int32, (tile, tile), 1)
    ).astype(BF16)
    gain = jnp.concatenate([params[4:5, :], params[5:6, :]], axis=1)
    shift = jnp.concatenate([params[6:7, :], params[7:8, :]], axis=1)

    def project(i):
        for k in range(seg_len // tile):
            at = slice(k * tile, (k + 1) * tile)
            whole_at = slice(i * seg_len + k * tile, i * seg_len + (k + 1) * tile)
            value = seg[i, at].astype(F32) + dot(att[i, at], out_w[...])
            residual[at, :] = value
            value = (norm_rows(value) * gain + shift).astype(BF16)
            low[whole_at, :] = value
            for b in range(width // tile):
                low_t[b * tile : (b + 1) * tile, whole_at] = dot_nt(
                    eye, value[:, b * tile : (b + 1) * tile]
                ).astype(BF16)

    def hidden(i, between):
        whole_at = slice(i * seg_len, (i + 1) * seg_len)
        branch[...] = jnp.zeros_like(branch)
        terms[...] = jnp.zeros_like(terms)

        def one(f, carry):
            down_at = pl.ds(pl.multiple_of(f * LANES, LANES), LANES)
            up_at = pl.ds(pl.multiple_of(f * width, width), width)
            value, slope = gelu_parts(dot(low[whole_at, :], up[up_at, :]))
            value = value.astype(BF16)
            act[f, whole_at, :] = value
            back = dot_nt(cot[i], down[down_at, :]).astype(BF16).astype(F32)
            back = (back * slope).astype(BF16)
            pre[f, whole_at, :] = back
            branch[...] += dot(value, down[down_at, :])
            terms[...] += dot_nt(back, up[up_at, :])
            for k, steps in enumerate(between):

                @pl.when(f == k)
                def _(steps=steps):
                    for run, c in steps:
                        run(c)

            return carry

        lax.fori_loop(0, 4, one, 0)

    for name in ("att1", "out", "seg1"):
        loads[name].wait()
    project(1)
    scatter.add_core(0)
    scatter.start(2)
    gather.start(1)
    for name in ("cot1", "up", "down"):
        loads[name].wait()
    hidden(
        1,
        (
            ((scatter.add_core, 1), (gather.pass_y, 0)),
            ((scatter.add_core, 2), (scatter.add_y, 0), (gather.start, 2)),
            ((gather.pass_y, 1),),
            ((scatter.add_y, 1),),
        ),
    )
    cast[0] = terms[...].astype(BF16)
    terms_pair.start()
    cast[1] = branch[...].astype(BF16)
    store_branch = pltpu.make_async_copy(cast.at[1], branch_out, store_sem.at[0])
    store_branch.start()
    for name in ("att0", "seg0", "cot0"):
        loads[name].wait()
    project(0)
    scatter.add_z(0)
    hidden(
        0,
        (
            ((gather.pass_core, 0),),
            ((gather.pass_y, 2),),
            ((scatter.add_y, 2),),
            ((scatter.add_z, 1),),
        ),
    )
    branch[...] += residual[...]
    store_own = pltpu.make_async_copy(branch, own_out, store_sem.at[1])
    store_own.start()

    count = windows.shape[0]
    load_windows = pltpu.make_async_copy(windows, down.at[pl.ds(0, count)], made_sem.at[2 * n])
    load_windows.start()

    block = tile // (4 * rows)

    def up_grad(f):
        for k in range(width // tile):
            grad = dot(low_t[k * tile : (k + 1) * tile, :], pre[f]).astype(BF16)
            up_grads[f, k * block : (k + 1) * block] = grad.reshape(block, 2, 2, rows, LANES)
        if f < 2:
            scatter.start(3 + f)

    up_grad(0)
    gather.pass_core(1)
    up_grad(1)
    scatter.add_core(3)
    scatter.add_z(2)
    up_grad(2)
    scatter.add_core(4)
    up_grad(3)
    store_rest = pltpu.make_async_copy(up_grads.at[pl.ds(2, 2)], up_rest, store_sem.at[4])
    store_rest.start()

    terms_pair.wait_recv()
    gain_grad = jnp.zeros((1, width), F32)
    shift_grad = jnp.zeros((1, width), F32)
    terms_pair.wait_send()
    for k in range(seg_len // tile):
        at = slice(k * tile, (k + 1) * tile)
        grad = terms[at, :] + terms_land[at, :].astype(F32)
        value = residual[at, :]
        mean = jnp.mean(value, axis=-1, keepdims=True)
        centred = value - mean
        rstd = lax.rsqrt(jnp.mean(centred * centred, axis=-1, keepdims=True) + 1e-05)
        xhat = centred * rstd
        gain_grad += jnp.sum(grad * xhat, axis=0, keepdims=True)
        shift_grad += jnp.sum(grad, axis=0, keepdims=True)
        grad = cot[0, at].astype(F32) + norm_back(xhat, rstd, grad * gain)
        residual[at, :] = grad
        grad = grad.astype(BF16)
        cast[0, at, :] = grad
        back = dot_nt(grad, out_w[...]).astype(BF16)
        mixed[0, at, :] = back[:, 0:LANES]
        mixed[1, at, :] = back[:, LANES:]
    mixed_pair.start()
    store_dout = pltpu.make_async_copy(mixed.at[x], dout.at[0], store_sem.at[2])
    store_dout.start()
    store_residual = pltpu.make_async_copy(residual, residual_out, store_sem.at[3])
    store_residual.start()
    small_out[...] = jnp.zeros_like(small_out)
    small_out[4:5, :] = gain_grad[:, 0:LANES]
    small_out[5:6, :] = gain_grad[:, LANES:]
    small_out[6:7, :] = shift_grad[:, 0:LANES]
    small_out[7:8, :] = shift_grad[:, LANES:]
    gather.pass_core(2)

    staged = [None, None]
    jobs = [(out_grads, k * tile, None, k) for k in range(width // tile)]
    jobs += [
        (down_grads, f * LANES + k * tile, f, k) for f in range(4) for k in range(LANES // tile)
    ]
    for j, (target, start, f, k) in enumerate(jobs):
        slot = j % 2
        at = slice(k * tile, (k + 1) * tile)
        if f is None:
            grad = dot_tn(att[0, :, at], cast[0])
        else:
            grad = dot_tn(act[f, 0:seg_len, at], cot[0]) + dot_tn(act[f, seg_len:, at], cot[1])
        if staged[slot] is not None:
            staged[slot].wait()
        stage[slot] = grad.astype(BF16)
        staged[slot] = pltpu.make_async_copy(
            stage.at[slot], target.at[pl.ds(start, tile)], stage_sem.at[slot]
        )
        staged[slot].start()
        if j == 3:
            scatter.add_y(3)
        if j == 10:
            scatter.add_y(4)
            scatter.add_z(3)
    for m in range(3):
        gather.arrive(m)
    load_comp = []
    for b in range(n):
        for half in range(2):
            load_comp.append(
                pltpu.make_async_copy(
                    comp_whole.at[b // 4, (b // 2) % 2, b % 2, half],
                    up.at[pl.ds((2 * b + half) * comp_rows, comp_rows)],
                    made_sem.at[2 * b + half],
                )
            )
            load_comp[-1].start()
    load_windows.wait()
    for copy in load_comp:
        copy.wait()
    made = jnp.zeros((count // 3, LANES), F32)
    for tap in range(3):
        made += dot(
            down[tap * (count // 3) : (tap + 1) * (count // 3), :],
            up[tap * width : (tap + 1) * width, :],
        )
    made_own[...] = made[: count // 6].astype(BF16)
    made_send[...] = made[count // 6 :].astype(BF16)
    made_pair.start()
    scatter.add_z(4)
    comp_pair.wait_recv()
    to = pl.ds(pl.multiple_of((1 - x) * LANES, LANES), LANES)
    comp_out[:, to] = comp_land[...].astype(F32)
    made_pair.wait_recv()
    made_out[:, to] = made_land[...]
    made_out[:, pl.ds(pl.multiple_of(x * LANES, LANES), LANES)] = made_own[...]
    for f in range(2):
        up_pairs[f].wait_recv()
        up_out[1 - x, f] = up_land[f].astype(F32)
    mixed_pair.wait_recv()
    for copy in [mixed_pair, comp_pair, made_pair, *up_pairs]:
        copy.wait_send()
    for copy in [*staged, store_branch, store_own, store_dout, store_residual, store_rest]:
        copy.wait()
    for c in range(5):
        scatter.close(c)
    for m in range(3):
        gather.close(m)


def comp_block(m, x, rows, stage, out, send, pair):
    def done(total):
        stage[m * rows : (m + 1) * rows, :] = total
        if m == 2:
            half = send.shape[0]
            upper, lower = stage[0:half, :], stage[half:, :]
            to = pl.ds(pl.multiple_of(x * LANES, LANES), LANES)
            out[:, to] = jnp.where(x == 0, upper, lower)
            send[...] = jnp.where(x == 0, lower, upper).astype(BF16)
            pair.start()

    return done


def up_block(f, x, out, send, pair):
    def done(total):
        half = send.shape[1]
        upper, lower = total[0:half], total[half:]
        out[x, f] = jnp.where(x == 0, upper, lower)
        send[f] = jnp.where(x == 0, lower, upper).astype(BF16)
        pair.start()

    return done


def feed_forward(
    n, att, segment, seg_other, cotangent, cot_other, out_w, up, down, params, comp, comp_shard, windows
):
    _, seg_len, width = att.shape
    rows = width // n
    half_rows = rows // 2
    nhi = n // 4
    comp_rows = comp.shape[3] // 2
    made_rows = windows.shape[0] // 6
    total = 2 * seg_len
    any_spec = pl.BlockSpec(memory_space=pl.ANY)
    vmem = pl.BlockSpec(memory_space=pltpu.VMEM)
    dma = pltpu.SemaphoreType.DMA
    f32 = lambda *shape: jax.ShapeDtypeStruct(shape, F32)
    bf = lambda *shape: jax.ShapeDtypeStruct(shape, BF16)
    return pl.pallas_call(
        functools.partial(feed_kernel, n),
        out_shape=(
            f32(seg_len, width),
            bf(seg_len, width),
            f32(seg_len, width),
            bf(2, seg_len, LANES),
            bf(width, width),
            bf(4 * LANES, width),
            bf(2, nhi, 2, 2, rows, LANES),
            f32(SMALL, LANES),
            f32(comp_rows, width),
            f32(2, 2, half_rows, LANES),
            bf(made_rows, width),
            bf(nhi, 2, 2, *comp_shard.shape),
        ),
        in_specs=[any_spec] * 8 + [vmem, any_spec, vmem, any_spec],
        out_specs=(any_spec,) * 7 + (vmem,) * 4 + (any_spec,),
        scratch_shapes=[
            pltpu.VMEM((2, seg_len, width), BF16),
            pltpu.VMEM((2, seg_len, width), BF16),
            pltpu.VMEM((2, seg_len, width), BF16),
            pltpu.VMEM((width, width), BF16),
            pltpu.VMEM((4 * width, LANES), BF16),
            pltpu.VMEM((4 * LANES, width), BF16),
            pltpu.VMEM((seg_len, width), F32),
            pltpu.VMEM((total, width), BF16),
            pltpu.VMEM((width, total), BF16),
            pltpu.VMEM((4, total, LANES), BF16),
            pltpu.VMEM((4, total, LANES), BF16),
            pltpu.VMEM((seg_len, width), F32),
            pltpu.VMEM((seg_len, width), F32),
            pltpu.VMEM((seg_len, width), BF16),
            pltpu.VMEM((2, seg_len, width), BF16),
            pltpu.VMEM((4, nhi, 2, 2, rows, LANES), BF16),
            pltpu.VMEM((2, seg_len, LANES), BF16),
            pltpu.VMEM((2, 256, width), BF16),
            pltpu.VMEM((2, half_rows, LANES), BF16),
            pltpu.VMEM((2, half_rows, LANES), BF16),
            pltpu.VMEM((3 * rows, LANES), F32),
            pltpu.VMEM((comp_rows, LANES), BF16),
            pltpu.VMEM((comp_rows, LANES), BF16),
            pltpu.VMEM((made_rows, LANES), BF16),
            pltpu.VMEM((made_rows, LANES), BF16),
            pltpu.VMEM((made_rows, LANES), BF16),
            dma((2 * n + 1,)),
            dma((9,)),
            dma((5,)),
            dma((2,)),
            dma((6,)),
            dma((6,)),
        ]
        + Scatter.scratch(5, nhi, rows)
        + Gather.semaphores(3, nhi),
        compiler_params=pltpu.CompilerParams(
            vmem_limit_bytes=VMEM_LIMIT, collective_id=2, has_side_effects=True
        ),
        name="feed_forward",
    )(att, segment, seg_other, cotangent, cot_other, out_w, up, down, params, comp, comp_shard, windows)


def norm_back(xhat, rstd, grad):
    a = jnp.mean(grad, axis=-1, keepdims=True)
    b = jnp.mean(grad * xhat, axis=-1, keepdims=True)
    return rstd * (grad - a - xhat * b)


def backward_kernel(
    n,
    past,
    seg_len,
    dout,
    kv,
    q,
    wide,
    near,
    place_keys,
    xhat_hbm,
    query_w,
    key_w,
    value_w,
    table_hbm,
    params,
    segment,
    seg_other,
    residual_hbm,
    small_in,
    own_sum,
    branch,
    up,
    down,
    out,
    result_out,
    segment_out,
    query_out,
    key_out,
    value_out,
    place_out,
    out_out,
    down_out,
    up_out,
    small_out,
    xhat_t,
    table_t,
    residual_grad,
    load_sem,
    up_send,
    up_land,
    flat,
    raw,
    sums,
    place_sum,
    input_grad,
    dkv,
    columns,
    gain_sum,
    shift_sum,
    head_grads,
    context_land,
    context_send,
    branch_land,
    own_rows_sum,
    own_sem,
    seg_rows,
    seg_sem,
    out_keep,
    out_send,
    out_land,
    small_mine,
    small_c,
    small_y,
    small_z,
    small_x,
    pair_send,
    pair_recv,
    small_send,
    small_recv,
    land_c,
    land_y,
    land_z,
    mine,
    mine_sem,
    *sems,
):
    step = pl.program_id(0)
    x = lax.axis_index("head")
    core, low, high, nhi = place(n)
    head = lax.rem(step, 4)
    tile = 256
    context = past + seg_len
    width = flat.shape[0]
    rows = width // n
    half_rows = rows // 2
    scale = 1.0 / math.sqrt(128)
    flip = (
        lax.broadcasted_iota(jnp.int32, (HALF, HALF), 0)
        + lax.broadcasted_iota(jnp.int32, (HALF, HALF), 1)
        == HALF - 1
    ).astype(BF16)

    def pair(src, dst, k):
        return pltpu.make_async_remote_copy(
            src_ref=src,
            dst_ref=dst,
            send_sem=pair_send.at[k],
            recv_sem=pair_recv.at[k],
            device_id={"head": 1 - x},
            device_id_type=MESH,
        )

    context_pair = pair(context_send, context_land, 0)
    branch_pair = pair(branch, branch_land, 1)
    out_pairs = [pair(out_send.at[b], out_land.at[b], 2 + b) for b in range(2)]
    load_own = pltpu.make_async_copy(own_sum, own_rows_sum, own_sem)
    up_pairs = [pair(up_send.at[f], up_land.at[f], 4 + f) for f in range(2)]
    load_xhat = [
        pltpu.make_async_copy(xhat_hbm.at[1 - i], xhat_t, load_sem.at[0]) for i in range(2)
    ]
    load_table = pltpu.make_async_copy(table_hbm, table_t, load_sem.at[1])
    load_residual = pltpu.make_async_copy(residual_hbm, residual_grad, load_sem.at[2])
    load_other = pltpu.make_async_copy(seg_other, seg_rows, seg_sem)
    load_segment = pltpu.make_async_copy(segment.at[0], seg_rows, seg_sem)

    def down_done(a, b):
        def done(total):
            down_out[a * rows : (a + 1) * rows, b * LANES : (b + 1) * LANES] = total

        return done

    def out_done(b):
        def done(total):
            upper, lower = total[0:half_rows], total[half_rows:]
            out_keep[b] = jnp.where(x == 0, upper, lower)
            out_send[b] = jnp.where(x == 0, lower, upper).astype(BF16)
            out_pairs[b].start()

        return done

    def head_done(h):
        def done(total):
            for j, ref in enumerate((query_out, key_out, value_out, place_out)):
                ref[:, h * 128 : (h + 1) * 128] = total[:, j * 128 : (j + 1) * 128]

        return done

    parts = [(up.at[f], False, up_block(f, x, up_out, up_send, up_pairs[f])) for f in range(2)]
    for a in range(2):
        for b in range(2):
            at, to = pl.ds(a * rows, rows), pl.ds(b * LANES, LANES)
            parts.append((down.at[:, :, :, at, to], False, down_done(a, b)))
    parts += [
        (out.at[:, :, :, :, pl.ds(b * LANES, LANES)], False, out_done(b)) for b in range(2)
    ]
    parts += [(head_grads.at[h], True, head_done(h)) for h in range(4)]
    scatter = Scatter(
        n,
        [
            (part, here, land_c.at[c], land_y.at[c], land_z.at[c], done)
            for c, (part, here, done) in enumerate(parts)
        ],
        mine,
        mine_sem,
        sems,
    )
    count = len(parts)

    @pl.when(step == 0)
    def _():
        barrier = pltpu.get_barrier_semaphore()
        pl.semaphore_signal(barrier, inc=1, device_id={"head": 1 - x}, device_id_type=MESH)
        meet(core, low, high, nhi, 1)
        load_xhat[0].start()
        load_other.start()
        load_own.start()
        load_table.start()
        load_residual.start()
        branch_pair.start()
        for j in range(2):
            line = jnp.concatenate([params[2 * j : 2 * j + 1, :], params[2 * j + 1 : 2 * j + 2, :]], axis=1)
            columns[j] = jnp.broadcast_to(line, (128, width)).T
        raw[...] = jnp.zeros_like(raw)
        sums[...] = jnp.zeros_like(sums)
        place_sum[...] = jnp.zeros_like(place_sum)
        gain_sum[...] = jnp.zeros_like(gain_sum)
        shift_sum[...] = jnp.zeros_like(shift_sum)
        small_mine[...] = small_in[...]

    @pl.when(head == 0)
    def _():
        input_grad[...] = jnp.zeros_like(input_grad)

    start, add_core, add_y, add_z = scatter.start, scatter.add_core, scatter.add_y, scatter.add_z
    before = {
        0: ((start, 0), (start, 1), (add_core, 0), (start, 2)),
        1: ((add_core, 1), (start, 3), (add_y, 0)),
        2: ((add_core, 3), (start, 5), (add_y, 1), (add_z, 0)),
        3: ((add_core, 5), (start, 7), (add_z, 1)),
        4: ((add_core, 7), (add_y, 4)),
        5: ((start, 8), (add_y, 5)),
        6: ((start, 9), (add_z, 5)),
        7: ((start, 10), (add_z, 6)),
    }
    within = {
        1: ((add_core, 2), (start, 4)),
        2: ((add_core, 4), (start, 6), (add_y, 2)),
        3: ((add_core, 6), (add_y, 3), (add_z, 2)),
        4: ((add_z, 3),),
        5: ((add_core, 8), (add_y, 6), (add_z, 4)),
        6: ((add_core, 9), (add_y, 7)),
        7: ((add_core, 10), (add_y, 8), (add_z, 7)),
    }

    def run(table):
        for k, steps in table.items():

            @pl.when(step == k)
            def _(steps=steps):
                for do, c in steps:
                    do(c)

    run(before)

    for j, mat in enumerate((query_w, key_w, value_w)):
        flat[:, j * 128 : (j + 1) * 128] = mat[...]

    query_grads = []
    key_rows = []
    value_rows = []
    place_rows = []
    bias_at = pl.ds(pl.multiple_of(head * 128, 128), 128)
    for part, weights_ref, key_start, key_count, place_start in (
        (0, wide, 0, past + HALF, 0),
        (1, near, past, seg_len, past - HALF),
    ):
        at = slice(part * HALF, (part + 1) * HALF)
        keys_at = slice(key_start, key_start + key_count)
        attn = weights_ref[0, 0]
        grad = dot(flip, dout[0, at]).astype(BF16)
        value_rows.append(dot_tn(grad, attn))
        weights_grad = dot_nt(grad, kv[0, 0, keys_at, 128:256])
        attn = attn.astype(F32)
        row = jnp.sum(weights_grad * attn, axis=1, keepdims=True)
        scores_f = attn * (weights_grad - row) * scale
        scores_grad = scores_f.astype(BF16)
        content_grad = dot(scores_grad, kv[0, 0, keys_at, 0:128]).astype(BF16)
        key_rows.append(dot_tn(q[0, 0, at, 0:128], scores_grad))
        by_place = pltpu.roll(scores_f, 0, 1, stride=1, stride_axis=0).astype(BF16)
        place_grad = dot(by_place, place_keys[0, place_start : place_start + key_count])
        place_grad = place_grad.astype(BF16)
        place_rows.append(dot_tn(q[0, 0, at, 128:256], by_place))
        content_f = content_grad.astype(F32)
        place_f = place_grad.astype(F32)
        small_mine[8:9, bias_at] += jnp.sum(content_f, axis=0, keepdims=True)
        small_mine[9:10, bias_at] += jnp.sum(place_f, axis=0, keepdims=True)
        query_grads.append(dot(flip, (content_f + place_f).astype(BF16)).astype(BF16))

    for j, (wide_rows, near_rows) in enumerate((key_rows, value_rows)):
        at = slice(j * 128, (j + 1) * 128)
        dkv[at, 0:past] = wide_rows[:, 0:past].astype(BF16)
        dkv[at, past : past + HALF] = (wide_rows[:, past:] + near_rows[:, 0:HALF]).astype(BF16)
        dkv[at, past + HALF :] = near_rows[:, HALF:].astype(BF16)
    split = past - HALF
    for at, rows_grad in (
        (slice(0, split), place_rows[0][:, 0:split]),
        (slice(split, None), place_rows[0][:, split:] + place_rows[1]),
    ):
        place_sum[head, :, at] = (
            place_sum[head, :, at].astype(F32) + rows_grad.astype(BF16).astype(F32)
        ).astype(BF16)
    dq = jnp.concatenate(query_grads, axis=0)
    stacked = jnp.concatenate([dq, dkv[:, past:].astype(F32).T.astype(BF16)], axis=1)

    run(within)

    @pl.when(step == 0)
    def _():
        load_xhat[0].wait()

    @pl.when(step == 4)
    def _():
        load_xhat[1].wait()
        load_table.wait()

    ones = jnp.ones((8, context), BF16)
    sums[head, :, 0:128] += dot(ones[:, 0:seg_len], dq)
    sums[head, :, 128:384] += dot_nt(ones, dkv[...])
    for k in range(width // tile):
        at = slice(k * tile, (k + 1) * tile)
        raw[head, at, 0:128] += dot(xhat_t[at, past:], dq)
        raw[head, at, 128:384] += dot_nt(xhat_t[at, :], dkv[...])
        input_grad[:, at] += dot_nt(stacked, flat[at, 0:384])

    @pl.when(step >= 4)
    def _():
        place_low = place_sum[head]
        block = tile // (4 * rows)
        total = sums[head, 0:1, :]
        for k in range(width // tile):
            at = slice(k * tile, (k + 1) * tile)
            to = slice(k * block, (k + 1) * block)
            got = raw[head, at, :]
            mats = flat[at, 0:384].astype(F32)
            for acc, term in ((gain_sum, mats * got), (shift_sum, mats * total)):
                acc[at, :] += term[:, 0:128] + term[:, 128:256] + term[:, 256:384]
            grad = (columns[0, at, 0:1] * got + columns[1, at, 0:1] * total).astype(BF16)
            head_grads[head, to, :, :, :, 0:384] = grad.reshape(block, 2, 2, rows, 384)
            grad = dot_nt(table_t[at, :], place_low).astype(BF16)
            head_grads[head, to, :, :, :, 384:512] = grad.reshape(block, 2, 2, rows, 128)

    def own_rows(k):
        gain = jnp.concatenate([params[0:1, :], params[1:2, :]], axis=1)
        at = slice(k * tile, (k + 1) * tile)
        values = seg_rows[at, :].astype(F32)
        mean = jnp.mean(values, axis=-1, keepdims=True)
        centred = values - mean
        rstd = lax.rsqrt(jnp.mean(centred * centred, axis=-1, keepdims=True) + 1e-05)
        return norm_back(centred * rstd, rstd, input_grad[at, :] * gain)

    @pl.when(step == 4)
    def _():
        load_segment.start()

    @pl.when(step == 3)
    def _():
        load_xhat[1].start()
        load_other.wait()
        for k in range(seg_len // tile):
            context_send[k * tile : (k + 1) * tile, :] = own_rows(k).astype(BF16)
        context_pair.start()

    @pl.when(step == 5)
    def _():
        branch_pair.wait_recv()
        load_own.wait()
        for k in range(seg_len // tile):
            at = slice(k * tile, (k + 1) * tile)
            result_out[0, at] = (own_rows_sum[at, :] + branch_land[at, :].astype(F32)).astype(BF16)

    @pl.when(step == 7)
    def _():
        start(11)
        one = jnp.ones((8, 128), F32)
        for acc, row in ((gain_sum, 0), (shift_sum, 2)):
            line = lax.dot_general(
                one,
                acc[...],
                (((1,), (1,)), ((), ())),
                precision=lax.Precision.HIGHEST,
                preferred_element_type=F32,
            )
            small_mine[row : row + 1, :] = line[0:1, 0:LANES]
            small_mine[row + 1 : row + 2, :] = line[0:1, LANES:]

        def to_dp(src, dst, k, index):
            return remote(src, dst, small_send.at[k], small_recv.at[k], index)

        copies = [to_dp(small_mine, small_c.at[1], 0, high * 4 + low * 2 + (1 - core))]
        copies[0].start()
        add_core(11)
        add_y(9)
        load_segment.wait()
        load_residual.wait()
        context_pair.wait_recv()
        for k in range(seg_len // tile):
            at = slice(k * tile, (k + 1) * tile)
            segment_out[0, at] = (
                residual_grad[at, :] + own_rows(k) + context_land[at, :].astype(F32)
            ).astype(BF16)
        add_z(8)
        copies[0].wait_recv()
        small_c[0] = small_mine[...] + small_c[1]
        copies.append(to_dp(small_c.at[0], small_y.at[1], 1, high * 4 + (1 - low) * 2 + core))
        copies[1].start()
        copies[1].wait_recv()
        small_y[0] = small_c[0] + small_y[1]
        along = []
        for k in range(1, nhi):
            to = lax.rem(high + k, nhi) * 4 + low * 2 + core
            along.append(to_dp(small_y.at[0], small_z.at[k], 2 + k, to))
        for copy in along:
            copy.start()
        add_y(10)
        for copy in along:
            copy.wait_recv()
        line = small_y[0]
        for k in range(1, nhi):
            line = line + small_z[k]
        small_z[0] = line
        last = pltpu.make_async_remote_copy(
            src_ref=small_z.at[0],
            dst_ref=small_x,
            send_sem=small_send.at[2],
            recv_sem=small_recv.at[2],
            device_id={"head": 1 - x},
            device_id_type=MESH,
        )
        last.start()
        add_z(9)
        add_y(11)
        add_z(10)
        add_z(11)
        for f in range(2):
            up_pairs[f].wait_recv()
            up_out[1 - x, f] = up_land[f].astype(F32)
        for b in range(2):
            out_pairs[b].wait_recv()
            out_out[:, b * LANES : (b + 1) * LANES] = out_keep[b] + out_land[b].astype(F32)
        last.wait_recv()
        line = lax.broadcasted_iota(jnp.int32, (SMALL, LANES), 0)
        small_out[...] = small_z[0] + jnp.where(line < 8, small_x[...], 0.0)
        for copy in [context_pair, branch_pair, *up_pairs, *out_pairs, *copies, *along, last]:
            copy.wait_send()
        for c in range(count):
            scatter.close(c)


def attention_backward(
    n, dout, kv, q, wide, near, place_keys, xhat_t, mats, table_t, params, segment,
    seg_other, residual_grad, small_in, own_sum, branch, up, down, out,
):
    _, seg_len, width = segment.shape
    context = kv.shape[2]
    past = context - seg_len
    rows = width // n
    nhi = n // 4
    half_rows = rows // 2
    seq = lambda t: 1 - t // 4
    head = lambda t: lax.rem(t, 4)
    by_both = lambda t: (head(t), seq(t), 0, 0)
    single = pl.Buffered(1)
    any_spec = pl.BlockSpec(memory_space=pl.ANY)
    dma = pltpu.SemaphoreType.DMA
    f32 = lambda *shape: jax.ShapeDtypeStruct(shape, F32)
    lead = (nhi, 2, 2)
    full = lambda shape: pl.BlockSpec(shape, lambda t: (0,) * len(shape), pipeline_mode=single)
    outs = (
        jax.ShapeDtypeStruct((1, seg_len, width), BF16),
        jax.ShapeDtypeStruct((1, seg_len, width), BF16),
        f32(rows, LANES),
        f32(rows, LANES),
        f32(rows, LANES),
        f32(rows, LANES),
        f32(half_rows, width),
        f32(2 * rows, width),
        f32(2, 2, half_rows, LANES),
        f32(SMALL, LANES),
    )
    return pl.pallas_call(
        functools.partial(backward_kernel, n, past, seg_len),
        grid=(8,),
        out_shape=outs,
        in_specs=[
            pl.BlockSpec((1, seg_len, 128), lambda t: (seq(t), 0, head(t))),
            pl.BlockSpec((1, 1, context, 256), by_both),
            pl.BlockSpec((1, 1, seg_len, 256), by_both),
            pl.BlockSpec((1, 1, HALF, past + HALF), by_both),
            pl.BlockSpec((1, 1, HALF, seg_len), by_both),
            pl.BlockSpec((1, past + HALF, 128), lambda t: (head(t), 0, 0)),
            any_spec,
            *[pl.BlockSpec((width, 128), lambda t: (0, head(t)))] * 3,
            any_spec,
            full((SMALL, LANES)),
            any_spec,
            any_spec,
            any_spec,
            full((SMALL, LANES)),
            any_spec,
            any_spec,
            any_spec,
            any_spec,
            any_spec,
        ],
        out_specs=tuple(full(o.shape) for o in outs),
        scratch_shapes=[
            pltpu.VMEM((width, context), BF16),
            pltpu.VMEM(table_t.shape, BF16),
            pltpu.VMEM((seg_len, width), F32),
            dma((3,)),
            pltpu.VMEM((2, half_rows, LANES), BF16),
            pltpu.VMEM((2, half_rows, LANES), BF16),
            pltpu.VMEM((width, 384), BF16),
            pltpu.VMEM((4, width, 384), F32),
            pltpu.VMEM((4, 8, 384), F32),
            pltpu.VMEM((4, 128, past + HALF), BF16),
            pltpu.VMEM((seg_len, width), F32),
            pltpu.VMEM((256, context), BF16),
            pltpu.VMEM((2, width, 128), F32),
            pltpu.VMEM((width, 128), F32),
            pltpu.VMEM((width, 128), F32),
            pltpu.VMEM((4,) + lead + (rows, LANES), BF16),
            pltpu.VMEM((seg_len, width), BF16),
            pltpu.VMEM((seg_len, width), BF16),
            pltpu.VMEM((seg_len, width), BF16),
            pltpu.VMEM((seg_len, width), F32),
            dma(()),
            pltpu.VMEM((seg_len, width), BF16),
            dma(()),
            pltpu.VMEM((2, half_rows, LANES), F32),
            pltpu.VMEM((2, half_rows, LANES), BF16),
            pltpu.VMEM((2, half_rows, LANES), BF16),
            pltpu.VMEM((SMALL, LANES), F32),
            pltpu.VMEM((2, SMALL, LANES), F32),
            pltpu.VMEM((2, SMALL, LANES), F32),
            pltpu.VMEM((nhi, SMALL, LANES), F32),
            pltpu.VMEM((SMALL, LANES), F32),
            dma((6,)),
            dma((6,)),
            dma((2 + nhi,)),
            dma((2 + nhi,)),
        ]
        + Scatter.scratch(12, nhi, rows),
        compiler_params=pltpu.CompilerParams(
            vmem_limit_bytes=VMEM_LIMIT,
            dimension_semantics=("arbitrary",),
            collective_id=1,
            has_side_effects=True,
        ),
        name="attention_backward",
    )(
        dout, kv, q, wide, near, place_keys, xhat_t, *mats, table_t,
        params, segment, seg_other,
        residual_grad, small_in, own_sum, branch, up, down, out,
    )


def finish_kernel(n, *refs):
    count = (len(refs) - 1) // 2
    ups, refs = refs[:2], refs[1:]
    up_out = refs[count]
    size = LANES // (n // 4)
    for f in range(4):
        for j in range(n // 4):
            for half in range(2):
                to = ((f * (n // 4) + j) * 2 + half) * size
                up_out[:, to : to + size] = ups[f // 2][
                    half, f % 2, :, j * size : (j + 1) * size
                ]
    for src, dst in zip(refs[1:count], refs[count + 1 :]):
        dst[...] = src[...]


def finish(n, ups, others):
    vmem = pl.BlockSpec(memory_space=pltpu.VMEM)
    same = [jax.ShapeDtypeStruct(a.shape, a.dtype) for a in others]
    out = jax.ShapeDtypeStruct((ups[0].shape[2], 8 * LANES), F32)
    return pl.pallas_call(
        functools.partial(finish_kernel, n),
        out_shape=(out, *same),
        in_specs=[vmem] * (2 + len(others)),
        out_specs=(vmem,) * (1 + len(others)),
        compiler_params=pltpu.CompilerParams(vmem_limit_bytes=VMEM_LIMIT),
        name="finish",
    )(*ups, *others)


def body(
    n,
    segment,
    memory,
    compressed,
    doc_lengths,
    memory_valid,
    query_weight,
    key_weight,
    value_weight,
    position_weight,
    content_bias,
    position_bias,
    output_weight,
    up_weight,
    down_weight,
    compress_weight,
    norm_gain,
    norm_shift,
    post_gain,
    post_shift,
    cotangent,
    compress_cotangent,
):
    x = lax.axis_index("head")
    dp = lax.axis_index("dp")
    first = x == 0
    nhi = n // 4
    width = segment.shape[2]
    seg_len = segment.shape[1]
    past = memory.shape[1] + compressed.shape[1]
    context = past + seg_len
    rows = query_weight.shape[0]
    half_rows = output_weight.shape[0]
    new_count = compress_cotangent.shape[1]
    comp_rows = compress_weight.shape[0]

    per = content_bias.shape[1]
    vectors = jnp.stack([norm_gain, norm_shift, post_gain, post_shift])
    here = jnp.arange(2 * n, dtype=jnp.int32)[None, :, None] == dp * 2 + x
    norms = jnp.where(here, vectors[:, None, :], 0).reshape(8, LANES)
    here = jnp.arange(n, dtype=jnp.int32)[None, None, :, None] == dp
    bias = jnp.stack([content_bias, position_bias])[:, :, None, :]
    bias = jnp.where(here, bias, 0).reshape(2, LANES)
    small = jnp.concatenate([norms, bias, jnp.zeros((SMALL - 10, LANES), BF16)])
    pad_rows = -(-new_count // 16) * 16
    comp_cot = jnp.pad(compress_cotangent[0], ((0, pad_rows - new_count), (0, 0)))
    table = position_rows(context, width, past + HALF)

    (
        att, seg_other, cot_other, xhat_t, windows, comp_grads, comp_shard, params, kv, q, wide, near,
        place_keys, query_whole, key_whole, value_whole, _, out_whole, up_whole, down_whole, _,
    ) = attention_forward(
        n, doc_lengths, memory_valid, compressed, memory, segment, cotangent, comp_cot,
        (query_weight, key_weight, value_weight, position_weight),
        output_weight, up_weight, down_weight, compress_weight, small, jnp.asarray(table),
    )

    lead = (nhi, 2, 2)
    (
        own_sum, branch, residual_grad, dout, out_grads, down_grads, up_rest, small_in, comp_done,
        up_first, made, _,
    ) = feed_forward(
        n, att, segment, seg_other, cotangent, cot_other, out_whole.reshape(width, width),
        up_whole.reshape(4 * width, LANES), down_whole.reshape(4 * LANES, width), params,
        comp_grads.reshape(lead + (3 * rows, LANES)), comp_shard, windows.reshape(-1, width),
    )

    mats = [w.reshape(width, LANES) for w in (query_whole, key_whole, value_whole)]
    result, segment_grad, *matrices, up_last, small_done = attention_backward(
        n, dout, kv, q, wide, near, place_keys, xhat_t, mats, jnp.asarray(table.T.copy()),
        params, segment, seg_other, residual_grad, small_in, own_sum, branch,
        up_rest,
        down_grads.reshape(lead + (2 * rows, 2 * LANES)),
        out_grads.reshape(lead + (rows, 2 * LANES)),
    )

    up_final, result, segment_grad, *matrices, comp_final = finish(
        n, (up_first, up_last), (result, segment_grad, *matrices, comp_done)
    )
    query_final, key_final, value_final, place_final, out_final, down_final = matrices
    vectors = lax.dynamic_slice_in_dim(
        small_done[0:8].reshape(4, width), (dp * 2 + x) * half_rows, half_rows, 1
    )
    biases = lax.dynamic_slice_in_dim(small_done[8:10].reshape(2, 4, 128), dp * per, per, 2)
    return (
        result,
        made[None, :new_count],
        segment_grad,
        query_final,
        key_final,
        value_final,
        place_final,
        biases[0],
        biases[1],
        out_final,
        up_final,
        down_final,
        comp_final,
        vectors[0],
        vectors[1],
        vectors[2],
        vectors[3],
    )


def solution(mesh):
    split = P(("dp", "head"))
    wide = P(("dp", "head"), None)
    deep = P(("dp", "head"), None, None)
    return jax.shard_map(
        functools.partial(body, mesh.shape["dp"]),
        mesh=mesh,
        in_specs=(
            deep,
            P("dp", None, None),
            P("dp", None, None),
            P("dp", None),
            P("dp"),
            P("dp", "head"),
            P("dp", "head"),
            P("dp", "head"),
            P("dp", "head"),
            P("head", "dp"),
            P("head", "dp"),
            wide,
            wide,
            wide,
            wide,
            split,
            split,
            split,
            split,
            deep,
            deep,
        ),
        out_specs=(
            deep,
            deep,
            deep,
            P("dp", "head"),
            P("dp", "head"),
            P("dp", "head"),
            P("dp", "head"),
            P("head", "dp"),
            P("head", "dp"),
            wide,
            wide,
            wide,
            wide,
            split,
            split,
            split,
            split,
        ),
        check_vma=False,
    )
```

```python
import functools
import math

import jax
import jax.numpy as jnp
import numpy as np
from jax import lax
from jax.experimental import pallas as pl
from jax.experimental.pallas import tpu as pltpu
from jax.sharding import PartitionSpec as P

F32 = jnp.float32
BF16 = jnp.bfloat16
MESH = pl.DeviceIdType.MESH
VMEM_LIMIT = 62 * 1024 * 1024
HALF = 256
LANES = 512
SMALL = 16


def dot(a, b):
    return lax.dot_general(a, b, (((1,), (0,)), ((), ())), preferred_element_type=F32)


def dot_nt(a, b):
    return lax.dot_general(a, b, (((1,), (1,)), ((), ())), preferred_element_type=F32)


def dot_tn(a, b):
    return lax.dot_general(a, b, (((0,), (0,)), ((), ())), preferred_element_type=F32)


def position_rows(context, width, used):
    distance = np.arange(context, dtype=np.float32)[:, None]
    frequency = np.exp(
        np.arange(width // 2, dtype=np.float32) * np.float32(-2.0 * math.log(10000.0) / width)
    )
    phases = distance * frequency[None, :].astype(np.float32)
    table = np.concatenate([np.sin(phases), np.cos(phases)], axis=1)
    return table[::-1][context - used :].astype(jnp.bfloat16)


def place(n):
    me = lax.axis_index("dp")
    core = lax.rem(me, 2)
    low = lax.rem(me // 2, 2)
    high = me // 4
    return core, low, high, n // 4


def meet(core, low, high, nhi, more=0):
    barrier = pltpu.get_barrier_semaphore()

    def tell(index):
        pl.semaphore_signal(barrier, inc=1, device_id={"dp": index}, device_id_type=MESH)

    for k in range(1, nhi):
        tell(lax.rem(high + k, nhi) * 4 + low * 2 + core)
    tell(high * 4 + (1 - low) * 2 + core)
    tell(high * 4 + low * 2 + (1 - core))
    pl.semaphore_wait(barrier, nhi + 1 + more)


def remote(src, dst, send, recv, index):
    return pltpu.make_async_remote_copy(
        src_ref=src,
        dst_ref=dst,
        send_sem=send,
        recv_sem=recv,
        device_id={"dp": index},
        device_id_type=MESH,
    )


class Gather:
    def __init__(self, n, pairs, sems):
        self.core, self.low, self.high, self.nhi = place(n)
        self.pairs = pairs
        (self.zs, self.zr, self.ys, self.yr, self.cs, self.cr, self.own) = sems
        order = sorted(range(1, self.nhi), key=lambda k: (min(k, self.nhi - k), k))
        self.order = order

    def z_copy(self, c, k):
        shard, whole = self.pairs[c]
        return remote(
            shard,
            whole.at[self.high, self.low, self.core],
            self.zs.at[c, k],
            self.zr.at[c, k],
            lax.rem(self.high + k, self.nhi) * 4 + self.low * 2 + self.core,
        )

    def own_copy(self, c):
        shard, whole = self.pairs[c]
        return pltpu.make_async_copy(
            shard, whole.at[self.high, self.low, self.core], self.own.at[c]
        )

    def y_copy(self, c, k):
        shard, whole = self.pairs[c]
        at = whole.at[lax.rem(self.high + k, self.nhi), self.low, self.core]
        return remote(
            shard if k == 0 else at,
            at,
            self.ys.at[c, k],
            self.yr.at[c, k],
            self.high * 4 + (1 - self.low) * 2 + self.core,
        )

    def c_copy(self, c):
        _, whole = self.pairs[c]
        part = whole.at[:, :, self.core]
        return remote(
            part,
            part,
            self.cs.at[c],
            self.cr.at[c],
            self.high * 4 + self.low * 2 + (1 - self.core),
        )

    def start(self, c):
        for k in self.order:
            self.z_copy(c, k).start()
        self.y_copy(c, 0).start()
        self.own_copy(c).start()

    def pass_y(self, c):
        for k in self.order:
            self.z_copy(c, self.nhi - k).wait_recv()
            self.y_copy(c, k).start()

    def pass_core(self, c):
        self.own_copy(c).wait()
        for k in range(self.nhi):
            self.y_copy(c, k).wait_recv()
        self.c_copy(c).start()

    def arrive(self, c):
        self.c_copy(c).wait_recv()

    def close(self, c):
        for k in self.order:
            self.z_copy(c, k).wait_send()
        for k in range(self.nhi):
            self.y_copy(c, k).wait_send()
        self.c_copy(c).wait_send()

    @staticmethod
    def semaphores(count, nhi):
        dma = pltpu.SemaphoreType.DMA
        return [dma((count, nhi))] * 4 + [dma((count,))] * 3


class Scatter:
    def __init__(self, n, items, mine, mine_sem, sems):
        self.core, self.low, self.high, self.nhi = place(n)
        self.items = items
        self.mine, self.mine_sem = mine, mine_sem
        (self.cs, self.cr, self.ys, self.yr, self.zs, self.zr) = sems

    def c_copy(self, c):
        return remote(
            self.items[c][0].at[:, :, 1 - self.core],
            self.items[c][2],
            self.cs.at[c],
            self.cr.at[c],
            self.high * 4 + self.low * 2 + (1 - self.core),
        )

    def mine_copy(self, c):
        slot = c % 2
        return pltpu.make_async_copy(
            self.items[c][0].at[:, :, self.core], self.mine.at[slot], self.mine_sem.at[slot]
        )

    def y_copy(self, c):
        return remote(
            self.items[c][2].at[:, 1 - self.low],
            self.items[c][3],
            self.ys.at[c],
            self.yr.at[c],
            self.high * 4 + (1 - self.low) * 2 + self.core,
        )

    def z_copies(self, c):
        return [
            remote(
                self.items[c][3].at[lax.rem(self.high + k, self.nhi)],
                self.items[c][4].at[k - 1],
                self.zs.at[c, k - 1],
                self.zr.at[c, k - 1],
                lax.rem(self.high + k, self.nhi) * 4 + self.low * 2 + self.core,
            )
            for k in range(1, self.nhi)
        ]

    def start(self, c):
        self.c_copy(c).start()
        if not self.items[c][1]:
            self.mine_copy(c).start()

    def add_core(self, c):
        here = self.items[c][1]
        if not here:
            self.mine_copy(c).wait()
        self.c_copy(c).wait_recv()
        land = self.items[c][2]

        def body(i, carry):
            for j in range(2):
                own = self.items[c][0][i, j, self.core] if here else self.mine[c % 2, i, j]
                land[i, j] = land[i, j] + own
            return carry

        lax.fori_loop(0, self.nhi, body, 0)
        self.y_copy(c).start()

    def add_y(self, c, go_on=True):
        self.y_copy(c).wait_recv()
        src, land = self.items[c][2], self.items[c][3]

        def body(i, carry):
            land[i] = land[i] + src[i, self.low]
            return carry

        lax.fori_loop(0, self.nhi, body, 0)
        if go_on:
            self.start_z(c)

    def start_z(self, c):
        for copy in self.z_copies(c):
            copy.start()

    def add_z(self, c):
        for copy in self.z_copies(c):
            copy.wait_recv()
        land, last, done = self.items[c][3:]
        total = land[self.high].astype(F32)
        for k in range(self.nhi - 1):
            total = total + last[k].astype(F32)
        done(total)

    def close(self, c, upper=True, last=True):
        if upper:
            self.c_copy(c).wait_send()
            self.y_copy(c).wait_send()
        if last:
            for copy in self.z_copies(c):
                copy.wait_send()

    @staticmethod
    def scratch(count, nhi, rows):
        dma = pltpu.SemaphoreType.DMA
        return [
            pltpu.VMEM((count, nhi, 2, rows, LANES), BF16),
            pltpu.VMEM((count, nhi, rows, LANES), BF16),
            pltpu.VMEM((count, nhi - 1, rows, LANES), BF16),
            pltpu.VMEM((2, nhi, 2, rows, LANES), BF16),
            dma((2,)),
            dma((count,)),
            dma((count,)),
            dma((count,)),
            dma((count,)),
            dma((count, nhi - 1)),
            dma((count, nhi - 1)),
        ]


def norm_rows(values):
    mean = jnp.mean(values, axis=-1, keepdims=True)
    centred = values - mean
    variance = jnp.mean(centred * centred, axis=-1, keepdims=True)
    return centred * lax.rsqrt(variance + 1e-05)


def attend_rows(query_content, query_place, keys, place_keys, first_seen, last_seen, scale):
    width = keys.shape[0]
    content = dot_nt(query_content, keys)
    by_place = pltpu.roll(
        dot_nt(query_place, place_keys), width - (HALF - 1), 1, stride=1, stride_axis=0
    )
    column = lax.broadcasted_iota(jnp.int32, (HALF, width), 1)
    seen = (column >= first_seen) & (column <= last_seen)
    scores = jnp.where(seen, (content + by_place) * (scale * math.log2(math.e)), -1e30)
    top = jnp.max(scores, axis=1, keepdims=True)
    expo = jnp.exp2(scores - top)
    return expo * (1.0 / jnp.sum(expo, axis=1, keepdims=True))


def forward_kernel(
    n,
    past,
    seg_len,
    docs,
    valid,
    compressed,
    memory,
    segment,
    cotangent,
    comp_cot,
    query_w,
    key_w,
    value_w,
    place_w,
    out_w,
    up_w,
    down_w,
    comp_w,
    small,
    table,
    attended,
    seg_other,
    cot_other,
    xhat_hbm,
    windows_hbm,
    comp_grads_hbm,
    comp_shard_hbm,
    params,
    kv_out,
    q_out,
    wide_out,
    near_out,
    place_out,
    query_whole,
    key_whole,
    value_whole,
    place_whole,
    out_whole,
    up_whole,
    down_whole,
    small_whole,
    out_shard,
    up_parts,
    up_shard,
    comp_shard,
    small_shard,
    normed,
    xhat_out,
    memory_f,
    windows,
    comp_rows_cot,
    comp_grads,
    past_rows,
    seg_rows,
    flat,
    small_rows,
    att,
    load_sem,
    flat_sem,
    own_sem,
    store_sem,
    pair_send,
    pair_recv,
    att_own,
    att_send,
    att_recv,
    *sems,
):
    step = pl.program_id(0)
    x = lax.axis_index("head")
    core, low, high, nhi = place(n)
    tile = 256
    width = normed.shape[2]
    context = past + seg_len
    head = jnp.maximum(step - 2, 0) // 2
    half = comp_w.shape[1] // 2

    items = [(small_shard, small_whole)]
    items += [(query_w, query_whole), (key_w, key_whole), (value_w, value_whole), (place_w, place_whole)]
    for b in range(2):
        to = pl.ds(b * LANES, LANES)
        items.append((out_shard.at[:, :, to], out_whole.at[:, :, :, :, :, to]))
    items += [(up_shard.at[f], up_whole.at[f]) for f in range(4)]
    mid = down_w.shape[0] // 2
    for part in range(2):
        for b in range(2):
            at, to = pl.ds(part * mid, mid), pl.ds(b * LANES, LANES)
            items.append((down_w.at[at, to], down_whole.at[:, :, :, at, to]))
    gather = Gather(n, items, sems)
    count = len(items)
    needs = {5: 1, 7: 2}
    pad_rows = comp_cot.shape[0]

    def pair(src, dst, k):
        return pltpu.make_async_remote_copy(
            src_ref=src,
            dst_ref=dst,
            send_sem=pair_send.at[k],
            recv_sem=pair_recv.at[k],
            device_id={"head": 1 - x},
            device_id_type=MESH,
        )

    mine_at = pl.ds(pl.multiple_of(x * half, half), half)
    other_at = pl.ds(pl.multiple_of((1 - x) * half, half), half)
    pairs = [
        pair(small, small_shard.at[x], 0),
        pair(out_w, out_shard.at[x], 1),
        pair(up_parts.at[1 - x], up_shard.at[:, x], 2),
        pair(comp_w.at[:, other_at], comp_shard.at[x], 3),
        pair(segment.at[0], seg_other, 4),
        pair(cotangent.at[0], cot_other, 5),
        pair(comp_cot.at[:, other_at], comp_rows_cot.at[1], 6),
    ]
    owns = [
        pltpu.make_async_copy(small, small_shard.at[x], own_sem.at[0]),
        pltpu.make_async_copy(out_w, out_shard.at[x], own_sem.at[1]),
        pltpu.make_async_copy(up_parts.at[x], up_shard.at[:, x], own_sem.at[2]),
        pltpu.make_async_copy(comp_w.at[:, mine_at], comp_shard.at[x], own_sem.at[3]),
        pltpu.make_async_copy(comp_cot.at[:, mine_at], comp_rows_cot.at[0], own_sem.at[4]),
    ]
    loads = []
    for i in range(2):
        s = lax.rem(x + i, 2)
        loads.append(pltpu.make_async_copy(compressed.at[s], past_rows.at[i, 0], load_sem.at[i, 0]))
        loads.append(pltpu.make_async_copy(memory.at[s], past_rows.at[i, 1], load_sem.at[i, 1]))
    loads.append(pltpu.make_async_copy(segment.at[0], seg_rows.at[0], load_sem.at[0, 2]))
    load_other = pltpu.make_async_copy(seg_other, seg_rows.at[1], load_sem.at[1, 2])
    store_xhat = pltpu.make_async_copy(xhat_out, xhat_hbm, store_sem.at[0])
    store_windows = pltpu.make_async_copy(windows, windows_hbm, store_sem.at[1])
    store_grads = pltpu.make_async_copy(comp_grads, comp_grads_hbm, store_sem.at[2])
    store_shard = pltpu.make_async_copy(comp_shard, comp_shard_hbm, store_sem.at[3])

    joined = set()

    def join(k):
        if k not in joined:
            joined.add(k)
            owns[k].wait()
            pairs[k].wait_recv()

    def tick(t):
        lead = t + 3
        if lead < count:
            if lead in needs:
                join(needs[lead])
            gather.start(lead)
        if t < count:
            gather.pass_y(t)
        if 0 <= t - 1 < count:
            gather.pass_core(t - 1)
        if 0 <= t - 2 < count and t != 6:
            gather.arrive(t - 2)

    def flat_copies(h, slot):
        at = pl.ds(h * 128, 128)
        return [
            pltpu.make_async_copy(
                whole.at[:, :, :, :, at],
                flat.at[slot, :, :, :, :, pl.ds(j * 128, 128)],
                flat_sem.at[slot, j],
            )
            for j, whole in enumerate((query_whole, key_whole, value_whole, place_whole))
        ]

    def norm_into(i, values, at):
        eye = (
            lax.broadcasted_iota(jnp.int32, (tile, tile), 0)
            == lax.broadcasted_iota(jnp.int32, (tile, tile), 1)
        ).astype(BF16)
        gain = jnp.concatenate([params[0:1, :], params[1:2, :]], axis=1)
        shift = jnp.concatenate([params[2:3, :], params[3:4, :]], axis=1)
        xhat = norm_rows(values.astype(F32))
        normed[i, pl.ds(at, tile)] = (xhat * gain + shift).astype(BF16)
        xhat = xhat.astype(BF16)
        for b in range(width // tile):
            xhat_out[i, b * tile : (b + 1) * tile, pl.ds(at, tile)] = dot_nt(
                eye, xhat[:, b * tile : (b + 1) * tile]
            ).astype(BF16)

    def norm_past(i):
        per = past // 2 // tile

        def one(k, carry):
            at = pl.multiple_of(k * tile, tile)
            inner = pl.multiple_of(lax.rem(k, per) * tile, tile)
            norm_into(i, past_rows[i, k // per, pl.ds(inner, tile)], at)
            return carry

        lax.fori_loop(0, past // tile, one, 0)

    def norm_segment(i):
        def one(k, carry):
            at = pl.multiple_of(k * tile, tile)
            norm_into(i, seg_rows[i, pl.ds(at, tile)], past + at)
            return carry

        lax.fori_loop(0, seg_len // tile, one, 0)

    @pl.when(step == 0)
    def _():
        barrier = pltpu.get_barrier_semaphore()
        pl.semaphore_signal(
            barrier, inc=1, device_id={"head": 1 - x}, device_id_type=MESH
        )
        meet(core, low, high, nhi, 1)
        for k in (0, 1):
            pairs[k].start()
            owns[k].start()
        gather.start(1)
        size = LANES // (n // 4)
        for half_at in range(2):
            for f in range(4):
                for j in range(n // 4):
                    at = ((f * (n // 4) + j) * 2 + half_at) * size
                    up_parts[half_at, f, :, j * size : (j + 1) * size] = up_w[:, at : at + size]
        for k in (2, 6, 3, 4, 5):
            pairs[k].start()
        for copy in owns[2:]:
            copy.start()
        for copy in loads:
            copy.start()
        join(0)
        gather.start(0)
        gather.start(2)
        tick(0)
        tick(1)
        tick(2)
        summed = pltpu.make_async_copy(small_whole, small_rows, load_sem.at[0, 3])
        summed.start()
        summed.wait()
        both = jnp.sum(small_rows[...].reshape(n, 2, SMALL, LANES).astype(F32), axis=0)
        row = lax.broadcasted_iota(jnp.int32, (SMALL, LANES), 0)
        by_head = jnp.where(x == 0, both[0], both[1])
        params[...] = jnp.where(row < 8, both[0] + both[1], by_head)
        for copy in (loads[0], loads[1], loads[4]):
            copy.wait()
        norm_past(0)
        tick(3)
        norm_segment(0)

    @pl.when(step == 1)
    def _():
        for copy in loads[2:4]:
            copy.wait()
        norm_past(1)
        tick(4)
        tick(5)
        gather.arrive(4)
        for copy in flat_copies(0, 0):
            copy.start()

    for k in range(2, 10):

        @pl.when(step == k)
        def _(k=k):
            h, slot = (k - 2) // 2, ((k - 2) // 2) % 2
            if k % 2 == 0:
                for copy in flat_copies(h, slot):
                    copy.wait()
                if h < 3:
                    for copy in flat_copies(h + 1, 1 - slot):
                        copy.start()
            if k == 3:
                pairs[4].wait_recv()
                load_other.start()
                load_other.wait()
                norm_segment(1)
                store_xhat.start()
                join(3)
                store_shard.start()

    def att_pair(h, i):
        at = pl.ds(pl.multiple_of(x * LANES + h * 128, 128), 128)
        return pltpu.make_async_remote_copy(
            src_ref=att.at[h, i],
            dst_ref=attended.at[1 - i, :, at],
            send_sem=att_send.at[h, i],
            recv_sem=att_recv.at[h, i],
            device_id={"head": 1 - x},
            device_id_type=MESH,
        )

    def att_local(h, i):
        at = pl.ds(pl.multiple_of(x * LANES + h * 128, 128), 128)
        return pltpu.make_async_copy(att.at[h, i], attended.at[i, :, at], att_own.at[h, i])

    @pl.when(step >= 2)
    def _():
        i = lax.rem(step, 2)
        s = lax.rem(x + i, 2)
        slot = lax.rem(head, 2)

        def weights(a, b):
            return flat[slot, :, :, :, :, a:b].reshape(width, b - a)

        @pl.when(i == 0)
        def _():
            mat = weights(384, 512)
            for k in range(table.shape[0] // tile):
                place_out[0, k * tile : (k + 1) * tile] = dot(
                    table[k * tile : (k + 1) * tile], mat
                ).astype(BF16)

        mat = weights(128, 384)
        for k in range(context // tile):
            kv_out[0, 0, k * tile : (k + 1) * tile] = dot(
                normed[i, pl.ds(k * tile, tile)], mat
            ).astype(BF16)
        mat = weights(0, 128)
        bias_at = pl.ds(pl.multiple_of(head * 128, 128), 128)
        for k in range(seg_len // tile):
            queries = dot(normed[i, pl.ds(past + k * tile, tile)], mat)
            at = slice(k * tile, (k + 1) * tile)
            q_out[0, 0, at, 0:128] = (queries + params[8:9, bias_at]).astype(BF16)
            q_out[0, 0, at, 128:256] = (queries + params[9:10, bias_at]).astype(BF16)

        flip = (
            lax.broadcasted_iota(jnp.int32, (HALF, HALF), 0)
            + lax.broadcasted_iota(jnp.int32, (HALF, HALF), 1)
            == HALF - 1
        ).astype(BF16)
        scale = 1.0 / math.sqrt(128)
        for part, out, key_start, key_count, place_start in (
            (0, wide_out, 0, past + HALF, 0),
            (1, near_out, past, seg_len, past - HALF),
        ):
            token = lax.broadcasted_iota(jnp.int32, (HALF, 1), 0) + part * HALF
            end, first = 0, past - valid[s]
            for doc in range(3):
                end = end + docs[s, doc]
                first = jnp.where(token >= end, past + end, first)
            at = slice(part * HALF, (part + 1) * HALF)
            weights_low = attend_rows(
                q_out[0, 0, at, 0:128],
                q_out[0, 0, at, 128:256],
                kv_out[0, 0, key_start : key_start + key_count, 0:128],
                place_out[0, place_start : place_start + key_count],
                first - key_start,
                token + (past - key_start),
                scale,
            ).astype(BF16)
            out[0, 0] = dot(flip, weights_low).astype(BF16)
            q_out[0, 0, at] = dot(flip, q_out[0, 0, at]).astype(BF16)
            att[head, i, at] = dot(
                weights_low, kv_out[0, 0, key_start : key_start + key_count, 128:256]
            ).astype(BF16)
        att_pair(head, i).start()
        att_local(head, i).start()

    for k in range(2, 10):
        pl.when(step == k)(functools.partial(tick, k + 4))

    @pl.when(step == pl.num_programs(0) - 1)
    def _():
        memory_f[:, past // 2 :, :] = jnp.zeros((width // 128, 16, 128), F32)
        for i in range(2):
            for b in range(width // 128):
                at = slice(b * 128, (b + 1) * 128)
                memory_f[b, 0 : past // 2, :] = past_rows[i, 1, :, at].astype(F32)
                for tap in range(3):
                    windows[tap, i * pad_rows : (i + 1) * pad_rows, at] = memory_f[
                        b, pl.ds(tap, pad_rows, stride=3), :
                    ].astype(BF16)
        store_windows.start()
        owns[4].wait()
        pairs[6].wait_recv()
        tick(14)
        comp_rows_both = comp_rows_cot[...].reshape(2 * pad_rows, LANES)
        for tap in range(3):
            for k in range(width // tile):
                at = slice(k * tile, (k + 1) * tile)
                comp_grads[tap * width + k * tile : tap * width + (k + 1) * tile, :] = dot_tn(
                    windows[tap, :, at], comp_rows_both
                ).astype(BF16)
        store_grads.start()
        for t in range(15, count + 2):
            tick(t)
        for copy in (store_xhat, store_windows, store_grads, store_shard):
            copy.wait()
        for h in range(4):
            for i in range(2):
                att_local(h, i).wait()
                att_pair(h, i).wait()
        for copy in pairs:
            copy.wait_send()
        pairs[5].wait_recv()
        for c in range(count):
            gather.close(c)


def attention_forward(
    n, docs, valid, compressed, memory, segment, cotangent, comp_cot, mats, out_w, up_w, down_w,
    comp_w, small, table,
):
    _, seg_len, width = segment.shape
    past = compressed.shape[1] + memory.shape[1]
    context = past + seg_len
    nhi = n // 4
    lead = (nhi, 2, 2)
    half_rows = out_w.shape[0]
    comp_rows = comp_w.shape[0]
    pad_rows = comp_cot.shape[0]
    any_spec = pl.BlockSpec(memory_space=pl.ANY)
    smem = pl.BlockSpec(memory_space=pltpu.SMEM)
    single = pl.Buffered(1)
    bf = lambda *shape: jax.ShapeDtypeStruct(shape, BF16)
    head = lambda t: jnp.maximum(t - 2, 0) // 2
    which = lambda t: lax.rem(jnp.maximum(t, 2), 2)
    by_both = lambda t: (head(t), which(t), 0, 0)
    dma = pltpu.SemaphoreType.DMA
    full = lambda shape: pl.BlockSpec(shape, lambda t: (0,) * len(shape), pipeline_mode=single)
    count = 15
    return pl.pallas_call(
        functools.partial(forward_kernel, n, past, seg_len),
        grid=(10,),
        out_shape=(
            bf(2, seg_len, width),
            bf(seg_len, width),
            bf(seg_len, width),
            bf(2, width, context),
            bf(3, 2 * pad_rows, width),
            bf(3 * width, LANES),
            bf(2, comp_rows, LANES),
            jax.ShapeDtypeStruct((SMALL, LANES), F32),
            bf(4, 2, context, 256),
            bf(4, 2, seg_len, 256),
            bf(4, 2, HALF, past + HALF),
            bf(4, 2, HALF, seg_len),
            bf(4, past + HALF, 128),
            *[bf(*lead, *w.shape) for w in mats],
            bf(*lead, 2, half_rows, width),
            bf(4, *lead, 2, half_rows, LANES),
            bf(*lead, *down_w.shape),
            bf(*lead, 2, SMALL, LANES),
        ),
        in_specs=[smem, smem]
        + [any_spec] * 5
        + [full(a.shape) for a in (*mats, out_w, up_w, down_w, comp_w, small)]
        + [pl.BlockSpec(table.shape, lambda t: (0, 0), pipeline_mode=single)],
        out_specs=(
            *[any_spec] * 6,
            any_spec,
            pl.BlockSpec((SMALL, LANES), lambda t: (0, 0)),
            pl.BlockSpec((1, 1, context, 256), by_both),
            pl.BlockSpec((1, 1, seg_len, 256), by_both),
            pl.BlockSpec((1, 1, HALF, past + HALF), by_both),
            pl.BlockSpec((1, 1, HALF, seg_len), by_both),
            pl.BlockSpec((1, past + HALF, 128), lambda t: (head(t), 0, 0)),
            *[any_spec] * 8,
        ),
        scratch_shapes=[
            pltpu.VMEM((2, half_rows, width), BF16),
            pltpu.VMEM((2, 4, half_rows, LANES), BF16),
            pltpu.VMEM((4, 2, half_rows, LANES), BF16),
            pltpu.VMEM((2, comp_rows, LANES), BF16),
            pltpu.VMEM((2, SMALL, LANES), BF16),
            pltpu.VMEM((2, context, width), BF16),
            pltpu.VMEM((2, width, context), BF16),
            pltpu.VMEM((width // 128, past // 2 + 16, 128), F32),
            pltpu.VMEM((3, 2 * pad_rows, width), BF16),
            pltpu.VMEM((2, pad_rows, LANES), BF16),
            pltpu.VMEM((3 * width, LANES), BF16),
            pltpu.VMEM((2, 2, past // 2, width), BF16),
            pltpu.VMEM((2, seg_len, width), BF16),
            pltpu.VMEM((2,) + lead + (mats[0].shape[0], LANES), BF16),
            pltpu.VMEM(lead + (2, SMALL, LANES), BF16),
            pltpu.VMEM((4, 2, seg_len, 128), BF16),
            dma((2, 4)),
            dma((2, 4)),
            dma((6,)),
            dma((4,)),
            dma((7,)),
            dma((7,)),
            dma((4, 2)),
            dma((4, 2)),
            dma((4, 2)),
        ]
        + Gather.semaphores(count, nhi),
        compiler_params=pltpu.CompilerParams(
            vmem_limit_bytes=VMEM_LIMIT,
            dimension_semantics=("arbitrary",),
            collective_id=0,
            has_side_effects=True,
        ),
        name="attention_forward",
    )(
        docs, valid, compressed, memory, segment, cotangent, comp_cot, *mats, out_w, up_w, down_w,
        comp_w, small, table,
    )


def gelu_parts(v):
    c = math.sqrt(2.0 / math.pi)
    square = v * v
    t = jnp.tanh(c * (v + 0.044715 * square * v))
    half = 0.5 * (1.0 + t)
    value = v * half
    return value, half + value * (1.0 - half) * (2 * c + (6 * 0.044715 * c) * square)


def feed_kernel(
    n,
    att_in,
    segment,
    seg_other,
    cotangent,
    cot_other,
    out_in,
    up_in,
    down_in,
    params,
    comp,
    comp_shard,
    windows,
    own_out,
    branch_out,
    residual_out,
    dout,
    out_grads,
    down_grads,
    up_rest,
    small_out,
    comp_out,
    up_out,
    made_out,
    comp_whole,
    att,
    seg,
    cot,
    out_w,
    up,
    down,
    residual,
    low,
    low_t,
    act,
    pre,
    branch,
    terms,
    terms_land,
    cast,
    up_grads,
    mixed,
    stage,
    up_send,
    up_land,
    comp_stage,
    comp_send,
    comp_land,
    made_own,
    made_send,
    made_land,
    made_sem,
    load_sem,
    store_sem,
    stage_sem,
    pair_send,
    pair_recv,
    land_c,
    land_y,
    land_z,
    mine,
    mine_sem,
    *sems,
):
    sems, gather_sems = sems[:6], sems[6:]
    x = lax.axis_index("head")
    core, low_y, high, nhi = place(n)
    tile = 256
    _, seg_len, width = att.shape
    rows = width // n
    half_rows = rows // 2
    comp_rows = comp_send.shape[0]

    def pair(src, dst, k):
        return pltpu.make_async_remote_copy(
            src_ref=src,
            dst_ref=dst,
            send_sem=pair_send.at[k],
            recv_sem=pair_recv.at[k],
            device_id={"head": 1 - x},
            device_id_type=MESH,
        )

    terms_pair = pair(cast.at[0], terms_land, 0)
    mixed_pair = pair(mixed.at[1 - x], dout.at[1], 1)
    comp_pair = pair(comp_send, comp_land, 2)
    up_pairs = [pair(up_send.at[f], up_land.at[f], 3 + f) for f in range(2)]
    made_pair = pair(made_send, made_land, 5)
    scatter = Scatter(
        n,
        [
            (part, here, land_c.at[c], land_y.at[c], land_z.at[c], done)
            for c, (part, here, done) in enumerate(
                [
                    (
                        comp.at[:, :, :, pl.ds(m * rows, rows)],
                        False,
                        comp_block(m, x, rows, comp_stage, comp_out, comp_send, comp_pair),
                    )
                    for m in range(3)
                ]
                + [
                    (up_grads.at[f], True, up_block(f, x, up_out, up_send, up_pairs[f]))
                    for f in range(2)
                ]
                + [(up_grads.at[f], True, None) for f in range(2, 4)]
            )
        ],
        mine,
        mine_sem,
        sems,
    )

    third = comp_rows // 3
    gather = Gather(
        n,
        [
            (
                comp_shard.at[:, pl.ds(m * third, third)],
                comp_whole.at[:, :, :, :, pl.ds(m * third, third)],
            )
            for m in range(3)
        ],
        gather_sems,
    )

    def load(src, dst, k):
        return pltpu.make_async_copy(src, dst, load_sem.at[k])

    loads = {
        "att1": load(att_in.at[1], att.at[1], 0),
        "out": load(out_in, out_w, 1),
        "seg1": load(seg_other, seg.at[1], 2),
        "cot1": load(cot_other, cot.at[1], 3),
        "up": load(up_in, up, 4),
        "down": load(down_in, down, 5),
        "att0": load(att_in.at[0], att.at[0], 6),
        "seg0": load(segment.at[0], seg.at[0], 7),
        "cot0": load(cotangent.at[0], cot.at[0], 8),
    }
    for copy in loads.values():
        copy.start()
    barrier = pltpu.get_barrier_semaphore()
    pl.semaphore_signal(barrier, inc=1, device_id={"head": 1 - x}, device_id_type=MESH)
    meet(core, low_y, high, nhi, 1)
    scatter.start(0)
    scatter.start(1)
    gather.start(0)

    eye = (
        lax.broadcasted_iota(jnp.int32, (tile, tile), 0)
        == lax.broadcasted_iota(jnp.int32, (tile, tile), 1)
    ).astype(BF16)
    gain = jnp.concatenate([params[4:5, :], params[5:6, :]], axis=1)
    shift = jnp.concatenate([params[6:7, :], params[7:8, :]], axis=1)

    def project(i):
        for k in range(seg_len // tile):
            at = slice(k * tile, (k + 1) * tile)
            whole_at = slice(i * seg_len + k * tile, i * seg_len + (k + 1) * tile)
            value = seg[i, at].astype(F32) + dot(att[i, at], out_w[...])
            residual[at, :] = value
            value = (norm_rows(value) * gain + shift).astype(BF16)
            low[whole_at, :] = value
            for b in range(width // tile):
                low_t[b * tile : (b + 1) * tile, whole_at] = dot_nt(
                    eye, value[:, b * tile : (b + 1) * tile]
                ).astype(BF16)

    def hidden(i, between):
        whole_at = slice(i * seg_len, (i + 1) * seg_len)
        branch[...] = jnp.zeros_like(branch)
        terms[...] = jnp.zeros_like(terms)

        def one(f, carry):
            down_at = pl.ds(pl.multiple_of(f * LANES, LANES), LANES)
            up_at = pl.ds(pl.multiple_of(f * width, width), width)
            value, slope = gelu_parts(dot(low[whole_at, :], up[up_at, :]))
            value = value.astype(BF16)
            act[f, whole_at, :] = value
            back = dot_nt(cot[i], down[down_at, :]).astype(BF16).astype(F32)
            back = (back * slope).astype(BF16)
            pre[f, whole_at, :] = back
            branch[...] += dot(value, down[down_at, :])
            terms[...] += dot_nt(back, up[up_at, :])
            for k, steps in enumerate(between):

                @pl.when(f == k)
                def _(steps=steps):
                    for run, c in steps:
                        run(c)

            return carry

        lax.fori_loop(0, 4, one, 0)

    for name in ("att1", "out", "seg1"):
        loads[name].wait()
    project(1)
    scatter.add_core(0)
    scatter.start(2)
    gather.start(1)
    for name in ("cot1", "up", "down"):
        loads[name].wait()
    hidden(
        1,
        (
            ((scatter.add_core, 1), (gather.pass_y, 0)),
            ((scatter.add_core, 2), (scatter.add_y, 0), (gather.start, 2)),
            ((gather.pass_y, 1),),
            ((scatter.add_y, 1),),
        ),
    )
    cast[0] = terms[...].astype(BF16)
    terms_pair.start()
    cast[1] = branch[...].astype(BF16)
    store_branch = pltpu.make_async_copy(cast.at[1], branch_out, store_sem.at[0])
    store_branch.start()
    for name in ("att0", "seg0", "cot0"):
        loads[name].wait()
    project(0)
    scatter.add_z(0)
    hidden(
        0,
        (
            ((gather.pass_core, 0),),
            ((gather.pass_y, 2),),
            ((scatter.add_y, 2),),
            ((scatter.add_z, 1),),
        ),
    )
    branch[...] += residual[...]
    store_own = pltpu.make_async_copy(branch, own_out, store_sem.at[1])
    store_own.start()

    count = windows.shape[0]
    load_windows = pltpu.make_async_copy(windows, down.at[pl.ds(0, count)], made_sem.at[2 * n])
    load_windows.start()

    block = tile // (4 * rows)

    def up_grad(f):
        for k in range(width // tile):
            grad = dot(low_t[k * tile : (k + 1) * tile, :], pre[f]).astype(BF16)
            up_grads[f, k * block : (k + 1) * block] = grad.reshape(block, 2, 2, rows, LANES)
        scatter.start(3 + f)

    up_grad(0)
    gather.pass_core(1)
    up_grad(1)
    scatter.add_core(3)
    scatter.add_z(2)
    up_grad(2)
    scatter.add_core(4)
    up_grad(3)
    scatter.add_core(5)
    store_rest = [
        pltpu.make_async_copy(land_y.at[5 + f], up_rest.at[f], store_sem.at[4 + f]) for f in range(2)
    ]

    terms_pair.wait_recv()
    gain_grad = jnp.zeros((1, width), F32)
    shift_grad = jnp.zeros((1, width), F32)
    terms_pair.wait_send()
    for k in range(seg_len // tile):
        at = slice(k * tile, (k + 1) * tile)
        grad = terms[at, :] + terms_land[at, :].astype(F32)
        value = residual[at, :]
        mean = jnp.mean(value, axis=-1, keepdims=True)
        centred = value - mean
        rstd = lax.rsqrt(jnp.mean(centred * centred, axis=-1, keepdims=True) + 1e-05)
        xhat = centred * rstd
        gain_grad += jnp.sum(grad * xhat, axis=0, keepdims=True)
        shift_grad += jnp.sum(grad, axis=0, keepdims=True)
        grad = cot[0, at].astype(F32) + norm_back(xhat, rstd, grad * gain)
        residual[at, :] = grad
        grad = grad.astype(BF16)
        cast[0, at, :] = grad
        back = dot_nt(grad, out_w[...]).astype(BF16)
        mixed[0, at, :] = back[:, 0:LANES]
        mixed[1, at, :] = back[:, LANES:]
    mixed_pair.start()
    store_dout = pltpu.make_async_copy(mixed.at[x], dout.at[0], store_sem.at[2])
    store_dout.start()
    store_residual = pltpu.make_async_copy(residual, residual_out, store_sem.at[3])
    store_residual.start()
    small_out[...] = jnp.zeros_like(small_out)
    small_out[4:5, :] = gain_grad[:, 0:LANES]
    small_out[5:6, :] = gain_grad[:, LANES:]
    small_out[6:7, :] = shift_grad[:, 0:LANES]
    small_out[7:8, :] = shift_grad[:, LANES:]
    scatter.add_core(6)
    gather.pass_core(2)

    staged = [None, None]
    jobs = [(out_grads, k * tile, None, k) for k in range(width // tile)]
    jobs += [
        (down_grads, f * LANES + k * tile, f, k) for f in range(4) for k in range(LANES // tile)
    ]
    for j, (target, start, f, k) in enumerate(jobs):
        slot = j % 2
        at = slice(k * tile, (k + 1) * tile)
        if f is None:
            grad = dot_tn(att[0, :, at], cast[0])
        else:
            grad = dot_tn(act[f, 0:seg_len, at], cot[0]) + dot_tn(act[f, seg_len:, at], cot[1])
        if staged[slot] is not None:
            staged[slot].wait()
        stage[slot] = grad.astype(BF16)
        staged[slot] = pltpu.make_async_copy(
            stage.at[slot], target.at[pl.ds(start, tile)], stage_sem.at[slot]
        )
        staged[slot].start()
        if j == 3:
            scatter.add_y(3)
        if j == 10:
            scatter.add_y(4)
            scatter.add_z(3)
    scatter.add_y(5, False)
    store_rest[0].start()
    for m in range(3):
        gather.arrive(m)
    load_comp = []
    for b in range(n):
        for half in range(2):
            load_comp.append(
                pltpu.make_async_copy(
                    comp_whole.at[b // 4, (b // 2) % 2, b % 2, half],
                    up.at[pl.ds((2 * b + half) * comp_rows, comp_rows)],
                    made_sem.at[2 * b + half],
                )
            )
            load_comp[-1].start()
    load_windows.wait()
    for copy in load_comp:
        copy.wait()
    made = jnp.zeros((count // 3, LANES), F32)
    for tap in range(3):
        made += dot(
            down[tap * (count // 3) : (tap + 1) * (count // 3), :],
            up[tap * width : (tap + 1) * width, :],
        )
    made_own[...] = made[: count // 6].astype(BF16)
    made_send[...] = made[count // 6 :].astype(BF16)
    made_pair.start()
    scatter.add_z(4)
    scatter.add_y(6, False)
    store_rest[1].start()
    comp_pair.wait_recv()
    to = pl.ds(pl.multiple_of((1 - x) * LANES, LANES), LANES)
    comp_out[:, to] = comp_land[...].astype(F32)
    made_pair.wait_recv()
    made_out[:, to] = made_land[...]
    made_out[:, pl.ds(pl.multiple_of(x * LANES, LANES), LANES)] = made_own[...]
    for f in range(2):
        up_pairs[f].wait_recv()
        up_out[1 - x, f] = up_land[f].astype(F32)
    mixed_pair.wait_recv()
    for copy in [mixed_pair, comp_pair, made_pair, *up_pairs]:
        copy.wait_send()
    for copy in [*staged, store_branch, store_own, store_dout, store_residual, *store_rest]:
        copy.wait()
    for c in range(7):
        scatter.close(c, last=c < 5)
    for m in range(3):
        gather.close(m)


def comp_block(m, x, rows, stage, out, send, pair):
    def done(total):
        stage[m * rows : (m + 1) * rows, :] = total
        if m == 2:
            half = send.shape[0]
            upper, lower = stage[0:half, :], stage[half:, :]
            to = pl.ds(pl.multiple_of(x * LANES, LANES), LANES)
            out[:, to] = jnp.where(x == 0, upper, lower)
            send[...] = jnp.where(x == 0, lower, upper).astype(BF16)
            pair.start()

    return done


def up_block(f, x, out, send, pair):
    def done(total):
        half = send.shape[1]
        upper, lower = total[0:half], total[half:]
        out[x, f] = jnp.where(x == 0, upper, lower)
        send[f] = jnp.where(x == 0, lower, upper).astype(BF16)
        pair.start()

    return done


def feed_forward(
    n, att, segment, seg_other, cotangent, cot_other, out_w, up, down, params, comp, comp_shard, windows
):
    _, seg_len, width = att.shape
    rows = width // n
    half_rows = rows // 2
    nhi = n // 4
    comp_rows = comp.shape[3] // 2
    made_rows = windows.shape[0] // 6
    total = 2 * seg_len
    any_spec = pl.BlockSpec(memory_space=pl.ANY)
    vmem = pl.BlockSpec(memory_space=pltpu.VMEM)
    dma = pltpu.SemaphoreType.DMA
    f32 = lambda *shape: jax.ShapeDtypeStruct(shape, F32)
    bf = lambda *shape: jax.ShapeDtypeStruct(shape, BF16)
    return pl.pallas_call(
        functools.partial(feed_kernel, n),
        out_shape=(
            f32(seg_len, width),
            bf(seg_len, width),
            f32(seg_len, width),
            bf(2, seg_len, LANES),
            bf(width, width),
            bf(4 * LANES, width),
            bf(2, nhi, rows, LANES),
            f32(SMALL, LANES),
            f32(comp_rows, width),
            f32(2, 2, half_rows, LANES),
            bf(made_rows, width),
            bf(nhi, 2, 2, *comp_shard.shape),
        ),
        in_specs=[any_spec] * 8 + [vmem, any_spec, vmem, any_spec],
        out_specs=(any_spec,) * 7 + (vmem,) * 4 + (any_spec,),
        scratch_shapes=[
            pltpu.VMEM((2, seg_len, width), BF16),
            pltpu.VMEM((2, seg_len, width), BF16),
            pltpu.VMEM((2, seg_len, width), BF16),
            pltpu.VMEM((width, width), BF16),
            pltpu.VMEM((4 * width, LANES), BF16),
            pltpu.VMEM((4 * LANES, width), BF16),
            pltpu.VMEM((seg_len, width), F32),
            pltpu.VMEM((total, width), BF16),
            pltpu.VMEM((width, total), BF16),
            pltpu.VMEM((4, total, LANES), BF16),
            pltpu.VMEM((4, total, LANES), BF16),
            pltpu.VMEM((seg_len, width), F32),
            pltpu.VMEM((seg_len, width), F32),
            pltpu.VMEM((seg_len, width), BF16),
            pltpu.VMEM((2, seg_len, width), BF16),
            pltpu.VMEM((4, nhi, 2, 2, rows, LANES), BF16),
            pltpu.VMEM((2, seg_len, LANES), BF16),
            pltpu.VMEM((2, 256, width), BF16),
            pltpu.VMEM((2, half_rows, LANES), BF16),
            pltpu.VMEM((2, half_rows, LANES), BF16),
            pltpu.VMEM((3 * rows, LANES), F32),
            pltpu.VMEM((comp_rows, LANES), BF16),
            pltpu.VMEM((comp_rows, LANES), BF16),
            pltpu.VMEM((made_rows, LANES), BF16),
            pltpu.VMEM((made_rows, LANES), BF16),
            pltpu.VMEM((made_rows, LANES), BF16),
            dma((2 * n + 1,)),
            dma((9,)),
            dma((6,)),
            dma((2,)),
            dma((6,)),
            dma((6,)),
        ]
        + Scatter.scratch(7, nhi, rows)
        + Gather.semaphores(3, nhi),
        compiler_params=pltpu.CompilerParams(
            vmem_limit_bytes=VMEM_LIMIT, collective_id=2, has_side_effects=True
        ),
        name="feed_forward",
    )(att, segment, seg_other, cotangent, cot_other, out_w, up, down, params, comp, comp_shard, windows)


def norm_back(xhat, rstd, grad):
    a = jnp.mean(grad, axis=-1, keepdims=True)
    b = jnp.mean(grad * xhat, axis=-1, keepdims=True)
    return rstd * (grad - a - xhat * b)


def backward_kernel(
    n,
    past,
    seg_len,
    dout,
    kv,
    q,
    wide,
    near,
    place_keys,
    xhat_hbm,
    query_w,
    key_w,
    value_w,
    table_hbm,
    params,
    segment,
    seg_other,
    residual_hbm,
    small_in,
    own_sum,
    branch,
    up,
    down,
    out,
    result_out,
    segment_out,
    query_out,
    key_out,
    value_out,
    place_out,
    out_out,
    down_out,
    up_out,
    small_out,
    xhat_t,
    table_t,
    residual_grad,
    load_sem,
    up_send,
    up_land,
    flat,
    raw,
    sums,
    place_sum,
    input_grad,
    dkv,
    columns,
    gain_sum,
    shift_sum,
    head_grads,
    context_land,
    context_send,
    branch_land,
    own_rows_sum,
    own_sem,
    seg_rows,
    seg_sem,
    out_keep,
    out_send,
    out_land,
    small_mine,
    small_c,
    small_y,
    small_z,
    small_x,
    pair_send,
    pair_recv,
    small_send,
    small_recv,
    land_c,
    land_y,
    land_z,
    mine,
    mine_sem,
    *sems,
):
    step = pl.program_id(0)
    x = lax.axis_index("head")
    core, low, high, nhi = place(n)
    head = lax.rem(step, 4)
    tile = 256
    context = past + seg_len
    width = flat.shape[0]
    rows = width // n
    half_rows = rows // 2
    scale = 1.0 / math.sqrt(128)
    flip = (
        lax.broadcasted_iota(jnp.int32, (HALF, HALF), 0)
        + lax.broadcasted_iota(jnp.int32, (HALF, HALF), 1)
        == HALF - 1
    ).astype(BF16)

    def pair(src, dst, k):
        return pltpu.make_async_remote_copy(
            src_ref=src,
            dst_ref=dst,
            send_sem=pair_send.at[k],
            recv_sem=pair_recv.at[k],
            device_id={"head": 1 - x},
            device_id_type=MESH,
        )

    context_pair = pair(context_send, context_land, 0)
    branch_pair = pair(branch, branch_land, 1)
    out_pairs = [pair(out_send.at[b], out_land.at[b], 2 + b) for b in range(2)]
    load_own = pltpu.make_async_copy(own_sum, own_rows_sum, own_sem)
    up_pairs = [pair(up_send.at[f], up_land.at[f], 4 + f) for f in range(2)]
    load_xhat = [
        pltpu.make_async_copy(xhat_hbm.at[1 - i], xhat_t, load_sem.at[0]) for i in range(2)
    ]
    load_up = [
        pltpu.make_async_copy(up.at[f], land_y.at[f], load_sem.at[3 + f]) for f in range(2)
    ]
    load_table = pltpu.make_async_copy(table_hbm, table_t, load_sem.at[1])
    load_residual = pltpu.make_async_copy(residual_hbm, residual_grad, load_sem.at[2])
    load_other = pltpu.make_async_copy(seg_other, seg_rows, seg_sem)
    load_segment = pltpu.make_async_copy(segment.at[0], seg_rows, seg_sem)

    def down_done(a, b):
        def done(total):
            down_out[a * rows : (a + 1) * rows, b * LANES : (b + 1) * LANES] = total

        return done

    def out_done(b):
        def done(total):
            upper, lower = total[0:half_rows], total[half_rows:]
            out_keep[b] = jnp.where(x == 0, upper, lower)
            out_send[b] = jnp.where(x == 0, lower, upper).astype(BF16)
            out_pairs[b].start()

        return done

    def head_done(h):
        def done(total):
            for j, ref in enumerate((query_out, key_out, value_out, place_out)):
                ref[:, h * 128 : (h + 1) * 128] = total[:, j * 128 : (j + 1) * 128]

        return done

    parts = [(None, False, up_block(f, x, up_out, up_send, up_pairs[f])) for f in range(2)]
    for a in range(2):
        for b in range(2):
            at, to = pl.ds(a * rows, rows), pl.ds(b * LANES, LANES)
            parts.append((down.at[:, :, :, at, to], False, down_done(a, b)))
    parts += [
        (out.at[:, :, :, :, pl.ds(b * LANES, LANES)], False, out_done(b)) for b in range(2)
    ]
    parts += [(head_grads.at[h], True, head_done(h)) for h in range(4)]
    scatter = Scatter(
        n,
        [
            (part, here, land_c.at[c], land_y.at[c], land_z.at[c], done)
            for c, (part, here, done) in enumerate(parts)
        ],
        mine,
        mine_sem,
        sems,
    )
    count = len(parts)

    @pl.when(step == 0)
    def _():
        barrier = pltpu.get_barrier_semaphore()
        pl.semaphore_signal(barrier, inc=1, device_id={"head": 1 - x}, device_id_type=MESH)
        meet(core, low, high, nhi, 1)
        for copy in load_up:
            copy.start()
        load_xhat[0].start()
        load_other.start()
        load_own.start()
        load_table.start()
        load_residual.start()
        branch_pair.start()
        for j in range(2):
            line = jnp.concatenate([params[2 * j : 2 * j + 1, :], params[2 * j + 1 : 2 * j + 2, :]], axis=1)
            columns[j] = jnp.broadcast_to(line, (128, width)).T
        raw[...] = jnp.zeros_like(raw)
        sums[...] = jnp.zeros_like(sums)
        place_sum[...] = jnp.zeros_like(place_sum)
        gain_sum[...] = jnp.zeros_like(gain_sum)
        shift_sum[...] = jnp.zeros_like(shift_sum)
        small_mine[...] = small_in[...]

    @pl.when(head == 0)
    def _():
        input_grad[...] = jnp.zeros_like(input_grad)

    start, add_core, add_y, add_z = scatter.start, scatter.add_core, scatter.add_y, scatter.add_z
    before = {
        0: ((start, 2), (start, 3), (scatter.start_z, 0), (scatter.start_z, 1), (add_core, 2), (start, 4)),
        1: ((add_core, 3), (start, 5), (add_y, 2)),
        2: ((add_core, 5), (start, 7), (add_y, 3), (add_z, 1)),
        3: ((add_core, 7),),
        4: ((add_y, 6),),
        5: ((start, 8), (add_y, 7), (add_z, 5)),
        6: ((start, 9), (add_z, 6)),
        7: ((start, 10),),
    }
    within = {
        1: ((add_core, 4), (start, 6), (add_z, 0)),
        2: ((add_core, 6), (add_y, 4), (add_z, 2)),
        3: ((add_y, 5), (add_z, 3)),
        4: ((add_z, 4),),
        5: ((add_core, 8),),
        6: ((add_core, 9), (add_y, 8), (add_z, 7)),
        7: ((add_core, 10), (add_y, 9), (add_z, 8)),
    }

    def run(table):
        for k, steps in table.items():

            @pl.when(step == k)
            def _(steps=steps):
                for do, c in steps:
                    do(c)

    @pl.when(step == 0)
    def _():
        for copy in load_up:
            copy.wait()

    run(before)

    for j, mat in enumerate((query_w, key_w, value_w)):
        flat[:, j * 128 : (j + 1) * 128] = mat[...]

    query_grads = []
    key_rows = []
    value_rows = []
    place_rows = []
    bias_at = pl.ds(pl.multiple_of(head * 128, 128), 128)
    for part, weights_ref, key_start, key_count, place_start in (
        (0, wide, 0, past + HALF, 0),
        (1, near, past, seg_len, past - HALF),
    ):
        at = slice(part * HALF, (part + 1) * HALF)
        keys_at = slice(key_start, key_start + key_count)
        attn = weights_ref[0, 0]
        grad = dot(flip, dout[0, at]).astype(BF16)
        value_rows.append(dot_tn(grad, attn))
        weights_grad = dot_nt(grad, kv[0, 0, keys_at, 128:256])
        attn = attn.astype(F32)
        row = jnp.sum(weights_grad * attn, axis=1, keepdims=True)
        scores_f = attn * (weights_grad - row) * scale
        scores_grad = scores_f.astype(BF16)
        content_grad = dot(scores_grad, kv[0, 0, keys_at, 0:128]).astype(BF16)
        key_rows.append(dot_tn(q[0, 0, at, 0:128], scores_grad))
        by_place = pltpu.roll(scores_f, 0, 1, stride=1, stride_axis=0).astype(BF16)
        place_grad = dot(by_place, place_keys[0, place_start : place_start + key_count])
        place_grad = place_grad.astype(BF16)
        place_rows.append(dot_tn(q[0, 0, at, 128:256], by_place))
        content_f = content_grad.astype(F32)
        place_f = place_grad.astype(F32)
        small_mine[8:9, bias_at] += jnp.sum(content_f, axis=0, keepdims=True)
        small_mine[9:10, bias_at] += jnp.sum(place_f, axis=0, keepdims=True)
        query_grads.append(dot(flip, (content_f + place_f).astype(BF16)).astype(BF16))

    for j, (wide_rows, near_rows) in enumerate((key_rows, value_rows)):
        at = slice(j * 128, (j + 1) * 128)
        dkv[at, 0:past] = wide_rows[:, 0:past].astype(BF16)
        dkv[at, past : past + HALF] = (wide_rows[:, past:] + near_rows[:, 0:HALF]).astype(BF16)
        dkv[at, past + HALF :] = near_rows[:, HALF:].astype(BF16)
    split = past - HALF
    for at, rows_grad in (
        (slice(0, split), place_rows[0][:, 0:split]),
        (slice(split, None), place_rows[0][:, split:] + place_rows[1]),
    ):
        place_sum[head, :, at] = (
            place_sum[head, :, at].astype(F32) + rows_grad.astype(BF16).astype(F32)
        ).astype(BF16)
    dq = jnp.concatenate(query_grads, axis=0)
    stacked = jnp.concatenate([dq, dkv[:, past:].astype(F32).T.astype(BF16)], axis=1)

    run(within)

    @pl.when(step == 0)
    def _():
        load_xhat[0].wait()

    @pl.when(step == 4)
    def _():
        load_xhat[1].wait()
        load_table.wait()

    ones = jnp.ones((8, context), BF16)
    sums[head, :, 0:128] += dot(ones[:, 0:seg_len], dq)
    sums[head, :, 128:384] += dot_nt(ones, dkv[...])
    for k in range(width // tile):
        at = slice(k * tile, (k + 1) * tile)
        raw[head, at, 0:128] += dot(xhat_t[at, past:], dq)
        raw[head, at, 128:384] += dot_nt(xhat_t[at, :], dkv[...])
        input_grad[:, at] += dot_nt(stacked, flat[at, 0:384])

    @pl.when(step >= 4)
    def _():
        place_low = place_sum[head]
        block = tile // (4 * rows)
        total = sums[head, 0:1, :]
        for k in range(width // tile):
            at = slice(k * tile, (k + 1) * tile)
            to = slice(k * block, (k + 1) * block)
            got = raw[head, at, :]
            mats = flat[at, 0:384].astype(F32)
            for acc, term in ((gain_sum, mats * got), (shift_sum, mats * total)):
                acc[at, :] += term[:, 0:128] + term[:, 128:256] + term[:, 256:384]
            grad = (columns[0, at, 0:1] * got + columns[1, at, 0:1] * total).astype(BF16)
            head_grads[head, to, :, :, :, 0:384] = grad.reshape(block, 2, 2, rows, 384)
            grad = dot_nt(table_t[at, :], place_low).astype(BF16)
            head_grads[head, to, :, :, :, 384:512] = grad.reshape(block, 2, 2, rows, 128)

    def own_rows(k):
        gain = jnp.concatenate([params[0:1, :], params[1:2, :]], axis=1)
        at = slice(k * tile, (k + 1) * tile)
        values = seg_rows[at, :].astype(F32)
        mean = jnp.mean(values, axis=-1, keepdims=True)
        centred = values - mean
        rstd = lax.rsqrt(jnp.mean(centred * centred, axis=-1, keepdims=True) + 1e-05)
        return norm_back(centred * rstd, rstd, input_grad[at, :] * gain)

    @pl.when(step == 4)
    def _():
        load_segment.start()

    @pl.when(step == 3)
    def _():
        load_xhat[1].start()
        load_other.wait()
        for k in range(seg_len // tile):
            context_send[k * tile : (k + 1) * tile, :] = own_rows(k).astype(BF16)
        context_pair.start()

    @pl.when(step == 5)
    def _():
        branch_pair.wait_recv()
        load_own.wait()
        for k in range(seg_len // tile):
            at = slice(k * tile, (k + 1) * tile)
            result_out[0, at] = (own_rows_sum[at, :] + branch_land[at, :].astype(F32)).astype(BF16)

    @pl.when(step == 7)
    def _():
        start(11)
        one = jnp.ones((8, 128), F32)
        for acc, row in ((gain_sum, 0), (shift_sum, 2)):
            line = lax.dot_general(
                one,
                acc[...],
                (((1,), (1,)), ((), ())),
                precision=lax.Precision.HIGHEST,
                preferred_element_type=F32,
            )
            small_mine[row : row + 1, :] = line[0:1, 0:LANES]
            small_mine[row + 1 : row + 2, :] = line[0:1, LANES:]

        def to_dp(src, dst, k, index):
            return remote(src, dst, small_send.at[k], small_recv.at[k], index)

        copies = [to_dp(small_mine, small_c.at[1], 0, high * 4 + low * 2 + (1 - core))]
        copies[0].start()
        add_core(11)
        load_segment.wait()
        load_residual.wait()
        context_pair.wait_recv()
        for k in range(seg_len // tile):
            at = slice(k * tile, (k + 1) * tile)
            segment_out[0, at] = (
                residual_grad[at, :] + own_rows(k) + context_land[at, :].astype(F32)
            ).astype(BF16)
        add_y(10)
        copies[0].wait_recv()
        small_c[0] = small_mine[...] + small_c[1]
        copies.append(to_dp(small_c.at[0], small_y.at[1], 1, high * 4 + (1 - low) * 2 + core))
        copies[1].start()
        copies[1].wait_recv()
        small_y[0] = small_c[0] + small_y[1]
        along = []
        for k in range(1, nhi):
            to = lax.rem(high + k, nhi) * 4 + low * 2 + core
            along.append(to_dp(small_y.at[0], small_z.at[k], 2 + k, to))
        for copy in along:
            copy.start()
        add_z(9)
        add_y(11)
        for copy in along:
            copy.wait_recv()
        line = small_y[0]
        for k in range(1, nhi):
            line = line + small_z[k]
        small_z[0] = line
        last = pltpu.make_async_remote_copy(
            src_ref=small_z.at[0],
            dst_ref=small_x,
            send_sem=small_send.at[2],
            recv_sem=small_recv.at[2],
            device_id={"head": 1 - x},
            device_id_type=MESH,
        )
        last.start()
        add_z(10)
        add_z(11)
        for f in range(2):
            up_pairs[f].wait_recv()
            up_out[1 - x, f] = up_land[f].astype(F32)
        for b in range(2):
            out_pairs[b].wait_recv()
            out_out[:, b * LANES : (b + 1) * LANES] = out_keep[b] + out_land[b].astype(F32)
        last.wait_recv()
        line = lax.broadcasted_iota(jnp.int32, (SMALL, LANES), 0)
        small_out[...] = small_z[0] + jnp.where(line < 8, small_x[...], 0.0)
        for copy in [context_pair, branch_pair, *up_pairs, *out_pairs, *copies, *along, last]:
            copy.wait_send()
        for c in range(count):
            scatter.close(c, upper=c > 1)


def attention_backward(
    n, dout, kv, q, wide, near, place_keys, xhat_t, mats, table_t, params, segment,
    seg_other, residual_grad, small_in, own_sum, branch, up, down, out,
):
    _, seg_len, width = segment.shape
    context = kv.shape[2]
    past = context - seg_len
    rows = width // n
    nhi = n // 4
    half_rows = rows // 2
    seq = lambda t: 1 - t // 4
    head = lambda t: lax.rem(t, 4)
    by_both = lambda t: (head(t), seq(t), 0, 0)
    single = pl.Buffered(1)
    any_spec = pl.BlockSpec(memory_space=pl.ANY)
    dma = pltpu.SemaphoreType.DMA
    f32 = lambda *shape: jax.ShapeDtypeStruct(shape, F32)
    lead = (nhi, 2, 2)
    full = lambda shape: pl.BlockSpec(shape, lambda t: (0,) * len(shape), pipeline_mode=single)
    outs = (
        jax.ShapeDtypeStruct((1, seg_len, width), BF16),
        jax.ShapeDtypeStruct((1, seg_len, width), BF16),
        f32(rows, LANES),
        f32(rows, LANES),
        f32(rows, LANES),
        f32(rows, LANES),
        f32(half_rows, width),
        f32(2 * rows, width),
        f32(2, 2, half_rows, LANES),
        f32(SMALL, LANES),
    )
    return pl.pallas_call(
        functools.partial(backward_kernel, n, past, seg_len),
        grid=(8,),
        out_shape=outs,
        in_specs=[
            pl.BlockSpec((1, seg_len, 128), lambda t: (seq(t), 0, head(t))),
            pl.BlockSpec((1, 1, context, 256), by_both),
            pl.BlockSpec((1, 1, seg_len, 256), by_both),
            pl.BlockSpec((1, 1, HALF, past + HALF), by_both),
            pl.BlockSpec((1, 1, HALF, seg_len), by_both),
            pl.BlockSpec((1, past + HALF, 128), lambda t: (head(t), 0, 0)),
            any_spec,
            *[pl.BlockSpec((width, 128), lambda t: (0, head(t)))] * 3,
            any_spec,
            full((SMALL, LANES)),
            any_spec,
            any_spec,
            any_spec,
            full((SMALL, LANES)),
            any_spec,
            any_spec,
            any_spec,
            any_spec,
            any_spec,
        ],
        out_specs=tuple(full(o.shape) for o in outs),
        scratch_shapes=[
            pltpu.VMEM((width, context), BF16),
            pltpu.VMEM(table_t.shape, BF16),
            pltpu.VMEM((seg_len, width), F32),
            dma((5,)),
            pltpu.VMEM((2, half_rows, LANES), BF16),
            pltpu.VMEM((2, half_rows, LANES), BF16),
            pltpu.VMEM((width, 384), BF16),
            pltpu.VMEM((4, width, 384), F32),
            pltpu.VMEM((4, 8, 384), F32),
            pltpu.VMEM((4, 128, past + HALF), BF16),
            pltpu.VMEM((seg_len, width), F32),
            pltpu.VMEM((256, context), BF16),
            pltpu.VMEM((2, width, 128), F32),
            pltpu.VMEM((width, 128), F32),
            pltpu.VMEM((width, 128), F32),
            pltpu.VMEM((4,) + lead + (rows, LANES), BF16),
            pltpu.VMEM((seg_len, width), BF16),
            pltpu.VMEM((seg_len, width), BF16),
            pltpu.VMEM((seg_len, width), BF16),
            pltpu.VMEM((seg_len, width), F32),
            dma(()),
            pltpu.VMEM((seg_len, width), BF16),
            dma(()),
            pltpu.VMEM((2, half_rows, LANES), F32),
            pltpu.VMEM((2, half_rows, LANES), BF16),
            pltpu.VMEM((2, half_rows, LANES), BF16),
            pltpu.VMEM((SMALL, LANES), F32),
            pltpu.VMEM((2, SMALL, LANES), F32),
            pltpu.VMEM((2, SMALL, LANES), F32),
            pltpu.VMEM((nhi, SMALL, LANES), F32),
            pltpu.VMEM((SMALL, LANES), F32),
            dma((6,)),
            dma((6,)),
            dma((2 + nhi,)),
            dma((2 + nhi,)),
        ]
        + Scatter.scratch(12, nhi, rows),
        compiler_params=pltpu.CompilerParams(
            vmem_limit_bytes=VMEM_LIMIT,
            dimension_semantics=("arbitrary",),
            collective_id=1,
            has_side_effects=True,
        ),
        name="attention_backward",
    )(
        dout, kv, q, wide, near, place_keys, xhat_t, *mats, table_t,
        params, segment, seg_other,
        residual_grad, small_in, own_sum, branch, up, down, out,
    )


def finish_kernel(n, *refs):
    count = (len(refs) - 1) // 2
    ups, refs = refs[:2], refs[1:]
    up_out = refs[count]
    size = LANES // (n // 4)
    for f in range(4):
        for j in range(n // 4):
            for half in range(2):
                to = ((f * (n // 4) + j) * 2 + half) * size
                up_out[:, to : to + size] = ups[f // 2][
                    half, f % 2, :, j * size : (j + 1) * size
                ]
    for src, dst in zip(refs[1:count], refs[count + 1 :]):
        dst[...] = src[...]


def finish(n, ups, others):
    vmem = pl.BlockSpec(memory_space=pltpu.VMEM)
    same = [jax.ShapeDtypeStruct(a.shape, a.dtype) for a in others]
    out = jax.ShapeDtypeStruct((ups[0].shape[2], 8 * LANES), F32)
    return pl.pallas_call(
        functools.partial(finish_kernel, n),
        out_shape=(out, *same),
        in_specs=[vmem] * (2 + len(others)),
        out_specs=(vmem,) * (1 + len(others)),
        compiler_params=pltpu.CompilerParams(vmem_limit_bytes=VMEM_LIMIT),
        name="finish",
    )(*ups, *others)


def body(
    n,
    segment,
    memory,
    compressed,
    doc_lengths,
    memory_valid,
    query_weight,
    key_weight,
    value_weight,
    position_weight,
    content_bias,
    position_bias,
    output_weight,
    up_weight,
    down_weight,
    compress_weight,
    norm_gain,
    norm_shift,
    post_gain,
    post_shift,
    cotangent,
    compress_cotangent,
):
    x = lax.axis_index("head")
    dp = lax.axis_index("dp")
    first = x == 0
    nhi = n // 4
    width = segment.shape[2]
    seg_len = segment.shape[1]
    past = memory.shape[1] + compressed.shape[1]
    context = past + seg_len
    rows = query_weight.shape[0]
    half_rows = output_weight.shape[0]
    new_count = compress_cotangent.shape[1]
    comp_rows = compress_weight.shape[0]

    per = content_bias.shape[1]
    vectors = jnp.stack([norm_gain, norm_shift, post_gain, post_shift])
    here = jnp.arange(2 * n, dtype=jnp.int32)[None, :, None] == dp * 2 + x
    norms = jnp.where(here, vectors[:, None, :], 0).reshape(8, LANES)
    here = jnp.arange(n, dtype=jnp.int32)[None, None, :, None] == dp
    bias = jnp.stack([content_bias, position_bias])[:, :, None, :]
    bias = jnp.where(here, bias, 0).reshape(2, LANES)
    small = jnp.concatenate([norms, bias, jnp.zeros((SMALL - 10, LANES), BF16)])
    pad_rows = -(-new_count // 16) * 16
    comp_cot = jnp.pad(compress_cotangent[0], ((0, pad_rows - new_count), (0, 0)))
    table = position_rows(context, width, past + HALF)

    (
        att, seg_other, cot_other, xhat_t, windows, comp_grads, comp_shard, params, kv, q, wide, near,
        place_keys, query_whole, key_whole, value_whole, _, out_whole, up_whole, down_whole, _,
    ) = attention_forward(
        n, doc_lengths, memory_valid, compressed, memory, segment, cotangent, comp_cot,
        (query_weight, key_weight, value_weight, position_weight),
        output_weight, up_weight, down_weight, compress_weight, small, jnp.asarray(table),
    )

    lead = (nhi, 2, 2)
    (
        own_sum, branch, residual_grad, dout, out_grads, down_grads, up_rest, small_in, comp_done,
        up_first, made, _,
    ) = feed_forward(
        n, att, segment, seg_other, cotangent, cot_other, out_whole.reshape(width, width),
        up_whole.reshape(4 * width, LANES), down_whole.reshape(4 * LANES, width), params,
        comp_grads.reshape(lead + (3 * rows, LANES)), comp_shard, windows.reshape(-1, width),
    )

    mats = [w.reshape(width, LANES) for w in (query_whole, key_whole, value_whole)]
    result, segment_grad, *matrices, up_last, small_done = attention_backward(
        n, dout, kv, q, wide, near, place_keys, xhat_t, mats, jnp.asarray(table.T.copy()),
        params, segment, seg_other, residual_grad, small_in, own_sum, branch,
        up_rest,
        down_grads.reshape(lead + (2 * rows, 2 * LANES)),
        out_grads.reshape(lead + (rows, 2 * LANES)),
    )

    up_final, result, segment_grad, *matrices, comp_final = finish(
        n, (up_first, up_last), (result, segment_grad, *matrices, comp_done)
    )
    query_final, key_final, value_final, place_final, out_final, down_final = matrices
    vectors = lax.dynamic_slice_in_dim(
        small_done[0:8].reshape(4, width), (dp * 2 + x) * half_rows, half_rows, 1
    )
    biases = lax.dynamic_slice_in_dim(small_done[8:10].reshape(2, 4, 128), dp * per, per, 2)
    return (
        result,
        made[None, :new_count],
        segment_grad,
        query_final,
        key_final,
        value_final,
        place_final,
        biases[0],
        biases[1],
        out_final,
        up_final,
        down_final,
        comp_final,
        vectors[0],
        vectors[1],
        vectors[2],
        vectors[3],
    )


def solution(mesh):
    split = P(("dp", "head"))
    wide = P(("dp", "head"), None)
    deep = P(("dp", "head"), None, None)
    return jax.shard_map(
        functools.partial(body, mesh.shape["dp"]),
        mesh=mesh,
        in_specs=(
            deep,
            P("dp", None, None),
            P("dp", None, None),
            P("dp", None),
            P("dp"),
            P("dp", "head"),
            P("dp", "head"),
            P("dp", "head"),
            P("dp", "head"),
            P("head", "dp"),
            P("head", "dp"),
            wide,
            wide,
            wide,
            wide,
            split,
            split,
            split,
            split,
            deep,
            deep,
        ),
        out_specs=(
            deep,
            deep,
            deep,
            P("dp", "head"),
            P("dp", "head"),
            P("dp", "head"),
            P("dp", "head"),
            P("head", "dp"),
            P("head", "dp"),
            wide,
            wide,
            wide,
            wide,
            split,
            split,
            split,
            split,
        ),
        check_vma=False,
    )
```

```python
import functools
import math

import jax
import jax.numpy as jnp
import numpy as np
from jax import lax
from jax.experimental import pallas as pl
from jax.experimental.pallas import tpu as pltpu
from jax.sharding import PartitionSpec as P

F32 = jnp.float32
BF16 = jnp.bfloat16
MESH = pl.DeviceIdType.MESH
VMEM_LIMIT = 62 * 1024 * 1024
HALF = 256
LANES = 512
SMALL = 16


def dot(a, b):
    return lax.dot_general(a, b, (((1,), (0,)), ((), ())), preferred_element_type=F32)


def dot_nt(a, b):
    return lax.dot_general(a, b, (((1,), (1,)), ((), ())), preferred_element_type=F32)


def dot_tn(a, b):
    return lax.dot_general(a, b, (((0,), (0,)), ((), ())), preferred_element_type=F32)


def position_rows(context, width, used):
    distance = np.arange(context, dtype=np.float32)[:, None]
    frequency = np.exp(
        np.arange(width // 2, dtype=np.float32) * np.float32(-2.0 * math.log(10000.0) / width)
    )
    phases = distance * frequency[None, :].astype(np.float32)
    table = np.concatenate([np.sin(phases), np.cos(phases)], axis=1)
    return table[::-1][context - used :].astype(jnp.bfloat16)


def place(n):
    me = lax.axis_index("dp")
    core = lax.rem(me, 2)
    low = lax.rem(me // 2, 2)
    high = me // 4
    return core, low, high, n // 4


def meet(core, low, high, nhi, more=0):
    barrier = pltpu.get_barrier_semaphore()

    def tell(index):
        pl.semaphore_signal(barrier, inc=1, device_id={"dp": index}, device_id_type=MESH)

    for k in range(1, nhi):
        tell(lax.rem(high + k, nhi) * 4 + low * 2 + core)
    tell(high * 4 + (1 - low) * 2 + core)
    tell(high * 4 + low * 2 + (1 - core))
    pl.semaphore_wait(barrier, nhi + 1 + more)


def remote(src, dst, send, recv, index):
    return pltpu.make_async_remote_copy(
        src_ref=src,
        dst_ref=dst,
        send_sem=send,
        recv_sem=recv,
        device_id={"dp": index},
        device_id_type=MESH,
    )


class Gather:
    def __init__(self, n, pairs, sems):
        self.core, self.low, self.high, self.nhi = place(n)
        self.pairs = pairs
        (self.zs, self.zr, self.ys, self.yr, self.cs, self.cr, self.own) = sems
        order = sorted(range(1, self.nhi), key=lambda k: (min(k, self.nhi - k), k))
        self.order = order

    def z_copy(self, c, k):
        shard, whole = self.pairs[c]
        return remote(
            shard,
            whole.at[self.high, self.low, self.core],
            self.zs.at[c, k],
            self.zr.at[c, k],
            lax.rem(self.high + k, self.nhi) * 4 + self.low * 2 + self.core,
        )

    def own_copy(self, c):
        shard, whole = self.pairs[c]
        return pltpu.make_async_copy(
            shard, whole.at[self.high, self.low, self.core], self.own.at[c]
        )

    def y_copy(self, c, k):
        shard, whole = self.pairs[c]
        at = whole.at[lax.rem(self.high + k, self.nhi), self.low, self.core]
        return remote(
            shard if k == 0 else at,
            at,
            self.ys.at[c, k],
            self.yr.at[c, k],
            self.high * 4 + (1 - self.low) * 2 + self.core,
        )

    def c_copy(self, c):
        _, whole = self.pairs[c]
        part = whole.at[:, :, self.core]
        return remote(
            part,
            part,
            self.cs.at[c],
            self.cr.at[c],
            self.high * 4 + self.low * 2 + (1 - self.core),
        )

    def start(self, c):
        for k in self.order:
            self.z_copy(c, k).start()
        self.y_copy(c, 0).start()
        self.own_copy(c).start()

    def pass_y(self, c):
        for k in self.order:
            self.z_copy(c, self.nhi - k).wait_recv()
            self.y_copy(c, k).start()

    def pass_core(self, c):
        self.own_copy(c).wait()
        for k in range(self.nhi):
            self.y_copy(c, k).wait_recv()
        self.c_copy(c).start()

    def arrive(self, c):
        self.c_copy(c).wait_recv()

    def close(self, c):
        for k in self.order:
            self.z_copy(c, k).wait_send()
        for k in range(self.nhi):
            self.y_copy(c, k).wait_send()
        self.c_copy(c).wait_send()

    @staticmethod
    def semaphores(count, nhi):
        dma = pltpu.SemaphoreType.DMA
        return [dma((count, nhi))] * 4 + [dma((count,))] * 3


class Scatter:
    def __init__(self, n, items, mine, mine_sem, sems):
        self.core, self.low, self.high, self.nhi = place(n)
        self.items = items
        self.mine, self.mine_sem = mine, mine_sem
        (self.cs, self.cr, self.ys, self.yr, self.zs, self.zr) = sems

    def c_copy(self, c):
        return remote(
            self.items[c][0].at[:, :, 1 - self.core],
            self.items[c][2],
            self.cs.at[c],
            self.cr.at[c],
            self.high * 4 + self.low * 2 + (1 - self.core),
        )

    def mine_copy(self, c):
        slot = c % 2
        return pltpu.make_async_copy(
            self.items[c][0].at[:, :, self.core], self.mine.at[slot], self.mine_sem.at[slot]
        )

    def y_copy(self, c):
        return remote(
            self.items[c][2].at[:, 1 - self.low],
            self.items[c][3],
            self.ys.at[c],
            self.yr.at[c],
            self.high * 4 + (1 - self.low) * 2 + self.core,
        )

    def z_copies(self, c):
        return [
            remote(
                self.items[c][3].at[lax.rem(self.high + k, self.nhi)],
                self.items[c][4].at[k - 1],
                self.zs.at[c, k - 1],
                self.zr.at[c, k - 1],
                lax.rem(self.high + k, self.nhi) * 4 + self.low * 2 + self.core,
            )
            for k in range(1, self.nhi)
        ]

    def start(self, c):
        self.c_copy(c).start()
        if not self.items[c][1]:
            self.mine_copy(c).start()

    def add_core(self, c):
        here = self.items[c][1]
        if not here:
            self.mine_copy(c).wait()
        self.c_copy(c).wait_recv()
        land = self.items[c][2]

        def body(i, carry):
            for j in range(2):
                own = self.items[c][0][i, j, self.core] if here else self.mine[c % 2, i, j]
                land[i, j] = land[i, j] + own
            return carry

        lax.fori_loop(0, self.nhi, body, 0)
        self.y_copy(c).start()

    def add_y(self, c, go_on=True):
        self.y_copy(c).wait_recv()
        src, land = self.items[c][2], self.items[c][3]

        def body(i, carry):
            land[i] = land[i] + src[i, self.low]
            return carry

        lax.fori_loop(0, self.nhi, body, 0)
        if go_on:
            self.start_z(c)

    def start_z(self, c):
        for copy in self.z_copies(c):
            copy.start()

    def add_z(self, c):
        for copy in self.z_copies(c):
            copy.wait_recv()
        land, last, done = self.items[c][3:]
        total = land[self.high].astype(F32)
        for k in range(self.nhi - 1):
            total = total + last[k].astype(F32)
        done(total)

    def close(self, c, upper=True, last=True):
        if upper:
            self.c_copy(c).wait_send()
            self.y_copy(c).wait_send()
        if last:
            for copy in self.z_copies(c):
                copy.wait_send()

    @staticmethod
    def scratch(count, nhi, rows):
        dma = pltpu.SemaphoreType.DMA
        return [
            pltpu.VMEM((count, nhi, 2, rows, LANES), BF16),
            pltpu.VMEM((count, nhi, rows, LANES), BF16),
            pltpu.VMEM((count, nhi - 1, rows, LANES), BF16),
            pltpu.VMEM((2, nhi, 2, rows, LANES), BF16),
            dma((2,)),
            dma((count,)),
            dma((count,)),
            dma((count,)),
            dma((count,)),
            dma((count, nhi - 1)),
            dma((count, nhi - 1)),
        ]


def norm_rows(values):
    mean = jnp.mean(values, axis=-1, keepdims=True)
    centred = values - mean
    variance = jnp.mean(centred * centred, axis=-1, keepdims=True)
    return centred * lax.rsqrt(variance + 1e-05)


def attend_rows(query_content, query_place, keys, place_keys, first_seen, last_seen, scale):
    width = keys.shape[0]
    content = dot_nt(query_content, keys)
    by_place = pltpu.roll(
        dot_nt(query_place, place_keys), width - (HALF - 1), 1, stride=1, stride_axis=0
    )
    column = lax.broadcasted_iota(jnp.int32, (HALF, width), 1)
    seen = (column >= first_seen) & (column <= last_seen)
    scores = jnp.where(seen, (content + by_place) * (scale * math.log2(math.e)), -1e30)
    top = jnp.max(scores, axis=1, keepdims=True)
    expo = jnp.exp2(scores - top)
    return expo * (1.0 / jnp.sum(expo, axis=1, keepdims=True))


def forward_kernel(
    n,
    past,
    seg_len,
    docs,
    valid,
    compressed,
    memory,
    segment,
    cotangent,
    comp_cot,
    query_w,
    key_w,
    value_w,
    place_w,
    out_w,
    up_w,
    down_w,
    comp_w,
    small,
    table,
    attended,
    seg_other,
    cot_other,
    xhat_hbm,
    windows_hbm,
    comp_grads_hbm,
    comp_shard_hbm,
    params,
    kv_out,
    q_out,
    wide_out,
    near_out,
    place_out,
    query_whole,
    key_whole,
    value_whole,
    place_whole,
    out_whole,
    up_whole,
    down_whole,
    small_whole,
    out_shard,
    up_parts,
    up_shard,
    comp_shard,
    small_shard,
    normed,
    xhat_out,
    memory_f,
    windows,
    comp_rows_cot,
    comp_grads,
    past_rows,
    seg_rows,
    flat,
    small_rows,
    att,
    load_sem,
    flat_sem,
    own_sem,
    store_sem,
    pair_send,
    pair_recv,
    att_own,
    att_send,
    att_recv,
    *sems,
):
    step = pl.program_id(0)
    x = lax.axis_index("head")
    core, low, high, nhi = place(n)
    tile = 256
    width = normed.shape[2]
    context = past + seg_len
    head = jnp.maximum(step - 2, 0) // 2
    half = comp_w.shape[1] // 2

    items = [(small_shard, small_whole)]
    items += [(query_w, query_whole), (key_w, key_whole), (value_w, value_whole), (place_w, place_whole)]
    for b in range(2):
        to = pl.ds(b * LANES, LANES)
        items.append((out_shard.at[:, :, to], out_whole.at[:, :, :, :, :, to]))
    items += [(up_shard.at[f], up_whole.at[f]) for f in range(4)]
    mid = down_w.shape[0] // 2
    for part in range(2):
        for b in range(2):
            at, to = pl.ds(part * mid, mid), pl.ds(b * LANES, LANES)
            items.append((down_w.at[at, to], down_whole.at[:, :, :, at, to]))
    gather = Gather(n, items, sems)
    count = len(items)
    needs = {5: 1, 7: 2}
    pad_rows = comp_cot.shape[0]

    def pair(src, dst, k):
        return pltpu.make_async_remote_copy(
            src_ref=src,
            dst_ref=dst,
            send_sem=pair_send.at[k],
            recv_sem=pair_recv.at[k],
            device_id={"head": 1 - x},
            device_id_type=MESH,
        )

    mine_at = pl.ds(pl.multiple_of(x * half, half), half)
    other_at = pl.ds(pl.multiple_of((1 - x) * half, half), half)
    pairs = [
        pair(small, small_shard.at[x], 0),
        pair(out_w, out_shard.at[x], 1),
        pair(up_parts.at[1 - x], up_shard.at[:, x], 2),
        pair(comp_w.at[:, other_at], comp_shard.at[x], 3),
        pair(segment.at[0], seg_other, 4),
        pair(cotangent.at[0], cot_other, 5),
        pair(comp_cot.at[:, other_at], comp_rows_cot.at[1], 6),
    ]
    owns = [
        pltpu.make_async_copy(small, small_shard.at[x], own_sem.at[0]),
        pltpu.make_async_copy(out_w, out_shard.at[x], own_sem.at[1]),
        pltpu.make_async_copy(up_parts.at[x], up_shard.at[:, x], own_sem.at[2]),
        pltpu.make_async_copy(comp_w.at[:, mine_at], comp_shard.at[x], own_sem.at[3]),
        pltpu.make_async_copy(comp_cot.at[:, mine_at], comp_rows_cot.at[0], own_sem.at[4]),
    ]
    loads = []
    for i in range(2):
        s = lax.rem(x + i, 2)
        loads.append(pltpu.make_async_copy(compressed.at[s], past_rows.at[i, 0], load_sem.at[i, 0]))
        loads.append(pltpu.make_async_copy(memory.at[s], past_rows.at[i, 1], load_sem.at[i, 1]))
    loads.append(pltpu.make_async_copy(segment.at[0], seg_rows.at[0], load_sem.at[0, 2]))
    load_other = pltpu.make_async_copy(seg_other, seg_rows.at[1], load_sem.at[1, 2])
    store_xhat = pltpu.make_async_copy(xhat_out, xhat_hbm, store_sem.at[0])
    store_windows = pltpu.make_async_copy(windows, windows_hbm, store_sem.at[1])
    store_grads = pltpu.make_async_copy(comp_grads, comp_grads_hbm, store_sem.at[2])
    store_shard = pltpu.make_async_copy(comp_shard, comp_shard_hbm, store_sem.at[3])

    joined = set()

    def join(k):
        if k not in joined:
            joined.add(k)
            owns[k].wait()
            pairs[k].wait_recv()

    def tick(t):
        lead = t + 2
        if lead < count:
            if lead in needs:
                join(needs[lead])
            gather.start(lead)
        if t < count:
            gather.pass_y(t)
        if 0 <= t - 1 < count:
            gather.pass_core(t - 1)
        if 0 <= t - 2 < count and t != 6:
            gather.arrive(t - 2)

    def flat_copies(h, slot):
        at = pl.ds(h * 128, 128)
        return [
            pltpu.make_async_copy(
                whole.at[:, :, :, :, at],
                flat.at[slot, :, :, :, :, pl.ds(j * 128, 128)],
                flat_sem.at[slot, j],
            )
            for j, whole in enumerate((query_whole, key_whole, value_whole, place_whole))
        ]

    def norm_into(i, values, at):
        eye = (
            lax.broadcasted_iota(jnp.int32, (tile, tile), 0)
            == lax.broadcasted_iota(jnp.int32, (tile, tile), 1)
        ).astype(BF16)
        gain = jnp.concatenate([params[0:1, :], params[1:2, :]], axis=1)
        shift = jnp.concatenate([params[2:3, :], params[3:4, :]], axis=1)
        xhat = norm_rows(values.astype(F32))
        normed[i, pl.ds(at, tile)] = (xhat * gain + shift).astype(BF16)
        xhat = xhat.astype(BF16)
        for b in range(width // tile):
            xhat_out[i, b * tile : (b + 1) * tile, pl.ds(at, tile)] = dot_nt(
                eye, xhat[:, b * tile : (b + 1) * tile]
            ).astype(BF16)

    def norm_past(i):
        per = past // 2 // tile

        def one(k, carry):
            at = pl.multiple_of(k * tile, tile)
            inner = pl.multiple_of(lax.rem(k, per) * tile, tile)
            norm_into(i, past_rows[i, k // per, pl.ds(inner, tile)], at)
            return carry

        lax.fori_loop(0, past // tile, one, 0)

    def norm_segment(i):
        def one(k, carry):
            at = pl.multiple_of(k * tile, tile)
            norm_into(i, seg_rows[i, pl.ds(at, tile)], past + at)
            return carry

        lax.fori_loop(0, seg_len // tile, one, 0)

    @pl.when(step == 0)
    def _():
        barrier = pltpu.get_barrier_semaphore()
        pl.semaphore_signal(
            barrier, inc=1, device_id={"head": 1 - x}, device_id_type=MESH
        )
        meet(core, low, high, nhi, 1)
        for k in (0, 1):
            pairs[k].start()
            owns[k].start()
        gather.start(1)
        size = LANES // (n // 4)
        for half_at in range(2):
            for f in range(4):
                for j in range(n // 4):
                    at = ((f * (n // 4) + j) * 2 + half_at) * size
                    up_parts[half_at, f, :, j * size : (j + 1) * size] = up_w[:, at : at + size]
        for k in (2, 6, 3, 4, 5):
            pairs[k].start()
        for copy in owns[2:]:
            copy.start()
        for copy in loads:
            copy.start()
        join(0)
        gather.start(0)
        tick(0)
        tick(1)
        tick(2)
        summed = pltpu.make_async_copy(small_whole, small_rows, load_sem.at[0, 3])
        summed.start()
        summed.wait()
        both = jnp.sum(small_rows[...].reshape(n, 2, SMALL, LANES).astype(F32), axis=0)
        row = lax.broadcasted_iota(jnp.int32, (SMALL, LANES), 0)
        by_head = jnp.where(x == 0, both[0], both[1])
        params[...] = jnp.where(row < 8, both[0] + both[1], by_head)
        for copy in (loads[0], loads[1], loads[4]):
            copy.wait()
        norm_past(0)
        tick(3)
        norm_segment(0)

    @pl.when(step == 1)
    def _():
        for copy in loads[2:4]:
            copy.wait()
        norm_past(1)
        tick(4)
        tick(5)
        gather.arrive(4)
        for copy in flat_copies(0, 0):
            copy.start()

    for k in range(2, 10):

        @pl.when(step == k)
        def _(k=k):
            h, slot = (k - 2) // 2, ((k - 2) // 2) % 2
            if k % 2 == 0:
                for copy in flat_copies(h, slot):
                    copy.wait()
                if h < 3:
                    for copy in flat_copies(h + 1, 1 - slot):
                        copy.start()
            if k == 3:
                pairs[4].wait_recv()
                load_other.start()
                load_other.wait()
                norm_segment(1)
                store_xhat.start()
                join(3)
                store_shard.start()

    def att_pair(h, i):
        at = pl.ds(pl.multiple_of(x * LANES + h * 128, 128), 128)
        return pltpu.make_async_remote_copy(
            src_ref=att.at[h, i],
            dst_ref=attended.at[1 - i, :, at],
            send_sem=att_send.at[h, i],
            recv_sem=att_recv.at[h, i],
            device_id={"head": 1 - x},
            device_id_type=MESH,
        )

    def att_local(h, i):
        at = pl.ds(pl.multiple_of(x * LANES + h * 128, 128), 128)
        return pltpu.make_async_copy(att.at[h, i], attended.at[i, :, at], att_own.at[h, i])

    @pl.when(step >= 2)
    def _():
        i = lax.rem(step, 2)
        s = lax.rem(x + i, 2)
        slot = lax.rem(head, 2)

        def weights(a, b):
            return flat[slot, :, :, :, :, a:b].reshape(width, b - a)

        @pl.when(i == 0)
        def _():
            mat = weights(384, 512)
            for k in range(table.shape[0] // tile):
                place_out[0, k * tile : (k + 1) * tile] = dot(
                    table[k * tile : (k + 1) * tile], mat
                ).astype(BF16)

        mat = weights(128, 384)
        for k in range(context // tile):
            kv_out[0, 0, k * tile : (k + 1) * tile] = dot(
                normed[i, pl.ds(k * tile, tile)], mat
            ).astype(BF16)
        mat = weights(0, 128)
        bias_at = pl.ds(pl.multiple_of(head * 128, 128), 128)
        for k in range(seg_len // tile):
            queries = dot(normed[i, pl.ds(past + k * tile, tile)], mat)
            at = slice(k * tile, (k + 1) * tile)
            q_out[0, 0, at, 0:128] = (queries + params[8:9, bias_at]).astype(BF16)
            q_out[0, 0, at, 128:256] = (queries + params[9:10, bias_at]).astype(BF16)

        flip = (
            lax.broadcasted_iota(jnp.int32, (HALF, HALF), 0)
            + lax.broadcasted_iota(jnp.int32, (HALF, HALF), 1)
            == HALF - 1
        ).astype(BF16)
        scale = 1.0 / math.sqrt(128)
        for part, out, key_start, key_count, place_start in (
            (0, wide_out, 0, past + HALF, 0),
            (1, near_out, past, seg_len, past - HALF),
        ):
            token = lax.broadcasted_iota(jnp.int32, (HALF, 1), 0) + part * HALF
            end, first = 0, past - valid[s]
            for doc in range(3):
                end = end + docs[s, doc]
                first = jnp.where(token >= end, past + end, first)
            at = slice(part * HALF, (part + 1) * HALF)
            weights_low = attend_rows(
                q_out[0, 0, at, 0:128],
                q_out[0, 0, at, 128:256],
                kv_out[0, 0, key_start : key_start + key_count, 0:128],
                place_out[0, place_start : place_start + key_count],
                first - key_start,
                token + (past - key_start),
                scale,
            ).astype(BF16)
            out[0, 0] = dot(flip, weights_low).astype(BF16)
            q_out[0, 0, at] = dot(flip, q_out[0, 0, at]).astype(BF16)
            att[head, i, at] = dot(
                weights_low, kv_out[0, 0, key_start : key_start + key_count, 128:256]
            ).astype(BF16)
        att_pair(head, i).start()
        att_local(head, i).start()

    for k in range(2, 10):
        pl.when(step == k)(functools.partial(tick, k + 4))

    @pl.when(step == pl.num_programs(0) - 1)
    def _():
        memory_f[:, past // 2 :, :] = jnp.zeros((width // 128, 16, 128), F32)
        for i in range(2):
            for b in range(width // 128):
                at = slice(b * 128, (b + 1) * 128)
                memory_f[b, 0 : past // 2, :] = past_rows[i, 1, :, at].astype(F32)
                for tap in range(3):
                    windows[tap, i * pad_rows : (i + 1) * pad_rows, at] = memory_f[
                        b, pl.ds(tap, pad_rows, stride=3), :
                    ].astype(BF16)
        store_windows.start()
        owns[4].wait()
        pairs[6].wait_recv()
        tick(14)
        comp_rows_both = comp_rows_cot[...].reshape(2 * pad_rows, LANES)
        for tap in range(3):
            for k in range(width // tile):
                at = slice(k * tile, (k + 1) * tile)
                comp_grads[tap * width + k * tile : tap * width + (k + 1) * tile, :] = dot_tn(
                    windows[tap, :, at], comp_rows_both
                ).astype(BF16)
        store_grads.start()
        for t in range(15, count + 2):
            tick(t)
        for copy in (store_xhat, store_windows, store_grads, store_shard):
            copy.wait()
        for h in range(4):
            for i in range(2):
                att_local(h, i).wait()
                att_pair(h, i).wait()
        for copy in pairs:
            copy.wait_send()
        pairs[5].wait_recv()
        for c in range(count):
            gather.close(c)


def attention_forward(
    n, docs, valid, compressed, memory, segment, cotangent, comp_cot, mats, out_w, up_w, down_w,
    comp_w, small, table,
):
    _, seg_len, width = segment.shape
    past = compressed.shape[1] + memory.shape[1]
    context = past + seg_len
    nhi = n // 4
    lead = (nhi, 2, 2)
    half_rows = out_w.shape[0]
    comp_rows = comp_w.shape[0]
    pad_rows = comp_cot.shape[0]
    any_spec = pl.BlockSpec(memory_space=pl.ANY)
    smem = pl.BlockSpec(memory_space=pltpu.SMEM)
    single = pl.Buffered(1)
    bf = lambda *shape: jax.ShapeDtypeStruct(shape, BF16)
    head = lambda t: jnp.maximum(t - 2, 0) // 2
    which = lambda t: lax.rem(jnp.maximum(t, 2), 2)
    by_both = lambda t: (head(t), which(t), 0, 0)
    dma = pltpu.SemaphoreType.DMA
    full = lambda shape: pl.BlockSpec(shape, lambda t: (0,) * len(shape), pipeline_mode=single)
    count = 15
    return pl.pallas_call(
        functools.partial(forward_kernel, n, past, seg_len),
        grid=(10,),
        out_shape=(
            bf(2, seg_len, width),
            bf(seg_len, width),
            bf(seg_len, width),
            bf(2, width, context),
            bf(3, 2 * pad_rows, width),
            bf(3 * width, LANES),
            bf(2, comp_rows, LANES),
            jax.ShapeDtypeStruct((SMALL, LANES), F32),
            bf(4, 2, context, 256),
            bf(4, 2, seg_len, 256),
            bf(4, 2, HALF, past + HALF),
            bf(4, 2, HALF, seg_len),
            bf(4, past + HALF, 128),
            *[bf(*lead, *w.shape) for w in mats],
            bf(*lead, 2, half_rows, width),
            bf(4, *lead, 2, half_rows, LANES),
            bf(*lead, *down_w.shape),
            bf(*lead, 2, SMALL, LANES),
        ),
        in_specs=[smem, smem]
        + [any_spec] * 5
        + [full(a.shape) for a in (*mats, out_w, up_w, down_w, comp_w, small)]
        + [pl.BlockSpec(table.shape, lambda t: (0, 0), pipeline_mode=single)],
        out_specs=(
            *[any_spec] * 6,
            any_spec,
            pl.BlockSpec((SMALL, LANES), lambda t: (0, 0)),
            pl.BlockSpec((1, 1, context, 256), by_both),
            pl.BlockSpec((1, 1, seg_len, 256), by_both),
            pl.BlockSpec((1, 1, HALF, past + HALF), by_both),
            pl.BlockSpec((1, 1, HALF, seg_len), by_both),
            pl.BlockSpec((1, past + HALF, 128), lambda t: (head(t), 0, 0)),
            *[any_spec] * 8,
        ),
        scratch_shapes=[
            pltpu.VMEM((2, half_rows, width), BF16),
            pltpu.VMEM((2, 4, half_rows, LANES), BF16),
            pltpu.VMEM((4, 2, half_rows, LANES), BF16),
            pltpu.VMEM((2, comp_rows, LANES), BF16),
            pltpu.VMEM((2, SMALL, LANES), BF16),
            pltpu.VMEM((2, context, width), BF16),
            pltpu.VMEM((2, width, context), BF16),
            pltpu.VMEM((width // 128, past // 2 + 16, 128), F32),
            pltpu.VMEM((3, 2 * pad_rows, width), BF16),
            pltpu.VMEM((2, pad_rows, LANES), BF16),
            pltpu.VMEM((3 * width, LANES), BF16),
            pltpu.VMEM((2, 2, past // 2, width), BF16),
            pltpu.VMEM((2, seg_len, width), BF16),
            pltpu.VMEM((2,) + lead + (mats[0].shape[0], LANES), BF16),
            pltpu.VMEM(lead + (2, SMALL, LANES), BF16),
            pltpu.VMEM((4, 2, seg_len, 128), BF16),
            dma((2, 4)),
            dma((2, 4)),
            dma((6,)),
            dma((4,)),
            dma((7,)),
            dma((7,)),
            dma((4, 2)),
            dma((4, 2)),
            dma((4, 2)),
        ]
        + Gather.semaphores(count, nhi),
        compiler_params=pltpu.CompilerParams(
            vmem_limit_bytes=VMEM_LIMIT,
            dimension_semantics=("arbitrary",),
            collective_id=0,
            has_side_effects=True,
        ),
        name="attention_forward",
    )(
        docs, valid, compressed, memory, segment, cotangent, comp_cot, *mats, out_w, up_w, down_w,
        comp_w, small, table,
    )


def gelu_parts(v):
    c = math.sqrt(2.0 / math.pi)
    square = v * v
    t = jnp.tanh(c * (v + 0.044715 * square * v))
    half = 0.5 * (1.0 + t)
    value = v * half
    return value, half + value * (1.0 - half) * (2 * c + (6 * 0.044715 * c) * square)


def feed_kernel(
    n,
    att_in,
    segment,
    seg_other,
    cotangent,
    cot_other,
    out_in,
    up_in,
    down_in,
    params,
    comp,
    comp_shard,
    windows,
    own_out,
    branch_out,
    residual_out,
    dout,
    out_grads,
    down_grads,
    up_rest,
    small_out,
    comp_out,
    up_out,
    made_out,
    comp_whole,
    att,
    seg,
    cot,
    out_w,
    up,
    down,
    residual,
    low,
    low_t,
    act,
    pre,
    branch,
    terms,
    terms_land,
    cast,
    up_grads,
    mixed,
    stage,
    up_send,
    up_land,
    comp_stage,
    comp_send,
    comp_land,
    made_own,
    made_send,
    made_land,
    made_sem,
    load_sem,
    store_sem,
    stage_sem,
    pair_send,
    pair_recv,
    land_c,
    land_y,
    land_z,
    mine,
    mine_sem,
    *sems,
):
    sems, gather_sems = sems[:6], sems[6:]
    x = lax.axis_index("head")
    core, low_y, high, nhi = place(n)
    tile = 256
    _, seg_len, width = att.shape
    rows = width // n
    half_rows = rows // 2
    comp_rows = comp_send.shape[0]

    def pair(src, dst, k):
        return pltpu.make_async_remote_copy(
            src_ref=src,
            dst_ref=dst,
            send_sem=pair_send.at[k],
            recv_sem=pair_recv.at[k],
            device_id={"head": 1 - x},
            device_id_type=MESH,
        )

    terms_pair = pair(cast.at[0], terms_land, 0)
    mixed_pair = pair(mixed.at[1 - x], dout.at[1], 1)
    comp_pair = pair(comp_send, comp_land, 2)
    up_pairs = [pair(up_send.at[f], up_land.at[f], 3 + f) for f in range(2)]
    made_pair = pair(made_send, made_land, 5)
    scatter = Scatter(
        n,
        [
            (part, here, land_c.at[c], land_y.at[c], land_z.at[c], done)
            for c, (part, here, done) in enumerate(
                [
                    (
                        comp.at[:, :, :, pl.ds(m * rows, rows)],
                        False,
                        comp_block(m, x, rows, comp_stage, comp_out, comp_send, comp_pair),
                    )
                    for m in range(3)
                ]
                + [
                    (up_grads.at[f], True, up_block(f, x, up_out, up_send, up_pairs[f]))
                    for f in range(2)
                ]
                + [(up_grads.at[f], True, None) for f in range(2, 4)]
            )
        ],
        mine,
        mine_sem,
        sems,
    )

    third = comp_rows // 3
    gather = Gather(
        n,
        [
            (
                comp_shard.at[:, pl.ds(m * third, third)],
                comp_whole.at[:, :, :, :, pl.ds(m * third, third)],
            )
            for m in range(3)
        ],
        gather_sems,
    )

    def load(src, dst, k):
        return pltpu.make_async_copy(src, dst, load_sem.at[k])

    loads = {
        "att1": load(att_in.at[1], att.at[1], 0),
        "out": load(out_in, out_w, 1),
        "seg1": load(seg_other, seg.at[1], 2),
        "cot1": load(cot_other, cot.at[1], 3),
        "up": load(up_in, up, 4),
        "down": load(down_in, down, 5),
        "att0": load(att_in.at[0], att.at[0], 6),
        "seg0": load(segment.at[0], seg.at[0], 7),
        "cot0": load(cotangent.at[0], cot.at[0], 8),
    }
    for copy in loads.values():
        copy.start()
    barrier = pltpu.get_barrier_semaphore()
    pl.semaphore_signal(barrier, inc=1, device_id={"head": 1 - x}, device_id_type=MESH)
    meet(core, low_y, high, nhi, 1)
    scatter.start(0)
    scatter.start(1)
    gather.start(0)

    eye = (
        lax.broadcasted_iota(jnp.int32, (tile, tile), 0)
        == lax.broadcasted_iota(jnp.int32, (tile, tile), 1)
    ).astype(BF16)
    gain = jnp.concatenate([params[4:5, :], params[5:6, :]], axis=1)
    shift = jnp.concatenate([params[6:7, :], params[7:8, :]], axis=1)

    def project(i):
        for k in range(seg_len // tile):
            at = slice(k * tile, (k + 1) * tile)
            whole_at = slice(i * seg_len + k * tile, i * seg_len + (k + 1) * tile)
            value = seg[i, at].astype(F32) + dot(att[i, at], out_w[...])
            residual[at, :] = value
            value = (norm_rows(value) * gain + shift).astype(BF16)
            low[whole_at, :] = value
            for b in range(width // tile):
                low_t[b * tile : (b + 1) * tile, whole_at] = dot_nt(
                    eye, value[:, b * tile : (b + 1) * tile]
                ).astype(BF16)

    def hidden(i, between):
        whole_at = slice(i * seg_len, (i + 1) * seg_len)
        branch[...] = jnp.zeros_like(branch)
        terms[...] = jnp.zeros_like(terms)

        def one(f, carry):
            down_at = pl.ds(pl.multiple_of(f * LANES, LANES), LANES)
            up_at = pl.ds(pl.multiple_of(f * width, width), width)
            value, slope = gelu_parts(dot(low[whole_at, :], up[up_at, :]))
            value = value.astype(BF16)
            act[f, whole_at, :] = value
            back = dot_nt(cot[i], down[down_at, :]).astype(BF16).astype(F32)
            back = (back * slope).astype(BF16)
            pre[f, whole_at, :] = back
            branch[...] += dot(value, down[down_at, :])
            terms[...] += dot_nt(back, up[up_at, :])
            for k, steps in enumerate(between):

                @pl.when(f == k)
                def _(steps=steps):
                    for run, c in steps:
                        run(c)

            return carry

        lax.fori_loop(0, 4, one, 0)

    for name in ("att1", "out", "seg1"):
        loads[name].wait()
    project(1)
    scatter.add_core(0)
    scatter.start(2)
    gather.start(1)
    for name in ("cot1", "up", "down"):
        loads[name].wait()
    hidden(
        1,
        (
            ((scatter.add_core, 1), (gather.pass_y, 0)),
            ((scatter.add_core, 2), (scatter.add_y, 0), (gather.start, 2)),
            ((gather.pass_y, 1),),
            ((scatter.add_y, 1),),
        ),
    )
    cast[0] = terms[...].astype(BF16)
    terms_pair.start()
    cast[1] = branch[...].astype(BF16)
    store_branch = pltpu.make_async_copy(cast.at[1], branch_out, store_sem.at[0])
    store_branch.start()
    for name in ("att0", "seg0", "cot0"):
        loads[name].wait()
    project(0)
    scatter.add_z(0)
    hidden(
        0,
        (
            ((gather.pass_core, 0),),
            ((gather.pass_y, 2),),
            ((scatter.add_y, 2),),
            ((scatter.add_z, 1),),
        ),
    )
    branch[...] += residual[...]
    store_own = pltpu.make_async_copy(branch, own_out, store_sem.at[1])
    store_own.start()

    count = windows.shape[0]
    load_windows = pltpu.make_async_copy(windows, down.at[pl.ds(0, count)], made_sem.at[2 * n])
    load_windows.start()

    block = tile // (4 * rows)

    def up_grad(f):
        for k in range(width // tile):
            grad = dot(low_t[k * tile : (k + 1) * tile, :], pre[f]).astype(BF16)
            up_grads[f, k * block : (k + 1) * block] = grad.reshape(block, 2, 2, rows, LANES)
        scatter.start(3 + f)

    up_grad(0)
    gather.pass_core(1)
    up_grad(1)
    scatter.add_core(3)
    scatter.add_z(2)
    up_grad(2)
    scatter.add_core(4)
    up_grad(3)
    scatter.add_core(5)
    store_rest = [
        pltpu.make_async_copy(land_y.at[5 + f], up_rest.at[f], store_sem.at[4 + f]) for f in range(2)
    ]

    terms_pair.wait_recv()
    gain_grad = jnp.zeros((1, width), F32)
    shift_grad = jnp.zeros((1, width), F32)
    terms_pair.wait_send()
    for k in range(seg_len // tile):
        at = slice(k * tile, (k + 1) * tile)
        grad = terms[at, :] + terms_land[at, :].astype(F32)
        value = residual[at, :]
        mean = jnp.mean(value, axis=-1, keepdims=True)
        centred = value - mean
        rstd = lax.rsqrt(jnp.mean(centred * centred, axis=-1, keepdims=True) + 1e-05)
        xhat = centred * rstd
        gain_grad += jnp.sum(grad * xhat, axis=0, keepdims=True)
        shift_grad += jnp.sum(grad, axis=0, keepdims=True)
        grad = cot[0, at].astype(F32) + norm_back(xhat, rstd, grad * gain)
        residual[at, :] = grad
        grad = grad.astype(BF16)
        cast[0, at, :] = grad
        back = dot_nt(grad, out_w[...]).astype(BF16)
        mixed[0, at, :] = back[:, 0:LANES]
        mixed[1, at, :] = back[:, LANES:]
    mixed_pair.start()
    store_dout = pltpu.make_async_copy(mixed.at[x], dout.at[0], store_sem.at[2])
    store_dout.start()
    store_residual = pltpu.make_async_copy(residual, residual_out, store_sem.at[3])
    store_residual.start()
    small_out[...] = jnp.zeros_like(small_out)
    small_out[4:5, :] = gain_grad[:, 0:LANES]
    small_out[5:6, :] = gain_grad[:, LANES:]
    small_out[6:7, :] = shift_grad[:, 0:LANES]
    small_out[7:8, :] = shift_grad[:, LANES:]
    scatter.add_core(6)
    gather.pass_core(2)

    staged = [None, None]
    jobs = [(out_grads, k * tile, None, k) for k in range(width // tile)]
    jobs += [
        (down_grads, f * LANES + k * tile, f, k) for f in range(4) for k in range(LANES // tile)
    ]
    for j, (target, start, f, k) in enumerate(jobs):
        slot = j % 2
        at = slice(k * tile, (k + 1) * tile)
        if f is None:
            grad = dot_tn(att[0, :, at], cast[0])
        else:
            grad = dot_tn(act[f, 0:seg_len, at], cot[0]) + dot_tn(act[f, seg_len:, at], cot[1])
        if staged[slot] is not None:
            staged[slot].wait()
        stage[slot] = grad.astype(BF16)
        staged[slot] = pltpu.make_async_copy(
            stage.at[slot], target.at[pl.ds(start, tile)], stage_sem.at[slot]
        )
        staged[slot].start()
        if j == 3:
            scatter.add_y(3)
        if j == 10:
            scatter.add_y(4)
            scatter.add_z(3)
    scatter.add_y(5, False)
    store_rest[0].start()
    for m in range(3):
        gather.arrive(m)
    load_comp = []
    for b in range(n):
        for half in range(2):
            load_comp.append(
                pltpu.make_async_copy(
                    comp_whole.at[b // 4, (b // 2) % 2, b % 2, half],
                    up.at[pl.ds((2 * b + half) * comp_rows, comp_rows)],
                    made_sem.at[2 * b + half],
                )
            )
            load_comp[-1].start()
    load_windows.wait()
    for copy in load_comp:
        copy.wait()
    made = jnp.zeros((count // 3, LANES), F32)
    for tap in range(3):
        made += dot(
            down[tap * (count // 3) : (tap + 1) * (count // 3), :],
            up[tap * width : (tap + 1) * width, :],
        )
    made_own[...] = made[: count // 6].astype(BF16)
    made_send[...] = made[count // 6 :].astype(BF16)
    made_pair.start()
    scatter.add_z(4)
    scatter.add_y(6, False)
    store_rest[1].start()
    comp_pair.wait_recv()
    to = pl.ds(pl.multiple_of((1 - x) * LANES, LANES), LANES)
    comp_out[:, to] = comp_land[...].astype(F32)
    made_pair.wait_recv()
    made_out[:, to] = made_land[...]
    made_out[:, pl.ds(pl.multiple_of(x * LANES, LANES), LANES)] = made_own[...]
    for f in range(2):
        up_pairs[f].wait_recv()
        up_out[1 - x, f] = up_land[f].astype(F32)
    mixed_pair.wait_recv()
    for copy in [mixed_pair, comp_pair, made_pair, *up_pairs]:
        copy.wait_send()
    for copy in [*staged, store_branch, store_own, store_dout, store_residual, *store_rest]:
        copy.wait()
    for c in range(7):
        scatter.close(c, last=c < 5)
    for m in range(3):
        gather.close(m)


def comp_block(m, x, rows, stage, out, send, pair):
    def done(total):
        stage[m * rows : (m + 1) * rows, :] = total
        if m == 2:
            half = send.shape[0]
            upper, lower = stage[0:half, :], stage[half:, :]
            to = pl.ds(pl.multiple_of(x * LANES, LANES), LANES)
            out[:, to] = jnp.where(x == 0, upper, lower)
            send[...] = jnp.where(x == 0, lower, upper).astype(BF16)
            pair.start()

    return done


def up_block(f, x, out, send, pair):
    def done(total):
        half = send.shape[1]
        upper, lower = total[0:half], total[half:]
        out[x, f] = jnp.where(x == 0, upper, lower)
        send[f] = jnp.where(x == 0, lower, upper).astype(BF16)
        pair.start()

    return done


def feed_forward(
    n, att, segment, seg_other, cotangent, cot_other, out_w, up, down, params, comp, comp_shard, windows
):
    _, seg_len, width = att.shape
    rows = width // n
    half_rows = rows // 2
    nhi = n // 4
    comp_rows = comp.shape[3] // 2
    made_rows = windows.shape[0] // 6
    total = 2 * seg_len
    any_spec = pl.BlockSpec(memory_space=pl.ANY)
    vmem = pl.BlockSpec(memory_space=pltpu.VMEM)
    dma = pltpu.SemaphoreType.DMA
    f32 = lambda *shape: jax.ShapeDtypeStruct(shape, F32)
    bf = lambda *shape: jax.ShapeDtypeStruct(shape, BF16)
    return pl.pallas_call(
        functools.partial(feed_kernel, n),
        out_shape=(
            f32(seg_len, width),
            bf(seg_len, width),
            f32(seg_len, width),
            bf(2, seg_len, LANES),
            bf(width, width),
            bf(4 * LANES, width),
            bf(2, nhi, rows, LANES),
            f32(SMALL, LANES),
            f32(comp_rows, width),
            f32(2, 2, half_rows, LANES),
            bf(made_rows, width),
            bf(nhi, 2, 2, *comp_shard.shape),
        ),
        in_specs=[any_spec] * 8 + [vmem, any_spec, vmem, any_spec],
        out_specs=(any_spec,) * 7 + (vmem,) * 4 + (any_spec,),
        scratch_shapes=[
            pltpu.VMEM((2, seg_len, width), BF16),
            pltpu.VMEM((2, seg_len, width), BF16),
            pltpu.VMEM((2, seg_len, width), BF16),
            pltpu.VMEM((width, width), BF16),
            pltpu.VMEM((4 * width, LANES), BF16),
            pltpu.VMEM((4 * LANES, width), BF16),
            pltpu.VMEM((seg_len, width), F32),
            pltpu.VMEM((total, width), BF16),
            pltpu.VMEM((width, total), BF16),
            pltpu.VMEM((4, total, LANES), BF16),
            pltpu.VMEM((4, total, LANES), BF16),
            pltpu.VMEM((seg_len, width), F32),
            pltpu.VMEM((seg_len, width), F32),
            pltpu.VMEM((seg_len, width), BF16),
            pltpu.VMEM((2, seg_len, width), BF16),
            pltpu.VMEM((4, nhi, 2, 2, rows, LANES), BF16),
            pltpu.VMEM((2, seg_len, LANES), BF16),
            pltpu.VMEM((2, 256, width), BF16),
            pltpu.VMEM((2, half_rows, LANES), BF16),
            pltpu.VMEM((2, half_rows, LANES), BF16),
            pltpu.VMEM((3 * rows, LANES), F32),
            pltpu.VMEM((comp_rows, LANES), BF16),
            pltpu.VMEM((comp_rows, LANES), BF16),
            pltpu.VMEM((made_rows, LANES), BF16),
            pltpu.VMEM((made_rows, LANES), BF16),
            pltpu.VMEM((made_rows, LANES), BF16),
            dma((2 * n + 1,)),
            dma((9,)),
            dma((6,)),
            dma((2,)),
            dma((6,)),
            dma((6,)),
        ]
        + Scatter.scratch(7, nhi, rows)
        + Gather.semaphores(3, nhi),
        compiler_params=pltpu.CompilerParams(
            vmem_limit_bytes=VMEM_LIMIT, collective_id=2, has_side_effects=True
        ),
        name="feed_forward",
    )(att, segment, seg_other, cotangent, cot_other, out_w, up, down, params, comp, comp_shard, windows)


def norm_back(xhat, rstd, grad):
    a = jnp.mean(grad, axis=-1, keepdims=True)
    b = jnp.mean(grad * xhat, axis=-1, keepdims=True)
    return rstd * (grad - a - xhat * b)


def backward_kernel(
    n,
    past,
    seg_len,
    dout,
    kv,
    q,
    wide,
    near,
    place_keys,
    xhat_hbm,
    query_w,
    key_w,
    value_w,
    table_hbm,
    params,
    segment,
    seg_other,
    residual_hbm,
    small_in,
    own_sum,
    branch,
    up,
    down,
    out,
    result_out,
    segment_out,
    query_out,
    key_out,
    value_out,
    place_out,
    out_out,
    down_out,
    up_out,
    small_out,
    xhat_t,
    table_t,
    residual_grad,
    load_sem,
    up_send,
    up_land,
    flat,
    raw,
    sums,
    place_sum,
    input_grad,
    dkv,
    columns,
    gain_sum,
    shift_sum,
    head_grads,
    context_land,
    context_send,
    branch_land,
    own_rows_sum,
    own_sem,
    seg_rows,
    seg_sem,
    out_keep,
    out_send,
    out_land,
    small_mine,
    small_c,
    small_y,
    small_z,
    small_x,
    pair_send,
    pair_recv,
    small_send,
    small_recv,
    land_c,
    land_y,
    land_z,
    mine,
    mine_sem,
    *sems,
):
    step = pl.program_id(0)
    x = lax.axis_index("head")
    core, low, high, nhi = place(n)
    head = lax.rem(step, 4)
    tile = 256
    context = past + seg_len
    width = flat.shape[0]
    rows = width // n
    half_rows = rows // 2
    scale = 1.0 / math.sqrt(128)
    flip = (
        lax.broadcasted_iota(jnp.int32, (HALF, HALF), 0)
        + lax.broadcasted_iota(jnp.int32, (HALF, HALF), 1)
        == HALF - 1
    ).astype(BF16)

    def pair(src, dst, k):
        return pltpu.make_async_remote_copy(
            src_ref=src,
            dst_ref=dst,
            send_sem=pair_send.at[k],
            recv_sem=pair_recv.at[k],
            device_id={"head": 1 - x},
            device_id_type=MESH,
        )

    context_pair = pair(context_send, context_land, 0)
    branch_pair = pair(branch, branch_land, 1)
    out_pairs = [pair(out_send.at[b], out_land.at[b], 2 + b) for b in range(2)]
    load_own = pltpu.make_async_copy(own_sum, own_rows_sum, own_sem)
    up_pairs = [pair(up_send.at[f], up_land.at[f], 4 + f) for f in range(2)]
    load_xhat = [
        pltpu.make_async_copy(xhat_hbm.at[1 - i], xhat_t, load_sem.at[0]) for i in range(2)
    ]
    load_up = [
        pltpu.make_async_copy(up.at[f], land_y.at[f], load_sem.at[3 + f]) for f in range(2)
    ]
    load_table = pltpu.make_async_copy(table_hbm, table_t, load_sem.at[1])
    load_residual = pltpu.make_async_copy(residual_hbm, residual_grad, load_sem.at[2])
    load_other = pltpu.make_async_copy(seg_other, seg_rows, seg_sem)
    load_segment = pltpu.make_async_copy(segment.at[0], seg_rows, seg_sem)

    def down_done(a, b):
        def done(total):
            down_out[a * rows : (a + 1) * rows, b * LANES : (b + 1) * LANES] = total

        return done

    def out_done(b):
        def done(total):
            upper, lower = total[0:half_rows], total[half_rows:]
            out_keep[b] = jnp.where(x == 0, upper, lower)
            out_send[b] = jnp.where(x == 0, lower, upper).astype(BF16)
            out_pairs[b].start()

        return done

    def head_done(h):
        def done(total):
            for j, ref in enumerate((query_out, key_out, value_out, place_out)):
                ref[:, h * 128 : (h + 1) * 128] = total[:, j * 128 : (j + 1) * 128]

        return done

    parts = [(None, False, up_block(f, x, up_out, up_send, up_pairs[f])) for f in range(2)]
    for a in range(2):
        for b in range(2):
            at, to = pl.ds(a * rows, rows), pl.ds(b * LANES, LANES)
            parts.append((down.at[:, :, :, at, to], False, down_done(a, b)))
    parts += [
        (out.at[:, :, :, :, pl.ds(b * LANES, LANES)], False, out_done(b)) for b in range(2)
    ]
    parts += [(head_grads.at[h], True, head_done(h)) for h in range(4)]
    scatter = Scatter(
        n,
        [
            (part, here, land_c.at[c], land_y.at[c], land_z.at[c], done)
            for c, (part, here, done) in enumerate(parts)
        ],
        mine,
        mine_sem,
        sems,
    )
    count = len(parts)

    @pl.when(step == 0)
    def _():
        barrier = pltpu.get_barrier_semaphore()
        pl.semaphore_signal(barrier, inc=1, device_id={"head": 1 - x}, device_id_type=MESH)
        meet(core, low, high, nhi, 1)
        for copy in load_up:
            copy.start()
        load_xhat[0].start()
        load_other.start()
        load_own.start()
        load_table.start()
        load_residual.start()
        branch_pair.start()
        for j in range(2):
            line = jnp.concatenate([params[2 * j : 2 * j + 1, :], params[2 * j + 1 : 2 * j + 2, :]], axis=1)
            columns[j] = jnp.broadcast_to(line, (128, width)).T
        raw[...] = jnp.zeros_like(raw)
        sums[...] = jnp.zeros_like(sums)
        place_sum[...] = jnp.zeros_like(place_sum)
        gain_sum[...] = jnp.zeros_like(gain_sum)
        shift_sum[...] = jnp.zeros_like(shift_sum)
        small_mine[...] = small_in[...]

    @pl.when(head == 0)
    def _():
        input_grad[...] = jnp.zeros_like(input_grad)

    start, add_core, add_y, add_z = scatter.start, scatter.add_core, scatter.add_y, scatter.add_z
    before = {
        0: ((start, 2), (start, 3), (scatter.start_z, 0), (scatter.start_z, 1), (add_core, 2), (start, 4)),
        1: ((add_core, 3), (start, 5), (add_y, 2)),
        2: ((add_core, 5), (start, 7), (add_y, 3), (add_z, 1)),
        3: ((add_core, 7),),
        4: ((add_y, 6),),
        5: ((start, 8), (add_y, 7), (add_z, 5)),
        6: ((start, 9), (add_z, 6)),
        7: ((start, 10),),
    }
    within = {
        1: ((add_core, 4), (start, 6), (add_z, 0)),
        2: ((add_core, 6), (add_y, 4), (add_z, 2)),
        3: ((add_y, 5), (add_z, 3)),
        4: ((add_z, 4),),
        5: ((add_core, 8),),
        6: ((add_core, 9), (add_y, 8), (add_z, 7)),
        7: ((add_core, 10), (add_y, 9), (add_z, 8)),
    }

    def run(table):
        for k, steps in table.items():

            @pl.when(step == k)
            def _(steps=steps):
                for do, c in steps:
                    do(c)

    @pl.when(step == 0)
    def _():
        for copy in load_up:
            copy.wait()

    run(before)

    for j, mat in enumerate((query_w, key_w, value_w)):
        flat[:, j * 128 : (j + 1) * 128] = mat[...]

    query_grads = []
    key_rows = []
    value_rows = []
    place_rows = []
    bias_at = pl.ds(pl.multiple_of(head * 128, 128), 128)
    for part, weights_ref, key_start, key_count, place_start in (
        (0, wide, 0, past + HALF, 0),
        (1, near, past, seg_len, past - HALF),
    ):
        at = slice(part * HALF, (part + 1) * HALF)
        keys_at = slice(key_start, key_start + key_count)
        attn = weights_ref[0, 0]
        grad = dot(flip, dout[0, at]).astype(BF16)
        value_rows.append(dot_tn(grad, attn))
        weights_grad = dot_nt(grad, kv[0, 0, keys_at, 128:256])
        attn = attn.astype(F32)
        row = jnp.sum(weights_grad * attn, axis=1, keepdims=True)
        scores_f = attn * (weights_grad - row) * scale
        scores_grad = scores_f.astype(BF16)
        content_grad = dot(scores_grad, kv[0, 0, keys_at, 0:128]).astype(BF16)
        key_rows.append(dot_tn(q[0, 0, at, 0:128], scores_grad))
        by_place = pltpu.roll(scores_f, 0, 1, stride=1, stride_axis=0).astype(BF16)
        place_grad = dot(by_place, place_keys[0, place_start : place_start + key_count])
        place_grad = place_grad.astype(BF16)
        place_rows.append(dot_tn(q[0, 0, at, 128:256], by_place))
        content_f = content_grad.astype(F32)
        place_f = place_grad.astype(F32)
        small_mine[8:9, bias_at] += jnp.sum(content_f, axis=0, keepdims=True)
        small_mine[9:10, bias_at] += jnp.sum(place_f, axis=0, keepdims=True)
        query_grads.append(dot(flip, (content_f + place_f).astype(BF16)).astype(BF16))

    for j, (wide_rows, near_rows) in enumerate((key_rows, value_rows)):
        at = slice(j * 128, (j + 1) * 128)
        dkv[at, 0:past] = wide_rows[:, 0:past].astype(BF16)
        dkv[at, past : past + HALF] = (wide_rows[:, past:] + near_rows[:, 0:HALF]).astype(BF16)
        dkv[at, past + HALF :] = near_rows[:, HALF:].astype(BF16)
    split = past - HALF
    for at, rows_grad in (
        (slice(0, split), place_rows[0][:, 0:split]),
        (slice(split, None), place_rows[0][:, split:] + place_rows[1]),
    ):
        place_sum[head, :, at] = (
            place_sum[head, :, at].astype(F32) + rows_grad.astype(BF16).astype(F32)
        ).astype(BF16)
    dq = jnp.concatenate(query_grads, axis=0)
    stacked = jnp.concatenate([dq, dkv[:, past:].astype(F32).T.astype(BF16)], axis=1)

    run(within)

    @pl.when(step == 0)
    def _():
        load_xhat[0].wait()

    @pl.when(step == 4)
    def _():
        load_xhat[1].wait()
        load_table.wait()

    ones = jnp.ones((8, context), BF16)
    sums[head, :, 0:128] += dot(ones[:, 0:seg_len], dq)
    sums[head, :, 128:384] += dot_nt(ones, dkv[...])
    for k in range(width // tile):
        at = slice(k * tile, (k + 1) * tile)
        raw[head, at, 0:128] += dot(xhat_t[at, past:], dq)
        raw[head, at, 128:384] += dot_nt(xhat_t[at, :], dkv[...])
        input_grad[:, at] += dot_nt(stacked, flat[at, 0:384])

    @pl.when(step >= 4)
    def _():
        place_low = place_sum[head]
        block = tile // (4 * rows)
        total = sums[head, 0:1, :]
        for k in range(width // tile):
            at = slice(k * tile, (k + 1) * tile)
            to = slice(k * block, (k + 1) * block)
            got = raw[head, at, :]
            mats = flat[at, 0:384].astype(F32)
            for acc, term in ((gain_sum, mats * got), (shift_sum, mats * total)):
                acc[at, :] += term[:, 0:128] + term[:, 128:256] + term[:, 256:384]
            grad = (columns[0, at, 0:1] * got + columns[1, at, 0:1] * total).astype(BF16)
            head_grads[head, to, :, :, :, 0:384] = grad.reshape(block, 2, 2, rows, 384)
            grad = dot_nt(table_t[at, :], place_low).astype(BF16)
            head_grads[head, to, :, :, :, 384:512] = grad.reshape(block, 2, 2, rows, 128)

    def own_rows(k):
        gain = jnp.concatenate([params[0:1, :], params[1:2, :]], axis=1)
        at = slice(k * tile, (k + 1) * tile)
        values = seg_rows[at, :].astype(F32)
        mean = jnp.mean(values, axis=-1, keepdims=True)
        centred = values - mean
        rstd = lax.rsqrt(jnp.mean(centred * centred, axis=-1, keepdims=True) + 1e-05)
        return norm_back(centred * rstd, rstd, input_grad[at, :] * gain)

    @pl.when(step == 4)
    def _():
        load_segment.start()

    @pl.when(step == 3)
    def _():
        load_xhat[1].start()
        load_other.wait()
        for k in range(seg_len // tile):
            context_send[k * tile : (k + 1) * tile, :] = own_rows(k).astype(BF16)
        context_pair.start()

    @pl.when(step == 5)
    def _():
        branch_pair.wait_recv()
        load_own.wait()
        for k in range(seg_len // tile):
            at = slice(k * tile, (k + 1) * tile)
            result_out[0, at] = (own_rows_sum[at, :] + branch_land[at, :].astype(F32)).astype(BF16)

    @pl.when(step == 7)
    def _():
        start(11)
        one = jnp.ones((8, 128), F32)
        for acc, row in ((gain_sum, 0), (shift_sum, 2)):
            line = lax.dot_general(
                one,
                acc[...],
                (((1,), (1,)), ((), ())),
                precision=lax.Precision.HIGHEST,
                preferred_element_type=F32,
            )
            small_mine[row : row + 1, :] = line[0:1, 0:LANES]
            small_mine[row + 1 : row + 2, :] = line[0:1, LANES:]

        def to_dp(src, dst, k, index):
            return remote(src, dst, small_send.at[k], small_recv.at[k], index)

        copies = [to_dp(small_mine, small_c.at[1], 0, high * 4 + low * 2 + (1 - core))]
        copies[0].start()
        add_core(11)
        load_segment.wait()
        load_residual.wait()
        context_pair.wait_recv()
        for k in range(seg_len // tile):
            at = slice(k * tile, (k + 1) * tile)
            segment_out[0, at] = (
                residual_grad[at, :] + own_rows(k) + context_land[at, :].astype(F32)
            ).astype(BF16)
        add_y(10)
        copies[0].wait_recv()
        small_c[0] = small_mine[...] + small_c[1]
        copies.append(to_dp(small_c.at[0], small_y.at[1], 1, high * 4 + (1 - low) * 2 + core))
        copies[1].start()
        copies[1].wait_recv()
        small_y[0] = small_c[0] + small_y[1]
        along = []
        for k in range(1, nhi):
            to = lax.rem(high + k, nhi) * 4 + low * 2 + core
            along.append(to_dp(small_y.at[0], small_z.at[k], 2 + k, to))
        for copy in along:
            copy.start()
        add_z(9)
        add_y(11)
        for copy in along:
            copy.wait_recv()
        line = small_y[0]
        for k in range(1, nhi):
            line = line + small_z[k]
        small_z[0] = line
        last = pltpu.make_async_remote_copy(
            src_ref=small_z.at[0],
            dst_ref=small_x,
            send_sem=small_send.at[2],
            recv_sem=small_recv.at[2],
            device_id={"head": 1 - x},
            device_id_type=MESH,
        )
        last.start()
        add_z(10)
        add_z(11)
        for f in range(2):
            up_pairs[f].wait_recv()
            up_out[1 - x, f] = up_land[f].astype(F32)
        for b in range(2):
            out_pairs[b].wait_recv()
            out_out[:, b * LANES : (b + 1) * LANES] = out_keep[b] + out_land[b].astype(F32)
        last.wait_recv()
        line = lax.broadcasted_iota(jnp.int32, (SMALL, LANES), 0)
        small_out[...] = small_z[0] + jnp.where(line < 8, small_x[...], 0.0)
        for copy in [context_pair, branch_pair, *up_pairs, *out_pairs, *copies, *along, last]:
            copy.wait_send()
        for c in range(count):
            scatter.close(c, upper=c > 1)


def attention_backward(
    n, dout, kv, q, wide, near, place_keys, xhat_t, mats, table_t, params, segment,
    seg_other, residual_grad, small_in, own_sum, branch, up, down, out,
):
    _, seg_len, width = segment.shape
    context = kv.shape[2]
    past = context - seg_len
    rows = width // n
    nhi = n // 4
    half_rows = rows // 2
    seq = lambda t: 1 - t // 4
    head = lambda t: lax.rem(t, 4)
    by_both = lambda t: (head(t), seq(t), 0, 0)
    single = pl.Buffered(1)
    any_spec = pl.BlockSpec(memory_space=pl.ANY)
    dma = pltpu.SemaphoreType.DMA
    f32 = lambda *shape: jax.ShapeDtypeStruct(shape, F32)
    lead = (nhi, 2, 2)
    full = lambda shape: pl.BlockSpec(shape, lambda t: (0,) * len(shape), pipeline_mode=single)
    outs = (
        jax.ShapeDtypeStruct((1, seg_len, width), BF16),
        jax.ShapeDtypeStruct((1, seg_len, width), BF16),
        f32(rows, LANES),
        f32(rows, LANES),
        f32(rows, LANES),
        f32(rows, LANES),
        f32(half_rows, width),
        f32(2 * rows, width),
        f32(2, 2, half_rows, LANES),
        f32(SMALL, LANES),
    )
    return pl.pallas_call(
        functools.partial(backward_kernel, n, past, seg_len),
        grid=(8,),
        out_shape=outs,
        in_specs=[
            pl.BlockSpec((1, seg_len, 128), lambda t: (seq(t), 0, head(t))),
            pl.BlockSpec((1, 1, context, 256), by_both),
            pl.BlockSpec((1, 1, seg_len, 256), by_both),
            pl.BlockSpec((1, 1, HALF, past + HALF), by_both),
            pl.BlockSpec((1, 1, HALF, seg_len), by_both),
            pl.BlockSpec((1, past + HALF, 128), lambda t: (head(t), 0, 0)),
            any_spec,
            *[pl.BlockSpec((width, 128), lambda t: (0, head(t)))] * 3,
            any_spec,
            full((SMALL, LANES)),
            any_spec,
            any_spec,
            any_spec,
            full((SMALL, LANES)),
            any_spec,
            any_spec,
            any_spec,
            any_spec,
            any_spec,
        ],
        out_specs=tuple(full(o.shape) for o in outs),
        scratch_shapes=[
            pltpu.VMEM((width, context), BF16),
            pltpu.VMEM(table_t.shape, BF16),
            pltpu.VMEM((seg_len, width), F32),
            dma((5,)),
            pltpu.VMEM((2, half_rows, LANES), BF16),
            pltpu.VMEM((2, half_rows, LANES), BF16),
            pltpu.VMEM((width, 384), BF16),
            pltpu.VMEM((4, width, 384), F32),
            pltpu.VMEM((4, 8, 384), F32),
            pltpu.VMEM((4, 128, past + HALF), BF16),
            pltpu.VMEM((seg_len, width), F32),
            pltpu.VMEM((256, context), BF16),
            pltpu.VMEM((2, width, 128), F32),
            pltpu.VMEM((width, 128), F32),
            pltpu.VMEM((width, 128), F32),
            pltpu.VMEM((4,) + lead + (rows, LANES), BF16),
            pltpu.VMEM((seg_len, width), BF16),
            pltpu.VMEM((seg_len, width), BF16),
            pltpu.VMEM((seg_len, width), BF16),
            pltpu.VMEM((seg_len, width), F32),
            dma(()),
            pltpu.VMEM((seg_len, width), BF16),
            dma(()),
            pltpu.VMEM((2, half_rows, LANES), F32),
            pltpu.VMEM((2, half_rows, LANES), BF16),
            pltpu.VMEM((2, half_rows, LANES), BF16),
            pltpu.VMEM((SMALL, LANES), F32),
            pltpu.VMEM((2, SMALL, LANES), F32),
            pltpu.VMEM((2, SMALL, LANES), F32),
            pltpu.VMEM((nhi, SMALL, LANES), F32),
            pltpu.VMEM((SMALL, LANES), F32),
            dma((6,)),
            dma((6,)),
            dma((2 + nhi,)),
            dma((2 + nhi,)),
        ]
        + Scatter.scratch(12, nhi, rows),
        compiler_params=pltpu.CompilerParams(
            vmem_limit_bytes=VMEM_LIMIT,
            dimension_semantics=("arbitrary",),
            collective_id=1,
            has_side_effects=True,
        ),
        name="attention_backward",
    )(
        dout, kv, q, wide, near, place_keys, xhat_t, *mats, table_t,
        params, segment, seg_other,
        residual_grad, small_in, own_sum, branch, up, down, out,
    )


def finish_kernel(n, *refs):
    count = (len(refs) - 1) // 2
    ups, refs = refs[:2], refs[1:]
    up_out = refs[count]
    size = LANES // (n // 4)
    for f in range(4):
        for j in range(n // 4):
            for half in range(2):
                to = ((f * (n // 4) + j) * 2 + half) * size
                up_out[:, to : to + size] = ups[f // 2][
                    half, f % 2, :, j * size : (j + 1) * size
                ]
    for src, dst in zip(refs[1:count], refs[count + 1 :]):
        dst[...] = src[...]


def finish(n, ups, others):
    vmem = pl.BlockSpec(memory_space=pltpu.VMEM)
    same = [jax.ShapeDtypeStruct(a.shape, a.dtype) for a in others]
    out = jax.ShapeDtypeStruct((ups[0].shape[2], 8 * LANES), F32)
    return pl.pallas_call(
        functools.partial(finish_kernel, n),
        out_shape=(out, *same),
        in_specs=[vmem] * (2 + len(others)),
        out_specs=(vmem,) * (1 + len(others)),
        compiler_params=pltpu.CompilerParams(vmem_limit_bytes=VMEM_LIMIT),
        name="finish",
    )(*ups, *others)


def body(
    n,
    segment,
    memory,
    compressed,
    doc_lengths,
    memory_valid,
    query_weight,
    key_weight,
    value_weight,
    position_weight,
    content_bias,
    position_bias,
    output_weight,
    up_weight,
    down_weight,
    compress_weight,
    norm_gain,
    norm_shift,
    post_gain,
    post_shift,
    cotangent,
    compress_cotangent,
):
    x = lax.axis_index("head")
    dp = lax.axis_index("dp")
    first = x == 0
    nhi = n // 4
    width = segment.shape[2]
    seg_len = segment.shape[1]
    past = memory.shape[1] + compressed.shape[1]
    context = past + seg_len
    rows = query_weight.shape[0]
    half_rows = output_weight.shape[0]
    new_count = compress_cotangent.shape[1]
    comp_rows = compress_weight.shape[0]

    per = content_bias.shape[1]
    vectors = jnp.stack([norm_gain, norm_shift, post_gain, post_shift])
    here = jnp.arange(2 * n, dtype=jnp.int32)[None, :, None] == dp * 2 + x
    norms = jnp.where(here, vectors[:, None, :], 0).reshape(8, LANES)
    here = jnp.arange(n, dtype=jnp.int32)[None, None, :, None] == dp
    bias = jnp.stack([content_bias, position_bias])[:, :, None, :]
    bias = jnp.where(here, bias, 0).reshape(2, LANES)
    small = jnp.concatenate([norms, bias, jnp.zeros((SMALL - 10, LANES), BF16)])
    pad_rows = -(-new_count // 16) * 16
    comp_cot = jnp.pad(compress_cotangent[0], ((0, pad_rows - new_count), (0, 0)))
    table = position_rows(context, width, past + HALF)

    (
        att, seg_other, cot_other, xhat_t, windows, comp_grads, comp_shard, params, kv, q, wide, near,
        place_keys, query_whole, key_whole, value_whole, _, out_whole, up_whole, down_whole, _,
    ) = attention_forward(
        n, doc_lengths, memory_valid, compressed, memory, segment, cotangent, comp_cot,
        (query_weight, key_weight, value_weight, position_weight),
        output_weight, up_weight, down_weight, compress_weight, small, jnp.asarray(table),
    )

    lead = (nhi, 2, 2)
    (
        own_sum, branch, residual_grad, dout, out_grads, down_grads, up_rest, small_in, comp_done,
        up_first, made, _,
    ) = feed_forward(
        n, att, segment, seg_other, cotangent, cot_other, out_whole.reshape(width, width),
        up_whole.reshape(4 * width, LANES), down_whole.reshape(4 * LANES, width), params,
        comp_grads.reshape(lead + (3 * rows, LANES)), comp_shard, windows.reshape(-1, width),
    )

    mats = [w.reshape(width, LANES) for w in (query_whole, key_whole, value_whole)]
    result, segment_grad, *matrices, up_last, small_done = attention_backward(
        n, dout, kv, q, wide, near, place_keys, xhat_t, mats, jnp.asarray(table.T.copy()),
        params, segment, seg_other, residual_grad, small_in, own_sum, branch,
        up_rest,
        down_grads.reshape(lead + (2 * rows, 2 * LANES)),
        out_grads.reshape(lead + (rows, 2 * LANES)),
    )

    up_final, result, segment_grad, *matrices, comp_final = finish(
        n, (up_first, up_last), (result, segment_grad, *matrices, comp_done)
    )
    query_final, key_final, value_final, place_final, out_final, down_final = matrices
    vectors = lax.dynamic_slice_in_dim(
        small_done[0:8].reshape(4, width), (dp * 2 + x) * half_rows, half_rows, 1
    )
    biases = lax.dynamic_slice_in_dim(small_done[8:10].reshape(2, 4, 128), dp * per, per, 2)
    return (
        result,
        made[None, :new_count],
        segment_grad,
        query_final,
        key_final,
        value_final,
        place_final,
        biases[0],
        biases[1],
        out_final,
        up_final,
        down_final,
        comp_final,
        vectors[0],
        vectors[1],
        vectors[2],
        vectors[3],
    )


def solution(mesh):
    split = P(("dp", "head"))
    wide = P(("dp", "head"), None)
    deep = P(("dp", "head"), None, None)
    return jax.shard_map(
        functools.partial(body, mesh.shape["dp"]),
        mesh=mesh,
        in_specs=(
            deep,
            P("dp", None, None),
            P("dp", None, None),
            P("dp", None),
            P("dp"),
            P("dp", "head"),
            P("dp", "head"),
            P("dp", "head"),
            P("dp", "head"),
            P("head", "dp"),
            P("head", "dp"),
            wide,
            wide,
            wide,
            wide,
            split,
            split,
            split,
            split,
            deep,
            deep,
        ),
        out_specs=(
            deep,
            deep,
            deep,
            P("dp", "head"),
            P("dp", "head"),
            P("dp", "head"),
            P("dp", "head"),
            P("head", "dp"),
            P("head", "dp"),
            wide,
            wide,
            wide,
            wide,
            split,
            split,
            split,
            split,
        ),
        check_vma=False,
    )
```
